32 devices in a mesh: seq: 8 (over z, x), fsdp: 4 (over y, core).
Axes of the slice: x: 2, y: 2, z: 4, core: 2. Of those that a mesh axis runs over, the one named last changes fastest.
Arguments:
- tokens: bfloat16 [2, 2048, 2048], P(None, 'seq'), may hold values from -6 to 6
- resets: int32 [2, 2048], P(None, 'seq'), may hold values 0 or 1
- norm_gain: bfloat16 [2048], replicated, may hold values from 0.5 to 1.5
- branch_weight: bfloat16 [2048, 2816], P('seq', 'fsdp'), may hold values from -0.125 to 0.125
- inner_weight: bfloat16 [2048, 2816], P('seq', 'fsdp'), may hold values from -0.125 to 0.125
- conv_weight: bfloat16 [4, 2816], P(None, 'fsdp'), may hold values from -3 to 3
- conv_bias: bfloat16 [2816], P('fsdp'), may hold values from -3 to 3
- gate_blocks: bfloat16 [16, 176, 176], P('fsdp'), may hold values from -0.4375 to 0.4375
- input_blocks: bfloat16 [16, 176, 176], P('fsdp'), may hold values from -0.4375 to 0.4375
- gate_bias: bfloat16 [2816], P('fsdp'), may hold values from -3 to 3
- input_bias: bfloat16 [2816], P('fsdp'), may hold values from -3 to 3
- decay_param: bfloat16 [2816], P('fsdp'), may hold values from 4 to 12
- out_weight: bfloat16 [2816, 2048], P('fsdp', 'seq'), may hold values from -0.109375 to 0.109375
- mlp_norm_gain: bfloat16 [2048], replicated, may hold values from 0.5 to 1.5
- gate_weight: bfloat16 [2048, 6144], P('seq', 'fsdp'), may hold values from -0.125 to 0.125
- up_weight: bfloat16 [2048, 6144], P('seq', 'fsdp'), may hold values from -0.125 to 0.125
- down_weight: bfloat16 [6144, 2048], P('fsdp', 'seq'), may hold values from -0.078125 to 0.078125
- cotangent: bfloat16 [2, 2048, 2048], P(None, 'seq'), may hold values from -6 to 6
Outputs:
- mixed: float32 [2, 2048, 2048], P(None, 'seq')
- tokens_grad: float32 [2, 2048, 2048], P(None, 'seq')
- norm_gain_grad: float32 [2048], replicated
- branch_weight_grad: float32 [2048, 2816], P('seq', 'fsdp')
- inner_weight_grad: float32 [2048, 2816], P('seq', 'fsdp')
- conv_weight_grad: float32 [4, 2816], P(None, 'fsdp')
- conv_bias_grad: float32 [2816], P('fsdp')
- gate_blocks_grad: float32 [16, 176, 176], P('fsdp')
- input_blocks_grad: float32 [16, 176, 176], P('fsdp')
- gate_bias_grad: float32 [2816], P('fsdp')
- input_bias_grad: float32 [2816], P('fsdp')
- decay_param_grad: float32 [2816], P('fsdp')
- out_weight_grad: float32 [2816, 2048], P('fsdp', 'seq')
- mlp_norm_gain_grad: float32 [2048], replicated
- gate_weight_grad: float32 [2048, 6144], P('seq', 'fsdp')
- up_weight_grad: float32 [2048, 6144], P('seq', 'fsdp')
- down_weight_grad: float32 [6144, 2048], P('fsdp', 'seq')
The draws below stay inside these ranges and needn't reach their ends.
All inputs are finite; a program needn't handle non-finite values. No bound on the sum of `resets` on one device may be relied on, other than what follows from the above.
Results may differ from the reference program's by a relative error of at most 0.0083.
Values may be sent and summed in bfloat16 or wider, within the bound.
A program may use at most 320 MiB of HBM per device.

```python
import jax
import jax.numpy as jnp
from jax import lax

D = 2048
R = 2816
H = 16
FF = 6144
MB = 2
BW = 176
S = 2048


def place_ends(entries, key, least, high):
    dims = entries.shape
    index_at = [jax.random.randint(jax.random.fold_in(key, axis), (), 0, dims[axis]) for axis in range(len(dims))]
    entries = entries.at[tuple(index_at)].set(least)
    longest = dims.index(max(dims))
    index_at[longest] = (index_at[longest] + 1) % dims[longest]
    return entries.at[tuple(index_at)].set(high)


def block_levels(rng, extent, split, least, high):
    factor_of, own = 1.0, jax.random.fold_in(rng, 6)
    for dim, shards_of in split:
        heights = jnp.exp(jax.random.uniform(jax.random.fold_in(own, dim), (shards_of,), jnp.float32, least / len(split), high / len(split)))
        factor_of = factor_of * jnp.repeat(heights, extent[dim] // shards_of).reshape([-1 if axis == dim else 1 for axis in range(len(extent))])
    return factor_of


def centred(own_key, shape, scale, bound, pieces=(), held_as=jnp.bfloat16):
    level = block_levels(own_key, shape, pieces, -0.22, 0.18) if pieces else 1.0
    drawn = jax.random.normal(own_key, shape, jnp.float32) * scale * level
    return jnp.minimum(jnp.maximum(drawn, -bound), bound).astype(held_as)


def setup_inputs(seed: int = 0) -> dict:
    streams_of = jax.random.split(jax.random.key(seed), 19)
    return {
        "tokens": centred(streams_of[0], (MB, S, D), 1.0, 6.0, ((1, 8),)),
        "resets": place_ends((jax.random.randint(streams_of[1], (MB, S), 0, 2048) < 1).astype(jnp.int32), jax.random.fold_in(streams_of[1], 1), 0, 1),
        "norm_gain": jnp.clip(1.0 + 0.1 * jax.random.normal(streams_of[2], (D,), jnp.float32), 0.5, 1.5).astype(jnp.bfloat16),
        "branch_weight": centred(streams_of[3], (D, R), D ** -0.5, 0.125, ((0, 8), (1, 4))),
        "inner_weight": centred(streams_of[4], (D, R), D ** -0.5, 0.125, ((0, 8), (1, 4))),
        "conv_weight": centred(streams_of[5], (4, R), 4 ** -0.5, 3.0, ((1, 4),)),
        "conv_bias": centred(streams_of[6], (R,), 0.5, 3.0, ((0, 4),)),
        "gate_blocks": centred(streams_of[7], (H, BW, BW), BW ** -0.5, 0.4375, ((0, 4),)),
        "input_blocks": centred(streams_of[8], (H, BW, BW), BW ** -0.5, 0.4375, ((0, 4),)),
        "gate_bias": centred(streams_of[9], (R,), 0.5, 3.0, ((0, 4),)),
        "input_bias": centred(streams_of[10], (R,), 0.5, 3.0, ((0, 4),)),
        "decay_param": jnp.clip(4.0 + 8.0 * jax.random.uniform(streams_of[11], (R,), jnp.float32) ** block_levels(streams_of[11], (R,), ((0, 4),), -0.2, 0.2), 4.0, 12.0).astype(jnp.bfloat16),
        "out_weight": centred(streams_of[12], (R, D), R ** -0.5, 0.109375, ((0, 4), (1, 8))),
        "mlp_norm_gain": jnp.clip(1.0 + 0.1 * jax.random.normal(streams_of[13], (D,), jnp.float32), 0.5, 1.5).astype(jnp.bfloat16),
        "gate_weight": centred(streams_of[14], (D, FF), D ** -0.5, 0.125, ((0, 8), (1, 4))),
        "up_weight": centred(streams_of[15], (D, FF), D ** -0.5, 0.125, ((0, 8), (1, 4))),
        "down_weight": centred(streams_of[16], (FF, D), FF ** -0.5, 0.078125, ((0, 4), (1, 8))),
        "cotangent": centred(streams_of[17], (MB, S, D), 1.0, 6.0, ((1, 8),)),
    }


eps = 1e-06
decay_scale = 8.0

@jax.custom_vjp
def low(v):
    return lax.optimization_barrier(v.astype(jnp.bfloat16)).astype(jnp.float32)

@jax.custom_vjp
def low_back(v):
    return v

def low_keep(v):
    return (low(v), None)

def low_pass(kept, grad):
    return (grad,)

def back_keep(v):
    return (v, None)

def back_low(kept, grad):
    return (low(grad),)
low.defvjp(low_keep, low_pass)
low_back.defvjp(back_keep, back_low)

def combine(earlier_map, later_map):
    return (earlier_map[0] * later_map[0], later_map[0] * earlier_map[1] + later_map[1])

def rms_norm(values, gain):
    return values * lax.rsqrt(lax.optimization_barrier(jnp.mean(values * values, axis=-1, keepdims=True)) + eps) * gain

def gelu_tanh(values):
    return jax.nn.gelu(values, approximate=True)

def gate_math(gate_pre, input_pre, conv_value, decay_param, reset_flags):
    rate_gate = jax.nn.sigmoid(gate_pre)
    inlet_gate = jax.nn.sigmoid(input_pre)
    log_decay = -decay_scale * jax.nn.softplus(-decay_param) * rate_gate
    fresh_start = reset_flags[:, None] > 0
    input_scale = jnp.where(fresh_start, 1.0, jnp.sqrt(-jnp.expm1(2.0 * log_decay)))
    carries = jnp.where(fresh_start, 0.0, jnp.exp(log_decay))
    return (carries, input_scale * inlet_gate * conv_value)

def matmul(left_side, right_side):
    return jnp.dot(left_side, right_side, precision=lax.Precision.HIGHEST)

def blockwise(values, blocks):
    shaped = values.reshape(values.shape[0], blocks.shape[0], blocks.shape[1])
    return jnp.einsum('shi,hij->shj', shaped, blocks, precision=lax.Precision.HIGHEST).reshape(values.shape[0], -1)

def residual_layer(values, reset_flags, weights):
    norm_gain, branch_weight, inner_weight, conv_weight, conv_bias, gate_blocks, input_blocks, gate_bias, input_bias, decay_param, out_weight, mlp_norm_gain, gate_weight, up_weight, down_weight = weights
    length = values.shape[0]
    normed = low(rms_norm(values, norm_gain))
    branch = gelu_tanh(low_back(matmul(normed, branch_weight)))
    inner_low = low(low_back(matmul(normed, inner_weight)))
    padded = jnp.concatenate([jnp.zeros((3, inner_low.shape[1]), jnp.float32), inner_low], 0)
    conv_sum = conv_bias + conv_weight[0] * padded[3:3 + length] + conv_weight[1] * padded[2:2 + length]
    conv_sum = conv_sum + conv_weight[2] * padded[1:1 + length] + conv_weight[3] * padded[0:length]
    conv_value = low(conv_sum)
    gate_pre = low_back(blockwise(conv_value, gate_blocks) + gate_bias)
    input_pre = low_back(blockwise(conv_value, input_blocks) + input_bias)
    carries, drives = gate_math(gate_pre, input_pre, conv_value, decay_param, reset_flags)
    _, states = lax.associative_scan(combine, (carries, drives), axis=0)
    mixed_low = low(states * branch)
    middle = values + low_back(matmul(mixed_low, out_weight))
    normed_two = low(rms_norm(middle, mlp_norm_gain))
    gate_mlp = low_back(matmul(normed_two, gate_weight))
    up_mlp = low_back(matmul(normed_two, up_weight))
    hidden_low = low(gelu_tanh(gate_mlp) * up_mlp)
    return middle + low_back(matmul(hidden_low, down_weight))

def reference(tokens, resets, norm_gain, branch_weight, inner_weight, conv_weight, conv_bias, gate_blocks, input_blocks, gate_bias, input_bias, decay_param, out_weight, mlp_norm_gain, gate_weight, up_weight, down_weight, cotangent):
    weights = tuple((member.astype(jnp.float32) for member in (norm_gain, branch_weight, inner_weight, conv_weight, conv_bias, gate_blocks, input_blocks, gate_bias, input_bias, decay_param, out_weight, mlp_norm_gain, gate_weight, up_weight, down_weight)))

    def one_sequence(totals, batch_item):
        sequence_rows, reset_flags, cot_rows = batch_item

        def forward(values, params):
            return residual_layer(values, reset_flags, params)
        result, pullback = jax.vjp(forward, sequence_rows.astype(jnp.float32), weights)
        input_grads, weight_grads = pullback(cot_rows.astype(jnp.float32))
        return (jax.tree.map(jnp.add, totals, weight_grads), (result, input_grads))
    empty_grads = jax.tree.map(jnp.zeros_like, weights)
    totals, (results, input_grads) = lax.scan(one_sequence, empty_grads, (tokens, resets, cotangent))
    return (results, input_grads, totals[0], totals[1], totals[2], totals[3], totals[4], totals[5], totals[6], totals[7], totals[8], totals[9], totals[10], totals[11], totals[12], totals[13], totals[14])
```

```python
import functools

import jax
import jax.numpy as jnp
from jax import lax
from jax.experimental import pallas as pl
from jax.experimental.pallas import tpu as pltpu
from jax.sharding import PartitionSpec as P

eps = 1e-06
decay_scale = 8.0
f32 = jnp.float32
bf16 = jnp.bfloat16
ring_limit = 16


def gelu_tanh(values):
    return jax.nn.gelu(values, approximate=True)


def gated_product(gate_pre, up_pre):
    return gelu_tanh(gate_pre) * up_pre


def gate_math(gate_pre, input_pre, conv_value, decay_param, fresh_start):
    rate_gate = jax.nn.sigmoid(gate_pre)
    inlet_gate = jax.nn.sigmoid(input_pre)
    log_decay = -decay_scale * jax.nn.softplus(-decay_param) * rate_gate
    input_scale = jnp.where(fresh_start, 1.0, jnp.sqrt(-jnp.expm1(2.0 * log_decay)))
    carries = jnp.where(fresh_start, 0.0, jnp.exp(log_decay))
    return (carries, input_scale * inlet_gate * conv_value)


def dot_nn(left, right):
    return jnp.dot(left, right, preferred_element_type=f32)


def dot_nt(left, right):
    return lax.dot_general(left, right, (((1,), (1,)), ((), ())), preferred_element_type=f32)


def dot_tn(left, right):
    return lax.dot_general(left, right, (((0,), (0,)), ((), ())), preferred_element_type=f32)


def inverse_rms(values):
    return lax.rsqrt(jnp.mean(values * values, axis=-1, keepdims=True) + eps)


def scan_body(backward, a_ref, b_ref, prod_ref, state_ref):
    batches, length, units = a_ref.shape
    tiles = length // 8
    rows = lax.broadcasted_iota(jnp.int32, (8, units), 0)

    def step(index, carry):
        tile = tiles - 1 - index if backward else index
        where_rows = pl.ds(pl.multiple_of(tile * 8, 8), 8)
        following = []
        for batch in range(batches):
            prod_in, state_in = carry[batch]
            a = a_ref[batch, where_rows, :]
            b = b_ref[batch, where_rows, :]
            for shift in (1, 2, 4):
                turn = 8 - shift if backward else shift
                inside = rows < 8 - shift if backward else rows >= shift
                a_moved = jnp.where(inside, pltpu.roll(a, turn, 0), 1.0)
                b_moved = jnp.where(inside, pltpu.roll(b, turn, 0), 0.0)
                b = a * b_moved + b
                a = a * a_moved
            b = b + a * state_in
            a = a * prod_in
            prod_ref[batch, where_rows, :] = a
            state_ref[batch, where_rows, :] = b
            edge = 0 if backward else 7
            following.append((a[edge : edge + 1], b[edge : edge + 1]))
        return tuple(following)

    first = tuple(
        (jnp.ones((1, units), f32), jnp.zeros((1, units), f32)) for _ in range(batches)
    )
    lax.fori_loop(0, tiles, step, first)


def local_scan(a, b, backward):
    shape = jax.ShapeDtypeStruct(a.shape, f32)
    elements = a.shape[0] * a.shape[1] * a.shape[2]
    return pl.pallas_call(
        functools.partial(scan_body, backward),
        out_shape=(shape, shape),
        in_specs=[pl.BlockSpec(memory_space=pltpu.VMEM)] * 2,
        out_specs=(pl.BlockSpec(memory_space=pltpu.VMEM),) * 2,
        compiler_params=pltpu.CompilerParams(vmem_limit_bytes=32 * 1024 * 1024),
        cost_estimate=pl.CostEstimate(
            flops=20 * elements, bytes_accessed=16 * elements, transcendentals=0
        ),
    )(a, b)


def move_body(table_ref, in_ref, out_ref):
    out_ref[...] = in_ref[...].astype(out_ref.dtype)


def move_slabs(values, table, dtype):
    rows, width = values.shape
    slabs = table.shape[0]
    return pl.pallas_call(
        move_body,
        out_shape=jax.ShapeDtypeStruct((rows, width), dtype),
        grid_spec=pltpu.PrefetchScalarGridSpec(
            num_scalar_prefetch=1,
            grid=(slabs,),
            in_specs=[pl.BlockSpec((rows, width // slabs), lambda k, where: (0, where[k]))],
            out_specs=pl.BlockSpec((rows, width // slabs), lambda k, where: (0, k)),
        ),
        cost_estimate=pl.CostEstimate(
            flops=0, bytes_accessed=8 * rows * width, transcendentals=0
        ),
    )(table, values)


class Ring:
    def __init__(self, count):
        self.count = count
        self.order = list(range(0, count, 2)) + list(range(count - 1, 0, -2))
        self.place = [self.order.index(i) for i in range(count)]
        self.forth = [(self.order[i], self.order[(i + 1) % count]) for i in range(count)]
        self.back = [(there, here) for here, there in self.forth]

    def tables(self):
        here = jnp.asarray(self.place, jnp.int32)[lax.axis_index("seq")]
        steps = jnp.arange(self.count, dtype=jnp.int32)
        to_ring = jnp.asarray(self.order, jnp.int32)[(here - steps) % self.count]
        to_plain = (here - jnp.asarray(self.place, jnp.int32)) % self.count
        return to_ring, to_plain

    def gather(self, forth_piece, back_piece):
        forth, back = [forth_piece], [back_piece]
        for _ in range(self.count - 1):
            forth.append(lax.ppermute(forth[-1], "seq", self.forth))
            back.append(lax.ppermute(back[-1], "seq", self.back))
        return forth, [back[-k % self.count] for k in range(self.count)]

    def scatter(self, forth_slabs, back_slabs):
        count = self.count
        forth, back = forth_slabs[1].astype(bf16), back_slabs[count - 1].astype(bf16)
        for step in range(2, count + 1):
            forth = lax.ppermute(forth, "seq", self.forth).astype(f32) + forth_slabs[step % count]
            back = lax.ppermute(back, "seq", self.back).astype(f32) + back_slabs[count - step]
            if step < count:
                forth, back = forth.astype(bf16), back.astype(bf16)
        return forth, back


def halves_summed(partial):
    count, mine = lax.axis_size("fsdp"), lax.axis_index("fsdp")
    bit = 1
    while bit < count:
        half = partial.shape[0] // 2
        upper = (mine // bit) % 2
        kept = lax.dynamic_slice_in_dim(partial, upper * half, half, 0)
        sent = lax.dynamic_slice_in_dim(partial, (1 - upper) * half, half, 0).astype(bf16)
        got = lax.ppermute(sent, "fsdp", [(i, i ^ bit) for i in range(count)])
        partial = kept + got.astype(f32)
        bit *= 2
    return partial


def own_rows(values):
    count, mine = lax.axis_size("fsdp"), lax.axis_index("fsdp")
    bit = 1
    while bit < count:
        half = values.shape[0] // 2
        values = lax.dynamic_slice_in_dim(values, ((mine // bit) % 2) * half, half, 0)
        bit *= 2
    return values


def halves_joined(own):
    count, mine = lax.axis_size("fsdp"), lax.axis_index("fsdp")
    bit = count // 2
    while bit:
        got = lax.ppermute(own, "fsdp", [(i, i ^ bit) for i in range(count)])
        upper = (mine // bit) % 2 > 0
        own = jnp.concatenate([jnp.where(upper, got, own), jnp.where(upper, own, got)], 0)
        bit //= 2
    return own


def passed_along(block, distance):
    devices = range(lax.axis_size("seq"))
    route = [(i - distance, i) for i in devices if i - distance in devices]
    return lax.ppermute(block, "seq", route)


def state_at_entry(prods, states, sign):
    pair = passed_along(jnp.stack([prods, states], 0), sign)
    distance = 1
    while distance < lax.axis_size("seq"):
        earlier = passed_along(pair, sign * distance)
        pair = jnp.stack([pair[0] * earlier[0], pair[1] + pair[0] * earlier[1]], 0)
        distance *= 2
    return pair[1]


def block_diagonal(blocks):
    count, width = blocks.shape[0], blocks.shape[1]
    return sum(
        jnp.pad(blocks[j], ((j * width, (count - 1 - j) * width),) * 2) for j in range(count)
    )


def diagonal_blocks(square, count):
    width = square.shape[0] // count
    return jnp.stack(
        [square[j * width : (j + 1) * width, j * width : (j + 1) * width] for j in range(count)], 0
    )


def local(
    tokens,
    resets,
    norm_gain,
    branch_weight,
    inner_weight,
    conv_weight,
    conv_bias,
    gate_blocks,
    input_blocks,
    gate_bias,
    input_bias,
    decay_param,
    out_weight,
    mlp_norm_gain,
    gate_weight,
    up_weight,
    down_weight,
    cotangent,
):
    count = lax.axis_size("seq")
    batches, length, width = tokens.shape
    slab = width // count
    units, hidden = conv_bias.shape[0], down_weight.shape[0]
    rows = batches * length
    ringed = count <= ring_limit
    out_turned, down_turned = out_weight.T, down_weight.T
    if ringed:
        ring = Ring(count)
        to_ring, to_plain = ring.tables()

        def moved(values, dtype):
            return move_slabs(values, to_ring, dtype)

        def restored(values, dtype):
            return move_slabs(values, to_plain, dtype)

        def gain_moved(gain):
            return gain.reshape(count, slab)[to_ring].reshape(width)

        def gain_restored(gain):
            return gain.reshape(count, slab)[to_plain].reshape(width)

        def gather(forth_piece, back_piece):
            forth, back = ring.gather(forth_piece, back_piece)
            return jnp.concatenate(forth, 0), jnp.concatenate(back, 0)

        def gather_rows(piece):
            forth, back = ring.gather(piece[: slab // 2], piece[slab // 2 :])
            return jnp.concatenate([part for pair in zip(forth, back) for part in pair], 0)

        def gather_columns(piece):
            middle = piece.shape[1] // 2
            forth, back = ring.gather(piece[:, :middle], piece[:, middle:])
            return jnp.concatenate(
                [jnp.concatenate(pair, 1) for pair in zip(forth, back)], 0
            )

        def slabs_of(whole):
            return [whole[k * slab : (k + 1) * slab] for k in range(count)]

        def scatter(forth_whole, back_whole):
            return ring.scatter(slabs_of(forth_whole), slabs_of(back_whole))

        def scatter_rows(whole):
            pieces = slabs_of(whole)
            parts = ring.scatter(
                [piece[: slab // 2] for piece in pieces], [piece[slab // 2 :] for piece in pieces]
            )
            return jnp.concatenate(parts, 0)

        def scatter_columns(whole):
            middle = whole.shape[1] // 2
            pieces = slabs_of(whole)
            parts = ring.scatter(
                [piece[:, :middle] for piece in pieces], [piece[:, middle:] for piece in pieces]
            )
            return jnp.concatenate(parts, 1)

    else:

        def moved(values, dtype):
            return values.astype(dtype)

        restored = moved

        def gain_moved(gain):
            return gain

        gain_restored = gain_moved

        def gather_rows(piece):
            return lax.all_gather(piece, "seq", axis=0, tiled=True)

        gather_columns = gather_rows

        def gather(forth_piece, back_piece):
            return gather_rows(forth_piece), gather_rows(back_piece)

        def scatter_rows(whole):
            return lax.psum_scatter(whole, "seq", scatter_dimension=0, tiled=True)

        scatter_columns = scatter_rows

        def scatter(forth_whole, back_whole):
            return scatter_rows(forth_whole), scatter_rows(back_whole)

    branch_all, inner_all = gather(branch_weight, inner_weight)
    out_all = gather_rows(out_turned)
    gate_all, up_all = gather(gate_weight, up_weight)
    down_all = gather_columns(down_turned)

    gain_one = gain_moved(norm_gain.astype(f32))
    gain_two = gain_moved(mlp_norm_gain.astype(f32))
    taps = conv_weight.astype(f32)
    decay = decay_param.astype(f32)
    gate_square, input_square = block_diagonal(gate_blocks), block_diagonal(input_blocks)
    fresh_start = resets[:, :, None] > 0

    tokens_low = moved(tokens.reshape(rows, width), bf16)
    cot_low = moved(cotangent.reshape(rows, width), bf16)
    values = tokens_low.astype(f32)
    normed = (values * inverse_rms(values) * gain_one).astype(bf16)
    inner_low = dot_nn(normed, inner_all).astype(bf16).reshape(batches, length, units)
    branch_pre = dot_nn(normed, branch_all).reshape(batches, length, units)
    edge_rows = passed_along(inner_low[:, -3:], 1)
    padded = jnp.concatenate([edge_rows, inner_low], 1).astype(f32)
    conv_sum = conv_bias.astype(f32) + taps[0] * padded[:, 3:] + taps[1] * padded[:, 2:-1]
    conv_sum = conv_sum + taps[2] * padded[:, 1:-2] + taps[3] * padded[:, :-3]
    conv_low = conv_sum.astype(bf16)
    conv_flat = conv_low.reshape(rows, units)
    gate_pre = dot_nn(conv_flat, gate_square).reshape(batches, length, units)
    gate_pre = gate_pre + gate_bias.astype(f32)
    input_pre = dot_nn(conv_flat, input_square).reshape(batches, length, units)
    input_pre = input_pre + input_bias.astype(f32)
    conv_value = conv_low.astype(f32)

    def gates(gate_pre, input_pre, conv_value, decay):
        return gate_math(gate_pre, input_pre, conv_value, decay, fresh_start)

    carries, drives = gates(gate_pre, input_pre, conv_value, decay)
    prods, local_state = local_scan(carries, drives, False)
    state_in = state_at_entry(prods[:, -1:], local_state[:, -1:], 1)
    states = local_state + prods * state_in

    branch, branch_pull = jax.vjp(gelu_tanh, branch_pre)
    mixed_low = (states * branch).astype(bf16).reshape(rows, units)
    own_middle = own_rows(tokens_low).astype(f32) + halves_summed(dot_nt(mixed_low, out_all))
    scale_two = inverse_rms(own_middle)
    unit_two = own_middle * scale_two
    normed_two = halves_joined((unit_two * gain_two).astype(bf16))

    gate_mlp = dot_nn(normed_two, gate_all)
    up_mlp = dot_nn(normed_two, up_all)
    activated, act_pull = jax.vjp(gated_product, gate_mlp, up_mlp)
    hidden_low = activated.astype(bf16)
    down_grad = scatter_columns(dot_tn(cot_low, hidden_low)).T
    grad_gate_mlp, grad_up_mlp = act_pull(dot_nn(cot_low, down_all))
    gate_mlp_low, up_mlp_low = grad_gate_mlp.astype(bf16), grad_up_mlp.astype(bf16)
    gate_grad, up_grad = scatter(dot_tn(normed_two, gate_mlp_low), dot_tn(normed_two, up_mlp_low))
    own_back = halves_summed(dot_nt(gate_mlp_low, gate_all) + dot_nt(up_mlp_low, up_all))
    own_mixed = own_middle + halves_summed(dot_nt(hidden_low, down_all))
    mixed = halves_joined(restored(own_mixed, bf16)).astype(f32).reshape(tokens.shape)

    gain_two_grad = jnp.sum(own_back * unit_two, 0)
    weighted = own_back * gain_two
    own_grad = own_rows(cot_low).astype(f32) + scale_two * (
        weighted - unit_two * jnp.mean(weighted * unit_two, axis=-1, keepdims=True)
    )
    middle_low = halves_joined(own_grad.astype(bf16))

    out_grad = scatter_rows(dot_tn(middle_low, mixed_low)).T
    grad_mixed = dot_nn(middle_low, out_all).reshape(batches, length, units)
    (grad_branch_pre,) = branch_pull(grad_mixed * states)
    branch_low = grad_branch_pre.astype(bf16).reshape(rows, units)
    following = jnp.concatenate([carries[:, 1:], jnp.ones_like(carries[:, :1])], 1)
    tail_prods, local_adjoint = local_scan(following, grad_mixed * branch, True)
    adjoint_in = state_at_entry(prods[:, -1:], carries[:, :1] * local_adjoint[:, :1], -1)
    adjoint = local_adjoint + tail_prods * adjoint_in
    state_before = jnp.concatenate([state_in, states[:, :-1]], 1)
    _, gate_pull = jax.vjp(gates, gate_pre, input_pre, conv_value, decay)
    grad_gate_pre, grad_input_pre, grad_conv, decay_grad = gate_pull(
        (adjoint * state_before, adjoint)
    )
    gate_low = grad_gate_pre.astype(bf16).reshape(rows, units)
    input_low = grad_input_pre.astype(bf16).reshape(rows, units)
    back_conv = dot_nt(gate_low, gate_square) + dot_nt(input_low, input_square)
    grad_conv = grad_conv + back_conv.reshape(batches, length, units)
    block_count = gate_blocks.shape[0]
    gate_blocks_grad = diagonal_blocks(dot_tn(conv_flat, gate_low), block_count)
    input_blocks_grad = diagonal_blocks(dot_tn(conv_flat, input_low), block_count)

    border = jnp.zeros((batches, 3, units), f32)
    spread = jnp.concatenate([border, grad_conv, border], 1)
    stop = length + 3
    grad_padded = taps[0] * spread[:, :stop] + taps[1] * spread[:, 1 : stop + 1]
    grad_padded = grad_padded + taps[2] * spread[:, 2 : stop + 2] + taps[3] * spread[:, 3:]
    returned = passed_along(grad_padded[:, :3], -1)
    grad_inner = jnp.concatenate(
        [grad_padded[:, 3:-3], grad_padded[:, -3:] + returned], 1
    )
    inner_grad_low = grad_inner.astype(bf16).reshape(rows, units)
    branch_grad, inner_grad = scatter(dot_tn(normed, branch_low), dot_tn(normed, inner_grad_low))
    own_front = halves_summed(dot_nt(branch_low, branch_all) + dot_nt(inner_grad_low, inner_all))

    own_values = own_rows(tokens_low).astype(f32)
    scale_one = inverse_rms(own_values)
    unit_one = own_values * scale_one
    gain_one_grad = jnp.sum(own_front * unit_one, 0)
    weighted = own_front * gain_one
    own_tokens = own_grad + scale_one * (
        weighted - unit_one * jnp.mean(weighted * unit_one, axis=-1, keepdims=True)
    )
    tokens_grad = halves_joined(restored(own_tokens, bf16)).astype(f32).reshape(tokens.shape)

    taps_grad = jnp.stack(
        [jnp.sum(grad_conv * padded[:, 3 - k : 3 - k + length], (0, 1)) for k in range(4)], 0
    )
    small = jnp.concatenate(
        [
            taps_grad,
            jnp.sum(grad_conv, (0, 1))[None],
            jnp.sum(gate_low.astype(f32), 0)[None],
            jnp.sum(input_low.astype(f32), 0)[None],
            decay_grad[None],
        ],
        0,
    )
    small, gate_blocks_grad, input_blocks_grad = lax.psum(
        (small, gate_blocks_grad, input_blocks_grad), "seq"
    )
    gains = jnp.stack([gain_restored(gain_one_grad), gain_restored(gain_two_grad)], 0)
    gains = lax.psum(gains, ("seq", "fsdp"))
    return (
        mixed,
        tokens_grad,
        gains[0],
        branch_grad,
        inner_grad,
        small[:4],
        small[4],
        gate_blocks_grad,
        input_blocks_grad,
        small[5],
        small[6],
        small[7],
        out_grad,
        gains[1],
        gate_grad,
        up_grad,
        down_grad,
    )


def solution(mesh):
    units, both = P("fsdp"), P("seq", "fsdp")
    blocks, turned = P("fsdp", None, None), P("fsdp", "seq")
    rows = P(None, "seq", None)
    return jax.shard_map(
        local,
        mesh=mesh,
        in_specs=(
            rows,
            P(None, "seq"),
            P(),
            both,
            both,
            P(None, "fsdp"),
            units,
            blocks,
            blocks,
            units,
            units,
            units,
            turned,
            P(),
            both,
            both,
            turned,
            rows,
        ),
        out_specs=(
            rows,
            rows,
            P(),
            both,
            both,
            P(None, "fsdp"),
            units,
            blocks,
            blocks,
            units,
            units,
            units,
            turned,
            P(),
            both,
            both,
            turned,
        ),
        check_vma=False,
    )
```

```python
import functools

import jax
import jax.numpy as jnp
from jax import lax
from jax.experimental import pallas as pl
from jax.experimental.pallas import tpu as pltpu
from jax.sharding import PartitionSpec as P

eps = 1e-06
decay_scale = 8.0
f32 = jnp.float32
bf16 = jnp.bfloat16
ring_limit = 16


def gelu_tanh(values):
    return jax.nn.gelu(values, approximate=True)


def gated_product(gate_pre, up_pre):
    return gelu_tanh(gate_pre) * up_pre


def gate_math(gate_pre, input_pre, conv_value, decay_param, fresh_start):
    rate_gate = jax.nn.sigmoid(gate_pre)
    inlet_gate = jax.nn.sigmoid(input_pre)
    log_decay = -decay_scale * jax.nn.softplus(-decay_param) * rate_gate
    input_scale = jnp.where(fresh_start, 1.0, jnp.sqrt(-jnp.expm1(2.0 * log_decay)))
    carries = jnp.where(fresh_start, 0.0, jnp.exp(log_decay))
    return (carries, input_scale * inlet_gate * conv_value)


def dot_nn(left, right):
    return jnp.dot(left, right, preferred_element_type=f32)


def dot_nt(left, right):
    return lax.dot_general(left, right, (((1,), (1,)), ((), ())), preferred_element_type=f32)


def dot_tn(left, right):
    return lax.dot_general(left, right, (((0,), (0,)), ((), ())), preferred_element_type=f32)


def inverse_rms(values):
    return lax.rsqrt(jnp.mean(values * values, axis=-1, keepdims=True) + eps)


def scan_body(backward, a_ref, b_ref, prod_ref, state_ref):
    batches, length, units = a_ref.shape
    tiles = length // 8
    rows = lax.broadcasted_iota(jnp.int32, (8, units), 0)

    def step(index, carry):
        tile = tiles - 1 - index if backward else index
        where_rows = pl.ds(pl.multiple_of(tile * 8, 8), 8)
        following = []
        for batch in range(batches):
            prod_in, state_in = carry[batch]
            a = a_ref[batch, where_rows, :]
            b = b_ref[batch, where_rows, :]
            for shift in (1, 2, 4):
                turn = 8 - shift if backward else shift
                inside = rows < 8 - shift if backward else rows >= shift
                a_moved = jnp.where(inside, pltpu.roll(a, turn, 0), 1.0)
                b_moved = jnp.where(inside, pltpu.roll(b, turn, 0), 0.0)
                b = a * b_moved + b
                a = a * a_moved
            b = b + a * state_in
            a = a * prod_in
            prod_ref[batch, where_rows, :] = a
            state_ref[batch, where_rows, :] = b
            edge = 0 if backward else 7
            following.append((a[edge : edge + 1], b[edge : edge + 1]))
        return tuple(following)

    first = tuple(
        (jnp.ones((1, units), f32), jnp.zeros((1, units), f32)) for _ in range(batches)
    )
    lax.fori_loop(0, tiles, step, first)


def local_scan(a, b, backward):
    shape = jax.ShapeDtypeStruct(a.shape, f32)
    elements = a.shape[0] * a.shape[1] * a.shape[2]
    return pl.pallas_call(
        functools.partial(scan_body, backward),
        out_shape=(shape, shape),
        in_specs=[pl.BlockSpec(memory_space=pltpu.VMEM)] * 2,
        out_specs=(pl.BlockSpec(memory_space=pltpu.VMEM),) * 2,
        compiler_params=pltpu.CompilerParams(vmem_limit_bytes=32 * 1024 * 1024),
        cost_estimate=pl.CostEstimate(
            flops=20 * elements, bytes_accessed=16 * elements, transcendentals=0
        ),
    )(a, b)


def move_body(table_ref, in_ref, out_ref):
    out_ref[...] = in_ref[...].astype(out_ref.dtype)


def move_slabs(values, table, dtype):
    rows, width = values.shape
    slabs = table.shape[0]
    return pl.pallas_call(
        move_body,
        out_shape=jax.ShapeDtypeStruct((rows, width), dtype),
        grid_spec=pltpu.PrefetchScalarGridSpec(
            num_scalar_prefetch=1,
            grid=(slabs,),
            in_specs=[pl.BlockSpec((rows, width // slabs), lambda k, where: (0, where[k]))],
            out_specs=pl.BlockSpec((rows, width // slabs), lambda k, where: (0, k)),
        ),
        cost_estimate=pl.CostEstimate(
            flops=0, bytes_accessed=8 * rows * width, transcendentals=0
        ),
    )(table, values)


class Ring:
    def __init__(self, count):
        self.count = count
        self.order = list(range(0, count, 2)) + list(range(count - 1, 0, -2))
        self.place = [self.order.index(i) for i in range(count)]
        self.forth = [(self.order[i], self.order[(i + 1) % count]) for i in range(count)]
        self.back = [(there, here) for here, there in self.forth]
        self.sent, self.awaited = [], []

    def tables(self):
        here = jnp.asarray(self.place, jnp.int32)[lax.axis_index("seq")]
        steps = jnp.arange(self.count, dtype=jnp.int32)
        to_ring = jnp.asarray(self.order, jnp.int32)[(here - steps) % self.count]
        to_plain = (here - jnp.asarray(self.place, jnp.int32)) % self.count
        return to_ring, to_plain

    def send(self, forth, back):
        earlier = list(self.sent[-2]) if len(self.sent) > 1 else []
        if earlier or self.awaited:
            forth, back = lax.optimization_barrier((forth, back, *earlier, *self.awaited))[:2]
        self.awaited = []
        self.sent.append(
            (lax.ppermute(forth, "seq", self.forth), lax.ppermute(back, "seq", self.back))
        )
        return self.sent[-1]

    def first(self, *values):
        self.awaited.extend(values)

    def then(self, value, under_way=1):
        if len(self.sent) <= under_way:
            return value
        return lax.optimization_barrier((value, *self.sent[-1 - under_way]))[0]


class Gather:
    def __init__(self, ring, forth, back):
        self.ring, self.forth, self.back = ring, [forth], [back]

    def step(self):
        forth, back = self.ring.send(self.forth[-1], self.back[-1])
        self.forth.append(forth)
        self.back.append(back)

    def slabs(self):
        count = self.ring.count
        return self.forth, [self.back[-k % count] for k in range(count)]


class Scatter:
    def __init__(self, ring, forth_slab, back_slab):
        self.ring, self.forth_slab, self.back_slab = ring, forth_slab, back_slab
        self.at = 1
        self.forth = forth_slab(1).astype(bf16)
        self.back = back_slab(ring.count - 1).astype(bf16)

    def step(self):
        count = self.ring.count
        forth, back = self.ring.send(self.forth, self.back)
        self.at += 1
        self.forth = forth.astype(f32) + self.forth_slab(self.at % count)
        self.back = back.astype(f32) + self.back_slab(count - self.at)
        if self.at < count:
            self.forth, self.back = self.forth.astype(bf16), self.back.astype(bf16)

    def sums(self):
        return self.forth, self.back


class PlainGather:
    def __init__(self, ring, forth, back):
        self.pieces = (forth, back)

    def step(self):
        pass

    def slabs(self):
        return tuple(list(lax.all_gather(piece, "seq")) for piece in self.pieces)


class PlainScatter:
    def __init__(self, ring, forth_slab, back_slab):
        self.terms = (forth_slab, back_slab)

    def step(self):
        pass

    def sums(self):
        count = lax.axis_size("seq")
        return tuple(
            lax.psum_scatter(
                jnp.concatenate([term(k) for k in range(count)], 0),
                "seq",
                scatter_dimension=0,
                tiled=True,
            )
            for term in self.terms
        )


def in_turn(*transfers):
    for transfer in transfers:
        transfer.step()


def swapped(values, axis, bit):
    return lax.ppermute(values, axis, [(i, i ^ bit) for i in range(lax.axis_size(axis))])


class Exchange:
    def __init__(self, ring, values, axis):
        self.ring, self.values, self.axis = ring, values, axis
        self.got = None
        count = lax.axis_size(axis)
        self.bits = [1 << i for i in range(count.bit_length() - 1)]
        self.stages = self.plan()

    def upper(self, bit):
        return (lax.axis_index(self.axis) // bit) % 2 > 0

    def step(self, under_way=None):
        if self.got is not None:
            got, bit, end = self.got
            self.got = None
            end(got if under_way is None else self.ring.then(got, under_way), bit)
        if self.stages:
            start, end, bit = self.stages.pop(0)
            self.got = (swapped(start(bit), self.axis, bit), bit, end)
        return self.values

    def run(self, under_way=None):
        while self.stages or self.got is not None:
            self.step(under_way)
        return self.values

    def start_half(self, bit):
        half = self.values.shape[0] // 2
        kept, sent = [
            jnp.where(self.upper(bit) == side, self.values[half:], self.values[:half])
            for side in (True, False)
        ]
        self.values = kept
        return sent.astype(bf16)

    def end_half(self, got, bit):
        self.values = self.values.astype(f32) + got.astype(f32)

    def start_join(self, bit):
        return self.values

    def end_join(self, got, bit):
        upper, own = self.upper(bit), self.values
        self.values = jnp.concatenate([jnp.where(upper, got, own), jnp.where(upper, own, got)], 0)

    def end_sum(self, got, bit):
        self.values = self.values + got

    def halving(self):
        return [(self.start_half, self.end_half, bit) for bit in self.bits]

    def joining(self):
        return [(self.start_join, self.end_join, bit) for bit in reversed(self.bits)]


class Halves(Exchange):
    def plan(self):
        return self.halving()


class Joined(Exchange):
    def plan(self):
        return self.joining()


class Everywhere(Exchange):
    def plan(self):
        stages = self.halving() + self.joining()
        middle = len(self.bits)

        def start_first_join(bit):
            self.values = self.values.astype(bf16)
            return self.values

        if stages:
            stages[middle] = (start_first_join, self.end_join, stages[middle][2])
        return stages


class SmallSum(Exchange):
    def plan(self):
        return [(self.start_join, self.end_sum, bit) for bit in self.bits]


def own_rows(values):
    count, mine = lax.axis_size("fsdp"), lax.axis_index("fsdp")
    bit = 1
    while bit < count:
        half = values.shape[0] // 2
        values = lax.dynamic_slice_in_dim(values, ((mine // bit) % 2) * half, half, 0)
        bit *= 2
    return values


def halves_joined(own):
    count, mine = lax.axis_size("fsdp"), lax.axis_index("fsdp")
    bit = count // 2
    while bit:
        got = lax.ppermute(own, "fsdp", [(i, i ^ bit) for i in range(count)])
        upper = (mine // bit) % 2 > 0
        own = jnp.concatenate([jnp.where(upper, got, own), jnp.where(upper, own, got)], 0)
        bit //= 2
    return own


def passed_along(block, distance):
    devices = range(lax.axis_size("seq"))
    route = [(i - distance, i) for i in devices if i - distance in devices]
    return lax.ppermute(block, "seq", route)


def joined_maps(earlier, later):
    return jnp.stack([earlier[0] * later[0], later[1] + later[0] * earlier[1]], 0)


class Entry:
    def __init__(self, prods, states, sign):
        self.pair, self.sign = jnp.stack([prods, states], 0), sign
        self.count = lax.axis_size("seq")
        self.direct = self.count <= ring_limit and self.count % 2 == 0
        if self.direct:
            self.other = swapped(self.pair, "seq", 1)

    def between(self, hold):
        if not self.direct:
            return
        self.other = hold(self.other)
        self.second = lax.axis_index("seq") % 2 == (1 if self.sign > 0 else 0)
        earlier = jnp.where(self.second, self.other, self.pair)
        later = jnp.where(self.second, self.pair, self.other)
        both = joined_maps(earlier, later)
        self.parts = [
            passed_along(both, self.sign * distance) for distance in range(self.count - 2, 0, -2)
        ]

    def state(self, hold):
        if self.direct:
            parts = [hold(self.parts[0])] + self.parts[1:]
            state = parts[0][1]
            for part in parts[1:]:
                state = part[1] + part[0] * state
            return jnp.where(self.second, self.other[1] + self.other[0] * state, state)
        pair = passed_along(self.pair, self.sign)
        distance = 1
        while distance < self.count:
            pair = joined_maps(passed_along(pair, self.sign * distance), pair)
            distance *= 2
        return pair[1]


def block_diagonal(blocks):
    count, width = blocks.shape[0], blocks.shape[1]
    return sum(
        jnp.pad(blocks[j], ((j * width, (count - 1 - j) * width),) * 2) for j in range(count)
    )


def rows_joined(slab_pairs):
    return jnp.concatenate([part for pair in zip(*slab_pairs) for part in pair], 0)


def diagonal_blocks(square, count):
    width = square.shape[0] // count
    return jnp.stack(
        [square[j * width : (j + 1) * width, j * width : (j + 1) * width] for j in range(count)], 0
    )


def local(
    tokens,
    resets,
    norm_gain,
    branch_weight,
    inner_weight,
    conv_weight,
    conv_bias,
    gate_blocks,
    input_blocks,
    gate_bias,
    input_bias,
    decay_param,
    out_weight,
    mlp_norm_gain,
    gate_weight,
    up_weight,
    down_weight,
    cotangent,
):
    count = lax.axis_size("seq")
    batches, length, width = tokens.shape
    slab = width // count
    units, hidden = conv_bias.shape[0], down_weight.shape[0]
    rows = batches * length
    ringed = count <= ring_limit
    half = slab // 2
    out_turned, down_turned = out_weight.T, down_weight.T
    ring = Ring(count)
    if ringed:
        gather, scatter = functools.partial(Gather, ring), functools.partial(Scatter, ring)
        to_ring, to_plain = ring.tables()

        def moved(values, dtype):
            return move_slabs(values, to_ring, dtype)

        def restored(values, dtype):
            return move_slabs(values, to_plain, dtype)

        def gain_moved(gain):
            return gain.reshape(count, slab)[to_ring].reshape(width)

        def gain_restored(gain):
            return gain.reshape(count, slab)[to_plain].reshape(width)

    else:
        gather, scatter = functools.partial(PlainGather, ring), functools.partial(PlainScatter, ring)

        def moved(values, dtype):
            return values.astype(dtype)

        restored = moved

        def gain_moved(gain):
            return gain

        gain_restored = gain_moved

    def slab_dots(turned, right, first=0, rows=slab):
        def term(k):
            start = k * slab + first
            return dot_nn(turned[start : start + rows], right)

        return term

    steps = count - 1
    front_weights = gather(branch_weight, inner_weight)
    out_weights = gather(out_turned[:half], out_turned[half:])
    mlp_weights = gather(gate_weight, up_weight)
    down_weights = gather(down_turned[:half], down_turned[half:])
    in_turn(front_weights, out_weights)
    tokens_low = moved(tokens.reshape(rows, width), bf16)
    ring.first(tokens_low)
    in_turn(front_weights, out_weights)
    gain_one = gain_moved(norm_gain.astype(f32))
    gain_two = gain_moved(mlp_norm_gain.astype(f32))
    values = ring.then(tokens_low, 2).astype(f32)
    normed = (values * inverse_rms(values) * gain_one).astype(bf16)
    ring.first(normed)
    in_turn(front_weights, out_weights)
    gate_square, input_square = block_diagonal(gate_blocks), block_diagonal(input_blocks)
    ring.first(gate_square, input_square)
    in_turn(front_weights, out_weights)
    cot_low = moved(ring.then(cotangent, 2).reshape(rows, width), bf16)
    ring.first(cot_low)
    for _ in range(steps - 4):
        in_turn(front_weights, out_weights)
    branch_all, inner_all = (jnp.concatenate(slabs, 0) for slabs in front_weights.slabs())
    out_all = rows_joined(out_weights.slabs())

    taps = conv_weight.astype(f32)
    decay = decay_param.astype(f32)
    fresh_start = resets[:, :, None] > 0
    in_turn(mlp_weights)
    inner_low = dot_nn(normed, inner_all).astype(bf16).reshape(batches, length, units)
    branch_pre = dot_nn(normed, branch_all).reshape(batches, length, units)
    edge_rows = passed_along(inner_low[:, -3:], 1)
    ring.first(inner_low, branch_pre)
    in_turn(down_weights)
    padded = jnp.concatenate([ring.then(edge_rows, 2), inner_low], 1).astype(f32)
    conv_sum = conv_bias.astype(f32) + taps[0] * padded[:, 3:] + taps[1] * padded[:, 2:-1]
    conv_sum = conv_sum + taps[2] * padded[:, 1:-2] + taps[3] * padded[:, :-3]
    conv_low = conv_sum.astype(bf16)
    conv_flat = conv_low.reshape(rows, units)
    gate_pre = dot_nn(conv_flat, gate_square).reshape(batches, length, units)
    gate_pre = gate_pre + gate_bias.astype(f32)
    input_pre = dot_nn(conv_flat, input_square).reshape(batches, length, units)
    input_pre = input_pre + input_bias.astype(f32)
    conv_value = conv_low.astype(f32)

    def gates(gate_pre, input_pre, conv_value, decay):
        return gate_math(gate_pre, input_pre, conv_value, decay, fresh_start)

    carries, drives = gates(gate_pre, input_pre, conv_value, decay)
    ring.first(carries, drives)
    in_turn(mlp_weights)
    prods, local_state = local_scan(ring.then(carries, 2), drives, False)
    entry = Entry(prods[:, -1:], local_state[:, -1:], 1)
    ring.first(prods)
    in_turn(down_weights)
    entry.between(ring.then)
    in_turn(mlp_weights)
    state_in = entry.state(lambda part: ring.then(part, 1))
    ring.first(state_in)
    in_turn(down_weights)
    states = local_state + prods * ring.then(state_in, 2)

    branch, branch_pull = jax.vjp(gelu_tanh, branch_pre)
    mixed_low = (states * branch).astype(bf16).reshape(rows, units)
    middle_sum = Halves(ring, dot_nt(mixed_low, out_all), "fsdp")
    middle_sum.step()
    ring.first(middle_sum.step())
    in_turn(mlp_weights, down_weights)
    own_middle = own_rows(tokens_low).astype(f32) + middle_sum.run(2)
    scale_two = inverse_rms(own_middle)
    unit_two = own_middle * scale_two
    normed_join = Joined(ring, (unit_two * gain_two).astype(bf16), "fsdp")
    ring.first(normed_join.step())
    in_turn(mlp_weights)
    normed_join.step(1)
    normed_two = normed_join.run()
    ring.first(normed_two)
    in_turn(down_weights, mlp_weights)
    in_turn(*[mlp_weights] * (steps - 6), *[down_weights] * (steps - 5))
    gate_all, up_all = (jnp.concatenate(slabs, 0) for slabs in mlp_weights.slabs())
    down_all = rows_joined(down_weights.slabs())

    gate_mlp = dot_nn(normed_two, gate_all)
    up_mlp = dot_nn(normed_two, up_all)
    activated, act_pull = jax.vjp(gated_product, gate_mlp, up_mlp)
    hidden_low = activated.astype(bf16)
    down_grads = scatter(
        slab_dots(cot_low.T, hidden_low, 0, half), slab_dots(cot_low.T, hidden_low, half, half)
    )
    in_turn(down_grads)
    grad_gate_mlp, grad_up_mlp = act_pull(dot_nn(ring.then(cot_low, 0), down_all))
    gate_mlp_low, up_mlp_low = grad_gate_mlp.astype(bf16), grad_up_mlp.astype(bf16)
    in_turn(down_grads)
    ring.first(gate_mlp_low, up_mlp_low)
    in_turn(down_grads)
    mlp_grads = scatter(
        slab_dots(normed_two.T, gate_mlp_low), slab_dots(normed_two.T, up_mlp_low)
    )
    in_turn(mlp_grads, down_grads)
    gate_mlp_low, up_mlp_low = lax.optimization_barrier(
        (ring.then(gate_mlp_low, 2), up_mlp_low)
    )
    back_sum = Halves(
        ring, dot_nt(gate_mlp_low, gate_all) + dot_nt(up_mlp_low, up_all), "fsdp"
    )
    back_sum.step()
    ring.first(back_sum.step())
    in_turn(mlp_grads, down_grads)
    own_back = back_sum.run(2)
    gain_two_grad = jnp.sum(own_back * unit_two, 0)
    weighted = own_back * gain_two
    own_grad = own_rows(cot_low).astype(f32) + scale_two * (
        weighted - unit_two * jnp.mean(weighted * unit_two, axis=-1, keepdims=True)
    )
    middle_join = Joined(ring, own_grad.astype(bf16), "fsdp")
    ring.first(middle_join.step())
    in_turn(mlp_grads, down_grads)
    middle_join.step(2)
    middle_low = middle_join.run()

    grad_mixed = dot_nn(middle_low, out_all).reshape(batches, length, units)
    (grad_branch_pre,) = branch_pull(grad_mixed * states)
    branch_low = grad_branch_pre.astype(bf16).reshape(rows, units)
    following = jnp.concatenate([carries[:, 1:], jnp.ones_like(carries[:, :1])], 1)
    tail_prods, local_adjoint = local_scan(following, grad_mixed * branch, True)
    entry = Entry(prods[:, -1:], carries[:, :1] * local_adjoint[:, :1], -1)
    ring.first(local_adjoint, branch_low)
    in_turn(mlp_grads)
    entry.between(ring.then)
    in_turn(down_grads)
    adjoint_in = entry.state(lambda part: ring.then(part, 1))
    adjoint = local_adjoint + tail_prods * adjoint_in
    state_before = jnp.concatenate([state_in, states[:, :-1]], 1)
    _, gate_pull = jax.vjp(gates, gate_pre, input_pre, conv_value, decay)
    grad_gate_pre, grad_input_pre, grad_conv, decay_grad = gate_pull(
        (adjoint * state_before, adjoint)
    )
    gate_low = grad_gate_pre.astype(bf16).reshape(rows, units)
    input_low = grad_input_pre.astype(bf16).reshape(rows, units)
    ring.first(gate_low, input_low)
    in_turn(mlp_grads)
    back_conv = dot_nt(gate_low, gate_square) + dot_nt(input_low, input_square)
    grad_conv = grad_conv + back_conv.reshape(batches, length, units)

    border = jnp.zeros((batches, 3, units), f32)
    spread = jnp.concatenate([border, grad_conv, border], 1)
    stop = length + 3
    grad_padded = taps[0] * spread[:, :stop] + taps[1] * spread[:, 1 : stop + 1]
    grad_padded = grad_padded + taps[2] * spread[:, 2 : stop + 2] + taps[3] * spread[:, 3:]
    returned = passed_along(grad_padded[:, :3], -1)
    ring.first(grad_padded)
    in_turn(mlp_grads)
    grad_inner = jnp.concatenate(
        [grad_padded[:, 3:-3], grad_padded[:, -3:] + ring.then(returned)], 1
    )
    inner_grad_low = grad_inner.astype(bf16).reshape(rows, units)
    in_turn(*[mlp_grads] * (steps - 6))
    out_grads = scatter(
        slab_dots(middle_low.T, mixed_low, 0, half), slab_dots(middle_low.T, mixed_low, half, half)
    )
    front_grads = scatter(
        slab_dots(normed.T, branch_low), slab_dots(normed.T, inner_grad_low)
    )
    in_turn(out_grads, front_grads)
    front_sum = Halves(
        ring,
        dot_nt(ring.then(branch_low), branch_all) + dot_nt(inner_grad_low, inner_all),
        "fsdp",
    )
    front_sum.step()
    front_sum.step()

    block_count = gate_blocks.shape[0]
    conv_again = ring.then(conv_flat)
    block_grads = jnp.concatenate(
        [
            diagonal_blocks(dot_tn(conv_again, gate_low), block_count),
            diagonal_blocks(dot_tn(conv_again, input_low), block_count),
        ],
        0,
    )
    block_width = block_grads.shape[-1]
    block_sum = Everywhere(ring, block_grads.reshape(-1, block_width), "seq")
    block_sum.step()
    taps_grad = jnp.stack(
        [jnp.sum(grad_conv * padded[:, 3 - k : 3 - k + length], (0, 1)) for k in range(4)], 0
    )
    small = jnp.concatenate(
        [
            taps_grad,
            jnp.sum(grad_conv, (0, 1))[None],
            jnp.sum(gate_low.astype(f32), 0)[None],
            jnp.sum(input_low.astype(f32), 0)[None],
            decay_grad[None],
        ],
        0,
    )
    in_turn(out_grads, front_grads)
    block_sum.step(1)
    own_front = front_sum.run(1)
    own_values = own_rows(tokens_low).astype(f32)
    scale_one = inverse_rms(own_values)
    unit_one = own_values * scale_one
    gain_one_grad = jnp.sum(own_front * unit_one, 0)
    weighted = own_front * gain_one
    own_tokens = own_grad + scale_one * (
        weighted - unit_one * jnp.mean(weighted * unit_one, axis=-1, keepdims=True)
    )
    gains = jnp.stack([gain_restored(gain_one_grad), gain_restored(gain_two_grad)], 0)
    small_sum = SmallSum(ring, jnp.concatenate([small.reshape(-1), gains.reshape(-1)]), "seq")
    tokens_join = Joined(ring, restored(own_tokens, bf16), "fsdp")
    tokens_join.step()
    small_sum.step()
    in_turn(out_grads, front_grads)
    block_sum.step(1)
    small_sum.step(1)
    tokens_join.step(1)
    tokens_grad = tokens_join.run().astype(f32).reshape(tokens.shape)
    in_turn(out_grads, front_grads)
    block_sum.step(1)
    small_sum.step(1)
    mixed_sum = Halves(ring, dot_nt(ring.then(hidden_low), down_all), "fsdp")
    mixed_sum.step()
    mixed_sum.step()
    in_turn(out_grads, front_grads)
    block_sum.step(1)
    small = small_sum.run(1)
    gains = small[8 * units :]
    small = small[: 8 * units].reshape(8, units)
    gains_sum = SmallSum(ring, gains, "fsdp")
    gains_sum.step()
    mixed_join = Joined(ring, restored(own_middle + mixed_sum.run(1), bf16), "fsdp")
    mixed_join.step()
    in_turn(out_grads, front_grads)
    block_sum.step(1)
    gains_sum.step(1)
    mixed_join.step(1)
    mixed = mixed_join.run().astype(f32).reshape(tokens.shape)
    in_turn(*[out_grads, front_grads] * (steps - 6))
    block_grads = block_sum.run(1).astype(f32)
    block_grads = block_grads.reshape(2, block_count, block_width, block_width)
    gains = gains_sum.run(1).reshape(2, width)
    branch_grad, inner_grad = front_grads.sums()
    gate_grad, up_grad = mlp_grads.sums()
    out_grad = jnp.concatenate(out_grads.sums(), 0)
    down_grad = jnp.concatenate(down_grads.sums(), 0)
    return (
        mixed,
        tokens_grad,
        gains[0],
        branch_grad,
        inner_grad,
        small[:4],
        small[4],
        block_grads[0],
        block_grads[1],
        small[5],
        small[6],
        small[7],
        out_grad.T,
        gains[1],
        gate_grad,
        up_grad,
        down_grad.T,
    )


def solution(mesh):
    units, both = P("fsdp"), P("seq", "fsdp")
    blocks, turned = P("fsdp", None, None), P("fsdp", "seq")
    rows = P(None, "seq", None)
    return jax.shard_map(
        local,
        mesh=mesh,
        in_specs=(
            rows,
            P(None, "seq"),
            P(),
            both,
            both,
            P(None, "fsdp"),
            units,
            blocks,
            blocks,
            units,
            units,
            units,
            turned,
            P(),
            both,
            both,
            turned,
            rows,
        ),
        out_specs=(
            rows,
            rows,
            P(),
            both,
            both,
            P(None, "fsdp"),
            units,
            blocks,
            blocks,
            units,
            units,
            units,
            turned,
            P(),
            both,
            both,
            turned,
        ),
        check_vma=False,
    )
```

```python
import functools

import jax
import jax.numpy as jnp
from jax import lax
from jax.experimental import pallas as pl
from jax.experimental.pallas import tpu as pltpu
from jax.sharding import PartitionSpec as P

eps = 1e-06
decay_scale = 8.0
f32 = jnp.float32
bf16 = jnp.bfloat16
ring_limit = 16


def gelu_tanh(values):
    return jax.nn.gelu(values, approximate=True)


def gated_product(gate_pre, up_pre):
    return gelu_tanh(gate_pre) * up_pre


def gate_math(gate_pre, input_pre, conv_value, decay_param, fresh_start):
    rate_gate = jax.nn.sigmoid(gate_pre)
    inlet_gate = jax.nn.sigmoid(input_pre)
    log_decay = -decay_scale * jax.nn.softplus(-decay_param) * rate_gate
    input_scale = jnp.where(fresh_start, 1.0, jnp.sqrt(-jnp.expm1(2.0 * log_decay)))
    carries = jnp.where(fresh_start, 0.0, jnp.exp(log_decay))
    return (carries, input_scale * inlet_gate * conv_value)


def dot_nn(left, right):
    return jnp.dot(left, right, preferred_element_type=f32)


def dot_nt(left, right):
    return lax.dot_general(left, right, (((1,), (1,)), ((), ())), preferred_element_type=f32)


def dot_tn(left, right):
    return lax.dot_general(left, right, (((0,), (0,)), ((), ())), preferred_element_type=f32)


def inverse_rms(values):
    return lax.rsqrt(jnp.mean(values * values, axis=-1, keepdims=True) + eps)


def scan_body(backward, a_ref, b_ref, prod_ref, state_ref):
    batches, length, units = a_ref.shape
    tiles = length // 8
    rows = lax.broadcasted_iota(jnp.int32, (8, units), 0)

    def step(index, carry):
        tile = tiles - 1 - index if backward else index
        where_rows = pl.ds(pl.multiple_of(tile * 8, 8), 8)
        following = []
        for batch in range(batches):
            prod_in, state_in = carry[batch]
            a = a_ref[batch, where_rows, :]
            b = b_ref[batch, where_rows, :]
            for shift in (1, 2, 4):
                turn = 8 - shift if backward else shift
                inside = rows < 8 - shift if backward else rows >= shift
                a_moved = jnp.where(inside, pltpu.roll(a, turn, 0), 1.0)
                b_moved = jnp.where(inside, pltpu.roll(b, turn, 0), 0.0)
                b = a * b_moved + b
                a = a * a_moved
            b = b + a * state_in
            a = a * prod_in
            prod_ref[batch, where_rows, :] = a
            state_ref[batch, where_rows, :] = b
            edge = 0 if backward else 7
            following.append((a[edge : edge + 1], b[edge : edge + 1]))
        return tuple(following)

    first = tuple(
        (jnp.ones((1, units), f32), jnp.zeros((1, units), f32)) for _ in range(batches)
    )
    lax.fori_loop(0, tiles, step, first)


def local_scan(a, b, backward):
    shape = jax.ShapeDtypeStruct(a.shape, f32)
    elements = a.shape[0] * a.shape[1] * a.shape[2]
    return pl.pallas_call(
        functools.partial(scan_body, backward),
        out_shape=(shape, shape),
        in_specs=[pl.BlockSpec(memory_space=pltpu.VMEM)] * 2,
        out_specs=(pl.BlockSpec(memory_space=pltpu.VMEM),) * 2,
        compiler_params=pltpu.CompilerParams(vmem_limit_bytes=32 * 1024 * 1024),
        cost_estimate=pl.CostEstimate(
            flops=20 * elements, bytes_accessed=16 * elements, transcendentals=0
        ),
    )(a, b)


def move_body(table_ref, in_ref, out_ref):
    out_ref[...] = in_ref[...].astype(out_ref.dtype)


def move_slabs(values, table, dtype):
    rows, width = values.shape
    slabs = table.shape[0]
    return pl.pallas_call(
        move_body,
        out_shape=jax.ShapeDtypeStruct((rows, width), dtype),
        grid_spec=pltpu.PrefetchScalarGridSpec(
            num_scalar_prefetch=1,
            grid=(slabs,),
            in_specs=[pl.BlockSpec((rows, width // slabs), lambda k, where: (0, where[k]))],
            out_specs=pl.BlockSpec((rows, width // slabs), lambda k, where: (0, k)),
        ),
        cost_estimate=pl.CostEstimate(
            flops=0, bytes_accessed=8 * rows * width, transcendentals=0
        ),
    )(table, values)


class Ring:
    def __init__(self, count):
        self.count = count
        self.order = list(range(0, count, 2)) + list(range(count - 1, 0, -2))
        self.place = [self.order.index(i) for i in range(count)]
        self.forth = [(self.order[i], self.order[(i + 1) % count]) for i in range(count)]
        self.back = [(there, here) for here, there in self.forth]
        self.sent, self.awaited = [], []

    def tables(self):
        here = jnp.asarray(self.place, jnp.int32)[lax.axis_index("seq")]
        steps = jnp.arange(self.count, dtype=jnp.int32)
        to_ring = jnp.asarray(self.order, jnp.int32)[(here - steps) % self.count]
        to_plain = (here - jnp.asarray(self.place, jnp.int32)) % self.count
        return to_ring, to_plain

    def send(self, forth, back):
        earlier = list(self.sent[-2]) if len(self.sent) > 1 else []
        if earlier or self.awaited:
            forth, back = lax.optimization_barrier((forth, back, *earlier, *self.awaited))[:2]
        self.awaited = []
        self.sent.append(
            (lax.ppermute(forth, "seq", self.forth), lax.ppermute(back, "seq", self.back))
        )
        return self.sent[-1]

    def first(self, *values):
        self.awaited.extend(values)

    def then(self, value, under_way=1):
        if len(self.sent) <= under_way:
            return value
        return lax.optimization_barrier((value, *self.sent[-1 - under_way]))[0]


class Gather:
    def __init__(self, ring, forth, back):
        self.ring, self.forth, self.back = ring, [forth], [back]

    def step(self):
        forth, back = self.ring.send(self.forth[-1], self.back[-1])
        self.forth.append(forth)
        self.back.append(back)

    def slabs(self):
        count = self.ring.count
        return self.forth, [self.back[-k % count] for k in range(count)]


class Scatter:
    def __init__(self, ring, forth_slab, back_slab):
        self.ring, self.forth_slab, self.back_slab = ring, forth_slab, back_slab
        self.at = 1
        self.forth = forth_slab(1).astype(bf16)
        self.back = back_slab(ring.count - 1).astype(bf16)

    def step(self):
        count = self.ring.count
        forth, back = self.ring.send(self.forth, self.back)
        self.at += 1
        self.forth = forth.astype(f32) + self.forth_slab(self.at % count)
        self.back = back.astype(f32) + self.back_slab(count - self.at)
        if self.at < count:
            self.forth, self.back = self.forth.astype(bf16), self.back.astype(bf16)

    def sums(self):
        return self.forth, self.back


class PlainGather:
    def __init__(self, ring, forth, back):
        self.pieces = (forth, back)

    def step(self):
        pass

    def slabs(self):
        return tuple(list(lax.all_gather(piece, "seq")) for piece in self.pieces)


class PlainScatter:
    def __init__(self, ring, forth_slab, back_slab):
        self.terms = (forth_slab, back_slab)

    def step(self):
        pass

    def sums(self):
        count = lax.axis_size("seq")
        return tuple(
            lax.psum_scatter(
                jnp.concatenate([term(k) for k in range(count)], 0),
                "seq",
                scatter_dimension=0,
                tiled=True,
            )
            for term in self.terms
        )


def in_turn(*transfers):
    for transfer in transfers:
        transfer.step()


def swapped(values, axis, bit):
    return lax.ppermute(values, axis, [(i, i ^ bit) for i in range(lax.axis_size(axis))])


class Exchange:
    def __init__(self, ring, values, axis):
        self.ring, self.values, self.axis = ring, values, axis
        self.got = None
        count = lax.axis_size(axis)
        self.bits = [1 << i for i in range(count.bit_length() - 1)]
        self.stages = self.plan()

    def upper(self, bit):
        return (lax.axis_index(self.axis) // bit) % 2 > 0

    def step(self, under_way=None):
        if self.got is not None:
            got, bit, end = self.got
            self.got = None
            end(got if under_way is None else self.ring.then(got, under_way), bit)
        if self.stages:
            start, end, bit = self.stages.pop(0)
            self.got = (swapped(start(bit), self.axis, bit), bit, end)
        return self.values

    def run(self, under_way=None):
        while self.stages or self.got is not None:
            self.step(under_way)
        return self.values

    def start_half(self, bit):
        half = self.values.shape[0] // 2
        kept, sent = [
            jnp.where(self.upper(bit) == side, self.values[half:], self.values[:half])
            for side in (True, False)
        ]
        self.values = kept
        return sent.astype(bf16)

    def end_half(self, got, bit):
        self.values = self.values.astype(f32) + got.astype(f32)

    def start_join(self, bit):
        return self.values

    def end_join(self, got, bit):
        upper, own = self.upper(bit), self.values
        self.values = jnp.concatenate([jnp.where(upper, got, own), jnp.where(upper, own, got)], 0)

    def end_sum(self, got, bit):
        self.values = self.values + got

    def halving(self):
        return [(self.start_half, self.end_half, bit) for bit in self.bits]

    def joining(self):
        return [(self.start_join, self.end_join, bit) for bit in reversed(self.bits)]


class Halves(Exchange):
    def plan(self):
        return self.halving()


class Joined(Exchange):
    def plan(self):
        return self.joining()


class Everywhere(Exchange):
    def plan(self):
        stages = self.halving() + self.joining()
        middle = len(self.bits)

        def start_first_join(bit):
            self.values = self.values.astype(bf16)
            return self.values

        if stages:
            stages[middle] = (start_first_join, self.end_join, stages[middle][2])
        return stages


class SmallSum(Exchange):
    def plan(self):
        return [(self.start_join, self.end_sum, bit) for bit in self.bits]


def own_rows(values):
    count, mine = lax.axis_size("fsdp"), lax.axis_index("fsdp")
    bit = 1
    while bit < count:
        half = values.shape[0] // 2
        values = lax.dynamic_slice_in_dim(values, ((mine // bit) % 2) * half, half, 0)
        bit *= 2
    return values


def halves_joined(own):
    count, mine = lax.axis_size("fsdp"), lax.axis_index("fsdp")
    bit = count // 2
    while bit:
        got = lax.ppermute(own, "fsdp", [(i, i ^ bit) for i in range(count)])
        upper = (mine // bit) % 2 > 0
        own = jnp.concatenate([jnp.where(upper, got, own), jnp.where(upper, own, got)], 0)
        bit //= 2
    return own


def passed_along(block, distance):
    devices = range(lax.axis_size("seq"))
    route = [(i - distance, i) for i in devices if i - distance in devices]
    return lax.ppermute(block, "seq", route)


def joined_maps(earlier, later):
    return jnp.stack([earlier[0] * later[0], later[1] + later[0] * earlier[1]], 0)


class Entry:
    def __init__(self, prods, states, sign):
        self.pair, self.sign = jnp.stack([prods, states], 0), sign
        self.count = lax.axis_size("seq")
        self.direct = self.count <= ring_limit and self.count % 2 == 0
        if self.direct:
            self.other = swapped(self.pair, "seq", 1)

    def between(self, hold):
        if not self.direct:
            return
        self.other = hold(self.other)
        self.second = lax.axis_index("seq") % 2 == (1 if self.sign > 0 else 0)
        earlier = jnp.where(self.second, self.other, self.pair)
        later = jnp.where(self.second, self.pair, self.other)
        both = joined_maps(earlier, later)
        self.parts = [
            passed_along(both, self.sign * distance) for distance in range(self.count - 2, 0, -2)
        ]

    def state(self, hold):
        if self.direct:
            parts = [hold(self.parts[0])] + self.parts[1:]
            state = parts[0][1]
            for part in parts[1:]:
                state = part[1] + part[0] * state
            return jnp.where(self.second, self.other[1] + self.other[0] * state, state)
        pair = passed_along(self.pair, self.sign)
        distance = 1
        while distance < self.count:
            pair = joined_maps(passed_along(pair, self.sign * distance), pair)
            distance *= 2
        return pair[1]


def ring_index(place, count):
    place = lax.rem(place + 2 * count, count)
    odd = place // (count // 2)
    return (1 - odd) * (2 * place) + odd * (2 * count - 1 - 2 * place)


def ring_place(index, count):
    odd = lax.rem(index, 2)
    return (1 - odd) * (index // 2) + odd * (count - 1 - index // 2)


def partner(index, bit):
    return index + bit * (1 - 2 * lax.rem(index // bit, 2))


class Copies:
    def __init__(self, send_sems, recv_sems):
        self.send_sems, self.recv_sems = send_sems, recv_sems
        self.started = []

    def start(self, source, target, device):
        slot = len(self.started)
        copy = pltpu.make_async_remote_copy(
            src_ref=source,
            dst_ref=target,
            send_sem=self.send_sems.at[slot],
            recv_sem=self.recv_sems.at[slot],
            device_id=device,
            device_id_type=pl.DeviceIdType.MESH,
        )
        copy.start()
        self.started.append(copy)
        return copy

    def end(self):
        for copy in self.started:
            copy.wait_send()


def greet(devices):
    barrier = pltpu.get_barrier_semaphore()
    for device in devices:
        pl.semaphore_signal(
            barrier, inc=1, device_id=device, device_id_type=pl.DeviceIdType.MESH
        )
    pl.semaphore_wait(barrier, len(devices))


tail_copies = 28 + 4 + 6 + 3 + 5


def tail_body(
    count,
    emb_ref,
    mixed_ref,
    normed_ref,
    branch_ref,
    inner_ref,
    branch_all_ref,
    inner_all_ref,
    values_ref,
    grad_ref,
    gain_ref,
    gain_two_ref,
    small_ref,
    blocks_ref,
    branch_out,
    inner_out,
    out_out,
    tokens_out,
    gains_out,
    small_out,
    blocks_out,
    wide_sent,
    wide_got,
    slim_sent,
    slim_got,
    half_sent,
    half_kept,
    half_got,
    own_sent,
    own_got,
    small_sums,
    small_got,
    gain_sums,
    gain_got,
    blocks_one,
    blocks_two,
    blocks_got_one,
    blocks_got_two,
    blocks_got_three,
    send_sems,
    recv_sems,
):
    index, unit = lax.axis_index("seq"), lax.axis_index("fsdp")
    place = ring_place(index, count)
    forth, back = {"seq": ring_index(place + 1, count)}, {"seq": ring_index(place - 1, count)}
    across = [{"seq": partner(index, bit)} for bit in (1, 2, 4)]
    beside = [{"fsdp": partner(unit, bit)} for bit in (1, 2)]
    copies = Copies(send_sems, recv_sems)
    slab = normed_ref.shape[0] // count
    half = slab // 2
    last = count - 1

    greet([forth, back] + across + beside)

    bits = [lax.rem(index // bit, 2) for bit in (1, 2, 4)]
    high = blocks_ref.shape[0]
    firsts = [high // 2, high // 4, high // 8]

    def rows_at(start, size):
        return pl.ds(pl.multiple_of(start, 16), size)

    blocks_copy = copies.start(
        blocks_ref.at[rows_at((1 - bits[0]) * firsts[0], firsts[0])], blocks_got_one, across[0]
    )
    small_sums[0] = small_ref[...]
    small_copy = copies.start(small_sums.at[0], small_got.at[0], across[0])

    def out_term(k, way):
        start = k * slab + way * half
        return jnp.dot(
            emb_ref[start : start + half, :], mixed_ref[...], preferred_element_type=f32
        )

    def front_term(k, way):
        right = inner_ref if way else branch_ref
        return jnp.dot(
            normed_ref[k * slab : (k + 1) * slab, :], right[...], preferred_element_type=f32
        )

    rings = {}

    def send(name, way, step, total):
        sent, got = (slim_sent, slim_got) if name == "out" else (wide_sent, wide_got)
        sent[way, step] = total.astype(bf16)
        rings[name, way] = copies.start(
            sent.at[way, step], got.at[way, step], back if way else forth
        )

    def term(name, way, step):
        k = (count - step) % count if way else step % count
        return out_term(k, way) if name == "out" else front_term(k, way)

    def serve(name, step):
        got = slim_got if name == "out" else wide_got
        for way in (0, 1):
            own = term(name, way, step)
            rings[name, way].wait_recv()
            total = got[way, step - 2].astype(f32) + own
            if step < count:
                send(name, way, step - 1, total)
            elif name == "out":
                out_out[way * half : (way + 1) * half, :] = total
            else:
                (inner_out if way else branch_out)[...] = total

    for name in ("out", "front"):
        for way in (0, 1):
            send(name, way, 0, term(name, way, 1))

    core, side = lax.rem(unit, 2), lax.rem(unit // 2, 2)
    rows = branch_ref.shape[0]
    mid, own = rows // 2, rows // 4

    def front_back(start, k):
        nt = (((1,), (1,)), ((), ()))
        columns = slice(k * slab, (k + 1) * slab)
        return lax.dot_general(
            branch_ref[rows_at(start, mid), :],
            branch_all_ref[columns, :],
            nt,
            preferred_element_type=f32,
        ) + lax.dot_general(
            inner_ref[rows_at(start, mid), :],
            inner_all_ref[columns, :],
            nt,
            preferred_element_type=f32,
        )

    for k in range(count):
        half_sent[:, k * slab : (k + 1) * slab] = front_back((1 - core) * mid, k).astype(bf16)
    half_copy = copies.start(half_sent, half_got, beside[0])
    serve("out", 2)
    for k in range(count):
        half_kept[:, k * slab : (k + 1) * slab] = front_back(core * mid, k)
    half_copy.wait_recv()
    other = rows_at((1 - side) * own, own)
    mine = rows_at(side * own, own)
    own_sent[...] = (half_kept[other, :] + half_got[other, :].astype(f32)).astype(bf16)
    own_copy = copies.start(own_sent, own_got, beside[1])
    serve("front", 2)

    blocks_copy.wait_recv()
    blocks_one[...] = (
        blocks_ref[rows_at(bits[0] * firsts[0], firsts[0]), :].astype(f32)
        + blocks_got_one[...].astype(f32)
    ).astype(bf16)
    blocks_copy = copies.start(
        blocks_one.at[rows_at((1 - bits[1]) * firsts[1], firsts[1])], blocks_got_two, across[1]
    )
    small_copy.wait_recv()
    small_sums[1] = small_sums[0] + small_got[0]
    small_copy = copies.start(small_sums.at[1], small_got.at[1], across[1])
    serve("out", 3)
    serve("front", 3)

    own_copy.wait_recv()
    values = values_ref[...]
    scale = lax.rsqrt(jnp.mean(values * values, axis=-1, keepdims=True) + eps)
    unit_values = values * scale
    front = half_kept[mine, :] + half_got[mine, :].astype(f32) + own_got[...].astype(f32)
    gain_grad = jnp.sum(front * unit_values, 0, keepdims=True)
    weighted = front * gain_ref[...]
    result = grad_ref[...] + scale * (
        weighted - unit_values * jnp.mean(weighted * unit_values, axis=-1, keepdims=True)
    )
    low = result.astype(bf16)
    own_at = rows_at(core * mid + side * own, own)
    gain_sums[0] = jnp.zeros_like(gain_sums[0])
    for k in range(count):
        to = pl.ds(pl.multiple_of(ring_index(place - k, count) * slab, slab), slab)
        part = slice(k * slab, (k + 1) * slab)
        tokens_out[own_at, to] = low[:, part]
        gain_sums[0, 0:1, to] = gain_grad[:, part]
        gain_sums[0, 1:2, to] = gain_two_ref[:, part]
    tokens_copy = copies.start(tokens_out.at[own_at], tokens_out.at[own_at], beside[1])
    gain_copy = copies.start(gain_sums.at[0], gain_got.at[0], across[0])
    serve("out", 4)
    serve("front", 4)

    blocks_copy.wait_recv()
    blocks_two[...] = (
        blocks_one[rows_at(bits[1] * firsts[1], firsts[1]), :].astype(f32)
        + blocks_got_two[...].astype(f32)
    ).astype(bf16)
    blocks_copy = copies.start(
        blocks_two.at[rows_at((1 - bits[2]) * firsts[2], firsts[2])], blocks_got_three, across[2]
    )
    small_copy.wait_recv()
    small_sums[2] = small_sums[1] + small_got[1]
    small_copy = copies.start(small_sums.at[2], small_got.at[2], across[2])
    gain_copy.wait_recv()
    gain_sums[1] = gain_sums[0] + gain_got[0]
    gain_copy = copies.start(gain_sums.at[1], gain_got.at[1], across[1])
    tokens_copy.wait_recv()
    both_at = rows_at(core * mid, mid)
    tokens_copy = copies.start(tokens_out.at[both_at], tokens_out.at[both_at], beside[0])
    serve("out", 5)
    serve("front", 5)

    blocks_copy.wait_recv()
    starts = [bits[0] * firsts[0]]
    for bit, first in zip(bits[1:], firsts[1:]):
        starts.append(starts[-1] + bit * first)
    at = [rows_at(start, first) for start, first in zip(starts, firsts)]
    blocks_out[at[2], :] = (
        blocks_two[rows_at(bits[2] * firsts[2], firsts[2]), :].astype(f32)
        + blocks_got_three[...].astype(f32)
    ).astype(bf16)
    blocks_copy = copies.start(blocks_out.at[at[2]], blocks_out.at[at[2]], across[2])
    gain_copy.wait_recv()
    gain_sums[2] = gain_sums[1] + gain_got[1]
    gain_copy = copies.start(gain_sums.at[2], gain_got.at[2], across[2])
    small_copy.wait_recv()
    small_out[...] = small_sums[2] + small_got[2]
    serve("out", 6)
    serve("front", 6)

    blocks_copy.wait_recv()
    blocks_copy = copies.start(blocks_out.at[at[1]], blocks_out.at[at[1]], across[1])
    gain_copy.wait_recv()
    gain_sums[3] = gain_sums[2] + gain_got[2]
    gain_copy = copies.start(gain_sums.at[3], gain_got.at[3], beside[0])
    serve("out", 7)
    gain_copy.wait_recv()
    gain_sums[4] = gain_sums[3] + gain_got[3]
    gain_copy = copies.start(gain_sums.at[4], gain_got.at[4], beside[1])
    serve("front", 7)
    blocks_copy.wait_recv()
    blocks_copy = copies.start(blocks_out.at[at[0]], blocks_out.at[at[0]], across[0])
    serve("out", 8)
    gain_copy.wait_recv()
    gains_out[...] = gain_sums[4] + gain_got[4]
    tokens_copy.wait_recv()
    blocks_copy.wait_recv()
    serve("front", 8)
    copies.end()


def tail(count, *operands, earlier):
    operands = lax.optimization_barrier((*operands, *earlier))[: len(operands)]
    emb, mixed, normed, *_ = operands
    small, blocks = operands[-2:]
    width, rows = emb.shape
    units = mixed.shape[1]
    slab = width // count
    high, block_width = blocks.shape
    whole = pl.BlockSpec(memory_space=pltpu.VMEM)
    grad = jax.ShapeDtypeStruct((slab, units), f32)
    steps = count - 1
    return pl.pallas_call(
        functools.partial(tail_body, count),
        out_shape=(
            grad,
            grad,
            grad,
            jax.ShapeDtypeStruct((rows, width), bf16),
            jax.ShapeDtypeStruct((8, width), f32),
            jax.ShapeDtypeStruct(small.shape, f32),
            jax.ShapeDtypeStruct(blocks.shape, bf16),
        ),
        in_specs=[whole] * len(operands),
        out_specs=(whole,) * 7,
        scratch_shapes=[
            pltpu.VMEM((2, steps, slab, units), bf16),
            pltpu.VMEM((2, steps, slab, units), bf16),
            pltpu.VMEM((2, steps, slab // 2, units), bf16),
            pltpu.VMEM((2, steps, slab // 2, units), bf16),
            pltpu.VMEM((rows // 2, width), bf16),
            pltpu.VMEM((rows // 2, width), f32),
            pltpu.VMEM((rows // 2, width), bf16),
            pltpu.VMEM((rows // 4, width), bf16),
            pltpu.VMEM((rows // 4, width), bf16),
            pltpu.VMEM((3, *small.shape), f32),
            pltpu.VMEM((3, *small.shape), f32),
            pltpu.VMEM((5, 8, width), f32),
            pltpu.VMEM((5, 8, width), f32),
            pltpu.VMEM((high // 2, block_width), bf16),
            pltpu.VMEM((high // 4, block_width), bf16),
            pltpu.VMEM((high // 2, block_width), bf16),
            pltpu.VMEM((high // 4, block_width), bf16),
            pltpu.VMEM((high // 8, block_width), bf16),
            pltpu.SemaphoreType.DMA((tail_copies,)),
            pltpu.SemaphoreType.DMA((tail_copies,)),
        ],
        compiler_params=pltpu.CompilerParams(
            collective_id=0, has_side_effects=True, vmem_limit_bytes=60 * 1024 * 1024
        ),
    )(*operands)


def block_diagonal(blocks):
    count, width = blocks.shape[0], blocks.shape[1]
    return sum(
        jnp.pad(blocks[j], ((j * width, (count - 1 - j) * width),) * 2) for j in range(count)
    )


def rows_joined(slab_pairs):
    return jnp.concatenate([part for pair in zip(*slab_pairs) for part in pair], 0)


def diagonal_blocks(square, count):
    width = square.shape[0] // count
    return jnp.stack(
        [square[j * width : (j + 1) * width, j * width : (j + 1) * width] for j in range(count)], 0
    )


def local(
    tokens,
    resets,
    norm_gain,
    branch_weight,
    inner_weight,
    conv_weight,
    conv_bias,
    gate_blocks,
    input_blocks,
    gate_bias,
    input_bias,
    decay_param,
    out_weight,
    mlp_norm_gain,
    gate_weight,
    up_weight,
    down_weight,
    cotangent,
):
    count = lax.axis_size("seq")
    batches, length, width = tokens.shape
    slab = width // count
    units, hidden = conv_bias.shape[0], down_weight.shape[0]
    rows = batches * length
    ringed = count <= ring_limit
    half = slab // 2
    out_turned, down_turned = out_weight.T, down_weight.T
    ring = Ring(count)
    if ringed:
        gather, scatter = functools.partial(Gather, ring), functools.partial(Scatter, ring)
        to_ring, to_plain = ring.tables()

        def moved(values, dtype):
            return move_slabs(values, to_ring, dtype)

        def restored(values, dtype):
            return move_slabs(values, to_plain, dtype)

        def gain_moved(gain):
            return gain.reshape(count, slab)[to_ring].reshape(width)

        def gain_restored(gain):
            return gain.reshape(count, slab)[to_plain].reshape(width)

    else:
        gather, scatter = functools.partial(PlainGather, ring), functools.partial(PlainScatter, ring)

        def moved(values, dtype):
            return values.astype(dtype)

        restored = moved

        def gain_moved(gain):
            return gain

        gain_restored = gain_moved

    def slab_dots(turned, right, first=0, rows=slab):
        def term(k):
            start = k * slab + first
            return dot_nn(turned[start : start + rows], right)

        return term

    steps = count - 1
    front_weights = gather(branch_weight, inner_weight)
    out_weights = gather(out_turned[:half], out_turned[half:])
    mlp_weights = gather(gate_weight, up_weight)
    down_weights = gather(down_turned[:half], down_turned[half:])
    in_turn(front_weights, out_weights)
    tokens_low = moved(tokens.reshape(rows, width), bf16)
    ring.first(tokens_low)
    in_turn(front_weights, out_weights)
    gain_one = gain_moved(norm_gain.astype(f32))
    gain_two = gain_moved(mlp_norm_gain.astype(f32))
    values = ring.then(tokens_low, 2).astype(f32)
    normed = (values * inverse_rms(values) * gain_one).astype(bf16)
    ring.first(normed)
    in_turn(front_weights, out_weights)
    gate_square, input_square = block_diagonal(gate_blocks), block_diagonal(input_blocks)
    ring.first(gate_square, input_square)
    in_turn(front_weights, out_weights)
    cot_low = moved(ring.then(cotangent, 2).reshape(rows, width), bf16)
    ring.first(cot_low)
    for _ in range(steps - 4):
        in_turn(front_weights, out_weights)
    branch_all, inner_all = (jnp.concatenate(slabs, 0) for slabs in front_weights.slabs())
    out_all = rows_joined(out_weights.slabs())

    taps = conv_weight.astype(f32)
    decay = decay_param.astype(f32)
    fresh_start = resets[:, :, None] > 0
    in_turn(mlp_weights)
    inner_low = dot_nn(normed, inner_all).astype(bf16).reshape(batches, length, units)
    branch_pre = dot_nn(normed, branch_all).reshape(batches, length, units)
    edge_rows = passed_along(inner_low[:, -3:], 1)
    ring.first(inner_low, branch_pre)
    in_turn(down_weights)
    padded = jnp.concatenate([ring.then(edge_rows, 2), inner_low], 1).astype(f32)
    conv_sum = conv_bias.astype(f32) + taps[0] * padded[:, 3:] + taps[1] * padded[:, 2:-1]
    conv_sum = conv_sum + taps[2] * padded[:, 1:-2] + taps[3] * padded[:, :-3]
    conv_low = conv_sum.astype(bf16)
    conv_flat = conv_low.reshape(rows, units)
    gate_pre = dot_nn(conv_flat, gate_square).reshape(batches, length, units)
    gate_pre = gate_pre + gate_bias.astype(f32)
    input_pre = dot_nn(conv_flat, input_square).reshape(batches, length, units)
    input_pre = input_pre + input_bias.astype(f32)
    conv_value = conv_low.astype(f32)

    def gates(gate_pre, input_pre, conv_value, decay):
        return gate_math(gate_pre, input_pre, conv_value, decay, fresh_start)

    carries, drives = gates(gate_pre, input_pre, conv_value, decay)
    ring.first(carries, drives)
    in_turn(mlp_weights)
    prods, local_state = local_scan(ring.then(carries, 2), drives, False)
    entry = Entry(prods[:, -1:], local_state[:, -1:], 1)
    ring.first(prods)
    in_turn(down_weights)
    entry.between(ring.then)
    in_turn(mlp_weights)
    state_in = entry.state(lambda part: ring.then(part, 1))
    ring.first(state_in)
    in_turn(down_weights)
    states = local_state + prods * ring.then(state_in, 2)

    branch, branch_pull = jax.vjp(gelu_tanh, branch_pre)
    mixed_low = (states * branch).astype(bf16).reshape(rows, units)
    middle_sum = Halves(ring, dot_nt(mixed_low, out_all), "fsdp")
    middle_sum.step()
    ring.first(middle_sum.step())
    in_turn(mlp_weights, down_weights)
    own_middle = own_rows(tokens_low).astype(f32) + middle_sum.run(2)
    scale_two = inverse_rms(own_middle)
    unit_two = own_middle * scale_two
    normed_join = Joined(ring, (unit_two * gain_two).astype(bf16), "fsdp")
    ring.first(normed_join.step())
    in_turn(mlp_weights)
    normed_join.step(1)
    normed_two = normed_join.run()
    ring.first(normed_two)
    in_turn(down_weights, mlp_weights)
    in_turn(*[mlp_weights] * (steps - 6), *[down_weights] * (steps - 5))
    gate_all, up_all = (jnp.concatenate(slabs, 0) for slabs in mlp_weights.slabs())
    down_all = rows_joined(down_weights.slabs())

    gate_mlp = dot_nn(normed_two, gate_all)
    up_mlp = dot_nn(normed_two, up_all)
    activated, act_pull = jax.vjp(gated_product, gate_mlp, up_mlp)
    hidden_low = activated.astype(bf16)
    down_grads = scatter(
        slab_dots(cot_low.T, hidden_low, 0, half), slab_dots(cot_low.T, hidden_low, half, half)
    )
    in_turn(down_grads)
    grad_gate_mlp, grad_up_mlp = act_pull(dot_nn(ring.then(cot_low, 0), down_all))
    gate_mlp_low, up_mlp_low = grad_gate_mlp.astype(bf16), grad_up_mlp.astype(bf16)
    in_turn(down_grads)
    ring.first(gate_mlp_low, up_mlp_low)
    in_turn(down_grads)
    mlp_grads = scatter(
        slab_dots(normed_two.T, gate_mlp_low), slab_dots(normed_two.T, up_mlp_low)
    )
    in_turn(mlp_grads, down_grads)
    gate_mlp_low, up_mlp_low = lax.optimization_barrier(
        (ring.then(gate_mlp_low, 2), up_mlp_low)
    )
    back_sum = Halves(
        ring, dot_nt(gate_mlp_low, gate_all) + dot_nt(up_mlp_low, up_all), "fsdp"
    )
    back_sum.step()
    ring.first(back_sum.step())
    in_turn(mlp_grads, down_grads)
    own_back = back_sum.run(2)
    gain_two_grad = jnp.sum(own_back * unit_two, 0)
    weighted = own_back * gain_two
    own_grad = own_rows(cot_low).astype(f32) + scale_two * (
        weighted - unit_two * jnp.mean(weighted * unit_two, axis=-1, keepdims=True)
    )
    middle_join = Joined(ring, own_grad.astype(bf16), "fsdp")
    ring.first(middle_join.step())
    in_turn(mlp_grads)
    mixed_sum = Halves(ring, dot_nt(ring.then(hidden_low, 2), down_all), "fsdp")
    mixed_sum.step()
    ring.first(mixed_sum.step())
    in_turn(down_grads)
    middle_join.step(2)
    middle_low = middle_join.run()

    grad_mixed = dot_nn(middle_low, out_all).reshape(batches, length, units)
    (grad_branch_pre,) = branch_pull(grad_mixed * states)
    branch_low = grad_branch_pre.astype(bf16).reshape(rows, units)
    following = jnp.concatenate([carries[:, 1:], jnp.ones_like(carries[:, :1])], 1)
    tail_prods, local_adjoint = local_scan(following, grad_mixed * branch, True)
    entry = Entry(prods[:, -1:], carries[:, :1] * local_adjoint[:, :1], -1)
    ring.first(local_adjoint, branch_low)
    in_turn(mlp_grads)
    entry.between(ring.then)
    in_turn(down_grads)
    adjoint_in = entry.state(lambda part: ring.then(part, 1))
    adjoint = local_adjoint + tail_prods * adjoint_in
    state_before = jnp.concatenate([state_in, states[:, :-1]], 1)
    _, gate_pull = jax.vjp(gates, gate_pre, input_pre, conv_value, decay)
    grad_gate_pre, grad_input_pre, grad_conv, decay_grad = gate_pull(
        (adjoint * state_before, adjoint)
    )
    gate_low = grad_gate_pre.astype(bf16).reshape(rows, units)
    input_low = grad_input_pre.astype(bf16).reshape(rows, units)
    ring.first(gate_low, input_low)
    in_turn(mlp_grads)
    back_conv = dot_nt(gate_low, gate_square) + dot_nt(input_low, input_square)
    grad_conv = grad_conv + back_conv.reshape(batches, length, units)

    border = jnp.zeros((batches, 3, units), f32)
    spread = jnp.concatenate([border, grad_conv, border], 1)
    stop = length + 3
    grad_padded = taps[0] * spread[:, :stop] + taps[1] * spread[:, 1 : stop + 1]
    grad_padded = grad_padded + taps[2] * spread[:, 2 : stop + 2] + taps[3] * spread[:, 3:]
    returned = passed_along(grad_padded[:, :3], -1)
    mixed_join = Joined(ring, restored(own_middle + mixed_sum.run(1), bf16), "fsdp")
    ring.first(grad_padded, mixed_join.step())
    in_turn(mlp_grads)
    grad_inner = jnp.concatenate(
        [grad_padded[:, 3:-3], grad_padded[:, -3:] + ring.then(returned)], 1
    )
    inner_grad_low = grad_inner.astype(bf16).reshape(rows, units)
    in_turn(*[mlp_grads] * (steps - 6))

    block_count = gate_blocks.shape[0]
    block_grads = jnp.concatenate(
        [
            diagonal_blocks(dot_tn(conv_flat, gate_low), block_count),
            diagonal_blocks(dot_tn(conv_flat, input_low), block_count),
        ],
        0,
    )
    block_width = block_grads.shape[-1]
    taps_grad = jnp.stack(
        [jnp.sum(grad_conv * padded[:, 3 - k : 3 - k + length], (0, 1)) for k in range(4)], 0
    )
    small = jnp.concatenate(
        [
            taps_grad,
            jnp.sum(grad_conv, (0, 1))[None],
            jnp.sum(gate_low.astype(f32), 0)[None],
            jnp.sum(input_low.astype(f32), 0)[None],
            decay_grad[None],
        ],
        0,
    )
    mixed_join.step()
    mixed = mixed_join.run().astype(f32).reshape(tokens.shape)
    gate_grad, up_grad = mlp_grads.sums()
    own_values = own_rows(tokens_low).astype(f32)
    if ringed:
        branch_grad, inner_grad, out_grad, tokens_grad, gains, small, block_grads = tail(
            count,
            middle_low.T,
            mixed_low,
            normed.T,
            branch_low,
            inner_grad_low,
            branch_all,
            inner_all,
            own_values,
            own_grad,
            gain_one[None],
            gain_two_grad[None],
            small,
            block_grads.reshape(-1, block_width).astype(bf16),
            earlier=(gate_grad, up_grad, mixed),
        )
        block_grads = block_grads.astype(f32)
    else:
        out_grads = scatter(
            slab_dots(middle_low.T, mixed_low, 0, half),
            slab_dots(middle_low.T, mixed_low, half, half),
        )
        front_grads = scatter(
            slab_dots(normed.T, branch_low), slab_dots(normed.T, inner_grad_low)
        )
        branch_grad, inner_grad = front_grads.sums()
        out_grad = jnp.concatenate(out_grads.sums(), 0)
        own_front = Halves(
            ring, dot_nt(branch_low, branch_all) + dot_nt(inner_grad_low, inner_all), "fsdp"
        ).run()
        scale_one = inverse_rms(own_values)
        unit_one = own_values * scale_one
        weighted = own_front * gain_one
        own_tokens = own_grad + scale_one * (
            weighted - unit_one * jnp.mean(weighted * unit_one, axis=-1, keepdims=True)
        )
        gains = jnp.stack([jnp.sum(own_front * unit_one, 0), gain_two_grad], 0)
        gains = lax.psum(gains, ("seq", "fsdp"))
        small, block_grads = lax.psum((small, block_grads), "seq")
        tokens_grad = Joined(ring, own_tokens.astype(bf16), "fsdp").run()
    tokens_grad = tokens_grad.astype(f32).reshape(tokens.shape)
    block_grads = block_grads.reshape(2, block_count, block_width, block_width)
    down_grad = jnp.concatenate(down_grads.sums(), 0)
    return (
        mixed,
        tokens_grad,
        gains[0],
        branch_grad,
        inner_grad,
        small[:4],
        small[4],
        block_grads[0],
        block_grads[1],
        small[5],
        small[6],
        small[7],
        out_grad.T,
        gains[1],
        gate_grad,
        up_grad,
        down_grad.T,
    )


def solution(mesh):
    units, both = P("fsdp"), P("seq", "fsdp")
    blocks, turned = P("fsdp", None, None), P("fsdp", "seq")
    rows = P(None, "seq", None)
    return jax.shard_map(
        local,
        mesh=mesh,
        in_specs=(
            rows,
            P(None, "seq"),
            P(),
            both,
            both,
            P(None, "fsdp"),
            units,
            blocks,
            blocks,
            units,
            units,
            units,
            turned,
            P(),
            both,
            both,
            turned,
            rows,
        ),
        out_specs=(
            rows,
            rows,
            P(),
            both,
            both,
            P(None, "fsdp"),
            units,
            blocks,
            blocks,
            units,
            units,
            units,
            turned,
            P(),
            both,
            both,
            turned,
        ),
        check_vma=False,
    )
```

```python
import functools

import jax
import jax.numpy as jnp
from jax import lax
from jax.experimental import pallas as pl
from jax.experimental.pallas import tpu as pltpu
from jax.sharding import PartitionSpec as P

eps = 1e-06
decay_scale = 8.0
f32 = jnp.float32
bf16 = jnp.bfloat16
ring_count = 8


def gelu_tanh(values):
    return jax.nn.gelu(values, approximate=True)


def gated_product(gate_pre, up_pre):
    return gelu_tanh(gate_pre) * up_pre


def gate_math(gate_pre, input_pre, conv_value, decay_param, fresh_start):
    rate_gate = jax.nn.sigmoid(gate_pre)
    inlet_gate = jax.nn.sigmoid(input_pre)
    log_decay = -decay_scale * jax.nn.softplus(-decay_param) * rate_gate
    input_scale = jnp.where(fresh_start, 1.0, jnp.sqrt(-jnp.expm1(2.0 * log_decay)))
    carries = jnp.where(fresh_start, 0.0, jnp.exp(log_decay))
    return (carries, input_scale * inlet_gate * conv_value)


def dot_nn(left, right):
    return jnp.dot(left, right, preferred_element_type=f32)


def dot_nt(left, right):
    return lax.dot_general(left, right, (((1,), (1,)), ((), ())), preferred_element_type=f32)


def dot_tn(left, right):
    return lax.dot_general(left, right, (((0,), (0,)), ((), ())), preferred_element_type=f32)


def inverse_rms(values):
    return lax.rsqrt(jnp.mean(values * values, axis=-1, keepdims=True) + eps)


def scan_body(backward, a_ref, b_ref, prod_ref, state_ref):
    batches, length, units = a_ref.shape
    tiles = length // 8
    rows = lax.broadcasted_iota(jnp.int32, (8, units), 0)

    def step(index, carry):
        tile = tiles - 1 - index if backward else index
        where_rows = pl.ds(pl.multiple_of(tile * 8, 8), 8)
        following = []
        for batch in range(batches):
            prod_in, state_in = carry[batch]
            a = a_ref[batch, where_rows, :]
            b = b_ref[batch, where_rows, :]
            for shift in (1, 2, 4):
                turn = 8 - shift if backward else shift
                inside = rows < 8 - shift if backward else rows >= shift
                a_moved = jnp.where(inside, pltpu.roll(a, turn, 0), 1.0)
                b_moved = jnp.where(inside, pltpu.roll(b, turn, 0), 0.0)
                b = a * b_moved + b
                a = a * a_moved
            b = b + a * state_in
            a = a * prod_in
            prod_ref[batch, where_rows, :] = a
            state_ref[batch, where_rows, :] = b
            edge = 0 if backward else 7
            following.append((a[edge : edge + 1], b[edge : edge + 1]))
        return tuple(following)

    first = tuple(
        (jnp.ones((1, units), f32), jnp.zeros((1, units), f32)) for _ in range(batches)
    )
    lax.fori_loop(0, tiles, step, first)


def local_scan(a, b, backward):
    shape = jax.ShapeDtypeStruct(a.shape, f32)
    elements = a.shape[0] * a.shape[1] * a.shape[2]
    return pl.pallas_call(
        functools.partial(scan_body, backward),
        out_shape=(shape, shape),
        in_specs=[pl.BlockSpec(memory_space=pltpu.VMEM)] * 2,
        out_specs=(pl.BlockSpec(memory_space=pltpu.VMEM),) * 2,
        compiler_params=pltpu.CompilerParams(vmem_limit_bytes=32 * 1024 * 1024),
        cost_estimate=pl.CostEstimate(
            flops=20 * elements, bytes_accessed=16 * elements, transcendentals=0
        ),
    )(a, b)


def move_body(table_ref, in_ref, out_ref):
    out_ref[...] = in_ref[...].astype(out_ref.dtype)


def move_slabs(values, table, dtype):
    rows, width = values.shape
    slabs = table.shape[0]
    return pl.pallas_call(
        move_body,
        out_shape=jax.ShapeDtypeStruct((rows, width), dtype),
        grid_spec=pltpu.PrefetchScalarGridSpec(
            num_scalar_prefetch=1,
            grid=(slabs,),
            in_specs=[pl.BlockSpec((rows, width // slabs), lambda k, where: (0, where[k]))],
            out_specs=pl.BlockSpec((rows, width // slabs), lambda k, where: (0, k)),
        ),
        cost_estimate=pl.CostEstimate(
            flops=0, bytes_accessed=8 * rows * width, transcendentals=0
        ),
    )(table, values)


class Ring:
    def __init__(self, count):
        self.count = count
        self.order = list(range(0, count, 2)) + list(range(count - 1, 0, -2))
        self.place = [self.order.index(i) for i in range(count)]
        self.forth = [(self.order[i], self.order[(i + 1) % count]) for i in range(count)]
        self.back = [(there, here) for here, there in self.forth]
        self.sent, self.awaited = [], []

    def tables(self):
        here = jnp.asarray(self.place, jnp.int32)[lax.axis_index("seq")]
        steps = jnp.arange(self.count, dtype=jnp.int32)
        to_ring = jnp.asarray(self.order, jnp.int32)[(here - steps) % self.count]
        to_plain = (here - jnp.asarray(self.place, jnp.int32)) % self.count
        return to_ring, to_plain

    def send(self, forth, back):
        earlier = list(self.sent[-2]) if len(self.sent) > 1 else []
        if earlier or self.awaited:
            forth, back = lax.optimization_barrier((forth, back, *earlier, *self.awaited))[:2]
        self.awaited = []
        self.sent.append(
            (lax.ppermute(forth, "seq", self.forth), lax.ppermute(back, "seq", self.back))
        )
        return self.sent[-1]

    def first(self, *values):
        self.awaited.extend(values)

    def then(self, value, under_way=1):
        if len(self.sent) <= under_way:
            return value
        return lax.optimization_barrier((value, *self.sent[-1 - under_way]))[0]


class Gather:
    def __init__(self, ring, forth, back):
        self.ring, self.forth, self.back = ring, [forth], [back]

    def step(self):
        forth, back = self.ring.send(self.forth[-1], self.back[-1])
        self.forth.append(forth)
        self.back.append(back)

    def slabs(self):
        count = self.ring.count
        return self.forth, [self.back[-k % count] for k in range(count)]


class Scatter:
    def __init__(self, ring, forth_slab, back_slab):
        self.ring, self.forth_slab, self.back_slab = ring, forth_slab, back_slab
        self.at = 1
        self.forth = forth_slab(1).astype(bf16)
        self.back = back_slab(ring.count - 1).astype(bf16)

    def step(self):
        count = self.ring.count
        forth, back = self.ring.send(self.forth, self.back)
        self.at += 1
        self.forth = forth.astype(f32) + self.forth_slab(self.at % count)
        self.back = back.astype(f32) + self.back_slab(count - self.at)
        if self.at < count:
            self.forth, self.back = self.forth.astype(bf16), self.back.astype(bf16)

    def sums(self):
        return self.forth, self.back


class PlainGather:
    def __init__(self, ring, forth, back):
        self.pieces = (forth, back)

    def step(self):
        pass

    def slabs(self):
        return tuple(list(lax.all_gather(piece, "seq")) for piece in self.pieces)


class PlainScatter:
    def __init__(self, ring, forth_slab, back_slab):
        self.terms = (forth_slab, back_slab)

    def step(self):
        pass

    def sums(self):
        count = lax.axis_size("seq")
        return tuple(
            lax.psum_scatter(
                jnp.concatenate([term(k) for k in range(count)], 0),
                "seq",
                scatter_dimension=0,
                tiled=True,
            )
            for term in self.terms
        )


def in_turn(*transfers):
    for transfer in transfers:
        transfer.step()


def swapped(values, axis, bit):
    return lax.ppermute(values, axis, [(i, i ^ bit) for i in range(lax.axis_size(axis))])


class Exchange:
    def __init__(self, ring, values, axis):
        self.ring, self.values, self.axis = ring, values, axis
        self.got = None
        count = lax.axis_size(axis)
        self.bits = [1 << i for i in range(count.bit_length() - 1)]
        self.stages = self.plan()

    def upper(self, bit):
        return (lax.axis_index(self.axis) // bit) % 2 > 0

    def step(self, under_way=None):
        if self.got is not None:
            got, bit, end = self.got
            self.got = None
            end(got if under_way is None else self.ring.then(got, under_way), bit)
        if self.stages:
            start, end, bit = self.stages.pop(0)
            self.got = (swapped(start(bit), self.axis, bit), bit, end)
        return self.values

    def run(self, under_way=None):
        while self.stages or self.got is not None:
            self.step(under_way)
        return self.values

    def start_half(self, bit):
        half = self.values.shape[0] // 2
        kept, sent = [
            jnp.where(self.upper(bit) == side, self.values[half:], self.values[:half])
            for side in (True, False)
        ]
        self.values = kept
        return sent.astype(bf16)

    def end_half(self, got, bit):
        self.values = self.values.astype(f32) + got.astype(f32)

    def start_join(self, bit):
        return self.values

    def end_join(self, got, bit):
        upper, own = self.upper(bit), self.values
        self.values = jnp.concatenate([jnp.where(upper, got, own), jnp.where(upper, own, got)], 0)

    def end_sum(self, got, bit):
        self.values = self.values + got

    def halving(self):
        return [(self.start_half, self.end_half, bit) for bit in self.bits]

    def joining(self):
        return [(self.start_join, self.end_join, bit) for bit in reversed(self.bits)]


class Halves(Exchange):
    def plan(self):
        return self.halving()


class Joined(Exchange):
    def plan(self):
        return self.joining()


class Everywhere(Exchange):
    def plan(self):
        stages = self.halving() + self.joining()
        middle = len(self.bits)

        def start_first_join(bit):
            self.values = self.values.astype(bf16)
            return self.values

        if stages:
            stages[middle] = (start_first_join, self.end_join, stages[middle][2])
        return stages


class SmallSum(Exchange):
    def plan(self):
        return [(self.start_join, self.end_sum, bit) for bit in self.bits]


def own_rows(values):
    count, mine = lax.axis_size("fsdp"), lax.axis_index("fsdp")
    bit = 1
    while bit < count:
        half = values.shape[0] // 2
        values = lax.dynamic_slice_in_dim(values, ((mine // bit) % 2) * half, half, 0)
        bit *= 2
    return values


def halves_joined(own):
    count, mine = lax.axis_size("fsdp"), lax.axis_index("fsdp")
    bit = count // 2
    while bit:
        got = lax.ppermute(own, "fsdp", [(i, i ^ bit) for i in range(count)])
        upper = (mine // bit) % 2 > 0
        own = jnp.concatenate([jnp.where(upper, got, own), jnp.where(upper, own, got)], 0)
        bit //= 2
    return own


def passed_along(block, distance):
    devices = range(lax.axis_size("seq"))
    route = [(i - distance, i) for i in devices if i - distance in devices]
    return lax.ppermute(block, "seq", route)


def joined_maps(earlier, later):
    return jnp.stack([earlier[0] * later[0], later[1] + later[0] * earlier[1]], 0)


class Entry:
    def __init__(self, prods, states, sign):
        self.pair, self.sign = jnp.stack([prods, states], 0), sign
        self.count = lax.axis_size("seq")
        self.direct = self.count == ring_count
        if self.direct:
            self.other = swapped(self.pair, "seq", 1)

    def between(self, hold):
        if not self.direct:
            return
        self.other = hold(self.other)
        self.second = lax.axis_index("seq") % 2 == (1 if self.sign > 0 else 0)
        earlier = jnp.where(self.second, self.other, self.pair)
        later = jnp.where(self.second, self.pair, self.other)
        both = joined_maps(earlier, later)
        self.parts = [
            passed_along(both, self.sign * distance) for distance in range(self.count - 2, 0, -2)
        ]

    def state(self, hold):
        if self.direct:
            parts = [hold(self.parts[0])] + self.parts[1:]
            state = parts[0][1]
            for part in parts[1:]:
                state = part[1] + part[0] * state
            return jnp.where(self.second, self.other[1] + self.other[0] * state, state)
        pair = passed_along(self.pair, self.sign)
        distance = 1
        while distance < self.count:
            pair = joined_maps(passed_along(pair, self.sign * distance), pair)
            distance *= 2
        return pair[1]


def ring_index(place, count):
    place = lax.rem(place + 2 * count, count)
    odd = place // (count // 2)
    return (1 - odd) * (2 * place) + odd * (2 * count - 1 - 2 * place)


def ring_place(index, count):
    odd = lax.rem(index, 2)
    return (1 - odd) * (index // 2) + odd * (count - 1 - index // 2)


def partner(index, bit):
    return index + bit * (1 - 2 * lax.rem(index // bit, 2))


class Copies:
    def __init__(self, send_sems, recv_sems):
        self.send_sems, self.recv_sems = send_sems, recv_sems
        self.started, self.waiting = 0, []

    def start(self, source, target, device):
        slot = self.started
        copy = pltpu.make_async_remote_copy(
            src_ref=source,
            dst_ref=target,
            send_sem=self.send_sems.at[slot],
            recv_sem=self.recv_sems.at[slot],
            device_id=device,
            device_id_type=pl.DeviceIdType.MESH,
        )
        copy.start()
        self.started += 1
        self.waiting.append(copy)
        return copy

    def sent(self, copy):
        copy.wait_send()
        self.waiting.remove(copy)

    def end(self):
        for copy in self.waiting:
            copy.wait_send()


def greet(devices):
    barrier = pltpu.get_barrier_semaphore()
    for device in devices:
        pl.semaphore_signal(
            barrier, inc=1, device_id=device, device_id_type=pl.DeviceIdType.MESH
        )
    pl.semaphore_wait(barrier, len(devices))


tail_copies = 28 + 4 + 6 + 3 + 5


def tail_body(
    count,
    emb_ref,
    mixed_ref,
    normed_ref,
    branch_ref,
    inner_ref,
    branch_all_ref,
    inner_all_ref,
    values_ref,
    grad_ref,
    gain_ref,
    gain_two_ref,
    small_ref,
    blocks_ref,
    branch_out,
    inner_out,
    out_out,
    tokens_out,
    gains_out,
    small_out,
    blocks_out,
    wide_sent,
    wide_got,
    slim_sent,
    slim_got,
    half_sent,
    half_kept,
    half_got,
    own_sent,
    own_got,
    small_sums,
    small_got,
    gain_sums,
    gain_got,
    blocks_one,
    blocks_two,
    blocks_got_one,
    blocks_got_two,
    blocks_got_three,
    send_sems,
    recv_sems,
):
    index, unit = lax.axis_index("seq"), lax.axis_index("fsdp")
    place = ring_place(index, count)
    forth, back = {"seq": ring_index(place + 1, count)}, {"seq": ring_index(place - 1, count)}
    across = [{"seq": partner(index, bit)} for bit in (1, 2, 4)]
    beside = [{"fsdp": partner(unit, bit)} for bit in (1, 2)]
    copies = Copies(send_sems, recv_sems)
    slab = normed_ref.shape[0] // count
    half = slab // 2
    last = count - 1

    greet([forth, back] + across + beside)

    bits = [lax.rem(index // bit, 2) for bit in (1, 2, 4)]
    high = blocks_ref.shape[0]
    firsts = [high // 2, high // 4, high // 8]

    def rows_at(start, size):
        return pl.ds(pl.multiple_of(start, 16), size)

    blocks_copy = copies.start(
        blocks_ref.at[rows_at((1 - bits[0]) * firsts[0], firsts[0])], blocks_got_one, across[0]
    )
    small_sums[0] = small_ref[...]
    small_copy = copies.start(small_sums.at[0], small_got.at[0], across[0])

    def out_term(k, way):
        start = k * slab + way * half
        return jnp.dot(
            emb_ref[start : start + half, :], mixed_ref[...], preferred_element_type=f32
        )

    def front_term(k, way):
        right = inner_ref if way else branch_ref
        return jnp.dot(
            normed_ref[k * slab : (k + 1) * slab, :], right[...], preferred_element_type=f32
        )

    rings = {}

    def send(name, way, step, total):
        sent, got = (slim_sent, slim_got) if name == "out" else (wide_sent, wide_got)
        sent[way, step] = total.astype(bf16)
        rings[name, way] = copies.start(
            sent.at[way, step], got.at[way, step], back if way else forth
        )

    def term(name, way, step):
        k = (count - step) % count if way else step % count
        return out_term(k, way) if name == "out" else front_term(k, way)

    def serve(name, step):
        got = slim_got if name == "out" else wide_got
        for way in (0, 1):
            own = term(name, way, step)
            rings[name, way].wait_recv()
            total = got[way, step - 2].astype(f32) + own
            if step < count:
                send(name, way, step - 1, total)
            elif name == "out":
                out_out[way * half : (way + 1) * half, :] = total
            else:
                (inner_out if way else branch_out)[...] = total

    for name in ("out", "front"):
        for way in (0, 1):
            send(name, way, 0, term(name, way, 1))

    core, side = lax.rem(unit, 2), lax.rem(unit // 2, 2)
    rows = branch_ref.shape[0]
    mid, own = rows // 2, rows // 4

    def front_back(start, k):
        nt = (((1,), (1,)), ((), ()))
        columns = slice(k * slab, (k + 1) * slab)
        return lax.dot_general(
            branch_ref[rows_at(start, mid), :],
            branch_all_ref[columns, :],
            nt,
            preferred_element_type=f32,
        ) + lax.dot_general(
            inner_ref[rows_at(start, mid), :],
            inner_all_ref[columns, :],
            nt,
            preferred_element_type=f32,
        )

    for k in range(count):
        half_sent[:, k * slab : (k + 1) * slab] = front_back((1 - core) * mid, k).astype(bf16)
    half_copy = copies.start(half_sent, half_got, beside[0])
    serve("out", 2)
    for k in range(count):
        half_kept[:, k * slab : (k + 1) * slab] = front_back(core * mid, k)
    half_copy.wait_recv()
    other = rows_at((1 - side) * own, own)
    mine = rows_at(side * own, own)
    own_sent[...] = (half_kept[other, :] + half_got[other, :].astype(f32)).astype(bf16)
    own_copy = copies.start(own_sent, own_got, beside[1])
    serve("front", 2)

    blocks_copy.wait_recv()
    blocks_one[...] = (
        blocks_ref[rows_at(bits[0] * firsts[0], firsts[0]), :].astype(f32)
        + blocks_got_one[...].astype(f32)
    ).astype(bf16)
    blocks_copy = copies.start(
        blocks_one.at[rows_at((1 - bits[1]) * firsts[1], firsts[1])], blocks_got_two, across[1]
    )
    small_copy.wait_recv()
    small_sums[1] = small_sums[0] + small_got[0]
    small_copy = copies.start(small_sums.at[1], small_got.at[1], across[1])
    serve("out", 3)
    serve("front", 3)

    own_copy.wait_recv()
    values = values_ref[...]
    scale = lax.rsqrt(jnp.mean(values * values, axis=-1, keepdims=True) + eps)
    unit_values = values * scale
    front = half_kept[mine, :] + half_got[mine, :].astype(f32) + own_got[...].astype(f32)
    gain_grad = jnp.sum(front * unit_values, 0, keepdims=True)
    weighted = front * gain_ref[...]
    result = grad_ref[...] + scale * (
        weighted - unit_values * jnp.mean(weighted * unit_values, axis=-1, keepdims=True)
    )
    low = result.astype(bf16)
    own_at = rows_at(core * mid + side * own, own)
    gain_sums[0] = jnp.zeros_like(gain_sums[0])
    for k in range(count):
        to = pl.ds(pl.multiple_of(ring_index(place - k, count) * slab, slab), slab)
        part = slice(k * slab, (k + 1) * slab)
        tokens_out[own_at, to] = low[:, part]
        gain_sums[0, 0:1, to] = gain_grad[:, part]
        gain_sums[0, 1:2, to] = gain_two_ref[:, part]
    tokens_copy = copies.start(tokens_out.at[own_at], tokens_out.at[own_at], beside[1])
    gain_copy = copies.start(gain_sums.at[0], gain_got.at[0], across[0])
    serve("out", 4)
    serve("front", 4)

    blocks_copy.wait_recv()
    blocks_two[...] = (
        blocks_one[rows_at(bits[1] * firsts[1], firsts[1]), :].astype(f32)
        + blocks_got_two[...].astype(f32)
    ).astype(bf16)
    blocks_copy = copies.start(
        blocks_two.at[rows_at((1 - bits[2]) * firsts[2], firsts[2])], blocks_got_three, across[2]
    )
    small_copy.wait_recv()
    small_sums[2] = small_sums[1] + small_got[1]
    small_copy = copies.start(small_sums.at[2], small_got.at[2], across[2])
    gain_copy.wait_recv()
    gain_sums[1] = gain_sums[0] + gain_got[0]
    gain_copy = copies.start(gain_sums.at[1], gain_got.at[1], across[1])
    tokens_copy.wait_recv()
    both_at = rows_at(core * mid, mid)
    tokens_copy = copies.start(tokens_out.at[both_at], tokens_out.at[both_at], beside[0])
    serve("out", 5)
    serve("front", 5)

    blocks_copy.wait_recv()
    starts = [bits[0] * firsts[0]]
    for bit, first in zip(bits[1:], firsts[1:]):
        starts.append(starts[-1] + bit * first)
    at = [rows_at(start, first) for start, first in zip(starts, firsts)]
    blocks_out[at[2], :] = (
        blocks_two[rows_at(bits[2] * firsts[2], firsts[2]), :].astype(f32)
        + blocks_got_three[...].astype(f32)
    ).astype(bf16)
    blocks_copy = copies.start(blocks_out.at[at[2]], blocks_out.at[at[2]], across[2])
    gain_copy.wait_recv()
    gain_sums[2] = gain_sums[1] + gain_got[1]
    gain_copy = copies.start(gain_sums.at[2], gain_got.at[2], across[2])
    small_copy.wait_recv()
    small_out[...] = small_sums[2] + small_got[2]
    serve("out", 6)
    serve("front", 6)

    blocks_copy.wait_recv()
    blocks_copy = copies.start(blocks_out.at[at[1]], blocks_out.at[at[1]], across[1])
    gain_copy.wait_recv()
    gain_sums[3] = gain_sums[2] + gain_got[2]
    gain_copy = copies.start(gain_sums.at[3], gain_got.at[3], beside[0])
    serve("out", 7)
    gain_copy.wait_recv()
    gain_sums[4] = gain_sums[3] + gain_got[3]
    gain_copy = copies.start(gain_sums.at[4], gain_got.at[4], beside[1])
    serve("front", 7)
    blocks_copy.wait_recv()
    blocks_copy = copies.start(blocks_out.at[at[0]], blocks_out.at[at[0]], across[0])
    serve("out", 8)
    gain_copy.wait_recv()
    gains_out[...] = gain_sums[4] + gain_got[4]
    tokens_copy.wait_recv()
    blocks_copy.wait_recv()
    serve("front", 8)
    copies.end()


def tail(count, *operands):
    emb, mixed, normed, *_ = operands
    small, blocks = operands[-2:]
    width, rows = emb.shape
    units = mixed.shape[1]
    slab = width // count
    high, block_width = blocks.shape
    whole = pl.BlockSpec(memory_space=pltpu.VMEM)
    grad = jax.ShapeDtypeStruct((slab, units), f32)
    steps = count - 1
    return pl.pallas_call(
        functools.partial(tail_body, count),
        out_shape=(
            grad,
            grad,
            grad,
            jax.ShapeDtypeStruct((rows, width), bf16),
            jax.ShapeDtypeStruct((8, width), f32),
            jax.ShapeDtypeStruct(small.shape, f32),
            jax.ShapeDtypeStruct(blocks.shape, bf16),
        ),
        in_specs=[whole] * len(operands),
        out_specs=(whole,) * 7,
        scratch_shapes=[
            pltpu.VMEM((2, steps, slab, units), bf16),
            pltpu.VMEM((2, steps, slab, units), bf16),
            pltpu.VMEM((2, steps, slab // 2, units), bf16),
            pltpu.VMEM((2, steps, slab // 2, units), bf16),
            pltpu.VMEM((rows // 2, width), bf16),
            pltpu.VMEM((rows // 2, width), f32),
            pltpu.VMEM((rows // 2, width), bf16),
            pltpu.VMEM((rows // 4, width), bf16),
            pltpu.VMEM((rows // 4, width), bf16),
            pltpu.VMEM((3, *small.shape), f32),
            pltpu.VMEM((3, *small.shape), f32),
            pltpu.VMEM((5, 8, width), f32),
            pltpu.VMEM((5, 8, width), f32),
            pltpu.VMEM((high // 2, block_width), bf16),
            pltpu.VMEM((high // 4, block_width), bf16),
            pltpu.VMEM((high // 2, block_width), bf16),
            pltpu.VMEM((high // 4, block_width), bf16),
            pltpu.VMEM((high // 8, block_width), bf16),
            pltpu.SemaphoreType.DMA((tail_copies,)),
            pltpu.SemaphoreType.DMA((tail_copies,)),
        ],
        compiler_params=pltpu.CompilerParams(
            collective_id=0, has_side_effects=True, vmem_limit_bytes=60 * 1024 * 1024
        ),
    )(*operands)


def peers(count, units):
    index, unit = lax.axis_index("seq"), lax.axis_index("fsdp")
    along = [{"seq": lax.rem(index + distance, count)} for distance in range(1, count)]
    beside = [{"fsdp": partner(unit, 1 << i)} for i in range(units.bit_length() - 1)]
    return along, beside


def rows_at(start, size, multiple=16):
    return pl.ds(pl.multiple_of(start, multiple), size)


def dot_slabs(left, right_ref, slab, count):
    for k in range(count):
        columns = slice(k * slab, (k + 1) * slab)
        yield columns, lax.dot_general(
            left,
            right_ref[columns, :],
            (((1,), (1,)), ((), ())),
            preferred_element_type=f32,
        )


def scan_rows(a_ref, b_ref, prod_ref, state_ref, batches, backward):
    length, units = a_ref.shape[0] // batches, a_ref.shape[1]
    tiles = length // 8
    rows = lax.broadcasted_iota(jnp.int32, (8, units), 0)

    def step(index, carry):
        tile = tiles - 1 - index if backward else index
        following = []
        for batch in range(batches):
            prod_in, state_in, a_next = carry[batch]
            at = rows_at(batch * length + tile * 8, 8, 8)
            a, b = a_ref[at, :], b_ref[at, :]
            a_first = a[0:1]
            if backward:
                a = jnp.where(rows < 7, pltpu.roll(a, 7, 0), a_next)
            for shift in (1, 2, 4):
                turn = 8 - shift if backward else shift
                inside = rows < 8 - shift if backward else rows >= shift
                a_moved = jnp.where(inside, pltpu.roll(a, turn, 0), 1.0)
                b_moved = jnp.where(inside, pltpu.roll(b, turn, 0), 0.0)
                b = a * b_moved + b
                a = a * a_moved
            b = b + a * state_in
            a = a * prod_in
            prod_ref[at, :] = a
            state_ref[at, :] = b
            edge = 0 if backward else 7
            following.append((a[edge : edge + 1], b[edge : edge + 1], a_first))
        return tuple(following)

    one, zero = jnp.ones((1, units), f32), jnp.zeros((1, units), f32)
    maps = lax.fori_loop(0, tiles, step, ((one, zero, one),) * batches)
    return [(prod, state) for prod, state, _ in maps]


def entry_states(ends_ref, got_ref, index, count, batches, sign):
    states = []
    for batch in range(batches):
        state = jnp.zeros_like(ends_ref[0:1, :])
        for distance in range(count - 1, 0, -1):
            there = index - distance >= 0 if sign > 0 else index + distance < count
            prods = got_ref[distance - 1, batch : batch + 1, :]
            longer = got_ref[distance - 1, batches + batch : batches + batch + 1, :] + prods * state
            state = jnp.where(there, longer, 0.0)
        states.append(state)
    return states


head_copies = 9 * (ring_count - 1) + 5
row_block = 32


def head_body(
    count,
    fsdp,
    batches,
    tokens_ref,
    cot_ref,
    gain_one_ref,
    gain_two_ref,
    branch_ref,
    inner_ref,
    out_ref,
    gate_ref,
    up_ref,
    down_ref,
    taps_ref,
    vectors_ref,
    gate_square_ref,
    input_square_ref,
    fresh_ref,
    branch_all,
    inner_all,
    out_all,
    gate_all,
    up_all,
    down_all,
    cot_out,
    normed_out,
    branch_pre,
    padded,
    conv_low,
    gate_pre,
    input_pre,
    carries,
    states,
    ends,
    mixed_low,
    own_values,
    own_middle,
    normed_two,
    tokens_low,
    gains,
    prods,
    local_states,
    edges_sent,
    edges_got,
    ends_sent,
    ends_got,
    half_sent,
    half_kept,
    half_got,
    own_sent,
    own_got,
    local_sems,
    send_sems,
    recv_sems,
):
    index, unit = lax.axis_index("seq"), lax.axis_index("fsdp")
    place = ring_place(index, count)
    forth, back = {"seq": ring_index(place + 1, count)}, {"seq": ring_index(place - 1, count)}
    along, beside = peers(count, fsdp)
    copies = Copies(send_sems, recv_sems)
    rows, width = tokens_ref.shape
    units = branch_ref.shape[1]
    length, slab = rows // batches, width // count
    half = slab // 2
    core, side = lax.rem(unit, 2), lax.rem(unit // 2, 2)
    mid, own = rows // 2, rows // 4

    locals_of = []
    for source, target in zip(
        (branch_ref, inner_ref, out_ref, gate_ref, up_ref, down_ref),
        (branch_all, inner_all, out_all, gate_all, up_all, down_all),
    ):
        copy = pltpu.make_async_copy(
            source, target.at[pl.ds(0, slab)], local_sems.at[len(locals_of)]
        )
        copy.start()
        locals_of.append(copy)

    greet(along + beside)

    pairs = {
        "front": ((branch_ref, branch_all, 0, slab), (inner_ref, inner_all, 0, slab)),
        "out": ((out_ref, out_all, 0, half), (out_ref, out_all, half, half)),
        "mlp": ((gate_ref, gate_all, 0, slab), (up_ref, up_all, 0, slab)),
        "down": ((down_ref, down_all, 0, half), (down_ref, down_all, half, half)),
    }
    under_way = {}

    def start(name, step):
        for way in (0, 1):
            shard, whole, first, size = pairs[name][way]
            if step > 1:
                under_way[name, way].wait_recv()
            there = (count - step) % count if way else step
            here = (there + 1) % count if way else step - 1
            source = (
                shard.at[pl.ds(first, size)]
                if step == 1
                else whole.at[pl.ds(here * slab + first, size)]
            )
            under_way[name, way] = copies.start(
                source, whole.at[pl.ds(there * slab + first, size)], back if way else forth
            )

    def finish(name):
        for way in (0, 1):
            under_way[name, way].wait_recv()

    start("front", 1)
    start("out", 1)

    for k in range(count):
        plain = pl.ds(pl.multiple_of(ring_index(place - k, count) * slab, slab), slab)
        part = slice(k * slab, (k + 1) * slab)
        tokens_low[:, part] = tokens_ref[:, plain]
        gains[0:1, part] = gain_one_ref[:, plain]
        gains[1:2, part] = gain_two_ref[:, plain]
    start("front", 2)
    start("out", 2)

    def norm_block(block, carry):
        at = rows_at(block * row_block, row_block)
        values = tokens_low[at, :].astype(f32)
        scale = lax.rsqrt(jnp.mean(values * values, axis=-1, keepdims=True) + eps)
        normed_out[at, :] = (values * scale * gains[0:1, :]).astype(bf16)
        return carry

    lax.fori_loop(0, rows // row_block, norm_block, 0)
    own_values[...] = tokens_low[rows_at(core * mid + side * own, own), :].astype(f32)
    start("front", 3)
    start("out", 3)
    for k in range(count):
        plain = pl.ds(pl.multiple_of(ring_index(place - k, count) * slab, slab), slab)
        cot_out[:, k * slab : (k + 1) * slab] = cot_ref[:, plain]
    for step in range(4, count):
        start("front", step)
        start("out", step)
    start("mlp", 1)
    start("down", 1)
    for copy in locals_of:
        copy.wait()
    finish("front")

    for batch in range(batches):
        at = slice(batch * length, (batch + 1) * length)
        top = batch * (length + 8)
        inner = jnp.dot(normed_out[at, :], inner_all[...], preferred_element_type=f32)
        padded[top + 8 : top + 8 + length, :] = inner.astype(bf16).astype(f32)
        edges_sent[batch] = padded[top + length : top + length + 8, :]
    edge_copy = copies.start(edges_sent, edges_got, along[0])
    for batch in range(batches):
        at = slice(batch * length, (batch + 1) * length)
        branch_pre[at, :] = jnp.dot(
            normed_out[at, :], branch_all[...], preferred_element_type=f32
        )
    edge_copy.wait_recv()
    for batch in range(batches):
        top = batch * (length + 8)
        padded[top : top + 8, :] = jnp.where(index > 0, edges_got[batch], 0.0)
    start("mlp", 2)
    bias, gate_bias, input_bias, rate = [vectors_ref[i : i + 1, :] for i in range(4)]

    def conv_block(block, carry):
        batch = block // (length // row_block)
        wide = padded[rows_at(block * row_block + batch * 8, row_block + 8, 8), :]
        total = bias + taps_ref[0:1, :] * wide[8:] + taps_ref[1:2, :] * wide[7:-1]
        total = total + taps_ref[2:3, :] * wide[6:-2] + taps_ref[3:4, :] * wide[5:-3]
        conv_low[rows_at(block * row_block, row_block), :] = total.astype(bf16)
        return carry

    lax.fori_loop(0, rows // row_block, conv_block, 0)
    for batch in range(batches):
        at = slice(batch * length, (batch + 1) * length)
        conv = conv_low[at, :]
        gate_pre[at, :] = (
            jnp.dot(conv, gate_square_ref[...], preferred_element_type=f32) + gate_bias
        )
        input_pre[at, :] = (
            jnp.dot(conv, input_square_ref[...], preferred_element_type=f32) + input_bias
        )
    start("down", 2)

    def gate_block(block, carry):
        at = rows_at(block * row_block, row_block)
        rate_gate = jax.nn.sigmoid(gate_pre[at, :])
        inlet_gate = jax.nn.sigmoid(input_pre[at, :])
        log_decay = rate * rate_gate
        decay = jnp.exp(log_decay)
        fresh = fresh_ref[at, :] > 0
        scale = jnp.sqrt(-jnp.tanh(log_decay) * (1.0 + decay * decay))
        carries[at, :] = jnp.where(fresh, 0.0, decay)
        local_states[at, :] = (
            jnp.where(fresh, 1.0, scale) * inlet_gate * conv_low[at, :].astype(f32)
        )
        return carry

    lax.fori_loop(0, rows // row_block, gate_block, 0)
    scanned = scan_rows(carries, local_states, prods, local_states, batches, False)
    ends_sent[...] = jnp.zeros_like(ends_sent)
    for batch, (prod, state) in enumerate(scanned):
        ends_sent[batch : batch + 1, :] = prod
        ends_sent[batches + batch : batches + batch + 1, :] = state
    ends[...] = ends_sent[...]
    end_copies = [
        copies.start(ends_sent, ends_got.at[distance - 1], along[distance - 1])
        for distance in range(1, count)
    ]
    start("mlp", 3)
    for copy in end_copies:
        copy.wait_recv()
    entries = entry_states(ends, ends_got, index, count, batches, 1)

    for batch in range(batches):
        entry = entries[batch]
        top = batch * (length + 8)
        states[top : top + 8, :] = jnp.broadcast_to(entry, (8, units))

        def state_block(block, carry, batch=batch, entry=entry):
            at = rows_at(batch * length + block * row_block, row_block)
            state = local_states[at, :] + prods[at, :] * entry
            states[rows_at(8 + batch * (length + 8) + block * row_block, row_block, 8), :] = state
            mixed_low[at, :] = (state * gelu_tanh(branch_pre[at, :])).astype(bf16)
            return carry

        lax.fori_loop(0, length // row_block, state_block, 0)
    start("down", 3)
    finish("out")
    for part, result in dot_slabs(
        mixed_low[rows_at((1 - core) * mid, mid), :], out_all, slab, count
    ):
        half_sent[:, part] = result.astype(bf16)
    half_copy = copies.start(half_sent, half_got, beside[0])
    for part, result in dot_slabs(mixed_low[rows_at(core * mid, mid), :], out_all, slab, count):
        half_kept[:, part] = result
    half_copy.wait_recv()
    other, mine = rows_at((1 - side) * own, own), rows_at(side * own, own)
    own_sent[...] = (half_kept[other, :] + half_got[other, :].astype(f32)).astype(bf16)
    own_copy = copies.start(own_sent, own_got, beside[1])
    start("mlp", 4)
    start("down", 4)
    own_copy.wait_recv()
    middle = own_values[...] + (
        half_kept[mine, :] + half_got[mine, :].astype(f32) + own_got[...].astype(f32)
    )
    own_middle[...] = middle
    scale = lax.rsqrt(jnp.mean(middle * middle, axis=-1, keepdims=True) + eps)
    own_at, both_at = rows_at(core * mid + side * own, own), rows_at(core * mid, mid)
    normed_two[own_at, :] = (middle * scale * gains[1:2, :]).astype(bf16)
    join_copy = copies.start(normed_two.at[own_at], normed_two.at[own_at], beside[1])
    start("mlp", 5)
    join_copy.wait_recv()
    join_copy = copies.start(normed_two.at[both_at], normed_two.at[both_at], beside[0])
    start("down", 5)
    join_copy.wait_recv()
    for step in range(6, count):
        start("mlp", step)
        start("down", step)
    finish("mlp")
    finish("down")
    copies.end()


def head(count, fsdp, batches, *operands):
    tokens = operands[0]
    branch, gate = operands[4], operands[7]
    rows, width = tokens.shape
    slab, units = branch.shape
    hidden = gate.shape[1]
    length = rows // batches
    whole, place = pl.BlockSpec(memory_space=pltpu.VMEM), pl.BlockSpec(memory_space=pl.ANY)

    def array(dtype, *shape):
        return jax.ShapeDtypeStruct(shape, dtype)

    outs = (
        [array(bf16, width, units)] * 3
        + [array(bf16, width, hidden)] * 3
        + [array(bf16, rows, width)] * 2
        + [array(f32, rows, units), array(f32, rows + 8 * batches, units), array(bf16, rows, units)]
        + [array(f32, rows, units)] * 3
        + [array(f32, rows + 8 * batches, units)]
        + [array(f32, 8, units), array(bf16, rows, units)]
        + [array(f32, rows // 4, width)] * 2
        + [array(bf16, rows, width)]
    )
    return pl.pallas_call(
        functools.partial(head_body, count, fsdp, batches),
        out_shape=tuple(outs),
        in_specs=[whole] * 4 + [place] * 6 + [whole] * 5,
        out_specs=tuple([whole] * 3 + [place] * 3 + [whole] * (len(outs) - 6)),
        scratch_shapes=[
            pltpu.VMEM((rows, width), bf16),
            pltpu.VMEM((8, width), f32),
            pltpu.VMEM((rows, units), f32),
            pltpu.VMEM((rows, units), f32),
            pltpu.VMEM((batches, 8, units), f32),
            pltpu.VMEM((batches, 8, units), f32),
            pltpu.VMEM((8, units), f32),
            pltpu.VMEM((count - 1, 8, units), f32),
            pltpu.VMEM((rows // 2, width), bf16),
            pltpu.VMEM((rows // 2, width), f32),
            pltpu.VMEM((rows // 2, width), bf16),
            pltpu.VMEM((rows // 4, width), bf16),
            pltpu.VMEM((rows // 4, width), bf16),
            pltpu.SemaphoreType.DMA((6,)),
            pltpu.SemaphoreType.DMA((head_copies,)),
            pltpu.SemaphoreType.DMA((head_copies,)),
        ],
        compiler_params=pltpu.CompilerParams(
            collective_id=1, has_side_effects=True, vmem_limit_bytes=60 * 1024 * 1024
        ),
    )(*operands)


def gelu_slope(values):
    constant = 0.7978845608028654
    bent = jnp.tanh(constant * (values + 0.044715 * values * values * values))
    inner = constant * (1.0 + 3.0 * 0.044715 * values * values)
    return 0.5 * (1.0 + bent) + 0.5 * values * (1.0 - bent * bent) * inner


ring_slots = 3
back_sends = 2 * 2 * (ring_count - 1)
back_copies = 4 + 4 + (ring_count - 1) + 1


class RingSum:
    def __init__(self, terms, slots, sends, arrivals, credits, count, neighbours):
        self.terms, self.slots, self.count = terms, slots, count
        self.sends, self.arrivals, self.credits = sends, arrivals, credits
        self.neighbours = neighbours
        self.copies = [[], []]

    def send(self, way, step, total):
        here, there = (step - 1) % ring_slots, step % ring_slots
        self.slots[way, here] = total.astype(bf16)
        if step >= ring_slots:
            pl.semaphore_wait(self.credits.at[way], 1)
        copy = pltpu.make_async_remote_copy(
            src_ref=self.slots.at[way, here],
            dst_ref=self.slots.at[way, there],
            send_sem=self.sends.at[way, step - 1],
            recv_sem=self.arrivals.at[way, step - 1],
            device_id=self.neighbours[way],
            device_id_type=pl.DeviceIdType.MESH,
        )
        copy.start()
        self.copies[way].append(copy)
        if step >= 2:
            self.copies[way][step - 2].wait_send()
            if step + 1 < self.count:
                pl.semaphore_signal(
                    self.credits.at[way],
                    inc=1,
                    device_id=self.neighbours[1 - way],
                    device_id_type=pl.DeviceIdType.MESH,
                )

    def serve(self, step, end=None):
        for way in (0, 1):
            k = (self.count - step) % self.count if way else step % self.count
            own = self.terms[way](k)
            if step == 1:
                self.send(way, 1, own)
                continue
            self.copies[way][step - 2].wait_recv()
            total = self.slots[way, (step - 1) % ring_slots].astype(f32) + own
            if step < self.count:
                self.send(way, step, total)
            else:
                self.copies[way][step - 2].wait_send()
                end(way, total)


def back_body(
    count,
    fsdp,
    batches,
    cot_ref,
    hidden_ref,
    normed_ref,
    gate_low_ref,
    up_low_ref,
    branch_pre,
    padded,
    conv_low,
    gate_pre,
    input_pre,
    carries,
    states,
    ends_ref,
    gate_square_ref,
    input_square_ref,
    own_middle,
    fresh_ref,
    taps_ref,
    vectors_ref,
    gain_two_ref,
    gate_all,
    up_all,
    down_all,
    out_all,
    mixed_out,
    middle_low,
    own_grad,
    branch_low,
    inner_low,
    gate_low,
    input_low,
    small_out,
    gain_grad_out,
    gate_grad,
    up_grad,
    down_grad,
    half_sent,
    half_kept,
    half_got,
    own_sent,
    own_got,
    prods,
    adjoints,
    conv_grad,
    edges_sent,
    edges_got,
    ends_sent,
    ends_got,
    mlp_slots,
    down_slots,
    stream_one,
    stream_two,
    stream_out,
    stage,
    stream_sems,
    stage_sems,
    ring_sends,
    ring_arrivals,
    ring_credits,
    send_sems,
    recv_sems,
):
    index, unit = lax.axis_index("seq"), lax.axis_index("fsdp")
    place = ring_place(index, count)
    neighbours = (
        {"seq": ring_index(place + 1, count)},
        {"seq": ring_index(place - 1, count)},
    )
    along, beside = peers(count, fsdp)
    copies = Copies(send_sems, recv_sems)
    rows, width = cot_ref.shape
    units = branch_pre.shape[1]
    length, slab = rows // batches, width // count
    half = slab // 2
    core, side = lax.rem(unit, 2), lax.rem(unit // 2, 2)
    mid, own = rows // 2, rows // 4
    kept_at, sent_at = rows_at(core * mid, mid), rows_at((1 - core) * mid, mid)
    mine, other = rows_at(side * own, own), rows_at((1 - side) * own, own)
    own_at = rows_at(core * mid + side * own, own)
    tn = (((0,), (0,)), ((), ()))

    greet(along + beside)

    def mlp_term(right):
        return lambda k: lax.dot_general(
            normed_ref[:, k * slab : (k + 1) * slab], right[...], tn, preferred_element_type=f32
        )

    def down_term(first):
        return lambda k: lax.dot_general(
            cot_ref[:, k * slab + first : k * slab + first + half],
            hidden_ref[...],
            tn,
            preferred_element_type=f32,
        )

    mlp = RingSum(
        [mlp_term(gate_low_ref), mlp_term(up_low_ref)],
        mlp_slots,
        ring_sends.at[0],
        ring_arrivals.at[0],
        ring_credits.at[0],
        count,
        neighbours,
    )
    down = RingSum(
        [down_term(0), down_term(half)],
        down_slots,
        ring_sends.at[1],
        ring_arrivals.at[1],
        ring_credits.at[1],
        count,
        neighbours,
    )
    mlp.serve(1)
    down.serve(1)

    def streamed(sources, buffers, first_sem):
        def fetch(k):
            fetched = []
            for number, (source, buffer) in enumerate(zip(sources, buffers)):
                copy = pltpu.make_async_copy(
                    source.at[pl.ds(k * slab, slab)],
                    buffer.at[k % 2],
                    stream_sems.at[first_sem + number * count + k],
                )
                copy.start()
                fetched.append(copy)
            return fetched

        fetched = fetch(0)
        for k in range(count):
            for copy in fetched:
                copy.wait()
            if k + 1 < count:
                fetched = fetch(k + 1)
            yield k, [buffer[k % 2] for buffer in buffers]

    def nt(left, right):
        return lax.dot_general(
            left, right, (((1,), (1,)), ((), ())), preferred_element_type=f32
        )

    for k, (gate, up) in streamed((gate_all, up_all), (stream_one, stream_two), 0):
        part = slice(k * slab, (k + 1) * slab)
        half_sent[:, part] = (
            nt(gate_low_ref[sent_at, :], gate) + nt(up_low_ref[sent_at, :], up)
        ).astype(bf16)
        half_kept[:, part] = nt(gate_low_ref[kept_at, :], gate) + nt(up_low_ref[kept_at, :], up)
    half_copy = copies.start(half_sent, half_got, beside[0])
    half_copy.wait_recv()
    own_sent[...] = (half_kept[other, :] + half_got[other, :].astype(f32)).astype(bf16)
    own_copy = copies.start(own_sent, own_got, beside[1])
    mlp.serve(2)
    down.serve(2)
    own_copy.wait_recv()
    middle = own_middle[...]
    scale = lax.rsqrt(jnp.mean(middle * middle, axis=-1, keepdims=True) + eps)
    unit_values = middle * scale
    front = half_kept[mine, :] + half_got[mine, :].astype(f32) + own_got[...].astype(f32)
    gain_grad_out[...] = jnp.zeros_like(gain_grad_out)
    gain_grad_out[0:1, :] = jnp.sum(front * unit_values, 0, keepdims=True)
    weighted = front * gain_two_ref[...]
    result = cot_ref[own_at, :].astype(f32) + scale * (
        weighted - unit_values * jnp.mean(weighted * unit_values, axis=-1, keepdims=True)
    )
    own_grad[...] = result
    middle_low[own_at, :] = result.astype(bf16)
    join_copy = copies.start(middle_low.at[own_at], middle_low.at[own_at], beside[1])
    mlp.serve(3)
    join_copy.wait_recv()
    join_copy = copies.start(middle_low.at[kept_at], middle_low.at[kept_at], beside[0])
    down.serve(3)
    join_copy.wait_recv()

    for k, (out,) in streamed((out_all,), (stream_out,), 2 * count):
        for batch in range(batches):
            at = slice(batch * length, (batch + 1) * length)
            more = jnp.dot(
                middle_low[at, k * slab : (k + 1) * slab], out, preferred_element_type=f32
            )
            adjoints[at, :] = more if k == 0 else adjoints[at, :] + more

    def mixed_block(block, carry):
        batch = block // (length // row_block)
        at = rows_at(block * row_block, row_block)
        back, before = adjoints[at, :], branch_pre[at, :]
        state = states[rows_at(block * row_block + batch * 8 + 8, row_block, 8), :]
        branch_low[at, :] = (back * state * gelu_slope(before)).astype(bf16)
        adjoints[at, :] = back * gelu_tanh(before)
        return carry

    lax.fori_loop(0, rows // row_block, mixed_block, 0)
    scanned = scan_rows(carries, adjoints, prods, adjoints, batches, True)
    ends_sent[...] = ends_ref[...]
    for batch, (_, state) in enumerate(scanned):
        top = batch * length
        ends_sent[batches + batch : batches + batch + 1, :] = carries[top : top + 1, :] * state
    end_copies = [
        copies.start(ends_sent, ends_got.at[distance - 1], along[count - distance - 1])
        for distance in range(1, count)
    ]
    mlp.serve(4)
    for copy in end_copies:
        copy.wait_recv()
    entries = entry_states(ends_sent, ends_got, index, count, batches, -1)

    bias, gate_bias, input_bias, rate, slope = [vectors_ref[i : i + 1, :] for i in range(5)]
    zero = jnp.zeros((1, units), f32)
    sums = (zero, zero, zero)
    for batch in range(batches):
        entry = entries[batch]

        def gate_block(block, sums, batch=batch, entry=entry):
            top = batch * length + block * row_block
            at = rows_at(top, row_block)
            rate_gate = jax.nn.sigmoid(gate_pre[at, :])
            inlet_gate = jax.nn.sigmoid(input_pre[at, :])
            log_decay = rate * rate_gate
            decay = jnp.exp(log_decay)
            fresh = fresh_ref[at, :] > 0
            scale = jnp.sqrt(-jnp.tanh(log_decay) * (1.0 + decay * decay))
            conv = conv_low[at, :].astype(f32)
            lam = adjoints[at, :] + prods[at, :] * entry
            before = states[rows_at(top + batch * 8, row_block + 8, 8), :][7:-1]
            drawn = inlet_gate * conv
            log_grad = jnp.where(
                fresh, 0.0, lam * before * decay - lam * (decay * decay / scale) * drawn
            )
            passed = lam * jnp.where(fresh, 1.0, scale)
            gate_grad_low = (log_grad * rate * (rate_gate * (1.0 - rate_gate))).astype(bf16)
            input_grad_low = (passed * conv * (inlet_gate * (1.0 - inlet_gate))).astype(bf16)
            gate_low[at, :] = gate_grad_low
            input_low[at, :] = input_grad_low
            conv_grad[rows_at(top + batch * 8, row_block, 8), :] = passed * inlet_gate
            terms = (
                gate_grad_low.astype(f32),
                input_grad_low.astype(f32),
                log_grad * rate_gate,
            )
            return tuple(
                total + jnp.sum(more, 0, keepdims=True) for total, more in zip(sums, terms)
            )

        sums = lax.fori_loop(0, length // row_block, gate_block, sums)
        if batch == 0:
            down.serve(4)
    for batch in range(batches):
        at, top = slice(batch * length, (batch + 1) * length), batch * (length + 8)
        conv_grad[top : top + length, :] = (
            conv_grad[top : top + length, :]
            + nt(gate_low[at, :], gate_square_ref[...])
            + nt(input_low[at, :], input_square_ref[...])
        )
        edges_sent[batch] = conv_grad[top : top + 8, :]
    edge_copy = copies.start(edges_sent, edges_got, along[count - 2])
    mlp.serve(5)

    copies.sent(half_copy)
    copies.sent(own_copy)
    for k, (turned,) in streamed((down_all,), (stream_one,), 3 * count):
        part = slice(k * slab, (k + 1) * slab)
        half_sent[:, part] = nt(hidden_ref[sent_at, :], turned).astype(bf16)
        half_kept[:, part] = nt(hidden_ref[kept_at, :], turned)
    mixed_copy = copies.start(half_sent, half_got, beside[0])
    down.serve(5)

    edge_copy.wait_recv()
    for batch in range(batches):
        top = batch * (length + 8) + length
        conv_grad[top : top + 8, :] = jnp.where(index < count - 1, edges_got[batch], 0.0)

    def conv_block(block, sums):
        batch = block // (length // row_block)
        at = rows_at(block * row_block + batch * 8, row_block + 8, 8)
        wide, inner = conv_grad[at, :], padded[at, :]
        total = taps_ref[0:1, :] * wide[:-8] + taps_ref[1:2, :] * wide[1:-7]
        total = total + taps_ref[2:3, :] * wide[2:-6] + taps_ref[3:4, :] * wide[3:-5]
        inner_low[rows_at(block * row_block, row_block), :] = total.astype(bf16)
        near = wide[:-8]
        terms = [near * inner[8 - k : 8 - k + row_block] for k in range(4)] + [near]
        return tuple(
            total + jnp.sum(more, 0, keepdims=True) for total, more in zip(sums, terms)
        )

    conv_sums = lax.fori_loop(0, rows // row_block, conv_block, (zero,) * 5)
    for number, total in enumerate((*conv_sums, sums[0], sums[1], sums[2] * slope)):
        small_out[number : number + 1, :] = total

    mixed_copy.wait_recv()
    own_sent[...] = (half_kept[other, :] + half_got[other, :].astype(f32)).astype(bf16)
    own_copy = copies.start(own_sent, own_got, beside[1])
    mlp.serve(6)
    down.serve(6)
    own_copy.wait_recv()
    final = own_middle[...] + (
        half_kept[mine, :] + half_got[mine, :].astype(f32) + own_got[...].astype(f32)
    )
    final = final.astype(bf16)
    for k in range(count):
        to = pl.ds(pl.multiple_of(ring_index(place - k, count) * slab, slab), slab)
        mixed_out[own_at, to] = final[:, k * slab : (k + 1) * slab]
    join_copy = copies.start(mixed_out.at[own_at], mixed_out.at[own_at], beside[1])
    mlp.serve(7)
    join_copy.wait_recv()
    join_copy = copies.start(mixed_out.at[kept_at], mixed_out.at[kept_at], beside[0])
    down.serve(7)
    join_copy.wait_recv()

    def mlp_end(way, total):
        stage[...] = total
        copy = pltpu.make_async_copy(stage, up_grad if way else gate_grad, stage_sems.at[way])
        copy.start()
        copy.wait()

    def down_end(way, total):
        stage[way * half : (way + 1) * half, :] = total

    mlp.serve(8, mlp_end)
    down.serve(8, down_end)
    copy = pltpu.make_async_copy(stage, down_grad, stage_sems.at[2])
    copy.start()
    copy.wait()
    copies.end()


def back(count, fsdp, batches, *operands):
    cot, hidden = operands[0], operands[1]
    branch_pre = operands[5]
    rows, width = cot.shape
    units, inner = branch_pre.shape[1], hidden.shape[1]
    slab, length = width // count, rows // batches
    whole, place = pl.BlockSpec(memory_space=pltpu.VMEM), pl.BlockSpec(memory_space=pl.ANY)

    def array(dtype, *shape):
        return jax.ShapeDtypeStruct(shape, dtype)

    outs = [
        array(bf16, rows, width),
        array(bf16, rows, width),
        array(f32, rows // 4, width),
        *[array(bf16, rows, units)] * 4,
        array(f32, 8, units),
        array(f32, 8, width),
        *[array(f32, slab, inner)] * 3,
    ]
    return pl.pallas_call(
        functools.partial(back_body, count, fsdp, batches),
        out_shape=tuple(outs),
        in_specs=[whole] * (len(operands) - 4) + [place] * 4,
        out_specs=tuple([whole] * 9 + [place] * 3),
        scratch_shapes=[
            pltpu.VMEM((rows // 2, width), bf16),
            pltpu.VMEM((rows // 2, width), f32),
            pltpu.VMEM((rows // 2, width), bf16),
            pltpu.VMEM((rows // 4, width), bf16),
            pltpu.VMEM((rows // 4, width), bf16),
            pltpu.VMEM((rows, units), f32),
            pltpu.VMEM((rows, units), f32),
            pltpu.VMEM((rows + 8 * batches, units), f32),
            pltpu.VMEM((batches, 8, units), f32),
            pltpu.VMEM((batches, 8, units), f32),
            pltpu.VMEM((8, units), f32),
            pltpu.VMEM((count - 1, 8, units), f32),
            pltpu.VMEM((2, ring_slots, slab, inner), bf16),
            pltpu.VMEM((2, ring_slots, slab // 2, inner), bf16),
            pltpu.VMEM((2, slab, inner), bf16),
            pltpu.VMEM((2, slab, inner), bf16),
            pltpu.VMEM((2, slab, units), bf16),
            pltpu.VMEM((slab, inner), f32),
            pltpu.SemaphoreType.DMA((4 * count,)),
            pltpu.SemaphoreType.DMA((3,)),
            pltpu.SemaphoreType.DMA((2, 2, count - 1)),
            pltpu.SemaphoreType.DMA((2, 2, count - 1)),
            pltpu.SemaphoreType.REGULAR((2, 2)),
            pltpu.SemaphoreType.DMA((back_copies,)),
            pltpu.SemaphoreType.DMA((back_copies,)),
        ],
        compiler_params=pltpu.CompilerParams(
            collective_id=2, has_side_effects=True, vmem_limit_bytes=63 * 1024 * 1024
        ),
    )(*operands)


def block_diagonal(blocks):
    count, width = blocks.shape[0], blocks.shape[1]
    return sum(
        jnp.pad(blocks[j], ((j * width, (count - 1 - j) * width),) * 2) for j in range(count)
    )


def rows_joined(slab_pairs):
    return jnp.concatenate([part for pair in zip(*slab_pairs) for part in pair], 0)


def diagonal_blocks(square, count):
    width = square.shape[0] // count
    return jnp.stack(
        [square[j * width : (j + 1) * width, j * width : (j + 1) * width] for j in range(count)], 0
    )


def local(
    tokens,
    resets,
    norm_gain,
    branch_weight,
    inner_weight,
    conv_weight,
    conv_bias,
    gate_blocks,
    input_blocks,
    gate_bias,
    input_bias,
    decay_param,
    out_weight,
    mlp_norm_gain,
    gate_weight,
    up_weight,
    down_weight,
    cotangent,
):
    count = lax.axis_size("seq")
    batches, length, width = tokens.shape
    slab = width // count
    units, hidden = conv_bias.shape[0], down_weight.shape[0]
    rows = batches * length
    ringed = count == ring_count and lax.axis_size("fsdp") == 4
    half = slab // 2
    out_turned, down_turned = out_weight.T, down_weight.T
    ring = Ring(count)
    if ringed:
        gather, scatter = functools.partial(Gather, ring), functools.partial(Scatter, ring)
        to_ring, to_plain = ring.tables()

        def moved(values, dtype):
            return move_slabs(values, to_ring, dtype)

        def restored(values, dtype):
            return move_slabs(values, to_plain, dtype)

        def gain_moved(gain):
            return gain.reshape(count, slab)[to_ring].reshape(width)

        def gain_restored(gain):
            return gain.reshape(count, slab)[to_plain].reshape(width)

    else:
        gather, scatter = functools.partial(PlainGather, ring), functools.partial(PlainScatter, ring)

        def moved(values, dtype):
            return values.astype(dtype)

        restored = moved

        def gain_moved(gain):
            return gain

        gain_restored = gain_moved

    def slab_dots(turned, right, first=0, rows=slab):
        def term(k):
            start = k * slab + first
            return dot_nn(turned[start : start + rows], right)

        return term

    steps = count - 1
    taps = conv_weight.astype(f32)
    decay = decay_param.astype(f32)
    gate_square, input_square = block_diagonal(gate_blocks), block_diagonal(input_blocks)
    fresh_start = resets[:, :, None] > 0
    gain_one = gain_moved(norm_gain.astype(f32))
    gain_two = gain_moved(mlp_norm_gain.astype(f32))

    def gates(gate_pre, input_pre, conv_value, decay):
        return gate_math(gate_pre, input_pre, conv_value, decay, fresh_start)

    def by_sequence(values):
        return values.reshape(batches, -1, values.shape[-1])

    if ringed:
        vectors = jnp.stack(
            [
                conv_bias.astype(f32),
                gate_bias.astype(f32),
                input_bias.astype(f32),
                -decay_scale * jax.nn.softplus(-decay),
            ],
            0,
        )
        (
            branch_all,
            inner_all,
            out_all,
            gate_all,
            up_all,
            down_all,
            cot_low,
            normed,
            branch_pre,
            padded,
            conv_flat,
            gate_pre,
            input_pre,
            carries,
            states,
            ends,
            mixed_low,
            own_values,
            own_middle,
            normed_two,
        ) = head(
            count,
            lax.axis_size("fsdp"),
            batches,
            tokens.reshape(rows, width),
            cotangent.reshape(rows, width),
            norm_gain.astype(f32)[None],
            mlp_norm_gain.astype(f32)[None],
            branch_weight,
            inner_weight,
            out_turned,
            gate_weight,
            up_weight,
            down_turned,
            taps,
            vectors,
            gate_square,
            input_square,
            resets.reshape(rows, 1),
        )
        gate_mlp, up_mlp = dot_nn(normed_two, gate_all), dot_nn(normed_two, up_all)
        activated, act_pull = jax.vjp(gated_product, gate_mlp, up_mlp)
        hidden_low = activated.astype(bf16)
        grad_gate_mlp, grad_up_mlp = act_pull(dot_nn(cot_low, down_all))
        (
            mixed,
            middle_low,
            own_grad,
            branch_low,
            inner_grad_low,
            gate_low,
            input_low,
            small,
            gain_two_grad,
            gate_grad,
            up_grad,
            down_grad,
        ) = back(
            count,
            lax.axis_size("fsdp"),
            batches,
            cot_low,
            hidden_low,
            normed_two,
            grad_gate_mlp.astype(bf16),
            grad_up_mlp.astype(bf16),
            branch_pre,
            padded,
            conv_flat,
            gate_pre,
            input_pre,
            carries,
            states,
            ends,
            gate_square,
            input_square,
            own_middle,
            resets.reshape(rows, 1),
            taps,
            jnp.concatenate([vectors, decay_scale * jax.nn.sigmoid(-decay)[None]], 0),
            gain_two[None],
            gate_all,
            up_all,
            down_all,
            out_all,
        )
        block_count = gate_blocks.shape[0]
        block_grads = jnp.concatenate(
            [
                diagonal_blocks(dot_tn(conv_flat, gate_low), block_count),
                diagonal_blocks(dot_tn(conv_flat, input_low), block_count),
            ],
            0,
        )
        block_width = block_grads.shape[-1]
        branch_grad, inner_grad, out_grad, tokens_grad, gains, small, block_grads = tail(
            count,
            middle_low.T,
            mixed_low,
            normed.T,
            branch_low,
            inner_grad_low,
            branch_all,
            inner_all,
            own_values,
            own_grad,
            gain_one[None],
            gain_two_grad[:1],
            small,
            block_grads.reshape(-1, block_width).astype(bf16),
        )
        block_grads = block_grads.astype(f32).reshape(2, block_count, block_width, block_width)
        return (
            mixed.astype(f32).reshape(tokens.shape),
            tokens_grad.astype(f32).reshape(tokens.shape),
            gains[0],
            branch_grad,
            inner_grad,
            small[:4],
            small[4],
            block_grads[0],
            block_grads[1],
            small[5],
            small[6],
            small[7],
            out_grad.T,
            gains[1],
            gate_grad,
            up_grad,
            down_grad.T,
        )
    else:
        branch_all, inner_all, out_all, gate_all, up_all, down_all = [
            lax.all_gather(piece, "seq", axis=0, tiled=True)
            for piece in (
                branch_weight,
                inner_weight,
                out_turned,
                gate_weight,
                up_weight,
                down_turned,
            )
        ]
        tokens_low, cot_low = tokens.reshape(rows, width), cotangent.reshape(rows, width)
        values = tokens_low.astype(f32)
        normed = (values * inverse_rms(values) * gain_one).astype(bf16)
        inner_low = by_sequence(dot_nn(normed, inner_all).astype(bf16))
        branch_pre = by_sequence(dot_nn(normed, branch_all))
        edge_rows = passed_along(inner_low[:, -3:], 1)
        padded = jnp.concatenate([edge_rows, inner_low], 1).astype(f32)
        conv_sum = conv_bias.astype(f32) + taps[0] * padded[:, 3:] + taps[1] * padded[:, 2:-1]
        conv_sum = conv_sum + taps[2] * padded[:, 1:-2] + taps[3] * padded[:, :-3]
        conv_flat = conv_sum.astype(bf16).reshape(rows, units)
        gate_pre = by_sequence(dot_nn(conv_flat, gate_square) + gate_bias.astype(f32))
        input_pre = by_sequence(dot_nn(conv_flat, input_square) + input_bias.astype(f32))
        conv_value = by_sequence(conv_flat).astype(f32)
        carries, drives = gates(gate_pre, input_pre, conv_value, decay)
        prods, local_state = local_scan(carries, drives, False)
        prods_end = prods[:, -1:]
        state_in = Entry(prods_end, local_state[:, -1:], 1).state(None)
        states = local_state + prods * state_in
        mixed_low = (states * gelu_tanh(branch_pre)).astype(bf16).reshape(rows, units)
        own_values = own_rows(tokens_low).astype(f32)
        own_middle = own_values + Halves(ring, dot_nt(mixed_low, out_all), "fsdp").run()
        normed_two = own_middle * inverse_rms(own_middle) * gain_two
        normed_two = Joined(ring, normed_two.astype(bf16), "fsdp").run()
    branch, branch_pull = jax.vjp(gelu_tanh, branch_pre)
    scale_two = inverse_rms(own_middle)
    unit_two = own_middle * scale_two

    gate_mlp = dot_nn(normed_two, gate_all)
    up_mlp = dot_nn(normed_two, up_all)
    activated, act_pull = jax.vjp(gated_product, gate_mlp, up_mlp)
    hidden_low = activated.astype(bf16)
    down_grads = scatter(
        slab_dots(cot_low.T, hidden_low, 0, half), slab_dots(cot_low.T, hidden_low, half, half)
    )
    in_turn(down_grads)
    grad_gate_mlp, grad_up_mlp = act_pull(dot_nn(ring.then(cot_low, 0), down_all))
    gate_mlp_low, up_mlp_low = grad_gate_mlp.astype(bf16), grad_up_mlp.astype(bf16)
    in_turn(down_grads)
    ring.first(gate_mlp_low, up_mlp_low)
    in_turn(down_grads)
    mlp_grads = scatter(
        slab_dots(normed_two.T, gate_mlp_low), slab_dots(normed_two.T, up_mlp_low)
    )
    in_turn(mlp_grads, down_grads)
    gate_mlp_low, up_mlp_low = lax.optimization_barrier(
        (ring.then(gate_mlp_low, 2), up_mlp_low)
    )
    back_sum = Halves(
        ring, dot_nt(gate_mlp_low, gate_all) + dot_nt(up_mlp_low, up_all), "fsdp"
    )
    back_sum.step()
    ring.first(back_sum.step())
    in_turn(mlp_grads, down_grads)
    own_back = back_sum.run(2)
    gain_two_grad = jnp.sum(own_back * unit_two, 0)
    weighted = own_back * gain_two
    own_grad = own_rows(cot_low).astype(f32) + scale_two * (
        weighted - unit_two * jnp.mean(weighted * unit_two, axis=-1, keepdims=True)
    )
    middle_join = Joined(ring, own_grad.astype(bf16), "fsdp")
    ring.first(middle_join.step())
    in_turn(mlp_grads)
    mixed_sum = Halves(ring, dot_nt(ring.then(hidden_low, 2), down_all), "fsdp")
    mixed_sum.step()
    ring.first(mixed_sum.step())
    in_turn(down_grads)
    middle_join.step(2)
    middle_low = middle_join.run()

    grad_mixed = dot_nn(middle_low, out_all).reshape(batches, length, units)
    (grad_branch_pre,) = branch_pull(grad_mixed * states)
    branch_low = grad_branch_pre.astype(bf16).reshape(rows, units)
    following = jnp.concatenate([carries[:, 1:], jnp.ones_like(carries[:, :1])], 1)
    tail_prods, local_adjoint = local_scan(following, grad_mixed * branch, True)
    entry = Entry(prods_end, carries[:, :1] * local_adjoint[:, :1], -1)
    ring.first(local_adjoint, branch_low)
    in_turn(mlp_grads)
    entry.between(ring.then)
    in_turn(down_grads)
    adjoint_in = entry.state(lambda part: ring.then(part, 1))
    adjoint = local_adjoint + tail_prods * adjoint_in
    state_before = jnp.concatenate([state_in, states[:, :-1]], 1)
    _, gate_pull = jax.vjp(gates, gate_pre, input_pre, conv_value, decay)
    grad_gate_pre, grad_input_pre, grad_conv, decay_grad = gate_pull(
        (adjoint * state_before, adjoint)
    )
    gate_low = grad_gate_pre.astype(bf16).reshape(rows, units)
    input_low = grad_input_pre.astype(bf16).reshape(rows, units)
    ring.first(gate_low, input_low)
    in_turn(mlp_grads)
    back_conv = dot_nt(gate_low, gate_square) + dot_nt(input_low, input_square)
    grad_conv = grad_conv + back_conv.reshape(batches, length, units)

    border = jnp.zeros((batches, 3, units), f32)
    spread = jnp.concatenate([border, grad_conv, border], 1)
    stop = length + 3
    grad_padded = taps[0] * spread[:, :stop] + taps[1] * spread[:, 1 : stop + 1]
    grad_padded = grad_padded + taps[2] * spread[:, 2 : stop + 2] + taps[3] * spread[:, 3:]
    returned = passed_along(grad_padded[:, :3], -1)
    mixed_join = Joined(ring, restored(own_middle + mixed_sum.run(1), bf16), "fsdp")
    ring.first(grad_padded, mixed_join.step())
    in_turn(mlp_grads)
    grad_inner = jnp.concatenate(
        [grad_padded[:, 3:-3], grad_padded[:, -3:] + ring.then(returned)], 1
    )
    inner_grad_low = grad_inner.astype(bf16).reshape(rows, units)
    in_turn(*[mlp_grads] * (steps - 6))

    block_count = gate_blocks.shape[0]
    block_grads = jnp.concatenate(
        [
            diagonal_blocks(dot_tn(conv_flat, gate_low), block_count),
            diagonal_blocks(dot_tn(conv_flat, input_low), block_count),
        ],
        0,
    )
    block_width = block_grads.shape[-1]
    taps_grad = jnp.stack(
        [jnp.sum(grad_conv * padded[:, 3 - k : 3 - k + length], (0, 1)) for k in range(4)], 0
    )
    small = jnp.concatenate(
        [
            taps_grad,
            jnp.sum(grad_conv, (0, 1))[None],
            jnp.sum(gate_low.astype(f32), 0)[None],
            jnp.sum(input_low.astype(f32), 0)[None],
            decay_grad[None],
        ],
        0,
    )
    mixed_join.step()
    mixed = mixed_join.run().astype(f32).reshape(tokens.shape)
    gate_grad, up_grad = mlp_grads.sums()
    if ringed:
        branch_grad, inner_grad, out_grad, tokens_grad, gains, small, block_grads = tail(
            count,
            middle_low.T,
            mixed_low,
            normed.T,
            branch_low,
            inner_grad_low,
            branch_all,
            inner_all,
            own_values,
            own_grad,
            gain_one[None],
            gain_two_grad[None],
            small,
            block_grads.reshape(-1, block_width).astype(bf16),
        )
        block_grads = block_grads.astype(f32)
    else:
        out_grads = scatter(
            slab_dots(middle_low.T, mixed_low, 0, half),
            slab_dots(middle_low.T, mixed_low, half, half),
        )
        front_grads = scatter(
            slab_dots(normed.T, branch_low), slab_dots(normed.T, inner_grad_low)
        )
        branch_grad, inner_grad = front_grads.sums()
        out_grad = jnp.concatenate(out_grads.sums(), 0)
        own_front = Halves(
            ring, dot_nt(branch_low, branch_all) + dot_nt(inner_grad_low, inner_all), "fsdp"
        ).run()
        scale_one = inverse_rms(own_values)
        unit_one = own_values * scale_one
        weighted = own_front * gain_one
        own_tokens = own_grad + scale_one * (
            weighted - unit_one * jnp.mean(weighted * unit_one, axis=-1, keepdims=True)
        )
        gains = jnp.stack([jnp.sum(own_front * unit_one, 0), gain_two_grad], 0)
        gains = lax.psum(gains, ("seq", "fsdp"))
        small, block_grads = lax.psum((small, block_grads), "seq")
        tokens_grad = Joined(ring, own_tokens.astype(bf16), "fsdp").run()
    tokens_grad = tokens_grad.astype(f32).reshape(tokens.shape)
    block_grads = block_grads.reshape(2, block_count, block_width, block_width)
    down_grad = jnp.concatenate(down_grads.sums(), 0)
    return (
        mixed,
        tokens_grad,
        gains[0],
        branch_grad,
        inner_grad,
        small[:4],
        small[4],
        block_grads[0],
        block_grads[1],
        small[5],
        small[6],
        small[7],
        out_grad.T,
        gains[1],
        gate_grad,
        up_grad,
        down_grad.T,
    )


def solution(mesh):
    units, both = P("fsdp"), P("seq", "fsdp")
    blocks, turned = P("fsdp", None, None), P("fsdp", "seq")
    rows = P(None, "seq", None)
    return jax.shard_map(
        local,
        mesh=mesh,
        in_specs=(
            rows,
            P(None, "seq"),
            P(),
            both,
            both,
            P(None, "fsdp"),
            units,
            blocks,
            blocks,
            units,
            units,
            units,
            turned,
            P(),
            both,
            both,
            turned,
            rows,
        ),
        out_specs=(
            rows,
            rows,
            P(),
            both,
            both,
            P(None, "fsdp"),
            units,
            blocks,
            blocks,
            units,
            units,
            units,
            turned,
            P(),
            both,
            both,
            turned,
        ),
        check_vma=False,
    )
```

```python
import functools

import jax
import jax.numpy as jnp
from jax import lax
from jax.experimental import pallas as pl
from jax.experimental.pallas import tpu as pltpu
from jax.sharding import PartitionSpec as P

eps = 1e-06
decay_scale = 8.0
f32 = jnp.float32
bf16 = jnp.bfloat16
ring_count = 8


def gelu_tanh(values):
    return jax.nn.gelu(values, approximate=True)


def gated_product(gate_pre, up_pre):
    return gelu_tanh(gate_pre) * up_pre


def gate_math(gate_pre, input_pre, conv_value, decay_param, fresh_start):
    rate_gate = jax.nn.sigmoid(gate_pre)
    inlet_gate = jax.nn.sigmoid(input_pre)
    log_decay = -decay_scale * jax.nn.softplus(-decay_param) * rate_gate
    input_scale = jnp.where(fresh_start, 1.0, jnp.sqrt(-jnp.expm1(2.0 * log_decay)))
    carries = jnp.where(fresh_start, 0.0, jnp.exp(log_decay))
    return (carries, input_scale * inlet_gate * conv_value)


def dot_nn(left, right):
    return jnp.dot(left, right, preferred_element_type=f32)


def dot_nt(left, right):
    return lax.dot_general(left, right, (((1,), (1,)), ((), ())), preferred_element_type=f32)


def dot_tn(left, right):
    return lax.dot_general(left, right, (((0,), (0,)), ((), ())), preferred_element_type=f32)


def inverse_rms(values):
    return lax.rsqrt(jnp.mean(values * values, axis=-1, keepdims=True) + eps)


def scan_body(backward, a_ref, b_ref, prod_ref, state_ref):
    batches, length, units = a_ref.shape
    tiles = length // 8
    rows = lax.broadcasted_iota(jnp.int32, (8, units), 0)

    def step(index, carry):
        tile = tiles - 1 - index if backward else index
        where_rows = pl.ds(pl.multiple_of(tile * 8, 8), 8)
        following = []
        for batch in range(batches):
            prod_in, state_in = carry[batch]
            a = a_ref[batch, where_rows, :]
            b = b_ref[batch, where_rows, :]
            for shift in (1, 2, 4):
                turn = 8 - shift if backward else shift
                inside = rows < 8 - shift if backward else rows >= shift
                a_moved = jnp.where(inside, pltpu.roll(a, turn, 0), 1.0)
                b_moved = jnp.where(inside, pltpu.roll(b, turn, 0), 0.0)
                b = a * b_moved + b
                a = a * a_moved
            b = b + a * state_in
            a = a * prod_in
            prod_ref[batch, where_rows, :] = a
            state_ref[batch, where_rows, :] = b
            edge = 0 if backward else 7
            following.append((a[edge : edge + 1], b[edge : edge + 1]))
        return tuple(following)

    first = tuple(
        (jnp.ones((1, units), f32), jnp.zeros((1, units), f32)) for _ in range(batches)
    )
    lax.fori_loop(0, tiles, step, first)


def local_scan(a, b, backward):
    shape = jax.ShapeDtypeStruct(a.shape, f32)
    elements = a.shape[0] * a.shape[1] * a.shape[2]
    return pl.pallas_call(
        functools.partial(scan_body, backward),
        out_shape=(shape, shape),
        in_specs=[pl.BlockSpec(memory_space=pltpu.VMEM)] * 2,
        out_specs=(pl.BlockSpec(memory_space=pltpu.VMEM),) * 2,
        compiler_params=pltpu.CompilerParams(vmem_limit_bytes=32 * 1024 * 1024),
        cost_estimate=pl.CostEstimate(
            flops=20 * elements, bytes_accessed=16 * elements, transcendentals=0
        ),
    )(a, b)


def move_body(table_ref, in_ref, out_ref):
    out_ref[...] = in_ref[...].astype(out_ref.dtype)


def move_slabs(values, table, dtype):
    rows, width = values.shape
    slabs = table.shape[0]
    return pl.pallas_call(
        move_body,
        out_shape=jax.ShapeDtypeStruct((rows, width), dtype),
        grid_spec=pltpu.PrefetchScalarGridSpec(
            num_scalar_prefetch=1,
            grid=(slabs,),
            in_specs=[pl.BlockSpec((rows, width // slabs), lambda k, where: (0, where[k]))],
            out_specs=pl.BlockSpec((rows, width // slabs), lambda k, where: (0, k)),
        ),
        cost_estimate=pl.CostEstimate(
            flops=0, bytes_accessed=8 * rows * width, transcendentals=0
        ),
    )(table, values)


class Ring:
    def __init__(self, count):
        self.count = count
        self.order = list(range(0, count, 2)) + list(range(count - 1, 0, -2))
        self.place = [self.order.index(i) for i in range(count)]
        self.forth = [(self.order[i], self.order[(i + 1) % count]) for i in range(count)]
        self.back = [(there, here) for here, there in self.forth]
        self.sent, self.awaited = [], []

    def tables(self):
        here = jnp.asarray(self.place, jnp.int32)[lax.axis_index("seq")]
        steps = jnp.arange(self.count, dtype=jnp.int32)
        to_ring = jnp.asarray(self.order, jnp.int32)[(here - steps) % self.count]
        to_plain = (here - jnp.asarray(self.place, jnp.int32)) % self.count
        return to_ring, to_plain

    def send(self, forth, back):
        earlier = list(self.sent[-2]) if len(self.sent) > 1 else []
        if earlier or self.awaited:
            forth, back = lax.optimization_barrier((forth, back, *earlier, *self.awaited))[:2]
        self.awaited = []
        self.sent.append(
            (lax.ppermute(forth, "seq", self.forth), lax.ppermute(back, "seq", self.back))
        )
        return self.sent[-1]

    def first(self, *values):
        self.awaited.extend(values)

    def then(self, value, under_way=1):
        if len(self.sent) <= under_way:
            return value
        return lax.optimization_barrier((value, *self.sent[-1 - under_way]))[0]


class Gather:
    def __init__(self, ring, forth, back):
        self.ring, self.forth, self.back = ring, [forth], [back]

    def step(self):
        forth, back = self.ring.send(self.forth[-1], self.back[-1])
        self.forth.append(forth)
        self.back.append(back)

    def slabs(self):
        count = self.ring.count
        return self.forth, [self.back[-k % count] for k in range(count)]


class Scatter:
    def __init__(self, ring, forth_slab, back_slab):
        self.ring, self.forth_slab, self.back_slab = ring, forth_slab, back_slab
        self.at = 1
        self.forth = forth_slab(1).astype(bf16)
        self.back = back_slab(ring.count - 1).astype(bf16)

    def step(self):
        count = self.ring.count
        forth, back = self.ring.send(self.forth, self.back)
        self.at += 1
        self.forth = forth.astype(f32) + self.forth_slab(self.at % count)
        self.back = back.astype(f32) + self.back_slab(count - self.at)
        if self.at < count:
            self.forth, self.back = self.forth.astype(bf16), self.back.astype(bf16)

    def sums(self):
        return self.forth, self.back


class PlainGather:
    def __init__(self, ring, forth, back):
        self.pieces = (forth, back)

    def step(self):
        pass

    def slabs(self):
        return tuple(list(lax.all_gather(piece, "seq")) for piece in self.pieces)


class PlainScatter:
    def __init__(self, ring, forth_slab, back_slab):
        self.terms = (forth_slab, back_slab)

    def step(self):
        pass

    def sums(self):
        count = lax.axis_size("seq")
        return tuple(
            lax.psum_scatter(
                jnp.concatenate([term(k) for k in range(count)], 0),
                "seq",
                scatter_dimension=0,
                tiled=True,
            )
            for term in self.terms
        )


def in_turn(*transfers):
    for transfer in transfers:
        transfer.step()


def swapped(values, axis, bit):
    return lax.ppermute(values, axis, [(i, i ^ bit) for i in range(lax.axis_size(axis))])


class Exchange:
    def __init__(self, ring, values, axis):
        self.ring, self.values, self.axis = ring, values, axis
        self.got = None
        count = lax.axis_size(axis)
        self.bits = [1 << i for i in range(count.bit_length() - 1)]
        self.stages = self.plan()

    def upper(self, bit):
        return (lax.axis_index(self.axis) // bit) % 2 > 0

    def step(self, under_way=None):
        if self.got is not None:
            got, bit, end = self.got
            self.got = None
            end(got if under_way is None else self.ring.then(got, under_way), bit)
        if self.stages:
            start, end, bit = self.stages.pop(0)
            self.got = (swapped(start(bit), self.axis, bit), bit, end)
        return self.values

    def run(self, under_way=None):
        while self.stages or self.got is not None:
            self.step(under_way)
        return self.values

    def start_half(self, bit):
        half = self.values.shape[0] // 2
        kept, sent = [
            jnp.where(self.upper(bit) == side, self.values[half:], self.values[:half])
            for side in (True, False)
        ]
        self.values = kept
        return sent.astype(bf16)

    def end_half(self, got, bit):
        self.values = self.values.astype(f32) + got.astype(f32)

    def start_join(self, bit):
        return self.values

    def end_join(self, got, bit):
        upper, own = self.upper(bit), self.values
        self.values = jnp.concatenate([jnp.where(upper, got, own), jnp.where(upper, own, got)], 0)

    def end_sum(self, got, bit):
        self.values = self.values + got

    def halving(self):
        return [(self.start_half, self.end_half, bit) for bit in self.bits]

    def joining(self):
        return [(self.start_join, self.end_join, bit) for bit in reversed(self.bits)]


class Halves(Exchange):
    def plan(self):
        return self.halving()


class Joined(Exchange):
    def plan(self):
        return self.joining()


class Everywhere(Exchange):
    def plan(self):
        stages = self.halving() + self.joining()
        middle = len(self.bits)

        def start_first_join(bit):
            self.values = self.values.astype(bf16)
            return self.values

        if stages:
            stages[middle] = (start_first_join, self.end_join, stages[middle][2])
        return stages


class SmallSum(Exchange):
    def plan(self):
        return [(self.start_join, self.end_sum, bit) for bit in self.bits]


def own_rows(values):
    count, mine = lax.axis_size("fsdp"), lax.axis_index("fsdp")
    bit = 1
    while bit < count:
        half = values.shape[0] // 2
        values = lax.dynamic_slice_in_dim(values, ((mine // bit) % 2) * half, half, 0)
        bit *= 2
    return values


def halves_joined(own):
    count, mine = lax.axis_size("fsdp"), lax.axis_index("fsdp")
    bit = count // 2
    while bit:
        got = lax.ppermute(own, "fsdp", [(i, i ^ bit) for i in range(count)])
        upper = (mine // bit) % 2 > 0
        own = jnp.concatenate([jnp.where(upper, got, own), jnp.where(upper, own, got)], 0)
        bit //= 2
    return own


def passed_along(block, distance):
    devices = range(lax.axis_size("seq"))
    route = [(i - distance, i) for i in devices if i - distance in devices]
    return lax.ppermute(block, "seq", route)


def joined_maps(earlier, later):
    return jnp.stack([earlier[0] * later[0], later[1] + later[0] * earlier[1]], 0)


class Entry:
    def __init__(self, prods, states, sign):
        self.pair, self.sign = jnp.stack([prods, states], 0), sign
        self.count = lax.axis_size("seq")
        self.direct = self.count == ring_count
        if self.direct:
            self.other = swapped(self.pair, "seq", 1)

    def between(self, hold):
        if not self.direct:
            return
        self.other = hold(self.other)
        self.second = lax.axis_index("seq") % 2 == (1 if self.sign > 0 else 0)
        earlier = jnp.where(self.second, self.other, self.pair)
        later = jnp.where(self.second, self.pair, self.other)
        both = joined_maps(earlier, later)
        self.parts = [
            passed_along(both, self.sign * distance) for distance in range(self.count - 2, 0, -2)
        ]

    def state(self, hold):
        if self.direct:
            parts = [hold(self.parts[0])] + self.parts[1:]
            state = parts[0][1]
            for part in parts[1:]:
                state = part[1] + part[0] * state
            return jnp.where(self.second, self.other[1] + self.other[0] * state, state)
        pair = passed_along(self.pair, self.sign)
        distance = 1
        while distance < self.count:
            pair = joined_maps(passed_along(pair, self.sign * distance), pair)
            distance *= 2
        return pair[1]


def ring_index(place, count):
    place = lax.rem(place + 2 * count, count)
    odd = place // (count // 2)
    return (1 - odd) * (2 * place) + odd * (2 * count - 1 - 2 * place)


def ring_place(index, count):
    odd = lax.rem(index, 2)
    return (1 - odd) * (index // 2) + odd * (count - 1 - index // 2)


def partner(index, bit):
    return index + bit * (1 - 2 * lax.rem(index // bit, 2))


class Copies:
    def __init__(self, send_sems, recv_sems):
        self.send_sems, self.recv_sems = send_sems, recv_sems
        self.started, self.waiting = 0, []

    def start(self, source, target, device):
        slot = self.started
        copy = pltpu.make_async_remote_copy(
            src_ref=source,
            dst_ref=target,
            send_sem=self.send_sems.at[slot],
            recv_sem=self.recv_sems.at[slot],
            device_id=device,
            device_id_type=pl.DeviceIdType.MESH,
        )
        copy.start()
        self.started += 1
        self.waiting.append(copy)
        return copy

    def sent(self, copy):
        copy.wait_send()
        self.waiting.remove(copy)

    def end(self):
        for copy in self.waiting:
            copy.wait_send()


class Moves:
    def __init__(self, sems):
        self.sems, self.started, self.waiting = sems, 0, []

    def start(self, source, target):
        copy = pltpu.make_async_copy(source, target, self.sems.at[self.started])
        copy.start()
        self.started += 1
        self.waiting.append(copy)
        return copy

    def wait(self, number):
        for copy in self.waiting[:number]:
            copy.wait()
        self.waiting = self.waiting[number:]


def greet(devices):
    barrier = pltpu.get_barrier_semaphore()
    for device in devices:
        pl.semaphore_signal(
            barrier, inc=1, device_id=device, device_id_type=pl.DeviceIdType.MESH
        )
    pl.semaphore_wait(barrier, len(devices))


tail_copies = 28 + 4 + 6 + 3 + 5


def tail_body(
    count,
    emb_ref,
    mixed_ref,
    normed_ref,
    branch_ref,
    inner_ref,
    branch_all_in,
    inner_all_in,
    values_ref,
    grad_ref,
    gain_ref,
    gain_two_ref,
    small_ref,
    blocks_ref,
    branch_out,
    inner_out,
    out_out,
    tokens_out,
    gains_out,
    small_out,
    blocks_out,
    wide_sent,
    wide_got,
    slim_sent,
    slim_got,
    half_sent,
    half_kept,
    half_got,
    own_sent,
    own_got,
    small_sums,
    small_got,
    gain_sums,
    gain_got,
    blocks_one,
    blocks_two,
    blocks_got_one,
    blocks_got_two,
    blocks_got_three,
    branch_all_ref,
    inner_all_ref,
    move_sems,
    send_sems,
    recv_sems,
):
    index, unit = lax.axis_index("seq"), lax.axis_index("fsdp")
    place = ring_place(index, count)
    forth, back = {"seq": ring_index(place + 1, count)}, {"seq": ring_index(place - 1, count)}
    across = [{"seq": partner(index, bit)} for bit in (1, 2, 4)]
    beside = [{"fsdp": partner(unit, bit)} for bit in (1, 2)]
    copies = Copies(send_sems, recv_sems)
    rows, units = branch_ref.shape
    slab = normed_ref.shape[1] // count
    tn = (((0,), (0,)), ((), ()))
    moves = Moves(move_sems)
    moves.start(branch_all_in, branch_all_ref)
    moves.start(inner_all_in, inner_all_ref)

    greet([forth, back] + across + beside)

    bits = [lax.rem(index // bit, 2) for bit in (1, 2, 4)]
    high = blocks_ref.shape[0]
    firsts = [high // 2, high // 4, high // 8]

    blocks_copy = copies.start(
        blocks_ref.at[rows_at((1 - bits[0]) * firsts[0], firsts[0])], blocks_got_one, across[0]
    )
    small_sums[0] = small_ref[...]
    small_copy = copies.start(small_sums.at[0], small_got.at[0], across[0])

    cut = slim_got.shape[2]
    parts = (slice(0, cut), slice(cut, units))

    def out_term(k, way):
        return lax.dot_general(
            mixed_ref[:, parts[way]],
            emb_ref[:, k * slab : (k + 1) * slab],
            tn,
            preferred_element_type=f32,
        )

    def front_term(k, way):
        return lax.dot_general(
            (inner_ref if way else branch_ref)[...],
            normed_ref[:, k * slab : (k + 1) * slab],
            tn,
            preferred_element_type=f32,
        )

    rings = {}

    def send(name, way, step, total):
        sent, got = (slim_sent, slim_got) if name == "out" else (wide_sent, wide_got)
        there = pl.ds(0, total.shape[0])
        sent[way, step, there, :] = total.astype(bf16)
        rings[name, way] = copies.start(
            sent.at[way, step, there], got.at[way, step, there], back if way else forth
        )

    def term(name, way, step):
        k = (count - step) % count if way else step % count
        return out_term(k, way) if name == "out" else front_term(k, way)

    def serve(name, step):
        got = slim_got if name == "out" else wide_got
        terms = [term(name, way, step) for way in (0, 1)]
        for way, own in enumerate(terms):
            rings[name, way].wait_recv()
            total = got[way, step - 2, pl.ds(0, own.shape[0]), :].astype(f32) + own
            if step < count:
                send(name, way, step - 1, total)
            elif name == "out":
                out_out[parts[way], :] = total
            else:
                (inner_out if way else branch_out)[...] = total

    for name in ("out", "front"):
        for way in (0, 1):
            send(name, way, 0, term(name, way, 1))
    moves.wait(2)

    core, side = lax.rem(unit, 2), lax.rem(unit // 2, 2)
    mid, own = rows // 2, rows // 4

    def front_back(start, k):
        columns = slice(k * slab, (k + 1) * slab)
        return jnp.dot(
            branch_ref[rows_at(start, mid), :],
            branch_all_ref[:, columns],
            preferred_element_type=f32,
        ) + jnp.dot(
            inner_ref[rows_at(start, mid), :],
            inner_all_ref[:, columns],
            preferred_element_type=f32,
        )

    for k in range(count):
        half_sent[:, k * slab : (k + 1) * slab] = front_back((1 - core) * mid, k).astype(bf16)
    half_copy = copies.start(half_sent, half_got, beside[0])
    serve("out", 2)
    for k in range(count):
        half_kept[:, k * slab : (k + 1) * slab] = front_back(core * mid, k)
    half_copy.wait_recv()
    other = rows_at((1 - side) * own, own)
    mine = rows_at(side * own, own)
    own_sent[...] = (half_kept[other, :] + half_got[other, :].astype(f32)).astype(bf16)
    own_copy = copies.start(own_sent, own_got, beside[1])
    serve("front", 2)

    blocks_copy.wait_recv()
    blocks_one[...] = (
        blocks_ref[rows_at(bits[0] * firsts[0], firsts[0]), :].astype(f32)
        + blocks_got_one[...].astype(f32)
    ).astype(bf16)
    blocks_copy = copies.start(
        blocks_one.at[rows_at((1 - bits[1]) * firsts[1], firsts[1])], blocks_got_two, across[1]
    )
    small_copy.wait_recv()
    small_sums[1] = small_sums[0] + small_got[0]
    small_copy = copies.start(small_sums.at[1], small_got.at[1], across[1])
    serve("out", 3)
    serve("front", 3)

    own_copy.wait_recv()
    values = values_ref[...]
    scale = lax.rsqrt(jnp.mean(values * values, axis=-1, keepdims=True) + eps)
    unit_values = values * scale
    front = half_kept[mine, :] + half_got[mine, :].astype(f32) + own_got[...].astype(f32)
    gain_grad = jnp.sum(front * unit_values, 0, keepdims=True)
    weighted = front * gain_ref[...]
    result = grad_ref[...] + scale * (
        weighted - unit_values * jnp.mean(weighted * unit_values, axis=-1, keepdims=True)
    )
    low = result.astype(bf16)
    own_at = rows_at(core * mid + side * own, own)
    gain_sums[0] = jnp.zeros_like(gain_sums[0])
    for k in range(count):
        to = pl.ds(pl.multiple_of(ring_index(place - k, count) * slab, slab), slab)
        part = slice(k * slab, (k + 1) * slab)
        tokens_out[own_at, to] = low[:, part]
        gain_sums[0, 0:1, to] = gain_grad[:, part]
        gain_sums[0, 1:2, to] = gain_two_ref[:, part]
    tokens_copy = copies.start(tokens_out.at[own_at], tokens_out.at[own_at], beside[1])
    gain_copy = copies.start(gain_sums.at[0], gain_got.at[0], across[0])
    serve("out", 4)
    serve("front", 4)

    blocks_copy.wait_recv()
    blocks_two[...] = (
        blocks_one[rows_at(bits[1] * firsts[1], firsts[1]), :].astype(f32)
        + blocks_got_two[...].astype(f32)
    ).astype(bf16)
    blocks_copy = copies.start(
        blocks_two.at[rows_at((1 - bits[2]) * firsts[2], firsts[2])], blocks_got_three, across[2]
    )
    small_copy.wait_recv()
    small_sums[2] = small_sums[1] + small_got[1]
    small_copy = copies.start(small_sums.at[2], small_got.at[2], across[2])
    gain_copy.wait_recv()
    gain_sums[1] = gain_sums[0] + gain_got[0]
    gain_copy = copies.start(gain_sums.at[1], gain_got.at[1], across[1])
    tokens_copy.wait_recv()
    both_at = rows_at(core * mid, mid)
    tokens_copy = copies.start(tokens_out.at[both_at], tokens_out.at[both_at], beside[0])
    serve("out", 5)
    serve("front", 5)

    blocks_copy.wait_recv()
    starts = [bits[0] * firsts[0]]
    for bit, first in zip(bits[1:], firsts[1:]):
        starts.append(starts[-1] + bit * first)
    at = [rows_at(start, first) for start, first in zip(starts, firsts)]
    blocks_out[at[2], :] = (
        blocks_two[rows_at(bits[2] * firsts[2], firsts[2]), :].astype(f32)
        + blocks_got_three[...].astype(f32)
    ).astype(bf16)
    blocks_copy = copies.start(blocks_out.at[at[2]], blocks_out.at[at[2]], across[2])
    gain_copy.wait_recv()
    gain_sums[2] = gain_sums[1] + gain_got[1]
    gain_copy = copies.start(gain_sums.at[2], gain_got.at[2], across[2])
    small_copy.wait_recv()
    small_out[...] = small_sums[2] + small_got[2]
    serve("out", 6)
    serve("front", 6)

    blocks_copy.wait_recv()
    blocks_copy = copies.start(blocks_out.at[at[1]], blocks_out.at[at[1]], across[1])
    gain_copy.wait_recv()
    gain_sums[3] = gain_sums[2] + gain_got[2]
    gain_copy = copies.start(gain_sums.at[3], gain_got.at[3], beside[0])
    serve("out", 7)
    gain_copy.wait_recv()
    gain_sums[4] = gain_sums[3] + gain_got[3]
    gain_copy = copies.start(gain_sums.at[4], gain_got.at[4], beside[1])
    serve("front", 7)
    blocks_copy.wait_recv()
    blocks_copy = copies.start(blocks_out.at[at[0]], blocks_out.at[at[0]], across[0])
    serve("out", 8)
    gain_copy.wait_recv()
    gains_out[...] = gain_sums[4] + gain_got[4]
    tokens_copy.wait_recv()
    blocks_copy.wait_recv()
    serve("front", 8)
    copies.end()


def tail(count, *operands):
    emb, mixed, normed, *_ = operands
    small, blocks = operands[-2:]
    rows, width = emb.shape
    units = mixed.shape[1]
    slab, cut = width // count, -(-units // 256) * 128
    high, block_width = blocks.shape
    whole = pl.BlockSpec(memory_space=pltpu.VMEM)
    grad = jax.ShapeDtypeStruct((units, slab), f32)
    steps = count - 1
    return pl.pallas_call(
        functools.partial(tail_body, count),
        out_shape=(
            grad,
            grad,
            grad,
            jax.ShapeDtypeStruct((rows, width), bf16),
            jax.ShapeDtypeStruct((8, width), f32),
            jax.ShapeDtypeStruct(small.shape, f32),
            jax.ShapeDtypeStruct(blocks.shape, bf16),
        ),
        in_specs=[whole] * 5
        + [pl.BlockSpec(memory_space=pl.ANY)] * 2
        + [whole] * (len(operands) - 7),
        out_specs=(whole,) * 7,
        scratch_shapes=[
            pltpu.VMEM((2, steps, units, slab), bf16),
            pltpu.VMEM((2, steps, units, slab), bf16),
            pltpu.VMEM((2, steps, cut, slab), bf16),
            pltpu.VMEM((2, steps, cut, slab), bf16),
            pltpu.VMEM((rows // 2, width), bf16),
            pltpu.VMEM((rows // 2, width), f32),
            pltpu.VMEM((rows // 2, width), bf16),
            pltpu.VMEM((rows // 4, width), bf16),
            pltpu.VMEM((rows // 4, width), bf16),
            pltpu.VMEM((3, *small.shape), f32),
            pltpu.VMEM((3, *small.shape), f32),
            pltpu.VMEM((5, 8, width), f32),
            pltpu.VMEM((5, 8, width), f32),
            pltpu.VMEM((high // 2, block_width), bf16),
            pltpu.VMEM((high // 4, block_width), bf16),
            pltpu.VMEM((high // 2, block_width), bf16),
            pltpu.VMEM((high // 4, block_width), bf16),
            pltpu.VMEM((high // 8, block_width), bf16),
            pltpu.VMEM((units, width), bf16),
            pltpu.VMEM((units, width), bf16),
            pltpu.SemaphoreType.DMA((2,)),
            pltpu.SemaphoreType.DMA((tail_copies,)),
            pltpu.SemaphoreType.DMA((tail_copies,)),
        ],
        compiler_params=pltpu.CompilerParams(
            collective_id=0, has_side_effects=True, vmem_limit_bytes=60 * 1024 * 1024
        ),
    )(*operands)


def peers(count, units):
    index, unit = lax.axis_index("seq"), lax.axis_index("fsdp")
    along = [{"seq": lax.rem(index + distance, count)} for distance in range(1, count)]
    beside = [{"fsdp": partner(unit, 1 << i)} for i in range(units.bit_length() - 1)]
    return along, beside


def rows_at(start, size, multiple=16):
    return pl.ds(pl.multiple_of(start, multiple), size)


def dot_nt_here(left, right):
    return lax.dot_general(left, right, (((1,), (1,)), ((), ())), preferred_element_type=f32)


def dot_slabs(left, right_ref, slab, count):
    for k in range(count):
        columns = slice(k * slab, (k + 1) * slab)
        yield columns, jnp.dot(left, right_ref[:, columns], preferred_element_type=f32)


def scan_rows(a_ref, b_ref, prod_ref, state_ref, batches, backward):
    length, units = a_ref.shape[0] // batches, a_ref.shape[1]
    tiles = length // 8
    rows = lax.broadcasted_iota(jnp.int32, (8, units), 0)

    def step(index, carry):
        tile = tiles - 1 - index if backward else index
        following = []
        for batch in range(batches):
            prod_in, state_in, a_next = carry[batch]
            at = rows_at(batch * length + tile * 8, 8, 8)
            a, b = a_ref[at, :], b_ref[at, :]
            a_first = a[0:1]
            if backward:
                a = jnp.where(rows < 7, pltpu.roll(a, 7, 0), a_next)
            for shift in (1, 2, 4):
                turn = 8 - shift if backward else shift
                inside = rows < 8 - shift if backward else rows >= shift
                a_moved = jnp.where(inside, pltpu.roll(a, turn, 0), 1.0)
                b_moved = jnp.where(inside, pltpu.roll(b, turn, 0), 0.0)
                b = a * b_moved + b
                a = a * a_moved
            b = b + a * state_in
            a = a * prod_in
            prod_ref[at, :] = a
            state_ref[at, :] = b
            edge = 0 if backward else 7
            following.append((a[edge : edge + 1], b[edge : edge + 1], a_first))
        return tuple(following)

    one, zero = jnp.ones((1, units), f32), jnp.zeros((1, units), f32)
    maps = lax.fori_loop(0, tiles, step, ((one, zero, one),) * batches)
    return [(prod, state) for prod, state, _ in maps]


def entry_states(ends_ref, got_ref, index, count, batches, sign):
    states = []
    for batch in range(batches):
        state = jnp.zeros_like(ends_ref[0:1, :])
        for distance in range(count - 1, 0, -1):
            there = index - distance >= 0 if sign > 0 else index + distance < count
            prods = got_ref[distance - 1, batch : batch + 1, :]
            longer = got_ref[distance - 1, batches + batch : batches + batch + 1, :] + prods * state
            state = jnp.where(there, longer, 0.0)
        states.append(state)
    return states


head_copies = 9 * (ring_count - 1) + 5
row_block = 32


def head_body(
    count,
    fsdp,
    batches,
    tokens_ref,
    cot_ref,
    gain_one_ref,
    gain_two_ref,
    branch_ref,
    inner_ref,
    out_ref,
    gate_ref,
    up_ref,
    down_ref,
    taps_ref,
    vectors_ref,
    gate_blocks_ref,
    input_blocks_ref,
    fresh_ref,
    gate_all,
    up_all,
    down_all,
    branch_all_far,
    inner_all_far,
    out_all_far,
    cot_out_far,
    normed_out_far,
    branch_pre_far,
    padded_far,
    conv_low_far,
    gate_pre_far,
    input_pre_far,
    carries_far,
    states_far,
    mixed_low_far,
    gate_square_far,
    input_square_far,
    ends,
    own_values,
    own_middle,
    normed_two,
    branch_all,
    inner_all,
    out_all,
    cot_out,
    normed_out,
    branch_pre,
    padded,
    conv_low,
    gate_pre,
    input_pre,
    carries,
    states,
    mixed_low,
    gate_square_ref,
    input_square_ref,
    tokens_low,
    gains,
    prods,
    local_states,
    edges_sent,
    edges_got,
    ends_sent,
    ends_got,
    half_sent,
    half_kept,
    half_got,
    own_sent,
    own_got,
    local_sems,
    far_sems,
    send_sems,
    recv_sems,
):
    index, unit = lax.axis_index("seq"), lax.axis_index("fsdp")
    place = ring_place(index, count)
    forth, back = {"seq": ring_index(place + 1, count)}, {"seq": ring_index(place - 1, count)}
    along, beside = peers(count, fsdp)
    copies = Copies(send_sems, recv_sems)
    rows, width = tokens_ref.shape
    units, hidden = branch_ref.shape[0], down_ref.shape[0]
    length, slab = rows // batches, width // count
    core, side = lax.rem(unit, 2), lax.rem(unit // 2, 2)
    mid, own = rows // 2, rows // 4

    locals_of = []
    for source, target in zip(
        (branch_ref, inner_ref, out_ref, gate_ref, up_ref, down_ref),
        (branch_all, inner_all, out_all, gate_all, up_all, down_all),
    ):
        first = target.at[pl.ds(0, slab)]
        if source.shape[1] == slab:
            first = target.at[:, pl.ds(0, slab)]
        copy = pltpu.make_async_copy(source, first, local_sems.at[len(locals_of)])
        copy.start()
        locals_of.append(copy)

    greet(along + beside)

    pairs = {
        "front": ((branch_ref, branch_all, 0, units), (inner_ref, inner_all, 0, units)),
        "out": (
            (out_ref, out_all, 0, units // 2),
            (out_ref, out_all, units // 2, units // 2),
        ),
        "mlp": ((gate_ref, gate_all, None, None), (up_ref, up_all, None, None)),
        "down": (
            (down_ref, down_all, 0, hidden // 2),
            (down_ref, down_all, hidden // 2, hidden // 2),
        ),
    }
    under_way = {}

    def start(name, step):
        for way in (0, 1):
            shard, whole, first, size = pairs[name][way]

            def slab_at(k):
                if first is None:
                    return whole.at[pl.ds(k * slab, slab)]
                return whole.at[pl.ds(first, size), pl.ds(k * slab, slab)]

            if step > 1:
                under_way[name, way].wait_recv()
            there = (count - step) % count if way else step
            here = (there + 1) % count if way else step - 1
            if step > 1:
                source = slab_at(here)
            else:
                source = shard if first is None else shard.at[pl.ds(first, size)]
            under_way[name, way] = copies.start(source, slab_at(there), back if way else forth)

    def finish(name):
        for way in (0, 1):
            under_way[name, way].wait_recv()

    start("front", 1)
    start("out", 1)

    for k in range(count):
        plain = pl.ds(pl.multiple_of(ring_index(place - k, count) * slab, slab), slab)
        part = slice(k * slab, (k + 1) * slab)
        tokens_low[:, part] = tokens_ref[:, plain]
        gains[0:1, part] = gain_one_ref[:, plain]
        gains[1:2, part] = gain_two_ref[:, plain]
    start("front", 2)
    start("out", 2)

    def norm_block(block, carry):
        at = rows_at(block * row_block, row_block)
        values = tokens_low[at, :].astype(f32)
        scale = lax.rsqrt(jnp.mean(values * values, axis=-1, keepdims=True) + eps)
        normed_out[at, :] = (values * scale * gains[0:1, :]).astype(bf16)
        return carry

    lax.fori_loop(0, rows // row_block, norm_block, 0)
    own_values[...] = tokens_low[rows_at(core * mid + side * own, own), :].astype(f32)
    start("front", 3)
    start("out", 3)
    for blocks, square in (
        (gate_blocks_ref, gate_square_ref),
        (input_blocks_ref, input_square_ref),
    ):
        square[...] = jnp.zeros_like(square)
        size = blocks.shape[1]
        for j in range(blocks.shape[0]):
            square[j * size : (j + 1) * size, j * size : (j + 1) * size] = blocks[j]
    for k in range(count):
        plain = pl.ds(pl.multiple_of(ring_index(place - k, count) * slab, slab), slab)
        cot_out[:, k * slab : (k + 1) * slab] = cot_ref[:, plain]
    for step in range(4, count):
        start("front", step)
        start("out", step)
    start("mlp", 1)
    start("down", 1)
    for copy in locals_of:
        copy.wait()
    finish("front")

    for batch in range(batches):
        at = slice(batch * length, (batch + 1) * length)
        top = batch * (length + 8)
        inner = dot_nt_here(normed_out[at, :], inner_all[...])
        padded[top + 8 : top + 8 + length, :] = inner.astype(bf16).astype(f32)
        edges_sent[batch] = padded[top + length : top + length + 8, :]
    edge_copy = copies.start(edges_sent, edges_got, along[0])
    for batch in range(batches):
        at = slice(batch * length, (batch + 1) * length)
        branch_pre[at, :] = dot_nt_here(normed_out[at, :], branch_all[...])
    edge_copy.wait_recv()
    for batch in range(batches):
        top = batch * (length + 8)
        padded[top : top + 8, :] = jnp.where(index > 0, edges_got[batch], 0.0)
    start("mlp", 2)
    bias, gate_bias, input_bias, rate = [vectors_ref[i : i + 1, :] for i in range(4)]

    def conv_block(block, carry):
        batch = block // (length // row_block)
        wide = padded[rows_at(block * row_block + batch * 8, row_block + 8, 8), :]
        total = bias + taps_ref[0:1, :] * wide[8:] + taps_ref[1:2, :] * wide[7:-1]
        total = total + taps_ref[2:3, :] * wide[6:-2] + taps_ref[3:4, :] * wide[5:-3]
        conv_low[rows_at(block * row_block, row_block), :] = total.astype(bf16)
        return carry

    lax.fori_loop(0, rows // row_block, conv_block, 0)
    for batch in range(batches):
        at = slice(batch * length, (batch + 1) * length)
        conv = conv_low[at, :]
        gate_pre[at, :] = (
            jnp.dot(conv, gate_square_ref[...], preferred_element_type=f32) + gate_bias
        )
        input_pre[at, :] = (
            jnp.dot(conv, input_square_ref[...], preferred_element_type=f32) + input_bias
        )
    start("down", 2)

    def gate_block(block, carry):
        at = rows_at(block * row_block, row_block)
        rate_gate = jax.nn.sigmoid(gate_pre[at, :])
        inlet_gate = jax.nn.sigmoid(input_pre[at, :])
        log_decay = rate * rate_gate
        decay = jnp.exp(log_decay)
        fresh = fresh_ref[at, :] > 0
        scale = jnp.sqrt(-jnp.tanh(log_decay) * (1.0 + decay * decay))
        carries[at, :] = jnp.where(fresh, 0.0, decay)
        local_states[at, :] = (
            jnp.where(fresh, 1.0, scale) * inlet_gate * conv_low[at, :].astype(f32)
        )
        return carry

    lax.fori_loop(0, rows // row_block, gate_block, 0)
    scanned = scan_rows(carries, local_states, prods, local_states, batches, False)
    ends_sent[...] = jnp.zeros_like(ends_sent)
    for batch, (prod, state) in enumerate(scanned):
        ends_sent[batch : batch + 1, :] = prod
        ends_sent[batches + batch : batches + batch + 1, :] = state
    ends[...] = ends_sent[...]
    end_copies = [
        copies.start(ends_sent, ends_got.at[distance - 1], along[distance - 1])
        for distance in range(1, count)
    ]
    start("mlp", 3)
    for copy in end_copies:
        copy.wait_recv()
    entries = entry_states(ends, ends_got, index, count, batches, 1)

    for batch in range(batches):
        entry = entries[batch]
        top = batch * (length + 8)
        states[top : top + 8, :] = jnp.broadcast_to(entry, (8, units))

        def state_block(block, carry, batch=batch, entry=entry):
            at = rows_at(batch * length + block * row_block, row_block)
            state = local_states[at, :] + prods[at, :] * entry
            states[rows_at(8 + batch * (length + 8) + block * row_block, row_block, 8), :] = state
            mixed_low[at, :] = (state * gelu_tanh(branch_pre[at, :])).astype(bf16)
            return carry

        lax.fori_loop(0, length // row_block, state_block, 0)
    start("down", 3)
    finish("out")
    for part, result in dot_slabs(
        mixed_low[rows_at((1 - core) * mid, mid), :], out_all, slab, count
    ):
        half_sent[:, part] = result.astype(bf16)
    half_copy = copies.start(half_sent, half_got, beside[0])
    for part, result in dot_slabs(mixed_low[rows_at(core * mid, mid), :], out_all, slab, count):
        half_kept[:, part] = result
    half_copy.wait_recv()
    other, mine = rows_at((1 - side) * own, own), rows_at(side * own, own)
    own_sent[...] = (half_kept[other, :] + half_got[other, :].astype(f32)).astype(bf16)
    own_copy = copies.start(own_sent, own_got, beside[1])
    start("mlp", 4)
    start("down", 4)
    own_copy.wait_recv()
    middle = own_values[...] + (
        half_kept[mine, :] + half_got[mine, :].astype(f32) + own_got[...].astype(f32)
    )
    own_middle[...] = middle
    scale = lax.rsqrt(jnp.mean(middle * middle, axis=-1, keepdims=True) + eps)
    own_at, both_at = rows_at(core * mid + side * own, own), rows_at(core * mid, mid)
    normed_two[own_at, :] = (middle * scale * gains[1:2, :]).astype(bf16)
    join_copy = copies.start(normed_two.at[own_at], normed_two.at[own_at], beside[1])
    start("mlp", 5)
    join_copy.wait_recv()
    join_copy = copies.start(normed_two.at[both_at], normed_two.at[both_at], beside[0])
    start("down", 5)
    join_copy.wait_recv()
    for step in range(6, count):
        start("mlp", step)
        start("down", step)
    moves = Moves(far_sems)
    for source, target in (
        (branch_all, branch_all_far),
        (inner_all, inner_all_far),
        (out_all, out_all_far),
        (cot_out, cot_out_far),
        (normed_out, normed_out_far),
        (branch_pre, branch_pre_far),
        (padded, padded_far),
        (conv_low, conv_low_far),
        (gate_pre, gate_pre_far),
        (input_pre, input_pre_far),
        (carries, carries_far),
        (states, states_far),
        (mixed_low, mixed_low_far),
        (gate_square_ref, gate_square_far),
        (input_square_ref, input_square_far),
    ):
        moves.start(source, target)
    finish("mlp")
    finish("down")
    moves.wait(15)
    copies.end()


def head(count, fsdp, batches, *operands):
    tokens = operands[0]
    branch, gate = operands[4], operands[7]
    rows, width = tokens.shape
    units, hidden = branch.shape[0], gate.shape[1]
    whole, place = pl.BlockSpec(memory_space=pltpu.VMEM), pl.BlockSpec(memory_space=pl.ANY)

    def array(dtype, *shape):
        return jax.ShapeDtypeStruct(shape, dtype)

    kept = (
        [array(bf16, units, width)] * 3
        + [array(bf16, rows, width)] * 2
        + [array(f32, rows, units), array(f32, rows + 8 * batches, units), array(bf16, rows, units)]
        + [array(f32, rows, units)] * 3
        + [array(f32, rows + 8 * batches, units), array(bf16, rows, units)]
        + [array(bf16, units, units)] * 2
    )
    outs = (
        [array(bf16, width, hidden)] * 2
        + [array(bf16, hidden, width)]
        + kept
        + [array(f32, 8, units)]
        + [array(f32, rows // 4, width)] * 2
        + [array(bf16, rows, width)]
    )
    return pl.pallas_call(
        functools.partial(head_body, count, fsdp, batches),
        out_shape=tuple(outs),
        in_specs=[whole] * 4 + [place] * 6 + [whole] * 5,
        out_specs=tuple([place] * (len(outs) - 4) + [whole] * 4),
        scratch_shapes=[
            *[pltpu.VMEM(part.shape, part.dtype) for part in kept],
            pltpu.VMEM((rows, width), bf16),
            pltpu.VMEM((8, width), f32),
            pltpu.VMEM((rows, units), f32),
            pltpu.VMEM((rows, units), f32),
            pltpu.VMEM((batches, 8, units), f32),
            pltpu.VMEM((batches, 8, units), f32),
            pltpu.VMEM((8, units), f32),
            pltpu.VMEM((count - 1, 8, units), f32),
            pltpu.VMEM((rows // 2, width), bf16),
            pltpu.VMEM((rows // 2, width), f32),
            pltpu.VMEM((rows // 2, width), bf16),
            pltpu.VMEM((rows // 4, width), bf16),
            pltpu.VMEM((rows // 4, width), bf16),
            pltpu.SemaphoreType.DMA((6,)),
            pltpu.SemaphoreType.DMA((15,)),
            pltpu.SemaphoreType.DMA((head_copies,)),
            pltpu.SemaphoreType.DMA((head_copies,)),
        ],
        compiler_params=pltpu.CompilerParams(
            collective_id=1, has_side_effects=True, vmem_limit_bytes=60 * 1024 * 1024
        ),
    )(*operands)


def gelu_slope(values):
    constant = 0.7978845608028654
    bent = jnp.tanh(constant * (values + 0.044715 * values * values * values))
    inner = constant * (1.0 + 3.0 * 0.044715 * values * values)
    return 0.5 * (1.0 + bent) + 0.5 * values * (1.0 - bent * bent) * inner


ring_slots = 3
back_sends = 2 * 2 * (ring_count - 1)
back_copies = 4 + 4 + (ring_count - 1) + 1


class RingSum:
    def __init__(self, terms, slots, sends, arrivals, credits, count, neighbours):
        self.terms, self.slots, self.count = terms, slots, count
        self.sends, self.arrivals, self.credits = sends, arrivals, credits
        self.neighbours = neighbours
        self.copies = [[], []]

    def send(self, way, step, total):
        here, there = (step - 1) % ring_slots, step % ring_slots
        self.slots[way, here] = total.astype(bf16)
        if step >= ring_slots:
            pl.semaphore_wait(self.credits.at[way], 1)
        copy = pltpu.make_async_remote_copy(
            src_ref=self.slots.at[way, here],
            dst_ref=self.slots.at[way, there],
            send_sem=self.sends.at[way, step - 1],
            recv_sem=self.arrivals.at[way, step - 1],
            device_id=self.neighbours[way],
            device_id_type=pl.DeviceIdType.MESH,
        )
        copy.start()
        self.copies[way].append(copy)
        if step >= 2:
            self.copies[way][step - 2].wait_send()
            if step + 1 < self.count:
                pl.semaphore_signal(
                    self.credits.at[way],
                    inc=1,
                    device_id=self.neighbours[1 - way],
                    device_id_type=pl.DeviceIdType.MESH,
                )

    def serve(self, step, end=None):
        slabs = (step % self.count, (self.count - step) % self.count)
        terms = [term(k) for term, k in zip(self.terms, slabs)]
        for way, own in enumerate(terms):
            if step == 1:
                self.send(way, 1, own)
                continue
            self.copies[way][step - 2].wait_recv()
            total = self.slots[way, (step - 1) % ring_slots].astype(f32) + own
            if step < self.count:
                self.send(way, step, total)
            else:
                self.copies[way][step - 2].wait_send()
                end(way, total)


def back_body(
    count,
    fsdp,
    batches,
    cot_ref,
    hidden_ref,
    normed_ref,
    gate_low_ref,
    up_low_ref,
    ends_ref,
    own_middle,
    fresh_ref,
    taps_ref,
    vectors_ref,
    gain_two_ref,
    gate_all,
    up_all,
    down_all,
    out_all,
    branch_pre_in,
    padded_in,
    conv_low_in,
    gate_pre_in,
    input_pre_in,
    carries_in,
    states_in,
    gate_square_in,
    input_square_in,
    mixed_out,
    middle_low,
    own_grad,
    small_out,
    blocks_out,
    gain_grad_out,
    down_grad,
    branch_low_out,
    inner_low_out,
    gate_low_out,
    input_low_out,
    gate_grad,
    up_grad,
    half_sent,
    half_kept,
    half_got,
    own_sent,
    own_got,
    prods,
    adjoints,
    conv_grad,
    edges_sent,
    edges_got,
    ends_sent,
    ends_got,
    mlp_slots,
    down_slots,
    stream_one,
    stream_two,
    stream_out,
    stream_down,
    stage,
    branch_pre,
    padded,
    conv_low,
    gate_pre,
    input_pre,
    carries,
    states,
    gate_square_ref,
    input_square_ref,
    branch_low,
    inner_low,
    gate_low,
    input_low,
    move_sems,
    stream_sems,
    stage_sems,
    ring_sends,
    ring_arrivals,
    ring_credits,
    send_sems,
    recv_sems,
):
    index, unit = lax.axis_index("seq"), lax.axis_index("fsdp")
    place = ring_place(index, count)
    neighbours = (
        {"seq": ring_index(place + 1, count)},
        {"seq": ring_index(place - 1, count)},
    )
    along, beside = peers(count, fsdp)
    copies = Copies(send_sems, recv_sems)
    rows, width = cot_ref.shape
    units = branch_pre.shape[1]
    moves = Moves(move_sems)
    for source, target in (
        (branch_pre_in, branch_pre),
        (states_in, states),
        (carries_in, carries),
        (gate_pre_in, gate_pre),
        (input_pre_in, input_pre),
        (conv_low_in, conv_low),
        (gate_square_in, gate_square_ref),
        (input_square_in, input_square_ref),
        (padded_in, padded),
    ):
        moves.start(source, target)
    length, slab = rows // batches, width // count
    inner_half = hidden_ref.shape[1] // 2
    core, side = lax.rem(unit, 2), lax.rem(unit // 2, 2)
    mid, own = rows // 2, rows // 4
    kept_at, sent_at = rows_at(core * mid, mid), rows_at((1 - core) * mid, mid)
    mine, other = rows_at(side * own, own), rows_at((1 - side) * own, own)
    own_at = rows_at(core * mid + side * own, own)
    tn = (((0,), (0,)), ((), ()))

    greet(along + beside)

    def mlp_term(right):
        return lambda k: lax.dot_general(
            normed_ref[:, k * slab : (k + 1) * slab], right[...], tn, preferred_element_type=f32
        )

    def down_term(first):
        return lambda k: lax.dot_general(
            hidden_ref[:, first : first + inner_half],
            cot_ref[:, k * slab : (k + 1) * slab],
            tn,
            preferred_element_type=f32,
        )

    mlp = RingSum(
        [mlp_term(gate_low_ref), mlp_term(up_low_ref)],
        mlp_slots,
        ring_sends.at[0],
        ring_arrivals.at[0],
        ring_credits.at[0],
        count,
        neighbours,
    )
    down = RingSum(
        [down_term(0), down_term(inner_half)],
        down_slots,
        ring_sends.at[1],
        ring_arrivals.at[1],
        ring_credits.at[1],
        count,
        neighbours,
    )
    mlp.serve(1)
    down.serve(1)

    def streamed(sources, buffers, first_sem, columns=False):
        def fetch(k):
            fetched = []
            for number, (source, buffer) in enumerate(zip(sources, buffers)):
                here = pl.ds(k * slab, slab)
                copy = pltpu.make_async_copy(
                    source.at[:, here] if columns else source.at[here],
                    buffer.at[k % 2],
                    stream_sems.at[first_sem + number * count + k],
                )
                copy.start()
                fetched.append(copy)
            return fetched

        fetched = fetch(0)
        for k in range(count):
            for copy in fetched:
                copy.wait()
            if k + 1 < count:
                fetched = fetch(k + 1)
            yield k, [buffer[k % 2] for buffer in buffers]

    nt = dot_nt_here

    for k, (gate, up) in streamed((gate_all, up_all), (stream_one, stream_two), 0):
        part = slice(k * slab, (k + 1) * slab)
        half_sent[:, part] = (
            nt(gate_low_ref[sent_at, :], gate) + nt(up_low_ref[sent_at, :], up)
        ).astype(bf16)
        half_kept[:, part] = nt(gate_low_ref[kept_at, :], gate) + nt(up_low_ref[kept_at, :], up)
    half_copy = copies.start(half_sent, half_got, beside[0])
    half_copy.wait_recv()
    own_sent[...] = (half_kept[other, :] + half_got[other, :].astype(f32)).astype(bf16)
    own_copy = copies.start(own_sent, own_got, beside[1])
    mlp.serve(2)
    down.serve(2)
    own_copy.wait_recv()
    middle = own_middle[...]
    scale = lax.rsqrt(jnp.mean(middle * middle, axis=-1, keepdims=True) + eps)
    unit_values = middle * scale
    front = half_kept[mine, :] + half_got[mine, :].astype(f32) + own_got[...].astype(f32)
    gain_grad_out[...] = jnp.zeros_like(gain_grad_out)
    gain_grad_out[0:1, :] = jnp.sum(front * unit_values, 0, keepdims=True)
    weighted = front * gain_two_ref[...]
    result = cot_ref[own_at, :].astype(f32) + scale * (
        weighted - unit_values * jnp.mean(weighted * unit_values, axis=-1, keepdims=True)
    )
    own_grad[...] = result
    middle_low[own_at, :] = result.astype(bf16)
    join_copy = copies.start(middle_low.at[own_at], middle_low.at[own_at], beside[1])
    mlp.serve(3)
    join_copy.wait_recv()
    join_copy = copies.start(middle_low.at[kept_at], middle_low.at[kept_at], beside[0])
    down.serve(3)
    join_copy.wait_recv()

    for k, (out,) in streamed((out_all,), (stream_out,), 2 * count, True):
        for batch in range(batches):
            at = slice(batch * length, (batch + 1) * length)
            more = nt(middle_low[at, k * slab : (k + 1) * slab], out)
            adjoints[at, :] = more if k == 0 else adjoints[at, :] + more

    moves.wait(9)

    def mixed_block(block, carry):
        batch = block // (length // row_block)
        at = rows_at(block * row_block, row_block)
        back, before = adjoints[at, :], branch_pre[at, :]
        state = states[rows_at(block * row_block + batch * 8 + 8, row_block, 8), :]
        branch_low[at, :] = (back * state * gelu_slope(before)).astype(bf16)
        adjoints[at, :] = back * gelu_tanh(before)
        return carry

    lax.fori_loop(0, rows // row_block, mixed_block, 0)
    moves.start(branch_low, branch_low_out)
    scanned = scan_rows(carries, adjoints, prods, adjoints, batches, True)
    ends_sent[...] = ends_ref[...]
    for batch, (_, state) in enumerate(scanned):
        top = batch * length
        ends_sent[batches + batch : batches + batch + 1, :] = carries[top : top + 1, :] * state
    end_copies = [
        copies.start(ends_sent, ends_got.at[distance - 1], along[count - distance - 1])
        for distance in range(1, count)
    ]
    mlp.serve(4)
    for copy in end_copies:
        copy.wait_recv()
    entries = entry_states(ends_sent, ends_got, index, count, batches, -1)

    bias, gate_bias, input_bias, rate, slope = [vectors_ref[i : i + 1, :] for i in range(5)]
    zero = jnp.zeros((1, units), f32)
    sums = (zero, zero, zero)
    for batch in range(batches):
        entry = entries[batch]

        def gate_block(block, sums, batch=batch, entry=entry):
            top = batch * length + block * row_block
            at = rows_at(top, row_block)
            rate_gate = jax.nn.sigmoid(gate_pre[at, :])
            inlet_gate = jax.nn.sigmoid(input_pre[at, :])
            log_decay = rate * rate_gate
            decay = jnp.exp(log_decay)
            fresh = fresh_ref[at, :] > 0
            scale = jnp.sqrt(-jnp.tanh(log_decay) * (1.0 + decay * decay))
            conv = conv_low[at, :].astype(f32)
            lam = adjoints[at, :] + prods[at, :] * entry
            before = states[rows_at(top + batch * 8, row_block + 8, 8), :][7:-1]
            drawn = inlet_gate * conv
            log_grad = jnp.where(
                fresh, 0.0, lam * before * decay - lam * (decay * decay / scale) * drawn
            )
            passed = lam * jnp.where(fresh, 1.0, scale)
            gate_grad_low = (log_grad * rate * (rate_gate * (1.0 - rate_gate))).astype(bf16)
            input_grad_low = (passed * conv * (inlet_gate * (1.0 - inlet_gate))).astype(bf16)
            gate_low[at, :] = gate_grad_low
            input_low[at, :] = input_grad_low
            conv_grad[rows_at(top + batch * 8, row_block, 8), :] = passed * inlet_gate
            terms = (
                gate_grad_low.astype(f32),
                input_grad_low.astype(f32),
                log_grad * rate_gate,
            )
            return tuple(
                total + jnp.sum(more, 0, keepdims=True) for total, more in zip(sums, terms)
            )

        sums = lax.fori_loop(0, length // row_block, gate_block, sums)
        if batch == 0:
            down.serve(4)
    moves.start(gate_low, gate_low_out)
    moves.start(input_low, input_low_out)
    for batch in range(batches):
        at, top = slice(batch * length, (batch + 1) * length), batch * (length + 8)
        conv_grad[top : top + length, :] = (
            conv_grad[top : top + length, :]
            + nt(gate_low[at, :], gate_square_ref[...])
            + nt(input_low[at, :], input_square_ref[...])
        )
        edges_sent[batch] = conv_grad[top : top + 8, :]
    edge_copy = copies.start(edges_sent, edges_got, along[count - 2])
    mlp.serve(5)
    size = blocks_out.shape[1]
    for number, right in enumerate((gate_low, input_low)):
        square = lax.dot_general(conv_low[...], right[...], tn, preferred_element_type=f32)
        for j in range(units // size):
            at = slice(j * size, (j + 1) * size)
            first = number * units + j * size
            blocks_out[first : first + size, :] = square[at, at].astype(bf16)

    copies.sent(half_copy)
    copies.sent(own_copy)
    for k, (right,) in streamed((down_all,), (stream_down,), 3 * count, True):
        part = slice(k * slab, (k + 1) * slab)
        half_sent[:, part] = jnp.dot(
            hidden_ref[sent_at, :], right, preferred_element_type=f32
        ).astype(bf16)
        half_kept[:, part] = jnp.dot(
            hidden_ref[kept_at, :], right, preferred_element_type=f32
        )
    mixed_copy = copies.start(half_sent, half_got, beside[0])
    down.serve(5)

    edge_copy.wait_recv()
    for batch in range(batches):
        top = batch * (length + 8) + length
        conv_grad[top : top + 8, :] = jnp.where(index < count - 1, edges_got[batch], 0.0)

    def conv_block(block, sums):
        batch = block // (length // row_block)
        at = rows_at(block * row_block + batch * 8, row_block + 8, 8)
        wide, inner = conv_grad[at, :], padded[at, :]
        total = taps_ref[0:1, :] * wide[:-8] + taps_ref[1:2, :] * wide[1:-7]
        total = total + taps_ref[2:3, :] * wide[2:-6] + taps_ref[3:4, :] * wide[3:-5]
        inner_low[rows_at(block * row_block, row_block), :] = total.astype(bf16)
        near = wide[:-8]
        terms = [near * inner[8 - k : 8 - k + row_block] for k in range(4)] + [near]
        return tuple(
            total + jnp.sum(more, 0, keepdims=True) for total, more in zip(sums, terms)
        )

    conv_sums = lax.fori_loop(0, rows // row_block, conv_block, (zero,) * 5)
    moves.start(inner_low, inner_low_out)
    for number, total in enumerate((*conv_sums, sums[0], sums[1], sums[2] * slope)):
        small_out[number : number + 1, :] = total

    mixed_copy.wait_recv()
    own_sent[...] = (half_kept[other, :] + half_got[other, :].astype(f32)).astype(bf16)
    own_copy = copies.start(own_sent, own_got, beside[1])
    mlp.serve(6)
    down.serve(6)
    own_copy.wait_recv()
    final = own_middle[...] + (
        half_kept[mine, :] + half_got[mine, :].astype(f32) + own_got[...].astype(f32)
    )
    final = final.astype(bf16)
    for k in range(count):
        to = pl.ds(pl.multiple_of(ring_index(place - k, count) * slab, slab), slab)
        mixed_out[own_at, to] = final[:, k * slab : (k + 1) * slab]
    join_copy = copies.start(mixed_out.at[own_at], mixed_out.at[own_at], beside[1])
    mlp.serve(7)
    join_copy.wait_recv()
    join_copy = copies.start(mixed_out.at[kept_at], mixed_out.at[kept_at], beside[0])
    down.serve(7)
    join_copy.wait_recv()

    def mlp_end(way, total):
        stage[...] = total
        copy = pltpu.make_async_copy(stage, up_grad if way else gate_grad, stage_sems.at[way])
        copy.start()
        copy.wait()

    def down_end(way, total):
        down_grad[way * inner_half : (way + 1) * inner_half, :] = total

    mlp.serve(8, mlp_end)
    down.serve(8, down_end)
    moves.wait(4)
    copies.end()


def back(count, fsdp, batches, block_width, *operands):
    cot, hidden = operands[0], operands[1]
    late = operands[-9:]
    rows, width = cot.shape
    units, inner = late[0].shape[1], hidden.shape[1]
    slab = width // count
    whole, place = pl.BlockSpec(memory_space=pltpu.VMEM), pl.BlockSpec(memory_space=pl.ANY)

    def array(dtype, *shape):
        return jax.ShapeDtypeStruct(shape, dtype)

    outs = [
        array(bf16, rows, width),
        array(bf16, rows, width),
        array(f32, rows // 4, width),
        array(f32, 8, units),
        array(bf16, 2 * units, block_width),
        array(f32, 8, width),
        array(f32, inner, slab),
        *[array(bf16, rows, units)] * 4,
        *[array(f32, slab, inner)] * 2,
    ]
    return pl.pallas_call(
        functools.partial(back_body, count, fsdp, batches),
        out_shape=tuple(outs),
        in_specs=[whole] * (len(operands) - 13) + [place] * 13,
        out_specs=tuple([whole] * 7 + [place] * 6),
        scratch_shapes=[
            pltpu.VMEM((rows // 2, width), bf16),
            pltpu.VMEM((rows // 2, width), f32),
            pltpu.VMEM((rows // 2, width), bf16),
            pltpu.VMEM((rows // 4, width), bf16),
            pltpu.VMEM((rows // 4, width), bf16),
            pltpu.VMEM((rows, units), f32),
            pltpu.VMEM((rows, units), f32),
            pltpu.VMEM((rows + 8 * batches, units), f32),
            pltpu.VMEM((batches, 8, units), f32),
            pltpu.VMEM((batches, 8, units), f32),
            pltpu.VMEM((8, units), f32),
            pltpu.VMEM((count - 1, 8, units), f32),
            pltpu.VMEM((2, ring_slots, slab, inner), bf16),
            pltpu.VMEM((2, ring_slots, inner // 2, slab), bf16),
            pltpu.VMEM((2, slab, inner), bf16),
            pltpu.VMEM((2, slab, inner), bf16),
            pltpu.VMEM((2, units, slab), bf16),
            pltpu.VMEM((2, inner, slab), bf16),
            pltpu.VMEM((slab, inner), f32),
            *[pltpu.VMEM(part.shape, part.dtype) for part in late],
            *[pltpu.VMEM((rows, units), bf16)] * 4,
            pltpu.SemaphoreType.DMA((13,)),
            pltpu.SemaphoreType.DMA((4 * count,)),
            pltpu.SemaphoreType.DMA((2,)),
            pltpu.SemaphoreType.DMA((2, 2, count - 1)),
            pltpu.SemaphoreType.DMA((2, 2, count - 1)),
            pltpu.SemaphoreType.REGULAR((2, 2)),
            pltpu.SemaphoreType.DMA((back_copies,)),
            pltpu.SemaphoreType.DMA((back_copies,)),
        ],
        compiler_params=pltpu.CompilerParams(
            collective_id=2, has_side_effects=True, vmem_limit_bytes=63 * 1024 * 1024
        ),
    )(*operands)


def mlp_body(normed_ref, cot_ref, gate_ref, up_ref, down_ref, hidden_out, gate_out, up_out):
    gate = jnp.dot(normed_ref[...], gate_ref[...], preferred_element_type=f32)
    up = jnp.dot(normed_ref[...], up_ref[...], preferred_element_type=f32)
    back = dot_nt_here(cot_ref[...], down_ref[...])
    constant = 0.7978845608028654
    square = gate * gate
    bent = jnp.tanh(constant * (gate + 0.044715 * square * gate))
    half = 0.5 * (1.0 + bent)
    active = half * gate
    slope = half + 0.5 * gate * (1.0 - bent * bent) * (
        constant * (1.0 + 3.0 * 0.044715 * square)
    )
    hidden_out[...] = (active * up).astype(bf16)
    gate_out[...] = (back * up * slope).astype(bf16)
    up_out[...] = (back * active).astype(bf16)


def feed_forward(normed, cot, gate_all, up_all, down_all):
    rows, width = normed.shape
    hidden = gate_all.shape[1]
    wide = 256
    resident = pl.BlockSpec((rows, width), lambda j: (0, 0))
    columns = pl.BlockSpec((width, wide), lambda j: (0, j))
    result = pl.BlockSpec((rows, wide), lambda j: (0, j))
    return pl.pallas_call(
        mlp_body,
        grid=(hidden // wide,),
        out_shape=(jax.ShapeDtypeStruct((rows, hidden), bf16),) * 3,
        in_specs=[
            resident,
            resident,
            columns,
            columns,
            pl.BlockSpec((wide, width), lambda j: (j, 0)),
        ],
        out_specs=(result,) * 3,
        compiler_params=pltpu.CompilerParams(vmem_limit_bytes=62 * 1024 * 1024),
    )(normed, cot, gate_all, up_all, down_all)


def block_diagonal(blocks):
    count, width = blocks.shape[0], blocks.shape[1]
    return sum(
        jnp.pad(blocks[j], ((j * width, (count - 1 - j) * width),) * 2) for j in range(count)
    )


def rows_joined(slab_pairs):
    return jnp.concatenate([part for pair in zip(*slab_pairs) for part in pair], 0)


def diagonal_blocks(square, count):
    width = square.shape[0] // count
    return jnp.stack(
        [square[j * width : (j + 1) * width, j * width : (j + 1) * width] for j in range(count)], 0
    )


def local(
    tokens,
    resets,
    norm_gain,
    branch_weight,
    inner_weight,
    conv_weight,
    conv_bias,
    gate_blocks,
    input_blocks,
    gate_bias,
    input_bias,
    decay_param,
    out_weight,
    mlp_norm_gain,
    gate_weight,
    up_weight,
    down_weight,
    cotangent,
):
    count = lax.axis_size("seq")
    batches, length, width = tokens.shape
    slab = width // count
    units, hidden = conv_bias.shape[0], down_weight.shape[0]
    rows = batches * length
    ringed = count == ring_count and lax.axis_size("fsdp") == 4
    half = slab // 2
    out_turned, down_turned = out_weight.T, down_weight.T
    ring = Ring(count)
    if ringed:
        gather, scatter = functools.partial(Gather, ring), functools.partial(Scatter, ring)
        to_ring, to_plain = ring.tables()

        def moved(values, dtype):
            return move_slabs(values, to_ring, dtype)

        def restored(values, dtype):
            return move_slabs(values, to_plain, dtype)

        def gain_moved(gain):
            return gain.reshape(count, slab)[to_ring].reshape(width)

        def gain_restored(gain):
            return gain.reshape(count, slab)[to_plain].reshape(width)

    else:
        gather, scatter = functools.partial(PlainGather, ring), functools.partial(PlainScatter, ring)

        def moved(values, dtype):
            return values.astype(dtype)

        restored = moved

        def gain_moved(gain):
            return gain

        gain_restored = gain_moved

    def slab_dots(turned, right, first=0, rows=slab):
        def term(k):
            start = k * slab + first
            return dot_nn(turned[start : start + rows], right)

        return term

    steps = count - 1
    taps = conv_weight.astype(f32)
    decay = decay_param.astype(f32)
    fresh_start = resets[:, :, None] > 0
    gain_one = gain_moved(norm_gain.astype(f32))
    gain_two = gain_moved(mlp_norm_gain.astype(f32))

    def gates(gate_pre, input_pre, conv_value, decay):
        return gate_math(gate_pre, input_pre, conv_value, decay, fresh_start)

    def by_sequence(values):
        return values.reshape(batches, -1, values.shape[-1])

    if ringed:
        vectors = jnp.stack(
            [
                conv_bias.astype(f32),
                gate_bias.astype(f32),
                input_bias.astype(f32),
                -decay_scale * jax.nn.softplus(-decay),
            ],
            0,
        )
        (
            gate_all,
            up_all,
            down_all,
            branch_all,
            inner_all,
            out_all,
            cot_low,
            normed,
            branch_pre,
            padded,
            conv_flat,
            gate_pre,
            input_pre,
            carries,
            states,
            mixed_low,
            gate_square,
            input_square,
            ends,
            own_values,
            own_middle,
            normed_two,
        ) = head(
            count,
            lax.axis_size("fsdp"),
            batches,
            tokens.reshape(rows, width),
            cotangent.reshape(rows, width),
            norm_gain.astype(f32)[None],
            mlp_norm_gain.astype(f32)[None],
            branch_weight.T,
            inner_weight.T,
            out_weight,
            gate_weight,
            up_weight,
            down_weight,
            taps,
            vectors,
            gate_blocks,
            input_blocks,
            resets.reshape(rows, 1),
        )
        hidden_low, gate_mlp_low, up_mlp_low = feed_forward(
            normed_two, cot_low, gate_all, up_all, down_all
        )
        (
            mixed,
            middle_low,
            own_grad,
            small,
            block_grads,
            gain_two_grad,
            down_grad,
            branch_low,
            inner_grad_low,
            gate_low,
            input_low,
            gate_grad,
            up_grad,
        ) = back(
            count,
            lax.axis_size("fsdp"),
            batches,
            gate_blocks.shape[-1],
            cot_low,
            hidden_low,
            normed_two,
            gate_mlp_low,
            up_mlp_low,
            ends,
            own_middle,
            resets.reshape(rows, 1),
            taps,
            jnp.concatenate([vectors, decay_scale * jax.nn.sigmoid(-decay)[None]], 0),
            gain_two[None],
            gate_all,
            up_all,
            down_all,
            out_all,
            branch_pre,
            padded,
            conv_flat,
            gate_pre,
            input_pre,
            carries,
            states,
            gate_square,
            input_square,
        )
        block_count, block_width = gate_blocks.shape[:2]
        branch_grad, inner_grad, out_grad, tokens_grad, gains, small, block_grads = tail(
            count,
            middle_low,
            mixed_low,
            normed,
            branch_low,
            inner_grad_low,
            branch_all,
            inner_all,
            own_values,
            own_grad,
            gain_one[None],
            gain_two_grad[:1],
            small,
            block_grads,
        )
        block_grads = block_grads.astype(f32).reshape(2, block_count, block_width, block_width)
        return (
            mixed.astype(f32).reshape(tokens.shape),
            tokens_grad.astype(f32).reshape(tokens.shape),
            gains[0],
            branch_grad.T,
            inner_grad.T,
            small[:4],
            small[4],
            block_grads[0],
            block_grads[1],
            small[5],
            small[6],
            small[7],
            out_grad,
            gains[1],
            gate_grad,
            up_grad,
            down_grad,
        )
    else:
        branch_all, inner_all, out_all, gate_all, up_all, down_all = [
            lax.all_gather(piece, "seq", axis=0, tiled=True)
            for piece in (
                branch_weight,
                inner_weight,
                out_turned,
                gate_weight,
                up_weight,
                down_turned,
            )
        ]
        gate_square, input_square = block_diagonal(gate_blocks), block_diagonal(input_blocks)
        tokens_low, cot_low = tokens.reshape(rows, width), cotangent.reshape(rows, width)
        values = tokens_low.astype(f32)
        normed = (values * inverse_rms(values) * gain_one).astype(bf16)
        inner_low = by_sequence(dot_nn(normed, inner_all).astype(bf16))
        branch_pre = by_sequence(dot_nn(normed, branch_all))
        edge_rows = passed_along(inner_low[:, -3:], 1)
        padded = jnp.concatenate([edge_rows, inner_low], 1).astype(f32)
        conv_sum = conv_bias.astype(f32) + taps[0] * padded[:, 3:] + taps[1] * padded[:, 2:-1]
        conv_sum = conv_sum + taps[2] * padded[:, 1:-2] + taps[3] * padded[:, :-3]
        conv_flat = conv_sum.astype(bf16).reshape(rows, units)
        gate_pre = by_sequence(dot_nn(conv_flat, gate_square) + gate_bias.astype(f32))
        input_pre = by_sequence(dot_nn(conv_flat, input_square) + input_bias.astype(f32))
        conv_value = by_sequence(conv_flat).astype(f32)
        carries, drives = gates(gate_pre, input_pre, conv_value, decay)
        prods, local_state = local_scan(carries, drives, False)
        prods_end = prods[:, -1:]
        state_in = Entry(prods_end, local_state[:, -1:], 1).state(None)
        states = local_state + prods * state_in
        mixed_low = (states * gelu_tanh(branch_pre)).astype(bf16).reshape(rows, units)
        own_values = own_rows(tokens_low).astype(f32)
        own_middle = own_values + Halves(ring, dot_nt(mixed_low, out_all), "fsdp").run()
        normed_two = own_middle * inverse_rms(own_middle) * gain_two
        normed_two = Joined(ring, normed_two.astype(bf16), "fsdp").run()
    branch, branch_pull = jax.vjp(gelu_tanh, branch_pre)
    scale_two = inverse_rms(own_middle)
    unit_two = own_middle * scale_two

    gate_mlp = dot_nn(normed_two, gate_all)
    up_mlp = dot_nn(normed_two, up_all)
    activated, act_pull = jax.vjp(gated_product, gate_mlp, up_mlp)
    hidden_low = activated.astype(bf16)
    down_grads = scatter(
        slab_dots(cot_low.T, hidden_low, 0, half), slab_dots(cot_low.T, hidden_low, half, half)
    )
    in_turn(down_grads)
    grad_gate_mlp, grad_up_mlp = act_pull(dot_nn(ring.then(cot_low, 0), down_all))
    gate_mlp_low, up_mlp_low = grad_gate_mlp.astype(bf16), grad_up_mlp.astype(bf16)
    in_turn(down_grads)
    ring.first(gate_mlp_low, up_mlp_low)
    in_turn(down_grads)
    mlp_grads = scatter(
        slab_dots(normed_two.T, gate_mlp_low), slab_dots(normed_two.T, up_mlp_low)
    )
    in_turn(mlp_grads, down_grads)
    gate_mlp_low, up_mlp_low = lax.optimization_barrier(
        (ring.then(gate_mlp_low, 2), up_mlp_low)
    )
    back_sum = Halves(
        ring, dot_nt(gate_mlp_low, gate_all) + dot_nt(up_mlp_low, up_all), "fsdp"
    )
    back_sum.step()
    ring.first(back_sum.step())
    in_turn(mlp_grads, down_grads)
    own_back = back_sum.run(2)
    gain_two_grad = jnp.sum(own_back * unit_two, 0)
    weighted = own_back * gain_two
    own_grad = own_rows(cot_low).astype(f32) + scale_two * (
        weighted - unit_two * jnp.mean(weighted * unit_two, axis=-1, keepdims=True)
    )
    middle_join = Joined(ring, own_grad.astype(bf16), "fsdp")
    ring.first(middle_join.step())
    in_turn(mlp_grads)
    mixed_sum = Halves(ring, dot_nt(ring.then(hidden_low, 2), down_all), "fsdp")
    mixed_sum.step()
    ring.first(mixed_sum.step())
    in_turn(down_grads)
    middle_join.step(2)
    middle_low = middle_join.run()

    grad_mixed = dot_nn(middle_low, out_all).reshape(batches, length, units)
    (grad_branch_pre,) = branch_pull(grad_mixed * states)
    branch_low = grad_branch_pre.astype(bf16).reshape(rows, units)
    following = jnp.concatenate([carries[:, 1:], jnp.ones_like(carries[:, :1])], 1)
    tail_prods, local_adjoint = local_scan(following, grad_mixed * branch, True)
    entry = Entry(prods_end, carries[:, :1] * local_adjoint[:, :1], -1)
    ring.first(local_adjoint, branch_low)
    in_turn(mlp_grads)
    entry.between(ring.then)
    in_turn(down_grads)
    adjoint_in = entry.state(lambda part: ring.then(part, 1))
    adjoint = local_adjoint + tail_prods * adjoint_in
    state_before = jnp.concatenate([state_in, states[:, :-1]], 1)
    _, gate_pull = jax.vjp(gates, gate_pre, input_pre, conv_value, decay)
    grad_gate_pre, grad_input_pre, grad_conv, decay_grad = gate_pull(
        (adjoint * state_before, adjoint)
    )
    gate_low = grad_gate_pre.astype(bf16).reshape(rows, units)
    input_low = grad_input_pre.astype(bf16).reshape(rows, units)
    ring.first(gate_low, input_low)
    in_turn(mlp_grads)
    back_conv = dot_nt(gate_low, gate_square) + dot_nt(input_low, input_square)
    grad_conv = grad_conv + back_conv.reshape(batches, length, units)

    border = jnp.zeros((batches, 3, units), f32)
    spread = jnp.concatenate([border, grad_conv, border], 1)
    stop = length + 3
    grad_padded = taps[0] * spread[:, :stop] + taps[1] * spread[:, 1 : stop + 1]
    grad_padded = grad_padded + taps[2] * spread[:, 2 : stop + 2] + taps[3] * spread[:, 3:]
    returned = passed_along(grad_padded[:, :3], -1)
    mixed_join = Joined(ring, restored(own_middle + mixed_sum.run(1), bf16), "fsdp")
    ring.first(grad_padded, mixed_join.step())
    in_turn(mlp_grads)
    grad_inner = jnp.concatenate(
        [grad_padded[:, 3:-3], grad_padded[:, -3:] + ring.then(returned)], 1
    )
    inner_grad_low = grad_inner.astype(bf16).reshape(rows, units)
    in_turn(*[mlp_grads] * (steps - 6))

    block_count = gate_blocks.shape[0]
    block_grads = jnp.concatenate(
        [
            diagonal_blocks(dot_tn(conv_flat, gate_low), block_count),
            diagonal_blocks(dot_tn(conv_flat, input_low), block_count),
        ],
        0,
    )
    block_width = block_grads.shape[-1]
    taps_grad = jnp.stack(
        [jnp.sum(grad_conv * padded[:, 3 - k : 3 - k + length], (0, 1)) for k in range(4)], 0
    )
    small = jnp.concatenate(
        [
            taps_grad,
            jnp.sum(grad_conv, (0, 1))[None],
            jnp.sum(gate_low.astype(f32), 0)[None],
            jnp.sum(input_low.astype(f32), 0)[None],
            decay_grad[None],
        ],
        0,
    )
    mixed_join.step()
    mixed = mixed_join.run().astype(f32).reshape(tokens.shape)
    gate_grad, up_grad = mlp_grads.sums()
    if ringed:
        branch_grad, inner_grad, out_grad, tokens_grad, gains, small, block_grads = tail(
            count,
            middle_low.T,
            mixed_low,
            normed.T,
            branch_low,
            inner_grad_low,
            branch_all,
            inner_all,
            own_values,
            own_grad,
            gain_one[None],
            gain_two_grad[None],
            small,
            block_grads.reshape(-1, block_width).astype(bf16),
        )
        block_grads = block_grads.astype(f32)
    else:
        out_grads = scatter(
            slab_dots(middle_low.T, mixed_low, 0, half),
            slab_dots(middle_low.T, mixed_low, half, half),
        )
        front_grads = scatter(
            slab_dots(normed.T, branch_low), slab_dots(normed.T, inner_grad_low)
        )
        branch_grad, inner_grad = front_grads.sums()
        out_grad = jnp.concatenate(out_grads.sums(), 0)
        own_front = Halves(
            ring, dot_nt(branch_low, branch_all) + dot_nt(inner_grad_low, inner_all), "fsdp"
        ).run()
        scale_one = inverse_rms(own_values)
        unit_one = own_values * scale_one
        weighted = own_front * gain_one
        own_tokens = own_grad + scale_one * (
            weighted - unit_one * jnp.mean(weighted * unit_one, axis=-1, keepdims=True)
        )
        gains = jnp.stack([jnp.sum(own_front * unit_one, 0), gain_two_grad], 0)
        gains = lax.psum(gains, ("seq", "fsdp"))
        small, block_grads = lax.psum((small, block_grads), "seq")
        tokens_grad = Joined(ring, own_tokens.astype(bf16), "fsdp").run()
    tokens_grad = tokens_grad.astype(f32).reshape(tokens.shape)
    block_grads = block_grads.reshape(2, block_count, block_width, block_width)
    down_grad = jnp.concatenate(down_grads.sums(), 0)
    return (
        mixed,
        tokens_grad,
        gains[0],
        branch_grad,
        inner_grad,
        small[:4],
        small[4],
        block_grads[0],
        block_grads[1],
        small[5],
        small[6],
        small[7],
        out_grad.T,
        gains[1],
        gate_grad,
        up_grad,
        down_grad.T,
    )


def solution(mesh):
    units, both = P("fsdp"), P("seq", "fsdp")
    blocks, turned = P("fsdp", None, None), P("fsdp", "seq")
    rows = P(None, "seq", None)
    return jax.shard_map(
        local,
        mesh=mesh,
        in_specs=(
            rows,
            P(None, "seq"),
            P(),
            both,
            both,
            P(None, "fsdp"),
            units,
            blocks,
            blocks,
            units,
            units,
            units,
            turned,
            P(),
            both,
            both,
            turned,
            rows,
        ),
        out_specs=(
            rows,
            rows,
            P(),
            both,
            both,
            P(None, "fsdp"),
            units,
            blocks,
            blocks,
            units,
            units,
            units,
            turned,
            P(),
            both,
            both,
            turned,
        ),
        check_vma=False,
    )
```

```python
import functools

import jax
import jax.numpy as jnp
from jax import lax
from jax.experimental import pallas as pl
from jax.experimental.pallas import tpu as pltpu
from jax.sharding import PartitionSpec as P

eps = 1e-06
decay_scale = 8.0
f32 = jnp.float32
bf16 = jnp.bfloat16
ring_count = 8


def gelu_tanh(values):
    return jax.nn.gelu(values, approximate=True)


def gated_product(gate_pre, up_pre):
    return gelu_tanh(gate_pre) * up_pre


def gate_math(gate_pre, input_pre, conv_value, decay_param, fresh_start):
    rate_gate = jax.nn.sigmoid(gate_pre)
    inlet_gate = jax.nn.sigmoid(input_pre)
    log_decay = -decay_scale * jax.nn.softplus(-decay_param) * rate_gate
    input_scale = jnp.where(fresh_start, 1.0, jnp.sqrt(-jnp.expm1(2.0 * log_decay)))
    carries = jnp.where(fresh_start, 0.0, jnp.exp(log_decay))
    return (carries, input_scale * inlet_gate * conv_value)


def dot_nn(left, right):
    return jnp.dot(left, right, preferred_element_type=f32)


def dot_nt(left, right):
    return lax.dot_general(left, right, (((1,), (1,)), ((), ())), preferred_element_type=f32)


def dot_tn(left, right):
    return lax.dot_general(left, right, (((0,), (0,)), ((), ())), preferred_element_type=f32)


def inverse_rms(values):
    return lax.rsqrt(jnp.mean(values * values, axis=-1, keepdims=True) + eps)


def scan_body(backward, a_ref, b_ref, prod_ref, state_ref):
    batches, length, units = a_ref.shape
    tiles = length // 8
    rows = lax.broadcasted_iota(jnp.int32, (8, units), 0)

    def step(index, carry):
        tile = tiles - 1 - index if backward else index
        where_rows = pl.ds(pl.multiple_of(tile * 8, 8), 8)
        following = []
        for batch in range(batches):
            prod_in, state_in = carry[batch]
            a = a_ref[batch, where_rows, :]
            b = b_ref[batch, where_rows, :]
            for shift in (1, 2, 4):
                turn = 8 - shift if backward else shift
                inside = rows < 8 - shift if backward else rows >= shift
                a_moved = jnp.where(inside, pltpu.roll(a, turn, 0), 1.0)
                b_moved = jnp.where(inside, pltpu.roll(b, turn, 0), 0.0)
                b = a * b_moved + b
                a = a * a_moved
            b = b + a * state_in
            a = a * prod_in
            prod_ref[batch, where_rows, :] = a
            state_ref[batch, where_rows, :] = b
            edge = 0 if backward else 7
            following.append((a[edge : edge + 1], b[edge : edge + 1]))
        return tuple(following)

    first = tuple(
        (jnp.ones((1, units), f32), jnp.zeros((1, units), f32)) for _ in range(batches)
    )
    lax.fori_loop(0, tiles, step, first)


def local_scan(a, b, backward):
    shape = jax.ShapeDtypeStruct(a.shape, f32)
    elements = a.shape[0] * a.shape[1] * a.shape[2]
    return pl.pallas_call(
        functools.partial(scan_body, backward),
        out_shape=(shape, shape),
        in_specs=[pl.BlockSpec(memory_space=pltpu.VMEM)] * 2,
        out_specs=(pl.BlockSpec(memory_space=pltpu.VMEM),) * 2,
        compiler_params=pltpu.CompilerParams(vmem_limit_bytes=32 * 1024 * 1024),
        cost_estimate=pl.CostEstimate(
            flops=20 * elements, bytes_accessed=16 * elements, transcendentals=0
        ),
    )(a, b)


def move_body(table_ref, in_ref, out_ref):
    out_ref[...] = in_ref[...].astype(out_ref.dtype)


def move_slabs(values, table, dtype):
    rows, width = values.shape
    slabs = table.shape[0]
    return pl.pallas_call(
        move_body,
        out_shape=jax.ShapeDtypeStruct((rows, width), dtype),
        grid_spec=pltpu.PrefetchScalarGridSpec(
            num_scalar_prefetch=1,
            grid=(slabs,),
            in_specs=[pl.BlockSpec((rows, width // slabs), lambda k, where: (0, where[k]))],
            out_specs=pl.BlockSpec((rows, width // slabs), lambda k, where: (0, k)),
        ),
        cost_estimate=pl.CostEstimate(
            flops=0, bytes_accessed=8 * rows * width, transcendentals=0
        ),
    )(table, values)


class Ring:
    def __init__(self, count):
        self.count = count
        self.order = list(range(0, count, 2)) + list(range(count - 1, 0, -2))
        self.place = [self.order.index(i) for i in range(count)]
        self.forth = [(self.order[i], self.order[(i + 1) % count]) for i in range(count)]
        self.back = [(there, here) for here, there in self.forth]
        self.sent, self.awaited = [], []

    def tables(self):
        here = jnp.asarray(self.place, jnp.int32)[lax.axis_index("seq")]
        steps = jnp.arange(self.count, dtype=jnp.int32)
        to_ring = jnp.asarray(self.order, jnp.int32)[(here - steps) % self.count]
        to_plain = (here - jnp.asarray(self.place, jnp.int32)) % self.count
        return to_ring, to_plain

    def send(self, forth, back):
        earlier = list(self.sent[-2]) if len(self.sent) > 1 else []
        if earlier or self.awaited:
            forth, back = lax.optimization_barrier((forth, back, *earlier, *self.awaited))[:2]
        self.awaited = []
        self.sent.append(
            (lax.ppermute(forth, "seq", self.forth), lax.ppermute(back, "seq", self.back))
        )
        return self.sent[-1]

    def first(self, *values):
        self.awaited.extend(values)

    def then(self, value, under_way=1):
        if len(self.sent) <= under_way:
            return value
        return lax.optimization_barrier((value, *self.sent[-1 - under_way]))[0]


class Gather:
    def __init__(self, ring, forth, back):
        self.ring, self.forth, self.back = ring, [forth], [back]

    def step(self):
        forth, back = self.ring.send(self.forth[-1], self.back[-1])
        self.forth.append(forth)
        self.back.append(back)

    def slabs(self):
        count = self.ring.count
        return self.forth, [self.back[-k % count] for k in range(count)]


class Scatter:
    def __init__(self, ring, forth_slab, back_slab):
        self.ring, self.forth_slab, self.back_slab = ring, forth_slab, back_slab
        self.at = 1
        self.forth = forth_slab(1).astype(bf16)
        self.back = back_slab(ring.count - 1).astype(bf16)

    def step(self):
        count = self.ring.count
        forth, back = self.ring.send(self.forth, self.back)
        self.at += 1
        self.forth = forth.astype(f32) + self.forth_slab(self.at % count)
        self.back = back.astype(f32) + self.back_slab(count - self.at)
        if self.at < count:
            self.forth, self.back = self.forth.astype(bf16), self.back.astype(bf16)

    def sums(self):
        return self.forth, self.back


class PlainGather:
    def __init__(self, ring, forth, back):
        self.pieces = (forth, back)

    def step(self):
        pass

    def slabs(self):
        return tuple(list(lax.all_gather(piece, "seq")) for piece in self.pieces)


class PlainScatter:
    def __init__(self, ring, forth_slab, back_slab):
        self.terms = (forth_slab, back_slab)

    def step(self):
        pass

    def sums(self):
        count = lax.axis_size("seq")
        return tuple(
            lax.psum_scatter(
                jnp.concatenate([term(k) for k in range(count)], 0),
                "seq",
                scatter_dimension=0,
                tiled=True,
            )
            for term in self.terms
        )


def in_turn(*transfers):
    for transfer in transfers:
        transfer.step()


def swapped(values, axis, bit):
    return lax.ppermute(values, axis, [(i, i ^ bit) for i in range(lax.axis_size(axis))])


class Exchange:
    def __init__(self, ring, values, axis):
        self.ring, self.values, self.axis = ring, values, axis
        self.got = None
        count = lax.axis_size(axis)
        self.bits = [1 << i for i in range(count.bit_length() - 1)]
        self.stages = self.plan()

    def upper(self, bit):
        return (lax.axis_index(self.axis) // bit) % 2 > 0

    def step(self, under_way=None):
        if self.got is not None:
            got, bit, end = self.got
            self.got = None
            end(got if under_way is None else self.ring.then(got, under_way), bit)
        if self.stages:
            start, end, bit = self.stages.pop(0)
            self.got = (swapped(start(bit), self.axis, bit), bit, end)
        return self.values

    def run(self, under_way=None):
        while self.stages or self.got is not None:
            self.step(under_way)
        return self.values

    def start_half(self, bit):
        half = self.values.shape[0] // 2
        kept, sent = [
            jnp.where(self.upper(bit) == side, self.values[half:], self.values[:half])
            for side in (True, False)
        ]
        self.values = kept
        return sent.astype(bf16)

    def end_half(self, got, bit):
        self.values = self.values.astype(f32) + got.astype(f32)

    def start_join(self, bit):
        return self.values

    def end_join(self, got, bit):
        upper, own = self.upper(bit), self.values
        self.values = jnp.concatenate([jnp.where(upper, got, own), jnp.where(upper, own, got)], 0)

    def end_sum(self, got, bit):
        self.values = self.values + got

    def halving(self):
        return [(self.start_half, self.end_half, bit) for bit in self.bits]

    def joining(self):
        return [(self.start_join, self.end_join, bit) for bit in reversed(self.bits)]


class Halves(Exchange):
    def plan(self):
        return self.halving()


class Joined(Exchange):
    def plan(self):
        return self.joining()


class Everywhere(Exchange):
    def plan(self):
        stages = self.halving() + self.joining()
        middle = len(self.bits)

        def start_first_join(bit):
            self.values = self.values.astype(bf16)
            return self.values

        if stages:
            stages[middle] = (start_first_join, self.end_join, stages[middle][2])
        return stages


class SmallSum(Exchange):
    def plan(self):
        return [(self.start_join, self.end_sum, bit) for bit in self.bits]


def own_rows(values):
    count, mine = lax.axis_size("fsdp"), lax.axis_index("fsdp")
    bit = 1
    while bit < count:
        half = values.shape[0] // 2
        values = lax.dynamic_slice_in_dim(values, ((mine // bit) % 2) * half, half, 0)
        bit *= 2
    return values


def halves_joined(own):
    count, mine = lax.axis_size("fsdp"), lax.axis_index("fsdp")
    bit = count // 2
    while bit:
        got = lax.ppermute(own, "fsdp", [(i, i ^ bit) for i in range(count)])
        upper = (mine // bit) % 2 > 0
        own = jnp.concatenate([jnp.where(upper, got, own), jnp.where(upper, own, got)], 0)
        bit //= 2
    return own


def passed_along(block, distance):
    devices = range(lax.axis_size("seq"))
    route = [(i - distance, i) for i in devices if i - distance in devices]
    return lax.ppermute(block, "seq", route)


def joined_maps(earlier, later):
    return jnp.stack([earlier[0] * later[0], later[1] + later[0] * earlier[1]], 0)


class Entry:
    def __init__(self, prods, states, sign):
        self.pair, self.sign = jnp.stack([prods, states], 0), sign
        self.count = lax.axis_size("seq")
        self.direct = self.count == ring_count
        if self.direct:
            self.other = swapped(self.pair, "seq", 1)

    def between(self, hold):
        if not self.direct:
            return
        self.other = hold(self.other)
        self.second = lax.axis_index("seq") % 2 == (1 if self.sign > 0 else 0)
        earlier = jnp.where(self.second, self.other, self.pair)
        later = jnp.where(self.second, self.pair, self.other)
        both = joined_maps(earlier, later)
        self.parts = [
            passed_along(both, self.sign * distance) for distance in range(self.count - 2, 0, -2)
        ]

    def state(self, hold):
        if self.direct:
            parts = [hold(self.parts[0])] + self.parts[1:]
            state = parts[0][1]
            for part in parts[1:]:
                state = part[1] + part[0] * state
            return jnp.where(self.second, self.other[1] + self.other[0] * state, state)
        pair = passed_along(self.pair, self.sign)
        distance = 1
        while distance < self.count:
            pair = joined_maps(passed_along(pair, self.sign * distance), pair)
            distance *= 2
        return pair[1]


def ring_index(place, count):
    place = lax.rem(place + 2 * count, count)
    odd = place // (count // 2)
    return (1 - odd) * (2 * place) + odd * (2 * count - 1 - 2 * place)


def ring_place(index, count):
    odd = lax.rem(index, 2)
    return (1 - odd) * (index // 2) + odd * (count - 1 - index // 2)


def partner(index, bit):
    return index + bit * (1 - 2 * lax.rem(index // bit, 2))


class Copies:
    def __init__(self, send_sems, recv_sems):
        self.send_sems, self.recv_sems = send_sems, recv_sems
        self.started, self.waiting = 0, []

    def start(self, source, target, device):
        slot = self.started
        copy = pltpu.make_async_remote_copy(
            src_ref=source,
            dst_ref=target,
            send_sem=self.send_sems.at[slot],
            recv_sem=self.recv_sems.at[slot],
            device_id=device,
            device_id_type=pl.DeviceIdType.MESH,
        )
        copy.start()
        self.started += 1
        self.waiting.append(copy)
        return copy

    def sent(self, copy):
        copy.wait_send()
        self.waiting.remove(copy)

    def end(self):
        for copy in self.waiting:
            copy.wait_send()


class Moves:
    def __init__(self, sems):
        self.sems, self.started, self.waiting = sems, 0, []

    def start(self, source, target):
        copy = pltpu.make_async_copy(source, target, self.sems.at[self.started])
        copy.start()
        self.started += 1
        self.waiting.append(copy)
        return copy

    def wait(self, number):
        for copy in self.waiting[:number]:
            copy.wait()
        self.waiting = self.waiting[number:]


def greet(devices):
    barrier = pltpu.get_barrier_semaphore()
    for device in devices:
        pl.semaphore_signal(
            barrier, inc=1, device_id=device, device_id_type=pl.DeviceIdType.MESH
        )
    pl.semaphore_wait(barrier, len(devices))


tail_copies = 28 + 4 + 3 + 3 + 5


def tail_body(
    count,
    emb_ref,
    mixed_ref,
    normed_ref,
    branch_ref,
    inner_ref,
    branch_all_in,
    inner_all_in,
    values_ref,
    grad_ref,
    gain_ref,
    gain_two_ref,
    small_ref,
    blocks_ref,
    branch_out,
    inner_out,
    out_out,
    tokens_out,
    gains_out,
    small_out,
    blocks_out,
    wide_sent,
    wide_got,
    slim_sent,
    slim_got,
    half_sent,
    half_kept,
    half_got,
    own_sent,
    own_got,
    small_sums,
    small_got,
    gain_sums,
    gain_got,
    branch_all_ref,
    inner_all_ref,
    move_sems,
    send_sems,
    recv_sems,
):
    index, unit = lax.axis_index("seq"), lax.axis_index("fsdp")
    place = ring_place(index, count)
    forth, back = {"seq": ring_index(place + 1, count)}, {"seq": ring_index(place - 1, count)}
    across = [{"seq": partner(index, bit)} for bit in (1, 2, 4)]
    beside = [{"fsdp": partner(unit, bit)} for bit in (1, 2)]
    copies = Copies(send_sems, recv_sems)
    rows, units = branch_ref.shape
    slab = normed_ref.shape[1] // count
    tn = (((0,), (0,)), ((), ()))
    moves = Moves(move_sems)
    moves.start(branch_all_in, branch_all_ref)
    moves.start(inner_all_in, inner_all_ref)

    greet([forth, back] + across + beside)

    cut = slim_got.shape[2]
    parts = (slice(0, cut), slice(cut, units))

    def out_term(k, way):
        return lax.dot_general(
            mixed_ref[:, parts[way]],
            emb_ref[:, k * slab : (k + 1) * slab],
            tn,
            preferred_element_type=f32,
        )

    def front_term(k, way):
        return lax.dot_general(
            (inner_ref if way else branch_ref)[...],
            normed_ref[:, k * slab : (k + 1) * slab],
            tn,
            preferred_element_type=f32,
        )

    rings = {}

    def send(name, way, step, total):
        sent, got = (slim_sent, slim_got) if name == "out" else (wide_sent, wide_got)
        there = pl.ds(0, total.shape[0])
        sent[way, step, there, :] = total.astype(bf16)
        rings[name, way] = copies.start(
            sent.at[way, step, there], got.at[way, step, there], back if way else forth
        )

    def term(name, way, step):
        k = (count - step) % count if way else step % count
        return out_term(k, way) if name == "out" else front_term(k, way)

    def serve(name, step):
        got = slim_got if name == "out" else wide_got
        terms = [term(name, way, step) for way in (0, 1)]
        for way, own in enumerate(terms):
            rings[name, way].wait_recv()
            total = got[way, step - 2, pl.ds(0, own.shape[0]), :].astype(f32) + own
            if step < count:
                send(name, way, step - 1, total)
            elif name == "out":
                out_out[parts[way], :] = total
            else:
                (inner_out if way else branch_out)[...] = total

    for name in ("out", "front"):
        for way in (0, 1):
            send(name, way, 0, term(name, way, 1))
    moves.wait(2)

    high = blocks_out.shape[0]
    bits = [lax.rem(index // bit, 2) for bit in (1, 2, 4)]
    sizes = [high // 2, high // 4, high // 8]
    starts = [bits[0] * sizes[0]]
    for bit, size in zip(bits[1:], sizes[1:]):
        starts.append(starts[-1] + bit * size)
    at = [rows_at(start, size) for start, size in zip(starts, sizes)]
    blocks_out[at[2], :] = blocks_ref[...]
    blocks_copy = copies.start(blocks_out.at[at[2]], blocks_out.at[at[2]], across[2])
    small_sums[0] = small_ref[...]
    small_copy = copies.start(small_sums.at[0], small_got.at[0], across[0])

    core, side = lax.rem(unit, 2), lax.rem(unit // 2, 2)
    mid, own = rows // 2, rows // 4

    def front_back(start, k):
        columns = slice(k * slab, (k + 1) * slab)
        return jnp.dot(
            branch_ref[rows_at(start, mid), :],
            branch_all_ref[:, columns],
            preferred_element_type=f32,
        ) + jnp.dot(
            inner_ref[rows_at(start, mid), :],
            inner_all_ref[:, columns],
            preferred_element_type=f32,
        )

    for k in range(count):
        half_sent[:, k * slab : (k + 1) * slab] = front_back((1 - core) * mid, k).astype(bf16)
    half_copy = copies.start(half_sent, half_got, beside[0])
    serve("out", 2)
    for k in range(count):
        half_kept[:, k * slab : (k + 1) * slab] = front_back(core * mid, k)
    half_copy.wait_recv()
    other = rows_at((1 - side) * own, own)
    mine = rows_at(side * own, own)
    own_sent[...] = (half_kept[other, :] + half_got[other, :].astype(f32)).astype(bf16)
    own_copy = copies.start(own_sent, own_got, beside[1])
    serve("front", 2)

    blocks_copy.wait_recv()
    blocks_copy = copies.start(blocks_out.at[at[1]], blocks_out.at[at[1]], across[1])
    small_copy.wait_recv()
    small_sums[1] = small_sums[0] + small_got[0]
    small_copy = copies.start(small_sums.at[1], small_got.at[1], across[1])
    serve("out", 3)
    serve("front", 3)

    own_copy.wait_recv()
    values = values_ref[...]
    scale = lax.rsqrt(jnp.mean(values * values, axis=-1, keepdims=True) + eps)
    unit_values = values * scale
    front = half_kept[mine, :] + half_got[mine, :].astype(f32) + own_got[...].astype(f32)
    gain_grad = jnp.sum(front * unit_values, 0, keepdims=True)
    weighted = front * gain_ref[0:1, :]
    result = grad_ref[...] + scale * (
        weighted - unit_values * jnp.mean(weighted * unit_values, axis=-1, keepdims=True)
    )
    low = result.astype(bf16)
    own_at = rows_at(core * mid + side * own, own)
    gain_sums[0] = jnp.zeros_like(gain_sums[0])
    for k in range(count):
        to = pl.ds(pl.multiple_of(ring_index(place - k, count) * slab, slab), slab)
        part = slice(k * slab, (k + 1) * slab)
        tokens_out[own_at, to] = low[:, part]
        gain_sums[0, 0:1, to] = gain_grad[:, part]
        gain_sums[0, 1:2, to] = gain_two_ref[0:1, part]
    tokens_copy = copies.start(tokens_out.at[own_at], tokens_out.at[own_at], beside[1])
    gain_copy = copies.start(gain_sums.at[0], gain_got.at[0], across[0])
    serve("out", 4)
    serve("front", 4)

    blocks_copy.wait_recv()
    blocks_copy = copies.start(blocks_out.at[at[0]], blocks_out.at[at[0]], across[0])
    small_copy.wait_recv()
    small_sums[2] = small_sums[1] + small_got[1]
    small_copy = copies.start(small_sums.at[2], small_got.at[2], across[2])
    gain_copy.wait_recv()
    gain_sums[1] = gain_sums[0] + gain_got[0]
    gain_copy = copies.start(gain_sums.at[1], gain_got.at[1], across[1])
    tokens_copy.wait_recv()
    both_at = rows_at(core * mid, mid)
    tokens_copy = copies.start(tokens_out.at[both_at], tokens_out.at[both_at], beside[0])
    serve("out", 5)
    serve("front", 5)

    blocks_copy.wait_recv()
    gain_copy.wait_recv()
    gain_sums[2] = gain_sums[1] + gain_got[1]
    gain_copy = copies.start(gain_sums.at[2], gain_got.at[2], across[2])
    small_copy.wait_recv()
    small_out[...] = small_sums[2] + small_got[2]
    serve("out", 6)
    serve("front", 6)

    gain_copy.wait_recv()
    gain_sums[3] = gain_sums[2] + gain_got[2]
    gain_copy = copies.start(gain_sums.at[3], gain_got.at[3], beside[0])
    serve("out", 7)
    gain_copy.wait_recv()
    gain_sums[4] = gain_sums[3] + gain_got[3]
    gain_copy = copies.start(gain_sums.at[4], gain_got.at[4], beside[1])
    serve("front", 7)
    serve("out", 8)
    gain_copy.wait_recv()
    gains_out[...] = gain_sums[4] + gain_got[4]
    tokens_copy.wait_recv()
    serve("front", 8)
    copies.end()


def tail(count, *operands):
    emb, mixed, normed, *_ = operands
    small, blocks = operands[-2:]
    rows, width = emb.shape
    units = mixed.shape[1]
    slab, cut = width // count, -(-units // 256) * 128
    high, block_width = blocks.shape
    whole = pl.BlockSpec(memory_space=pltpu.VMEM)
    grad = jax.ShapeDtypeStruct((units, slab), f32)
    steps = count - 1
    return pl.pallas_call(
        functools.partial(tail_body, count),
        out_shape=(
            grad,
            grad,
            grad,
            jax.ShapeDtypeStruct((rows, width), bf16),
            jax.ShapeDtypeStruct((8, width), f32),
            jax.ShapeDtypeStruct(small.shape, f32),
            jax.ShapeDtypeStruct((8 * high, block_width), bf16),
        ),
        in_specs=[whole] * 5
        + [pl.BlockSpec(memory_space=pl.ANY)] * 2
        + [whole] * (len(operands) - 7),
        out_specs=(whole,) * 7,
        scratch_shapes=[
            pltpu.VMEM((2, steps, units, slab), bf16),
            pltpu.VMEM((2, steps, units, slab), bf16),
            pltpu.VMEM((2, steps, cut, slab), bf16),
            pltpu.VMEM((2, steps, cut, slab), bf16),
            pltpu.VMEM((rows // 2, width), bf16),
            pltpu.VMEM((rows // 2, width), f32),
            pltpu.VMEM((rows // 2, width), bf16),
            pltpu.VMEM((rows // 4, width), bf16),
            pltpu.VMEM((rows // 4, width), bf16),
            pltpu.VMEM((3, *small.shape), f32),
            pltpu.VMEM((3, *small.shape), f32),
            pltpu.VMEM((5, 8, width), f32),
            pltpu.VMEM((5, 8, width), f32),
            pltpu.VMEM((units, width), bf16),
            pltpu.VMEM((units, width), bf16),
            pltpu.SemaphoreType.DMA((2,)),
            pltpu.SemaphoreType.DMA((tail_copies,)),
            pltpu.SemaphoreType.DMA((tail_copies,)),
        ],
        compiler_params=pltpu.CompilerParams(
            collective_id=0, has_side_effects=True, vmem_limit_bytes=60 * 1024 * 1024
        ),
    )(*operands)


def peers(count, units):
    index, unit = lax.axis_index("seq"), lax.axis_index("fsdp")
    along = [{"seq": lax.rem(index + distance, count)} for distance in range(1, count)]
    beside = [{"fsdp": partner(unit, 1 << i)} for i in range(units.bit_length() - 1)]
    return along, beside


def rows_at(start, size, multiple=16):
    return pl.ds(pl.multiple_of(start, multiple), size)


def dot_nt_here(left, right):
    return lax.dot_general(left, right, (((1,), (1,)), ((), ())), preferred_element_type=f32)


def dot_slabs(left, right_ref, slab, count):
    for k in range(count):
        columns = slice(k * slab, (k + 1) * slab)
        yield columns, jnp.dot(left, right_ref[:, columns], preferred_element_type=f32)


def scan_rows(a_ref, b_ref, prod_ref, state_ref, batches, backward):
    length, units = a_ref.shape[0] // batches, a_ref.shape[1]
    tiles = length // 8
    rows = lax.broadcasted_iota(jnp.int32, (8, units), 0)

    def step(index, carry):
        tile = tiles - 1 - index if backward else index
        following = []
        for batch in range(batches):
            prod_in, state_in, a_next = carry[batch]
            at = rows_at(batch * length + tile * 8, 8, 8)
            a, b = a_ref[at, :], b_ref[at, :]
            a_first = a[0:1]
            if backward:
                a = jnp.where(rows < 7, pltpu.roll(a, 7, 0), a_next)
            for shift in (1, 2, 4):
                turn = 8 - shift if backward else shift
                inside = rows < 8 - shift if backward else rows >= shift
                a_moved = jnp.where(inside, pltpu.roll(a, turn, 0), 1.0)
                b_moved = jnp.where(inside, pltpu.roll(b, turn, 0), 0.0)
                b = a * b_moved + b
                a = a * a_moved
            b = b + a * state_in
            a = a * prod_in
            prod_ref[at, :] = a
            state_ref[at, :] = b
            edge = 0 if backward else 7
            following.append((a[edge : edge + 1], b[edge : edge + 1], a_first))
        return tuple(following)

    one, zero = jnp.ones((1, units), f32), jnp.zeros((1, units), f32)
    maps = lax.fori_loop(0, tiles, step, ((one, zero, one),) * batches)
    return [(prod, state) for prod, state, _ in maps]


def entry_states(ends_ref, got_ref, index, count, batches, sign):
    states = []
    for batch in range(batches):
        state = jnp.zeros_like(ends_ref[0:1, :])
        for distance in range(count - 1, 0, -1):
            there = index - distance >= 0 if sign > 0 else index + distance < count
            prods = got_ref[distance - 1, batch : batch + 1, :]
            longer = got_ref[distance - 1, batches + batch : batches + batch + 1, :] + prods * state
            state = jnp.where(there, longer, 0.0)
        states.append(state)
    return states


head_copies = 9 * (ring_count - 1) + 5
row_block = 32


def head_body(
    count,
    fsdp,
    batches,
    tokens_ref,
    cot_ref,
    branch_ref,
    inner_ref,
    out_ref,
    gate_ref,
    up_ref,
    down_ref,
    taps_ref,
    conv_bias_ref,
    gate_bias_ref,
    input_bias_ref,
    rate_ref,
    slope_ref,
    gain_one_ref,
    gain_two_ref,
    resets_ref,
    gate_blocks_ref,
    input_blocks_ref,
    gate_all,
    up_all,
    down_all,
    branch_all_far,
    inner_all_far,
    out_all_far,
    cot_out_far,
    normed_out_far,
    branch_pre_far,
    padded_far,
    conv_low_far,
    gate_pre_far,
    input_pre_far,
    carries_far,
    states_far,
    mixed_low_far,
    gate_square_far,
    input_square_far,
    ends,
    own_values,
    own_middle,
    normed_two,
    gains,
    packed_ref,
    fresh_ref,
    branch_all,
    inner_all,
    out_all,
    cot_out,
    normed_out,
    branch_pre,
    padded,
    conv_low,
    gate_pre,
    input_pre,
    carries,
    states,
    mixed_low,
    gate_square_ref,
    input_square_ref,
    tokens_low,
    prods,
    local_states,
    edges_sent,
    edges_got,
    ends_sent,
    ends_got,
    half_sent,
    half_kept,
    half_got,
    own_sent,
    own_got,
    local_sems,
    far_sems,
    send_sems,
    recv_sems,
):
    index, unit = lax.axis_index("seq"), lax.axis_index("fsdp")
    place = ring_place(index, count)
    forth, back = {"seq": ring_index(place + 1, count)}, {"seq": ring_index(place - 1, count)}
    along, beside = peers(count, fsdp)
    copies = Copies(send_sems, recv_sems)
    rows, width = tokens_ref.shape
    units, hidden = branch_ref.shape[0], down_ref.shape[0]
    length, slab = rows // batches, width // count
    core, side = lax.rem(unit, 2), lax.rem(unit // 2, 2)
    mid, own = rows // 2, rows // 4

    locals_of = []
    for source, target in zip(
        (branch_ref, inner_ref, out_ref, gate_ref, up_ref, down_ref),
        (branch_all, inner_all, out_all, gate_all, up_all, down_all),
    ):
        first = target.at[pl.ds(0, slab)]
        if source.shape[1] == slab:
            first = target.at[:, pl.ds(0, slab)]
        copy = pltpu.make_async_copy(source, first, local_sems.at[len(locals_of)])
        copy.start()
        locals_of.append(copy)

    greet(along + beside)

    pairs = {
        "front": ((branch_ref, branch_all, 0, units), (inner_ref, inner_all, 0, units)),
        "out": (
            (out_ref, out_all, 0, units // 2),
            (out_ref, out_all, units // 2, units // 2),
        ),
        "mlp": ((gate_ref, gate_all, None, None), (up_ref, up_all, None, None)),
        "down": (
            (down_ref, down_all, 0, hidden // 2),
            (down_ref, down_all, hidden // 2, hidden // 2),
        ),
    }
    under_way = {}

    def start(name, step):
        for way in (0, 1):
            shard, whole, first, size = pairs[name][way]

            def slab_at(k):
                if first is None:
                    return whole.at[pl.ds(k * slab, slab)]
                return whole.at[pl.ds(first, size), pl.ds(k * slab, slab)]

            if step > 1:
                under_way[name, way].wait_recv()
            there = (count - step) % count if way else step
            here = (there + 1) % count if way else step - 1
            if step > 1:
                source = slab_at(here)
            else:
                source = shard if first is None else shard.at[pl.ds(first, size)]
            under_way[name, way] = copies.start(source, slab_at(there), back if way else forth)

    def finish(name):
        for way in (0, 1):
            under_way[name, way].wait_recv()

    start("front", 1)
    start("out", 1)

    packed_ref[...] = jnp.zeros_like(packed_ref)
    packed_ref[0:4, :units] = taps_ref[...].astype(f32)
    vectors = (conv_bias_ref, gate_bias_ref, input_bias_ref, rate_ref, slope_ref)
    for row, vector in enumerate((*vectors, gain_one_ref, gain_two_ref)):
        size = vector.shape[0]
        packed_ref[row + 4 : row + 5, :size] = vector[...].astype(f32).reshape(1, size)
    flags = jnp.concatenate(
        [resets_ref[...].astype(f32), jnp.zeros((8 - batches, length), f32)], 0
    ).T
    for batch in range(batches):
        fresh_ref[batch * length : (batch + 1) * length, :] = flags[:, batch : batch + 1]

    for k in range(count):
        plain = pl.ds(pl.multiple_of(ring_index(place - k, count) * slab, slab), slab)
        part = slice(k * slab, (k + 1) * slab)
        tokens_low[:, part] = tokens_ref[:, plain]
        gains[0:1, part] = packed_ref[9:10, plain]
        gains[1:2, part] = packed_ref[10:11, plain]
    start("front", 2)
    start("out", 2)

    def norm_block(block, carry):
        at = rows_at(block * row_block, row_block)
        values = tokens_low[at, :].astype(f32)
        scale = lax.rsqrt(jnp.mean(values * values, axis=-1, keepdims=True) + eps)
        normed_out[at, :] = (values * scale * gains[0:1, :]).astype(bf16)
        return carry

    lax.fori_loop(0, rows // row_block, norm_block, 0)
    own_values[...] = tokens_low[rows_at(core * mid + side * own, own), :].astype(f32)
    start("front", 3)
    start("out", 3)
    for blocks, square in (
        (gate_blocks_ref, gate_square_ref),
        (input_blocks_ref, input_square_ref),
    ):
        square[...] = jnp.zeros_like(square)
        size = blocks.shape[1]
        for j in range(blocks.shape[0]):
            square[j * size : (j + 1) * size, j * size : (j + 1) * size] = blocks[j]
    for k in range(count):
        plain = pl.ds(pl.multiple_of(ring_index(place - k, count) * slab, slab), slab)
        cot_out[:, k * slab : (k + 1) * slab] = cot_ref[:, plain]
    for step in range(4, count):
        start("front", step)
        start("out", step)
    start("mlp", 1)
    start("down", 1)
    for copy in locals_of:
        copy.wait()
    finish("front")

    for batch in range(batches):
        at = slice(batch * length, (batch + 1) * length)
        top = batch * (length + 8)
        inner = dot_nt_here(normed_out[at, :], inner_all[...])
        padded[top + 8 : top + 8 + length, :] = inner.astype(bf16).astype(f32)
        edges_sent[batch] = padded[top + length : top + length + 8, :]
    edge_copy = copies.start(edges_sent, edges_got, along[0])
    for batch in range(batches):
        at = slice(batch * length, (batch + 1) * length)
        branch_pre[at, :] = dot_nt_here(normed_out[at, :], branch_all[...])
    edge_copy.wait_recv()
    for batch in range(batches):
        top = batch * (length + 8)
        padded[top : top + 8, :] = jnp.where(index > 0, edges_got[batch], 0.0)
    start("mlp", 2)
    bias, gate_bias, input_bias, rate = [packed_ref[i : i + 1, :units] for i in range(4, 8)]

    def conv_block(block, carry):
        batch = block // (length // row_block)
        wide = padded[rows_at(block * row_block + batch * 8, row_block + 8, 8), :]
        total = bias + packed_ref[0:1, :units] * wide[8:] + packed_ref[1:2, :units] * wide[7:-1]
        total = total + packed_ref[2:3, :units] * wide[6:-2] + packed_ref[3:4, :units] * wide[5:-3]
        conv_low[rows_at(block * row_block, row_block), :] = total.astype(bf16)
        return carry

    lax.fori_loop(0, rows // row_block, conv_block, 0)
    for batch in range(batches):
        at = slice(batch * length, (batch + 1) * length)
        conv = conv_low[at, :]
        gate_pre[at, :] = (
            jnp.dot(conv, gate_square_ref[...], preferred_element_type=f32) + gate_bias
        )
        input_pre[at, :] = (
            jnp.dot(conv, input_square_ref[...], preferred_element_type=f32) + input_bias
        )
    start("down", 2)

    def gate_block(block, carry):
        at = rows_at(block * row_block, row_block)
        rate_gate = jax.nn.sigmoid(gate_pre[at, :])
        inlet_gate = jax.nn.sigmoid(input_pre[at, :])
        log_decay = rate * rate_gate
        decay = jnp.exp(log_decay)
        fresh = fresh_ref[at, :] > 0
        scale = jnp.sqrt(-jnp.tanh(log_decay) * (1.0 + decay * decay))
        carries[at, :] = jnp.where(fresh, 0.0, decay)
        local_states[at, :] = (
            jnp.where(fresh, 1.0, scale) * inlet_gate * conv_low[at, :].astype(f32)
        )
        return carry

    lax.fori_loop(0, rows // row_block, gate_block, 0)
    scanned = scan_rows(carries, local_states, prods, local_states, batches, False)
    ends_sent[...] = jnp.zeros_like(ends_sent)
    for batch, (prod, state) in enumerate(scanned):
        ends_sent[batch : batch + 1, :] = prod
        ends_sent[batches + batch : batches + batch + 1, :] = state
    ends[...] = ends_sent[...]
    end_copies = [
        copies.start(ends_sent, ends_got.at[distance - 1], along[distance - 1])
        for distance in range(1, count)
    ]
    start("mlp", 3)
    for copy in end_copies:
        copy.wait_recv()
    entries = entry_states(ends, ends_got, index, count, batches, 1)

    for batch in range(batches):
        entry = entries[batch]
        top = batch * (length + 8)
        states[top : top + 8, :] = jnp.broadcast_to(entry, (8, units))

        def state_block(block, carry, batch=batch, entry=entry):
            at = rows_at(batch * length + block * row_block, row_block)
            state = local_states[at, :] + prods[at, :] * entry
            states[rows_at(8 + batch * (length + 8) + block * row_block, row_block, 8), :] = state
            mixed_low[at, :] = (state * gelu_tanh(branch_pre[at, :])).astype(bf16)
            return carry

        lax.fori_loop(0, length // row_block, state_block, 0)
    start("down", 3)
    finish("out")
    for part, result in dot_slabs(
        mixed_low[rows_at((1 - core) * mid, mid), :], out_all, slab, count
    ):
        half_sent[:, part] = result.astype(bf16)
    half_copy = copies.start(half_sent, half_got, beside[0])
    for part, result in dot_slabs(mixed_low[rows_at(core * mid, mid), :], out_all, slab, count):
        half_kept[:, part] = result
    half_copy.wait_recv()
    other, mine = rows_at((1 - side) * own, own), rows_at(side * own, own)
    own_sent[...] = (half_kept[other, :] + half_got[other, :].astype(f32)).astype(bf16)
    own_copy = copies.start(own_sent, own_got, beside[1])
    start("mlp", 4)
    start("down", 4)
    own_copy.wait_recv()
    middle = own_values[...] + (
        half_kept[mine, :] + half_got[mine, :].astype(f32) + own_got[...].astype(f32)
    )
    own_middle[...] = middle
    scale = lax.rsqrt(jnp.mean(middle * middle, axis=-1, keepdims=True) + eps)
    own_at, both_at = rows_at(core * mid + side * own, own), rows_at(core * mid, mid)
    normed_two[own_at, :] = (middle * scale * gains[1:2, :]).astype(bf16)
    join_copy = copies.start(normed_two.at[own_at], normed_two.at[own_at], beside[1])
    start("mlp", 5)
    join_copy.wait_recv()
    join_copy = copies.start(normed_two.at[both_at], normed_two.at[both_at], beside[0])
    start("down", 5)
    join_copy.wait_recv()
    for step in range(6, count):
        start("mlp", step)
        start("down", step)
    moves = Moves(far_sems)
    for source, target in (
        (branch_all, branch_all_far),
        (inner_all, inner_all_far),
        (out_all, out_all_far),
        (cot_out, cot_out_far),
        (normed_out, normed_out_far),
        (branch_pre, branch_pre_far),
        (padded, padded_far),
        (conv_low, conv_low_far),
        (gate_pre, gate_pre_far),
        (input_pre, input_pre_far),
        (carries, carries_far),
        (states, states_far),
        (mixed_low, mixed_low_far),
        (gate_square_ref, gate_square_far),
        (input_square_ref, input_square_far),
    ):
        moves.start(source, target)
    finish("mlp")
    finish("down")
    moves.wait(15)
    copies.end()


def head(count, fsdp, batches, *operands):
    tokens = operands[0]
    branch, gate = operands[2], operands[5]
    rows, width = tokens.shape
    units, hidden = branch.shape[0], gate.shape[1]
    whole, place = pl.BlockSpec(memory_space=pltpu.VMEM), pl.BlockSpec(memory_space=pl.ANY)

    def array(dtype, *shape):
        return jax.ShapeDtypeStruct(shape, dtype)

    kept = (
        [array(bf16, units, width)] * 3
        + [array(bf16, rows, width)] * 2
        + [array(f32, rows, units), array(f32, rows + 8 * batches, units), array(bf16, rows, units)]
        + [array(f32, rows, units)] * 3
        + [array(f32, rows + 8 * batches, units), array(bf16, rows, units)]
        + [array(bf16, units, units)] * 2
    )
    outs = (
        [array(bf16, width, hidden)] * 2
        + [array(bf16, hidden, width)]
        + kept
        + [array(f32, 8, units)]
        + [array(f32, rows // 4, width)] * 2
        + [array(bf16, rows, width), array(f32, 8, width)]
        + [array(f32, 16, width), array(f32, rows, 1)]
    )
    return pl.pallas_call(
        functools.partial(head_body, count, fsdp, batches),
        out_shape=tuple(outs),
        in_specs=[whole] * 2 + [place] * 6 + [whole] * 11,
        out_specs=tuple([place] * (len(outs) - 7) + [whole] * 7),
        scratch_shapes=[
            *[pltpu.VMEM(part.shape, part.dtype) for part in kept],
            pltpu.VMEM((rows, width), bf16),
            pltpu.VMEM((rows, units), f32),
            pltpu.VMEM((rows, units), f32),
            pltpu.VMEM((batches, 8, units), f32),
            pltpu.VMEM((batches, 8, units), f32),
            pltpu.VMEM((8, units), f32),
            pltpu.VMEM((count - 1, 8, units), f32),
            pltpu.VMEM((rows // 2, width), bf16),
            pltpu.VMEM((rows // 2, width), f32),
            pltpu.VMEM((rows // 2, width), bf16),
            pltpu.VMEM((rows // 4, width), bf16),
            pltpu.VMEM((rows // 4, width), bf16),
            pltpu.SemaphoreType.DMA((6,)),
            pltpu.SemaphoreType.DMA((15,)),
            pltpu.SemaphoreType.DMA((head_copies,)),
            pltpu.SemaphoreType.DMA((head_copies,)),
        ],
        compiler_params=pltpu.CompilerParams(
            collective_id=1, has_side_effects=True, vmem_limit_bytes=60 * 1024 * 1024
        ),
    )(*operands)


def gelu_slope(values):
    constant = 0.7978845608028654
    bent = jnp.tanh(constant * (values + 0.044715 * values * values * values))
    inner = constant * (1.0 + 3.0 * 0.044715 * values * values)
    return 0.5 * (1.0 + bent) + 0.5 * values * (1.0 - bent * bent) * inner


ring_slots = 3
back_sends = 2 * 2 * (ring_count - 1)
back_copies = 4 + 4 + (ring_count - 1) + 1 + 3


class RingSum:
    def __init__(self, terms, slots, sends, arrivals, credits, count, neighbours):
        self.terms, self.slots, self.count = terms, slots, count
        self.sends, self.arrivals, self.credits = sends, arrivals, credits
        self.neighbours = neighbours
        self.copies = [[], []]

    def send(self, way, step, total):
        here, there = (step - 1) % ring_slots, step % ring_slots
        self.slots[way, here] = total.astype(bf16)
        if step >= ring_slots:
            pl.semaphore_wait(self.credits.at[way], 1)
        copy = pltpu.make_async_remote_copy(
            src_ref=self.slots.at[way, here],
            dst_ref=self.slots.at[way, there],
            send_sem=self.sends.at[way, step - 1],
            recv_sem=self.arrivals.at[way, step - 1],
            device_id=self.neighbours[way],
            device_id_type=pl.DeviceIdType.MESH,
        )
        copy.start()
        self.copies[way].append(copy)
        if step >= 2:
            self.copies[way][step - 2].wait_send()
            if step + 1 < self.count:
                pl.semaphore_signal(
                    self.credits.at[way],
                    inc=1,
                    device_id=self.neighbours[1 - way],
                    device_id_type=pl.DeviceIdType.MESH,
                )

    def serve(self, step, end=None):
        slabs = (step % self.count, (self.count - step) % self.count)
        terms = [term(k) for term, k in zip(self.terms, slabs)]
        for way, own in enumerate(terms):
            if step == 1:
                self.send(way, 1, own)
                continue
            self.copies[way][step - 2].wait_recv()
            total = self.slots[way, (step - 1) % ring_slots].astype(f32) + own
            if step < self.count:
                self.send(way, step, total)
            else:
                self.copies[way][step - 2].wait_send()
                end(way, total)


def back_body(
    count,
    fsdp,
    batches,
    cot_ref,
    hidden_ref,
    normed_ref,
    gate_low_ref,
    up_low_ref,
    ends_ref,
    own_middle,
    fresh_ref,
    packed_ref,
    gains_ref,
    gate_all,
    up_all,
    down_all,
    out_all,
    branch_pre_in,
    padded_in,
    conv_low_in,
    gate_pre_in,
    input_pre_in,
    carries_in,
    states_in,
    gate_square_in,
    input_square_in,
    mixed_out,
    middle_low,
    own_grad,
    small_out,
    blocks_out,
    gain_grad_out,
    down_grad,
    branch_low_out,
    inner_low_out,
    gate_low_out,
    input_low_out,
    gate_grad,
    up_grad,
    half_sent,
    half_kept,
    half_got,
    own_sent,
    own_got,
    prods,
    adjoints,
    conv_grad,
    edges_sent,
    edges_got,
    ends_sent,
    ends_got,
    mlp_slots,
    down_slots,
    stream_one,
    stream_two,
    stream_out,
    stream_down,
    stage,
    branch_pre,
    padded,
    conv_low,
    gate_pre,
    input_pre,
    carries,
    states,
    gate_square_ref,
    input_square_ref,
    branch_low,
    inner_low,
    gate_low,
    input_low,
    blocks,
    blocks_one,
    blocks_two,
    blocks_got_one,
    blocks_got_two,
    blocks_got_three,
    move_sems,
    stream_sems,
    stage_sems,
    ring_sends,
    ring_arrivals,
    ring_credits,
    send_sems,
    recv_sems,
):
    index, unit = lax.axis_index("seq"), lax.axis_index("fsdp")
    place = ring_place(index, count)
    neighbours = (
        {"seq": ring_index(place + 1, count)},
        {"seq": ring_index(place - 1, count)},
    )
    along, beside = peers(count, fsdp)
    copies = Copies(send_sems, recv_sems)
    rows, width = cot_ref.shape
    units = branch_pre.shape[1]
    moves = Moves(move_sems)
    for source, target in (
        (branch_pre_in, branch_pre),
        (states_in, states),
        (carries_in, carries),
        (gate_pre_in, gate_pre),
        (input_pre_in, input_pre),
        (conv_low_in, conv_low),
        (gate_square_in, gate_square_ref),
        (input_square_in, input_square_ref),
        (padded_in, padded),
    ):
        moves.start(source, target)
    length, slab = rows // batches, width // count
    inner_half = hidden_ref.shape[1] // 2
    core, side = lax.rem(unit, 2), lax.rem(unit // 2, 2)
    mid, own = rows // 2, rows // 4
    kept_at, sent_at = rows_at(core * mid, mid), rows_at((1 - core) * mid, mid)
    mine, other = rows_at(side * own, own), rows_at((1 - side) * own, own)
    own_at = rows_at(core * mid + side * own, own)
    tn = (((0,), (0,)), ((), ()))

    greet(along + beside)

    def mlp_term(right):
        return lambda k: lax.dot_general(
            normed_ref[:, k * slab : (k + 1) * slab], right[...], tn, preferred_element_type=f32
        )

    def down_term(first):
        return lambda k: lax.dot_general(
            hidden_ref[:, first : first + inner_half],
            cot_ref[:, k * slab : (k + 1) * slab],
            tn,
            preferred_element_type=f32,
        )

    mlp = RingSum(
        [mlp_term(gate_low_ref), mlp_term(up_low_ref)],
        mlp_slots,
        ring_sends.at[0],
        ring_arrivals.at[0],
        ring_credits.at[0],
        count,
        neighbours,
    )
    down = RingSum(
        [down_term(0), down_term(inner_half)],
        down_slots,
        ring_sends.at[1],
        ring_arrivals.at[1],
        ring_credits.at[1],
        count,
        neighbours,
    )
    mlp.serve(1)
    down.serve(1)

    def streamed(sources, buffers, first_sem, columns=False):
        def fetch(k):
            fetched = []
            for number, (source, buffer) in enumerate(zip(sources, buffers)):
                here = pl.ds(k * slab, slab)
                copy = pltpu.make_async_copy(
                    source.at[:, here] if columns else source.at[here],
                    buffer.at[k % 2],
                    stream_sems.at[first_sem + number * count + k],
                )
                copy.start()
                fetched.append(copy)
            return fetched

        fetched = fetch(0)
        for k in range(count):
            for copy in fetched:
                copy.wait()
            if k + 1 < count:
                fetched = fetch(k + 1)
            yield k, [buffer[k % 2] for buffer in buffers]

    nt = dot_nt_here

    for k, (gate, up) in streamed((gate_all, up_all), (stream_one, stream_two), 0):
        part = slice(k * slab, (k + 1) * slab)
        half_sent[:, part] = (
            nt(gate_low_ref[sent_at, :], gate) + nt(up_low_ref[sent_at, :], up)
        ).astype(bf16)
        half_kept[:, part] = nt(gate_low_ref[kept_at, :], gate) + nt(up_low_ref[kept_at, :], up)
    half_copy = copies.start(half_sent, half_got, beside[0])
    half_copy.wait_recv()
    own_sent[...] = (half_kept[other, :] + half_got[other, :].astype(f32)).astype(bf16)
    own_copy = copies.start(own_sent, own_got, beside[1])
    mlp.serve(2)
    down.serve(2)
    own_copy.wait_recv()
    middle = own_middle[...]
    scale = lax.rsqrt(jnp.mean(middle * middle, axis=-1, keepdims=True) + eps)
    unit_values = middle * scale
    front = half_kept[mine, :] + half_got[mine, :].astype(f32) + own_got[...].astype(f32)
    gain_grad_out[...] = jnp.zeros_like(gain_grad_out)
    gain_grad_out[0:1, :] = jnp.sum(front * unit_values, 0, keepdims=True)
    weighted = front * gains_ref[1:2, :]
    result = cot_ref[own_at, :].astype(f32) + scale * (
        weighted - unit_values * jnp.mean(weighted * unit_values, axis=-1, keepdims=True)
    )
    own_grad[...] = result
    middle_low[own_at, :] = result.astype(bf16)
    join_copy = copies.start(middle_low.at[own_at], middle_low.at[own_at], beside[1])
    mlp.serve(3)
    join_copy.wait_recv()
    join_copy = copies.start(middle_low.at[kept_at], middle_low.at[kept_at], beside[0])
    down.serve(3)
    join_copy.wait_recv()

    for k, (out,) in streamed((out_all,), (stream_out,), 2 * count, True):
        for batch in range(batches):
            at = slice(batch * length, (batch + 1) * length)
            more = nt(middle_low[at, k * slab : (k + 1) * slab], out)
            adjoints[at, :] = more if k == 0 else adjoints[at, :] + more

    moves.wait(9)

    def mixed_block(block, carry):
        batch = block // (length // row_block)
        at = rows_at(block * row_block, row_block)
        back, before = adjoints[at, :], branch_pre[at, :]
        state = states[rows_at(block * row_block + batch * 8 + 8, row_block, 8), :]
        branch_low[at, :] = (back * state * gelu_slope(before)).astype(bf16)
        adjoints[at, :] = back * gelu_tanh(before)
        return carry

    lax.fori_loop(0, rows // row_block, mixed_block, 0)
    moves.start(branch_low, branch_low_out)
    scanned = scan_rows(carries, adjoints, prods, adjoints, batches, True)
    ends_sent[...] = ends_ref[...]
    for batch, (_, state) in enumerate(scanned):
        top = batch * length
        ends_sent[batches + batch : batches + batch + 1, :] = carries[top : top + 1, :] * state
    end_copies = [
        copies.start(ends_sent, ends_got.at[distance - 1], along[count - distance - 1])
        for distance in range(1, count)
    ]
    mlp.serve(4)
    for copy in end_copies:
        copy.wait_recv()
    entries = entry_states(ends_sent, ends_got, index, count, batches, -1)

    rate, slope = [packed_ref[i : i + 1, :units] for i in (7, 8)]
    zero = jnp.zeros((1, units), f32)
    sums = (zero, zero, zero)
    for batch in range(batches):
        entry = entries[batch]

        def gate_block(block, sums, batch=batch, entry=entry):
            top = batch * length + block * row_block
            at = rows_at(top, row_block)
            rate_gate = jax.nn.sigmoid(gate_pre[at, :])
            inlet_gate = jax.nn.sigmoid(input_pre[at, :])
            log_decay = rate * rate_gate
            decay = jnp.exp(log_decay)
            fresh = fresh_ref[at, :] > 0
            scale = jnp.sqrt(-jnp.tanh(log_decay) * (1.0 + decay * decay))
            conv = conv_low[at, :].astype(f32)
            lam = adjoints[at, :] + prods[at, :] * entry
            before = states[rows_at(top + batch * 8, row_block + 8, 8), :][7:-1]
            drawn = inlet_gate * conv
            log_grad = jnp.where(
                fresh, 0.0, lam * before * decay - lam * (decay * decay / scale) * drawn
            )
            passed = lam * jnp.where(fresh, 1.0, scale)
            gate_grad_low = (log_grad * rate * (rate_gate * (1.0 - rate_gate))).astype(bf16)
            input_grad_low = (passed * conv * (inlet_gate * (1.0 - inlet_gate))).astype(bf16)
            gate_low[at, :] = gate_grad_low
            input_low[at, :] = input_grad_low
            conv_grad[rows_at(top + batch * 8, row_block, 8), :] = passed * inlet_gate
            terms = (
                gate_grad_low.astype(f32),
                input_grad_low.astype(f32),
                log_grad * rate_gate,
            )
            return tuple(
                total + jnp.sum(more, 0, keepdims=True) for total, more in zip(sums, terms)
            )

        sums = lax.fori_loop(0, length // row_block, gate_block, sums)
        if batch == 0:
            down.serve(4)
    moves.start(gate_low, gate_low_out)
    moves.start(input_low, input_low_out)
    for batch in range(batches):
        at, top = slice(batch * length, (batch + 1) * length), batch * (length + 8)
        conv_grad[top : top + length, :] = (
            conv_grad[top : top + length, :]
            + nt(gate_low[at, :], gate_square_ref[...])
            + nt(input_low[at, :], input_square_ref[...])
        )
        edges_sent[batch] = conv_grad[top : top + 8, :]
    edge_copy = copies.start(edges_sent, edges_got, along[count - 2])
    mlp.serve(5)
    size = blocks.shape[1]
    for number, right in enumerate((gate_low, input_low)):
        square = lax.dot_general(conv_low[...], right[...], tn, preferred_element_type=f32)
        for j in range(units // size):
            at = slice(j * size, (j + 1) * size)
            first = number * units + j * size
            blocks[first : first + size, :] = square[at, at].astype(bf16)
    across = [{"seq": partner(index, bit)} for bit in (1, 2, 4)]
    bits = [lax.rem(index // bit, 2) for bit in (1, 2, 4)]
    firsts = [units, units // 2, units // 4]

    def halves(source, stage):
        kept = source[rows_at(bits[stage] * firsts[stage], firsts[stage]), :]
        sent = source.at[rows_at((1 - bits[stage]) * firsts[stage], firsts[stage])]
        got = (blocks_got_one, blocks_got_two, blocks_got_three)[stage]
        return kept, copies.start(sent, got, across[stage]), got

    def halved(kept, copy, got):
        copy.wait_recv()
        return (kept.astype(f32) + got[...].astype(f32)).astype(bf16)

    halving = halves(blocks, 0)

    copies.sent(half_copy)
    copies.sent(own_copy)
    for k, (right,) in streamed((down_all,), (stream_down,), 3 * count, True):
        part = slice(k * slab, (k + 1) * slab)
        half_sent[:, part] = jnp.dot(
            hidden_ref[sent_at, :], right, preferred_element_type=f32
        ).astype(bf16)
        half_kept[:, part] = jnp.dot(
            hidden_ref[kept_at, :], right, preferred_element_type=f32
        )
    mixed_copy = copies.start(half_sent, half_got, beside[0])
    down.serve(5)

    edge_copy.wait_recv()
    for batch in range(batches):
        top = batch * (length + 8) + length
        conv_grad[top : top + 8, :] = jnp.where(index < count - 1, edges_got[batch], 0.0)

    def conv_block(block, sums):
        batch = block // (length // row_block)
        at = rows_at(block * row_block + batch * 8, row_block + 8, 8)
        wide, inner = conv_grad[at, :], padded[at, :]
        total = packed_ref[0:1, :units] * wide[:-8] + packed_ref[1:2, :units] * wide[1:-7]
        total = total + packed_ref[2:3, :units] * wide[2:-6] + packed_ref[3:4, :units] * wide[3:-5]
        inner_low[rows_at(block * row_block, row_block), :] = total.astype(bf16)
        near = wide[:-8]
        terms = [near * inner[8 - k : 8 - k + row_block] for k in range(4)] + [near]
        return tuple(
            total + jnp.sum(more, 0, keepdims=True) for total, more in zip(sums, terms)
        )

    conv_sums = lax.fori_loop(0, rows // row_block, conv_block, (zero,) * 5)
    moves.start(inner_low, inner_low_out)
    for number, total in enumerate((*conv_sums, sums[0], sums[1], sums[2] * slope)):
        small_out[number : number + 1, :] = total

    mixed_copy.wait_recv()
    own_sent[...] = (half_kept[other, :] + half_got[other, :].astype(f32)).astype(bf16)
    own_copy = copies.start(own_sent, own_got, beside[1])
    mlp.serve(6)
    down.serve(6)
    blocks_one[...] = halved(*halving)
    halving = halves(blocks_one, 1)
    own_copy.wait_recv()
    final = own_middle[...] + (
        half_kept[mine, :] + half_got[mine, :].astype(f32) + own_got[...].astype(f32)
    )
    final = final.astype(bf16)
    for k in range(count):
        to = pl.ds(pl.multiple_of(ring_index(place - k, count) * slab, slab), slab)
        mixed_out[own_at, to] = final[:, k * slab : (k + 1) * slab]
    join_copy = copies.start(mixed_out.at[own_at], mixed_out.at[own_at], beside[1])
    mlp.serve(7)
    blocks_two[...] = halved(*halving)
    halving = halves(blocks_two, 2)
    join_copy.wait_recv()
    join_copy = copies.start(mixed_out.at[kept_at], mixed_out.at[kept_at], beside[0])
    down.serve(7)
    join_copy.wait_recv()

    def mlp_end(way, total):
        stage[...] = total
        copy = pltpu.make_async_copy(stage, up_grad if way else gate_grad, stage_sems.at[way])
        copy.start()
        copy.wait()

    def down_end(way, total):
        down_grad[way * inner_half : (way + 1) * inner_half, :] = total

    mlp.serve(8, mlp_end)
    blocks_out[...] = halved(*halving)
    down.serve(8, down_end)
    moves.wait(4)
    copies.end()


def back(count, fsdp, batches, block_width, *operands):
    cot, hidden = operands[0], operands[1]
    late = operands[-9:]
    rows, width = cot.shape
    units, inner = late[0].shape[1], hidden.shape[1]
    slab = width // count
    whole, place = pl.BlockSpec(memory_space=pltpu.VMEM), pl.BlockSpec(memory_space=pl.ANY)

    def array(dtype, *shape):
        return jax.ShapeDtypeStruct(shape, dtype)

    outs = [
        array(bf16, rows, width),
        array(bf16, rows, width),
        array(f32, rows // 4, width),
        array(f32, 8, units),
        array(bf16, units // 4, block_width),
        array(f32, 8, width),
        array(f32, inner, slab),
        *[array(bf16, rows, units)] * 4,
        *[array(f32, slab, inner)] * 2,
    ]
    return pl.pallas_call(
        functools.partial(back_body, count, fsdp, batches),
        out_shape=tuple(outs),
        in_specs=[whole] * (len(operands) - 13) + [place] * 13,
        out_specs=tuple([whole] * 7 + [place] * 6),
        scratch_shapes=[
            pltpu.VMEM((rows // 2, width), bf16),
            pltpu.VMEM((rows // 2, width), f32),
            pltpu.VMEM((rows // 2, width), bf16),
            pltpu.VMEM((rows // 4, width), bf16),
            pltpu.VMEM((rows // 4, width), bf16),
            pltpu.VMEM((rows, units), f32),
            pltpu.VMEM((rows, units), f32),
            pltpu.VMEM((rows + 8 * batches, units), f32),
            pltpu.VMEM((batches, 8, units), f32),
            pltpu.VMEM((batches, 8, units), f32),
            pltpu.VMEM((8, units), f32),
            pltpu.VMEM((count - 1, 8, units), f32),
            pltpu.VMEM((2, ring_slots, slab, inner), bf16),
            pltpu.VMEM((2, ring_slots, inner // 2, slab), bf16),
            pltpu.VMEM((2, slab, inner), bf16),
            pltpu.VMEM((2, slab, inner), bf16),
            pltpu.VMEM((2, units, slab), bf16),
            pltpu.VMEM((2, inner, slab), bf16),
            pltpu.VMEM((slab, inner), f32),
            *[pltpu.VMEM(part.shape, part.dtype) for part in late],
            *[pltpu.VMEM((rows, units), bf16)] * 4,
            *[
                pltpu.VMEM((2 * units // part, block_width), bf16)
                for part in (1, 2, 4, 2, 4, 8)
            ],
            pltpu.SemaphoreType.DMA((13,)),
            pltpu.SemaphoreType.DMA((4 * count,)),
            pltpu.SemaphoreType.DMA((2,)),
            pltpu.SemaphoreType.DMA((2, 2, count - 1)),
            pltpu.SemaphoreType.DMA((2, 2, count - 1)),
            pltpu.SemaphoreType.REGULAR((2, 2)),
            pltpu.SemaphoreType.DMA((back_copies,)),
            pltpu.SemaphoreType.DMA((back_copies,)),
        ],
        compiler_params=pltpu.CompilerParams(
            collective_id=2, has_side_effects=True, vmem_limit_bytes=63 * 1024 * 1024
        ),
    )(*operands)


def mlp_body(normed_ref, cot_ref, gate_ref, up_ref, down_ref, hidden_out, gate_out, up_out):
    gate = jnp.dot(normed_ref[...], gate_ref[...], preferred_element_type=f32)
    up = jnp.dot(normed_ref[...], up_ref[...], preferred_element_type=f32)
    back = dot_nt_here(cot_ref[...], down_ref[...])
    constant = 0.7978845608028654
    square = gate * gate
    bent = jnp.tanh(constant * (gate + 0.044715 * square * gate))
    half = 0.5 * (1.0 + bent)
    active = half * gate
    slope = half + 0.5 * gate * (1.0 - bent * bent) * (
        constant * (1.0 + 3.0 * 0.044715 * square)
    )
    hidden_out[...] = (active * up).astype(bf16)
    gate_out[...] = (back * up * slope).astype(bf16)
    up_out[...] = (back * active).astype(bf16)


def feed_forward(normed, cot, gate_all, up_all, down_all):
    rows, width = normed.shape
    hidden = gate_all.shape[1]
    wide = 256
    resident = pl.BlockSpec((rows, width), lambda j: (0, 0))
    columns = pl.BlockSpec((width, wide), lambda j: (0, j))
    result = pl.BlockSpec((rows, wide), lambda j: (0, j))
    return pl.pallas_call(
        mlp_body,
        grid=(hidden // wide,),
        out_shape=(jax.ShapeDtypeStruct((rows, hidden), bf16),) * 3,
        in_specs=[
            resident,
            resident,
            columns,
            columns,
            pl.BlockSpec((wide, width), lambda j: (j, 0)),
        ],
        out_specs=(result,) * 3,
        compiler_params=pltpu.CompilerParams(vmem_limit_bytes=62 * 1024 * 1024),
    )(normed, cot, gate_all, up_all, down_all)


def finish_body(large, *refs):
    small, gains = refs[large : large + 2]
    outs = refs[large + 2 :]
    for source, target in zip(refs[:large], outs):
        target[...] = source[...].astype(f32)
    taps, *vectors = outs[large:]
    taps[...] = small[0:4, :]
    for row, vector in enumerate(vectors[:4]):
        vector[...] = small[row + 4 : row + 5, :].reshape(vector.shape[0])
    for row, vector in enumerate(vectors[4:]):
        vector[...] = gains[row : row + 1, :].reshape(vector.shape[0])


def finish(blocks, small, gains, *arrays):
    parts = 4
    half, block_width = blocks.shape[0] // 2, blocks.shape[1]

    def rows_of(count, wide, first=0):
        return pl.BlockSpec((count // parts, wide), lambda j: (j + first, 0))

    def whole(*shape):
        return pl.BlockSpec(shape, lambda j: (0,) * len(shape))

    specs = [rows_of(*part.shape) for part in arrays]
    blocks_out = rows_of(half, block_width)
    vectors = [small.shape[1]] * 4 + [gains.shape[1]] * 2
    shapes = [part.shape for part in arrays] + [(half, block_width)] * 2
    shapes += [(4, small.shape[1])] + [(size,) for size in vectors]
    return pl.pallas_call(
        functools.partial(finish_body, len(arrays) + 2),
        grid=(parts,),
        out_shape=tuple(jax.ShapeDtypeStruct(shape, f32) for shape in shapes),
        in_specs=[
            *specs,
            blocks_out,
            rows_of(half, block_width, parts),
            whole(*small.shape),
            whole(*gains.shape),
        ],
        out_specs=(
            *specs,
            blocks_out,
            blocks_out,
            whole(4, small.shape[1]),
            *[whole(size) for size in vectors],
        ),
        compiler_params=pltpu.CompilerParams(vmem_limit_bytes=62 * 1024 * 1024),
    )(*arrays, blocks, blocks, small, gains)


def block_diagonal(blocks):
    count, width = blocks.shape[0], blocks.shape[1]
    return sum(
        jnp.pad(blocks[j], ((j * width, (count - 1 - j) * width),) * 2) for j in range(count)
    )


def rows_joined(slab_pairs):
    return jnp.concatenate([part for pair in zip(*slab_pairs) for part in pair], 0)


def diagonal_blocks(square, count):
    width = square.shape[0] // count
    return jnp.stack(
        [square[j * width : (j + 1) * width, j * width : (j + 1) * width] for j in range(count)], 0
    )


def local(
    tokens,
    resets,
    norm_gain,
    branch_weight,
    inner_weight,
    conv_weight,
    conv_bias,
    gate_blocks,
    input_blocks,
    gate_bias,
    input_bias,
    decay_param,
    out_weight,
    mlp_norm_gain,
    gate_weight,
    up_weight,
    down_weight,
    cotangent,
):
    count = lax.axis_size("seq")
    batches, length, width = tokens.shape
    slab = width // count
    units, hidden = conv_bias.shape[0], down_weight.shape[0]
    rows = batches * length
    ringed = count == ring_count and lax.axis_size("fsdp") == 4
    half = slab // 2
    out_turned, down_turned = out_weight.T, down_weight.T
    ring = Ring(count)
    if ringed:
        gather, scatter = functools.partial(Gather, ring), functools.partial(Scatter, ring)
        to_ring, to_plain = ring.tables()

        def moved(values, dtype):
            return move_slabs(values, to_ring, dtype)

        def restored(values, dtype):
            return move_slabs(values, to_plain, dtype)

        def gain_moved(gain):
            return gain.reshape(count, slab)[to_ring].reshape(width)

        def gain_restored(gain):
            return gain.reshape(count, slab)[to_plain].reshape(width)

    else:
        gather, scatter = functools.partial(PlainGather, ring), functools.partial(PlainScatter, ring)

        def moved(values, dtype):
            return values.astype(dtype)

        restored = moved

        def gain_moved(gain):
            return gain

        gain_restored = gain_moved

    def slab_dots(turned, right, first=0, rows=slab):
        def term(k):
            start = k * slab + first
            return dot_nn(turned[start : start + rows], right)

        return term

    steps = count - 1
    taps = conv_weight.astype(f32)
    decay = decay_param.astype(f32)
    fresh_start = resets[:, :, None] > 0
    gain_one = gain_moved(norm_gain.astype(f32))
    gain_two = gain_moved(mlp_norm_gain.astype(f32))

    def gates(gate_pre, input_pre, conv_value, decay):
        return gate_math(gate_pre, input_pre, conv_value, decay, fresh_start)

    def by_sequence(values):
        return values.reshape(batches, -1, values.shape[-1])

    if ringed:
        (
            gate_all,
            up_all,
            down_all,
            branch_all,
            inner_all,
            out_all,
            cot_low,
            normed,
            branch_pre,
            padded,
            conv_flat,
            gate_pre,
            input_pre,
            carries,
            states,
            mixed_low,
            gate_square,
            input_square,
            ends,
            own_values,
            own_middle,
            normed_two,
            ring_gains,
            packed,
            fresh,
        ) = head(
            count,
            lax.axis_size("fsdp"),
            batches,
            tokens.reshape(rows, width),
            cotangent.reshape(rows, width),
            branch_weight.T,
            inner_weight.T,
            out_weight,
            gate_weight,
            up_weight,
            down_weight,
            conv_weight,
            conv_bias,
            gate_bias,
            input_bias,
            -decay_scale * jax.nn.softplus(-decay),
            decay_scale * jax.nn.sigmoid(-decay),
            norm_gain,
            mlp_norm_gain,
            resets,
            gate_blocks,
            input_blocks,
        )
        hidden_low, gate_mlp_low, up_mlp_low = feed_forward(
            normed_two, cot_low, gate_all, up_all, down_all
        )
        (
            mixed,
            middle_low,
            own_grad,
            small,
            block_grads,
            gain_two_grad,
            down_grad,
            branch_low,
            inner_grad_low,
            gate_low,
            input_low,
            gate_grad,
            up_grad,
        ) = back(
            count,
            lax.axis_size("fsdp"),
            batches,
            gate_blocks.shape[-1],
            cot_low,
            hidden_low,
            normed_two,
            gate_mlp_low,
            up_mlp_low,
            ends,
            own_middle,
            fresh,
            packed,
            ring_gains,
            gate_all,
            up_all,
            down_all,
            out_all,
            branch_pre,
            padded,
            conv_flat,
            gate_pre,
            input_pre,
            carries,
            states,
            gate_square,
            input_square,
        )
        block_count, block_width = gate_blocks.shape[:2]
        branch_grad, inner_grad, out_grad, tokens_grad, gains, small, block_grads = tail(
            count,
            middle_low,
            mixed_low,
            normed,
            branch_low,
            inner_grad_low,
            branch_all,
            inner_all,
            own_values,
            own_grad,
            ring_gains,
            gain_two_grad,
            small,
            block_grads,
        )
        (
            mixed,
            tokens_grad,
            gate_grad,
            up_grad,
            down_grad,
            branch_grad,
            inner_grad,
            out_grad,
            gate_blocks_grad,
            input_blocks_grad,
            taps_grad,
            conv_bias_grad,
            gate_bias_grad,
            input_bias_grad,
            decay_grad,
            gain_one_grad,
            gain_two_grad,
        ) = finish(
            block_grads,
            small,
            gains,
            mixed,
            tokens_grad,
            gate_grad,
            up_grad,
            down_grad,
            branch_grad,
            inner_grad,
            out_grad,
        )
        return (
            mixed.reshape(tokens.shape),
            tokens_grad.reshape(tokens.shape),
            gain_one_grad,
            branch_grad.T,
            inner_grad.T,
            taps_grad,
            conv_bias_grad,
            gate_blocks_grad.reshape(block_count, block_width, block_width),
            input_blocks_grad.reshape(block_count, block_width, block_width),
            gate_bias_grad,
            input_bias_grad,
            decay_grad,
            out_grad,
            gain_two_grad,
            gate_grad,
            up_grad,
            down_grad,
        )
    else:
        branch_all, inner_all, out_all, gate_all, up_all, down_all = [
            lax.all_gather(piece, "seq", axis=0, tiled=True)
            for piece in (
                branch_weight,
                inner_weight,
                out_turned,
                gate_weight,
                up_weight,
                down_turned,
            )
        ]
        gate_square, input_square = block_diagonal(gate_blocks), block_diagonal(input_blocks)
        tokens_low, cot_low = tokens.reshape(rows, width), cotangent.reshape(rows, width)
        values = tokens_low.astype(f32)
        normed = (values * inverse_rms(values) * gain_one).astype(bf16)
        inner_low = by_sequence(dot_nn(normed, inner_all).astype(bf16))
        branch_pre = by_sequence(dot_nn(normed, branch_all))
        edge_rows = passed_along(inner_low[:, -3:], 1)
        padded = jnp.concatenate([edge_rows, inner_low], 1).astype(f32)
        conv_sum = conv_bias.astype(f32) + taps[0] * padded[:, 3:] + taps[1] * padded[:, 2:-1]
        conv_sum = conv_sum + taps[2] * padded[:, 1:-2] + taps[3] * padded[:, :-3]
        conv_flat = conv_sum.astype(bf16).reshape(rows, units)
        gate_pre = by_sequence(dot_nn(conv_flat, gate_square) + gate_bias.astype(f32))
        input_pre = by_sequence(dot_nn(conv_flat, input_square) + input_bias.astype(f32))
        conv_value = by_sequence(conv_flat).astype(f32)
        carries, drives = gates(gate_pre, input_pre, conv_value, decay)
        prods, local_state = local_scan(carries, drives, False)
        prods_end = prods[:, -1:]
        state_in = Entry(prods_end, local_state[:, -1:], 1).state(None)
        states = local_state + prods * state_in
        mixed_low = (states * gelu_tanh(branch_pre)).astype(bf16).reshape(rows, units)
        own_values = own_rows(tokens_low).astype(f32)
        own_middle = own_values + Halves(ring, dot_nt(mixed_low, out_all), "fsdp").run()
        normed_two = own_middle * inverse_rms(own_middle) * gain_two
        normed_two = Joined(ring, normed_two.astype(bf16), "fsdp").run()
    branch, branch_pull = jax.vjp(gelu_tanh, branch_pre)
    scale_two = inverse_rms(own_middle)
    unit_two = own_middle * scale_two

    gate_mlp = dot_nn(normed_two, gate_all)
    up_mlp = dot_nn(normed_two, up_all)
    activated, act_pull = jax.vjp(gated_product, gate_mlp, up_mlp)
    hidden_low = activated.astype(bf16)
    down_grads = scatter(
        slab_dots(cot_low.T, hidden_low, 0, half), slab_dots(cot_low.T, hidden_low, half, half)
    )
    in_turn(down_grads)
    grad_gate_mlp, grad_up_mlp = act_pull(dot_nn(ring.then(cot_low, 0), down_all))
    gate_mlp_low, up_mlp_low = grad_gate_mlp.astype(bf16), grad_up_mlp.astype(bf16)
    in_turn(down_grads)
    ring.first(gate_mlp_low, up_mlp_low)
    in_turn(down_grads)
    mlp_grads = scatter(
        slab_dots(normed_two.T, gate_mlp_low), slab_dots(normed_two.T, up_mlp_low)
    )
    in_turn(mlp_grads, down_grads)
    gate_mlp_low, up_mlp_low = lax.optimization_barrier(
        (ring.then(gate_mlp_low, 2), up_mlp_low)
    )
    back_sum = Halves(
        ring, dot_nt(gate_mlp_low, gate_all) + dot_nt(up_mlp_low, up_all), "fsdp"
    )
    back_sum.step()
    ring.first(back_sum.step())
    in_turn(mlp_grads, down_grads)
    own_back = back_sum.run(2)
    gain_two_grad = jnp.sum(own_back * unit_two, 0)
    weighted = own_back * gain_two
    own_grad = own_rows(cot_low).astype(f32) + scale_two * (
        weighted - unit_two * jnp.mean(weighted * unit_two, axis=-1, keepdims=True)
    )
    middle_join = Joined(ring, own_grad.astype(bf16), "fsdp")
    ring.first(middle_join.step())
    in_turn(mlp_grads)
    mixed_sum = Halves(ring, dot_nt(ring.then(hidden_low, 2), down_all), "fsdp")
    mixed_sum.step()
    ring.first(mixed_sum.step())
    in_turn(down_grads)
    middle_join.step(2)
    middle_low = middle_join.run()

    grad_mixed = dot_nn(middle_low, out_all).reshape(batches, length, units)
    (grad_branch_pre,) = branch_pull(grad_mixed * states)
    branch_low = grad_branch_pre.astype(bf16).reshape(rows, units)
    following = jnp.concatenate([carries[:, 1:], jnp.ones_like(carries[:, :1])], 1)
    tail_prods, local_adjoint = local_scan(following, grad_mixed * branch, True)
    entry = Entry(prods_end, carries[:, :1] * local_adjoint[:, :1], -1)
    ring.first(local_adjoint, branch_low)
    in_turn(mlp_grads)
    entry.between(ring.then)
    in_turn(down_grads)
    adjoint_in = entry.state(lambda part: ring.then(part, 1))
    adjoint = local_adjoint + tail_prods * adjoint_in
    state_before = jnp.concatenate([state_in, states[:, :-1]], 1)
    _, gate_pull = jax.vjp(gates, gate_pre, input_pre, conv_value, decay)
    grad_gate_pre, grad_input_pre, grad_conv, decay_grad = gate_pull(
        (adjoint * state_before, adjoint)
    )
    gate_low = grad_gate_pre.astype(bf16).reshape(rows, units)
    input_low = grad_input_pre.astype(bf16).reshape(rows, units)
    ring.first(gate_low, input_low)
    in_turn(mlp_grads)
    back_conv = dot_nt(gate_low, gate_square) + dot_nt(input_low, input_square)
    grad_conv = grad_conv + back_conv.reshape(batches, length, units)

    border = jnp.zeros((batches, 3, units), f32)
    spread = jnp.concatenate([border, grad_conv, border], 1)
    stop = length + 3
    grad_padded = taps[0] * spread[:, :stop] + taps[1] * spread[:, 1 : stop + 1]
    grad_padded = grad_padded + taps[2] * spread[:, 2 : stop + 2] + taps[3] * spread[:, 3:]
    returned = passed_along(grad_padded[:, :3], -1)
    mixed_join = Joined(ring, restored(own_middle + mixed_sum.run(1), bf16), "fsdp")
    ring.first(grad_padded, mixed_join.step())
    in_turn(mlp_grads)
    grad_inner = jnp.concatenate(
        [grad_padded[:, 3:-3], grad_padded[:, -3:] + ring.then(returned)], 1
    )
    inner_grad_low = grad_inner.astype(bf16).reshape(rows, units)
    in_turn(*[mlp_grads] * (steps - 6))

    block_count = gate_blocks.shape[0]
    block_grads = jnp.concatenate(
        [
            diagonal_blocks(dot_tn(conv_flat, gate_low), block_count),
            diagonal_blocks(dot_tn(conv_flat, input_low), block_count),
        ],
        0,
    )
    block_width = block_grads.shape[-1]
    taps_grad = jnp.stack(
        [jnp.sum(grad_conv * padded[:, 3 - k : 3 - k + length], (0, 1)) for k in range(4)], 0
    )
    small = jnp.concatenate(
        [
            taps_grad,
            jnp.sum(grad_conv, (0, 1))[None],
            jnp.sum(gate_low.astype(f32), 0)[None],
            jnp.sum(input_low.astype(f32), 0)[None],
            decay_grad[None],
        ],
        0,
    )
    mixed_join.step()
    mixed = mixed_join.run().astype(f32).reshape(tokens.shape)
    gate_grad, up_grad = mlp_grads.sums()
    if ringed:
        branch_grad, inner_grad, out_grad, tokens_grad, gains, small, block_grads = tail(
            count,
            middle_low.T,
            mixed_low,
            normed.T,
            branch_low,
            inner_grad_low,
            branch_all,
            inner_all,
            own_values,
            own_grad,
            gain_one[None],
            gain_two_grad[None],
            small,
            block_grads.reshape(-1, block_width).astype(bf16),
        )
        block_grads = block_grads.astype(f32)
    else:
        out_grads = scatter(
            slab_dots(middle_low.T, mixed_low, 0, half),
            slab_dots(middle_low.T, mixed_low, half, half),
        )
        front_grads = scatter(
            slab_dots(normed.T, branch_low), slab_dots(normed.T, inner_grad_low)
        )
        branch_grad, inner_grad = front_grads.sums()
        out_grad = jnp.concatenate(out_grads.sums(), 0)
        own_front = Halves(
            ring, dot_nt(branch_low, branch_all) + dot_nt(inner_grad_low, inner_all), "fsdp"
        ).run()
        scale_one = inverse_rms(own_values)
        unit_one = own_values * scale_one
        weighted = own_front * gain_one
        own_tokens = own_grad + scale_one * (
            weighted - unit_one * jnp.mean(weighted * unit_one, axis=-1, keepdims=True)
        )
        gains = jnp.stack([jnp.sum(own_front * unit_one, 0), gain_two_grad], 0)
        gains = lax.psum(gains, ("seq", "fsdp"))
        small, block_grads = lax.psum((small, block_grads), "seq")
        tokens_grad = Joined(ring, own_tokens.astype(bf16), "fsdp").run()
    tokens_grad = tokens_grad.astype(f32).reshape(tokens.shape)
    block_grads = block_grads.reshape(2, block_count, block_width, block_width)
    down_grad = jnp.concatenate(down_grads.sums(), 0)
    return (
        mixed,
        tokens_grad,
        gains[0],
        branch_grad,
        inner_grad,
        small[:4],
        small[4],
        block_grads[0],
        block_grads[1],
        small[5],
        small[6],
        small[7],
        out_grad.T,
        gains[1],
        gate_grad,
        up_grad,
        down_grad.T,
    )


def solution(mesh):
    units, both = P("fsdp"), P("seq", "fsdp")
    blocks, turned = P("fsdp", None, None), P("fsdp", "seq")
    rows = P(None, "seq", None)
    return jax.shard_map(
        local,
        mesh=mesh,
        in_specs=(
            rows,
            P(None, "seq"),
            P(),
            both,
            both,
            P(None, "fsdp"),
            units,
            blocks,
            blocks,
            units,
            units,
            units,
            turned,
            P(),
            both,
            both,
            turned,
            rows,
        ),
        out_specs=(
            rows,
            rows,
            P(),
            both,
            both,
            P(None, "fsdp"),
            units,
            blocks,
            blocks,
            units,
            units,
            units,
            turned,
            P(),
            both,
            both,
            turned,
        ),
        check_vma=False,
    )
```

```python
import functools

import jax
import jax.numpy as jnp
from jax import lax
from jax.experimental import pallas as pl
from jax.experimental.pallas import tpu as pltpu
from jax.sharding import PartitionSpec as P

eps = 1e-06
decay_scale = 8.0
f32 = jnp.float32
bf16 = jnp.bfloat16
ring_count = 8


def gelu_tanh(values):
    return jax.nn.gelu(values, approximate=True)


def gated_product(gate_pre, up_pre):
    return gelu_tanh(gate_pre) * up_pre


def gate_math(gate_pre, input_pre, conv_value, decay_param, fresh_start):
    rate_gate = jax.nn.sigmoid(gate_pre)
    inlet_gate = jax.nn.sigmoid(input_pre)
    log_decay = -decay_scale * jax.nn.softplus(-decay_param) * rate_gate
    input_scale = jnp.where(fresh_start, 1.0, jnp.sqrt(-jnp.expm1(2.0 * log_decay)))
    carries = jnp.where(fresh_start, 0.0, jnp.exp(log_decay))
    return (carries, input_scale * inlet_gate * conv_value)


def dot_nn(left, right):
    return jnp.dot(left, right, preferred_element_type=f32)


def dot_nt(left, right):
    return lax.dot_general(left, right, (((1,), (1,)), ((), ())), preferred_element_type=f32)


def dot_tn(left, right):
    return lax.dot_general(left, right, (((0,), (0,)), ((), ())), preferred_element_type=f32)


def inverse_rms(values):
    return lax.rsqrt(jnp.mean(values * values, axis=-1, keepdims=True) + eps)


def scan_body(backward, a_ref, b_ref, prod_ref, state_ref):
    batches, length, units = a_ref.shape
    tiles = length // 8
    rows = lax.broadcasted_iota(jnp.int32, (8, units), 0)

    def step(index, carry):
        tile = tiles - 1 - index if backward else index
        where_rows = pl.ds(pl.multiple_of(tile * 8, 8), 8)
        following = []
        for batch in range(batches):
            prod_in, state_in = carry[batch]
            a = a_ref[batch, where_rows, :]
            b = b_ref[batch, where_rows, :]
            for shift in (1, 2, 4):
                turn = 8 - shift if backward else shift
                inside = rows < 8 - shift if backward else rows >= shift
                a_moved = jnp.where(inside, pltpu.roll(a, turn, 0), 1.0)
                b_moved = jnp.where(inside, pltpu.roll(b, turn, 0), 0.0)
                b = a * b_moved + b
                a = a * a_moved
            b = b + a * state_in
            a = a * prod_in
            prod_ref[batch, where_rows, :] = a
            state_ref[batch, where_rows, :] = b
            edge = 0 if backward else 7
            following.append((a[edge : edge + 1], b[edge : edge + 1]))
        return tuple(following)

    first = tuple(
        (jnp.ones((1, units), f32), jnp.zeros((1, units), f32)) for _ in range(batches)
    )
    lax.fori_loop(0, tiles, step, first)


def local_scan(a, b, backward):
    shape = jax.ShapeDtypeStruct(a.shape, f32)
    elements = a.shape[0] * a.shape[1] * a.shape[2]
    return pl.pallas_call(
        functools.partial(scan_body, backward),
        out_shape=(shape, shape),
        in_specs=[pl.BlockSpec(memory_space=pltpu.VMEM)] * 2,
        out_specs=(pl.BlockSpec(memory_space=pltpu.VMEM),) * 2,
        compiler_params=pltpu.CompilerParams(vmem_limit_bytes=32 * 1024 * 1024),
        cost_estimate=pl.CostEstimate(
            flops=20 * elements, bytes_accessed=16 * elements, transcendentals=0
        ),
    )(a, b)


def move_body(table_ref, in_ref, out_ref):
    out_ref[...] = in_ref[...].astype(out_ref.dtype)


def move_slabs(values, table, dtype):
    rows, width = values.shape
    slabs = table.shape[0]
    return pl.pallas_call(
        move_body,
        out_shape=jax.ShapeDtypeStruct((rows, width), dtype),
        grid_spec=pltpu.PrefetchScalarGridSpec(
            num_scalar_prefetch=1,
            grid=(slabs,),
            in_specs=[pl.BlockSpec((rows, width // slabs), lambda k, where: (0, where[k]))],
            out_specs=pl.BlockSpec((rows, width // slabs), lambda k, where: (0, k)),
        ),
        cost_estimate=pl.CostEstimate(
            flops=0, bytes_accessed=8 * rows * width, transcendentals=0
        ),
    )(table, values)


class Ring:
    def __init__(self, count):
        self.count = count
        self.order = list(range(0, count, 2)) + list(range(count - 1, 0, -2))
        self.place = [self.order.index(i) for i in range(count)]
        self.forth = [(self.order[i], self.order[(i + 1) % count]) for i in range(count)]
        self.back = [(there, here) for here, there in self.forth]
        self.sent, self.awaited = [], []

    def tables(self):
        here = jnp.asarray(self.place, jnp.int32)[lax.axis_index("seq")]
        steps = jnp.arange(self.count, dtype=jnp.int32)
        to_ring = jnp.asarray(self.order, jnp.int32)[(here - steps) % self.count]
        to_plain = (here - jnp.asarray(self.place, jnp.int32)) % self.count
        return to_ring, to_plain

    def send(self, forth, back):
        earlier = list(self.sent[-2]) if len(self.sent) > 1 else []
        if earlier or self.awaited:
            forth, back = lax.optimization_barrier((forth, back, *earlier, *self.awaited))[:2]
        self.awaited = []
        self.sent.append(
            (lax.ppermute(forth, "seq", self.forth), lax.ppermute(back, "seq", self.back))
        )
        return self.sent[-1]

    def first(self, *values):
        self.awaited.extend(values)

    def then(self, value, under_way=1):
        if len(self.sent) <= under_way:
            return value
        return lax.optimization_barrier((value, *self.sent[-1 - under_way]))[0]


class Gather:
    def __init__(self, ring, forth, back):
        self.ring, self.forth, self.back = ring, [forth], [back]

    def step(self):
        forth, back = self.ring.send(self.forth[-1], self.back[-1])
        self.forth.append(forth)
        self.back.append(back)

    def slabs(self):
        count = self.ring.count
        return self.forth, [self.back[-k % count] for k in range(count)]


class Scatter:
    def __init__(self, ring, forth_slab, back_slab):
        self.ring, self.forth_slab, self.back_slab = ring, forth_slab, back_slab
        self.at = 1
        self.forth = forth_slab(1).astype(bf16)
        self.back = back_slab(ring.count - 1).astype(bf16)

    def step(self):
        count = self.ring.count
        forth, back = self.ring.send(self.forth, self.back)
        self.at += 1
        self.forth = forth.astype(f32) + self.forth_slab(self.at % count)
        self.back = back.astype(f32) + self.back_slab(count - self.at)
        if self.at < count:
            self.forth, self.back = self.forth.astype(bf16), self.back.astype(bf16)

    def sums(self):
        return self.forth, self.back


class PlainGather:
    def __init__(self, ring, forth, back):
        self.pieces = (forth, back)

    def step(self):
        pass

    def slabs(self):
        return tuple(list(lax.all_gather(piece, "seq")) for piece in self.pieces)


class PlainScatter:
    def __init__(self, ring, forth_slab, back_slab):
        self.terms = (forth_slab, back_slab)

    def step(self):
        pass

    def sums(self):
        count = lax.axis_size("seq")
        return tuple(
            lax.psum_scatter(
                jnp.concatenate([term(k) for k in range(count)], 0),
                "seq",
                scatter_dimension=0,
                tiled=True,
            )
            for term in self.terms
        )


def in_turn(*transfers):
    for transfer in transfers:
        transfer.step()


def swapped(values, axis, bit):
    return lax.ppermute(values, axis, [(i, i ^ bit) for i in range(lax.axis_size(axis))])


class Exchange:
    def __init__(self, ring, values, axis):
        self.ring, self.values, self.axis = ring, values, axis
        self.got = None
        count = lax.axis_size(axis)
        self.bits = [1 << i for i in range(count.bit_length() - 1)]
        self.stages = self.plan()

    def upper(self, bit):
        return (lax.axis_index(self.axis) // bit) % 2 > 0

    def step(self, under_way=None):
        if self.got is not None:
            got, bit, end = self.got
            self.got = None
            end(got if under_way is None else self.ring.then(got, under_way), bit)
        if self.stages:
            start, end, bit = self.stages.pop(0)
            self.got = (swapped(start(bit), self.axis, bit), bit, end)
        return self.values

    def run(self, under_way=None):
        while self.stages or self.got is not None:
            self.step(under_way)
        return self.values

    def start_half(self, bit):
        half = self.values.shape[0] // 2
        kept, sent = [
            jnp.where(self.upper(bit) == side, self.values[half:], self.values[:half])
            for side in (True, False)
        ]
        self.values = kept
        return sent.astype(bf16)

    def end_half(self, got, bit):
        self.values = self.values.astype(f32) + got.astype(f32)

    def start_join(self, bit):
        return self.values

    def end_join(self, got, bit):
        upper, own = self.upper(bit), self.values
        self.values = jnp.concatenate([jnp.where(upper, got, own), jnp.where(upper, own, got)], 0)

    def end_sum(self, got, bit):
        self.values = self.values + got

    def halving(self):
        return [(self.start_half, self.end_half, bit) for bit in self.bits]

    def joining(self):
        return [(self.start_join, self.end_join, bit) for bit in reversed(self.bits)]


class Halves(Exchange):
    def plan(self):
        return self.halving()


class Joined(Exchange):
    def plan(self):
        return self.joining()


class Everywhere(Exchange):
    def plan(self):
        stages = self.halving() + self.joining()
        middle = len(self.bits)

        def start_first_join(bit):
            self.values = self.values.astype(bf16)
            return self.values

        if stages:
            stages[middle] = (start_first_join, self.end_join, stages[middle][2])
        return stages


class SmallSum(Exchange):
    def plan(self):
        return [(self.start_join, self.end_sum, bit) for bit in self.bits]


def own_rows(values):
    count, mine = lax.axis_size("fsdp"), lax.axis_index("fsdp")
    bit = 1
    while bit < count:
        half = values.shape[0] // 2
        values = lax.dynamic_slice_in_dim(values, ((mine // bit) % 2) * half, half, 0)
        bit *= 2
    return values


def halves_joined(own):
    count, mine = lax.axis_size("fsdp"), lax.axis_index("fsdp")
    bit = count // 2
    while bit:
        got = lax.ppermute(own, "fsdp", [(i, i ^ bit) for i in range(count)])
        upper = (mine // bit) % 2 > 0
        own = jnp.concatenate([jnp.where(upper, got, own), jnp.where(upper, own, got)], 0)
        bit //= 2
    return own


def passed_along(block, distance):
    devices = range(lax.axis_size("seq"))
    route = [(i - distance, i) for i in devices if i - distance in devices]
    return lax.ppermute(block, "seq", route)


def joined_maps(earlier, later):
    return jnp.stack([earlier[0] * later[0], later[1] + later[0] * earlier[1]], 0)


class Entry:
    def __init__(self, prods, states, sign):
        self.pair, self.sign = jnp.stack([prods, states], 0), sign
        self.count = lax.axis_size("seq")
        self.direct = self.count == ring_count
        if self.direct:
            self.other = swapped(self.pair, "seq", 1)

    def between(self, hold):
        if not self.direct:
            return
        self.other = hold(self.other)
        self.second = lax.axis_index("seq") % 2 == (1 if self.sign > 0 else 0)
        earlier = jnp.where(self.second, self.other, self.pair)
        later = jnp.where(self.second, self.pair, self.other)
        both = joined_maps(earlier, later)
        self.parts = [
            passed_along(both, self.sign * distance) for distance in range(self.count - 2, 0, -2)
        ]

    def state(self, hold):
        if self.direct:
            parts = [hold(self.parts[0])] + self.parts[1:]
            state = parts[0][1]
            for part in parts[1:]:
                state = part[1] + part[0] * state
            return jnp.where(self.second, self.other[1] + self.other[0] * state, state)
        pair = passed_along(self.pair, self.sign)
        distance = 1
        while distance < self.count:
            pair = joined_maps(passed_along(pair, self.sign * distance), pair)
            distance *= 2
        return pair[1]


def ring_index(place, count):
    place = lax.rem(place + 2 * count, count)
    odd = place // (count // 2)
    return (1 - odd) * (2 * place) + odd * (2 * count - 1 - 2 * place)


def ring_place(index, count):
    odd = lax.rem(index, 2)
    return (1 - odd) * (index // 2) + odd * (count - 1 - index // 2)


def partner(index, bit):
    return index + bit * (1 - 2 * lax.rem(index // bit, 2))


class Copies:
    def __init__(self, send_sems, recv_sems):
        self.send_sems, self.recv_sems = send_sems, recv_sems
        self.started, self.waiting = 0, []

    def start(self, source, target, device):
        slot = self.started
        copy = pltpu.make_async_remote_copy(
            src_ref=source,
            dst_ref=target,
            send_sem=self.send_sems.at[slot],
            recv_sem=self.recv_sems.at[slot],
            device_id=device,
            device_id_type=pl.DeviceIdType.MESH,
        )
        copy.start()
        self.started += 1
        self.waiting.append(copy)
        return copy

    def sent(self, copy):
        copy.wait_send()
        self.waiting.remove(copy)

    def end(self):
        for copy in self.waiting:
            copy.wait_send()


class Moves:
    def __init__(self, sems):
        self.sems, self.started, self.waiting = sems, 0, []

    def start(self, source, target):
        copy = pltpu.make_async_copy(source, target, self.sems.at[self.started])
        copy.start()
        self.started += 1
        self.waiting.append(copy)
        return copy

    def wait(self, number):
        for copy in self.waiting[:number]:
            copy.wait()
        self.waiting = self.waiting[number:]


def greet(devices):
    for device in devices:
        pl.semaphore_signal(
            pltpu.get_barrier_semaphore(),
            inc=1,
            device_id=device,
            device_id_type=pl.DeviceIdType.MESH,
        )


def greeted(devices):
    pl.semaphore_wait(pltpu.get_barrier_semaphore(), len(devices))


tail_copies = 28 + 4 + 3 + 3 + 5


def tail_body(
    count,
    emb_ref,
    mixed_ref,
    normed_ref,
    branch_ref,
    inner_ref,
    branch_all_in,
    inner_all_in,
    values_in,
    grad_in,
    gain_ref,
    gain_two_ref,
    small_ref,
    blocks_ref,
    branch_out,
    inner_out,
    out_out,
    tokens_out,
    gains_out,
    small_out,
    blocks_out,
    wide_sent,
    wide_got,
    slim_sent,
    slim_got,
    half_sent,
    half_kept,
    half_got,
    own_sent,
    own_got,
    small_sums,
    small_got,
    gain_sums,
    gain_got,
    branch_all_ref,
    inner_all_ref,
    values_ref,
    grad_ref,
    move_sems,
    send_sems,
    recv_sems,
):
    index, unit = lax.axis_index("seq"), lax.axis_index("fsdp")
    place = ring_place(index, count)
    forth, back = {"seq": ring_index(place + 1, count)}, {"seq": ring_index(place - 1, count)}
    across = [{"seq": partner(index, bit)} for bit in (1, 2, 4)]
    beside = [{"fsdp": partner(unit, bit)} for bit in (1, 2)]
    copies = Copies(send_sems, recv_sems)
    rows, units = branch_ref.shape
    slab = normed_ref.shape[1] // count
    tn = (((0,), (0,)), ((), ()))
    moves = Moves(move_sems)
    moves.start(branch_all_in, branch_all_ref)
    moves.start(inner_all_in, inner_all_ref)
    moves.start(values_in, values_ref)
    moves.start(grad_in, grad_ref)

    others = [forth, back] + across + beside
    greet(others)

    cut = slim_got.shape[2]
    parts = (slice(0, cut), slice(cut, units))

    def out_term(k, way):
        return lax.dot_general(
            mixed_ref[:, parts[way]],
            emb_ref[:, k * slab : (k + 1) * slab],
            tn,
            preferred_element_type=f32,
        )

    def front_term(k, way):
        return lax.dot_general(
            (inner_ref if way else branch_ref)[...],
            normed_ref[:, k * slab : (k + 1) * slab],
            tn,
            preferred_element_type=f32,
        )

    rings = {}

    def send(name, way, step, total):
        sent, got = (slim_sent, slim_got) if name == "out" else (wide_sent, wide_got)
        there = pl.ds(0, total.shape[0])
        if step > 0:
            sent[way, step, there, :] = total.astype(bf16)
        rings[name, way] = copies.start(
            sent.at[way, step, there], got.at[way, step, there], back if way else forth
        )

    def term(name, way, step):
        k = (count - step) % count if way else step % count
        return out_term(k, way) if name == "out" else front_term(k, way)

    def serve(name, step):
        got = slim_got if name == "out" else wide_got
        terms = [term(name, way, step) for way in (0, 1)]
        for way, own in enumerate(terms):
            rings[name, way].wait_recv()
            total = got[way, step - 2, pl.ds(0, own.shape[0]), :].astype(f32) + own
            if step < count:
                send(name, way, step - 1, total)
            elif name == "out":
                out_out[parts[way], :] = total
            else:
                (inner_out if way else branch_out)[...] = total

    firsts = [(name, way, term(name, way, 1)) for name in ("out", "front") for way in (0, 1)]
    for name, way, first in firsts:
        sent = slim_sent if name == "out" else wide_sent
        sent[way, 0, pl.ds(0, first.shape[0]), :] = first.astype(bf16)
    greeted(others)
    for name, way, first in firsts:
        send(name, way, 0, first)
    moves.wait(2)

    high = blocks_out.shape[0]
    bits = [lax.rem(index // bit, 2) for bit in (1, 2, 4)]
    sizes = [high // 2, high // 4, high // 8]
    starts = [bits[0] * sizes[0]]
    for bit, size in zip(bits[1:], sizes[1:]):
        starts.append(starts[-1] + bit * size)
    at = [rows_at(start, size) for start, size in zip(starts, sizes)]
    blocks_out[at[2], :] = blocks_ref[...]
    blocks_copy = copies.start(blocks_out.at[at[2]], blocks_out.at[at[2]], across[2])
    small_sums[0] = small_ref[...]
    small_copy = copies.start(small_sums.at[0], small_got.at[0], across[0])

    core, side = lax.rem(unit, 2), lax.rem(unit // 2, 2)
    mid, own = rows // 2, rows // 4

    def front_back(start, k):
        columns = slice(k * slab, (k + 1) * slab)
        return jnp.dot(
            branch_ref[rows_at(start, mid), :],
            branch_all_ref[:, columns],
            preferred_element_type=f32,
        ) + jnp.dot(
            inner_ref[rows_at(start, mid), :],
            inner_all_ref[:, columns],
            preferred_element_type=f32,
        )

    for k in range(count):
        half_sent[:, k * slab : (k + 1) * slab] = front_back((1 - core) * mid, k).astype(bf16)
    half_copy = copies.start(half_sent, half_got, beside[0])
    serve("out", 2)
    for k in range(count):
        half_kept[:, k * slab : (k + 1) * slab] = front_back(core * mid, k)
    half_copy.wait_recv()
    other = rows_at((1 - side) * own, own)
    mine = rows_at(side * own, own)
    own_sent[...] = (half_kept[other, :] + half_got[other, :].astype(f32)).astype(bf16)
    own_copy = copies.start(own_sent, own_got, beside[1])
    serve("front", 2)

    blocks_copy.wait_recv()
    blocks_copy = copies.start(blocks_out.at[at[1]], blocks_out.at[at[1]], across[1])
    small_copy.wait_recv()
    small_sums[1] = small_sums[0] + small_got[0]
    small_copy = copies.start(small_sums.at[1], small_got.at[1], across[1])
    serve("out", 3)
    serve("front", 3)

    own_copy.wait_recv()
    moves.wait(2)
    values = values_ref[...]
    scale = lax.rsqrt(jnp.mean(values * values, axis=-1, keepdims=True) + eps)
    unit_values = values * scale
    front = half_kept[mine, :] + half_got[mine, :].astype(f32) + own_got[...].astype(f32)
    gain_grad = jnp.sum(front * unit_values, 0, keepdims=True)
    weighted = front * gain_ref[0:1, :]
    result = grad_ref[...] + scale * (
        weighted - unit_values * jnp.mean(weighted * unit_values, axis=-1, keepdims=True)
    )
    low = result.astype(bf16)
    own_at = rows_at(core * mid + side * own, own)
    gain_sums[0] = jnp.zeros_like(gain_sums[0])
    for k in range(count):
        to = pl.ds(pl.multiple_of(ring_index(place - k, count) * slab, slab), slab)
        part = slice(k * slab, (k + 1) * slab)
        tokens_out[own_at, to] = low[:, part]
        gain_sums[0, 0:1, to] = gain_grad[:, part]
        gain_sums[0, 1:2, to] = gain_two_ref[0:1, part]
    tokens_copy = copies.start(tokens_out.at[own_at], tokens_out.at[own_at], beside[1])
    gain_copy = copies.start(gain_sums.at[0], gain_got.at[0], across[0])
    serve("out", 4)
    serve("front", 4)

    blocks_copy.wait_recv()
    blocks_copy = copies.start(blocks_out.at[at[0]], blocks_out.at[at[0]], across[0])
    small_copy.wait_recv()
    small_sums[2] = small_sums[1] + small_got[1]
    small_copy = copies.start(small_sums.at[2], small_got.at[2], across[2])
    gain_copy.wait_recv()
    gain_sums[1] = gain_sums[0] + gain_got[0]
    gain_copy = copies.start(gain_sums.at[1], gain_got.at[1], across[1])
    tokens_copy.wait_recv()
    both_at = rows_at(core * mid, mid)
    tokens_copy = copies.start(tokens_out.at[both_at], tokens_out.at[both_at], beside[0])
    serve("out", 5)
    serve("front", 5)

    blocks_copy.wait_recv()
    gain_copy.wait_recv()
    gain_sums[2] = gain_sums[1] + gain_got[1]
    gain_copy = copies.start(gain_sums.at[2], gain_got.at[2], across[2])
    small_copy.wait_recv()
    small_out[...] = small_sums[2] + small_got[2]
    serve("out", 6)
    serve("front", 6)

    gain_copy.wait_recv()
    gain_sums[3] = gain_sums[2] + gain_got[2]
    gain_copy = copies.start(gain_sums.at[3], gain_got.at[3], beside[0])
    serve("out", 7)
    gain_copy.wait_recv()
    gain_sums[4] = gain_sums[3] + gain_got[3]
    gain_copy = copies.start(gain_sums.at[4], gain_got.at[4], beside[1])
    serve("front", 7)
    serve("out", 8)
    gain_copy.wait_recv()
    gains_out[...] = gain_sums[4] + gain_got[4]
    tokens_copy.wait_recv()
    serve("front", 8)
    copies.end()


def tail(count, *operands):
    emb, mixed, normed, *_ = operands
    small, blocks = operands[-2:]
    rows, width = emb.shape
    units = mixed.shape[1]
    slab, cut = width // count, -(-units // 256) * 128
    high, block_width = blocks.shape
    whole = pl.BlockSpec(memory_space=pltpu.VMEM)
    grad = jax.ShapeDtypeStruct((units, slab), f32)
    steps = count - 1
    return pl.pallas_call(
        functools.partial(tail_body, count),
        out_shape=(
            grad,
            grad,
            grad,
            jax.ShapeDtypeStruct((rows, width), bf16),
            jax.ShapeDtypeStruct((8, width), f32),
            jax.ShapeDtypeStruct(small.shape, f32),
            jax.ShapeDtypeStruct((8 * high, block_width), bf16),
        ),
        in_specs=[whole] * 5
        + [pl.BlockSpec(memory_space=pl.ANY)] * 4
        + [whole] * (len(operands) - 9),
        out_specs=(whole,) * 7,
        scratch_shapes=[
            pltpu.VMEM((2, steps, units, slab), bf16),
            pltpu.VMEM((2, steps, units, slab), bf16),
            pltpu.VMEM((2, steps, cut, slab), bf16),
            pltpu.VMEM((2, steps, cut, slab), bf16),
            pltpu.VMEM((rows // 2, width), bf16),
            pltpu.VMEM((rows // 2, width), f32),
            pltpu.VMEM((rows // 2, width), bf16),
            pltpu.VMEM((rows // 4, width), bf16),
            pltpu.VMEM((rows // 4, width), bf16),
            pltpu.VMEM((3, *small.shape), f32),
            pltpu.VMEM((3, *small.shape), f32),
            pltpu.VMEM((5, 8, width), f32),
            pltpu.VMEM((5, 8, width), f32),
            pltpu.VMEM((units, width), bf16),
            pltpu.VMEM((units, width), bf16),
            pltpu.VMEM((rows // 4, width), f32),
            pltpu.VMEM((rows // 4, width), f32),
            pltpu.SemaphoreType.DMA((4,)),
            pltpu.SemaphoreType.DMA((tail_copies,)),
            pltpu.SemaphoreType.DMA((tail_copies,)),
        ],
        compiler_params=pltpu.CompilerParams(
            collective_id=0, has_side_effects=True, vmem_limit_bytes=60 * 1024 * 1024
        ),
    )(*operands)


def peers(count, units):
    index, unit = lax.axis_index("seq"), lax.axis_index("fsdp")
    along = [{"seq": lax.rem(index + distance, count)} for distance in range(1, count)]
    beside = [{"fsdp": partner(unit, 1 << i)} for i in range(units.bit_length() - 1)]
    return along, beside


def rows_at(start, size, multiple=16):
    return pl.ds(pl.multiple_of(start, multiple), size)


def dot_nt_here(left, right):
    return lax.dot_general(left, right, (((1,), (1,)), ((), ())), preferred_element_type=f32)


def dot_slabs(left, right_ref, slab, count):
    for k in range(count):
        columns = slice(k * slab, (k + 1) * slab)
        yield columns, jnp.dot(left, right_ref[:, columns], preferred_element_type=f32)


def scan_rows(a_ref, b_ref, prod_ref, state_ref, batches, backward):
    length, units = a_ref.shape[0] // batches, a_ref.shape[1]
    tiles = length // 8
    rows = lax.broadcasted_iota(jnp.int32, (8, units), 0)

    def step(index, carry):
        tile = tiles - 1 - index if backward else index
        following = []
        for batch in range(batches):
            prod_in, state_in, a_next = carry[batch]
            at = rows_at(batch * length + tile * 8, 8, 8)
            a, b = a_ref[at, :], b_ref[at, :]
            a_first = a[0:1]
            if backward:
                a = jnp.where(rows < 7, pltpu.roll(a, 7, 0), a_next)
            for shift in (1, 2, 4):
                turn = 8 - shift if backward else shift
                inside = rows < 8 - shift if backward else rows >= shift
                a_moved = jnp.where(inside, pltpu.roll(a, turn, 0), 1.0)
                b_moved = jnp.where(inside, pltpu.roll(b, turn, 0), 0.0)
                b = a * b_moved + b
                a = a * a_moved
            b = b + a * state_in
            a = a * prod_in
            prod_ref[at, :] = a
            state_ref[at, :] = b
            edge = 0 if backward else 7
            following.append((a[edge : edge + 1], b[edge : edge + 1], a_first))
        return tuple(following)

    one, zero = jnp.ones((1, units), f32), jnp.zeros((1, units), f32)
    maps = lax.fori_loop(0, tiles, step, ((one, zero, one),) * batches)
    return [(prod, state) for prod, state, _ in maps]


def entry_states(ends_ref, got_ref, index, count, batches, sign):
    states = []
    for batch in range(batches):
        state = jnp.zeros_like(ends_ref[0:1, :])
        for distance in range(count - 1, 0, -1):
            there = index - distance >= 0 if sign > 0 else index + distance < count
            prods = got_ref[distance - 1, batch : batch + 1, :]
            longer = got_ref[distance - 1, batches + batch : batches + batch + 1, :] + prods * state
            state = jnp.where(there, longer, 0.0)
        states.append(state)
    return states


head_copies = 9 * (ring_count - 1) + 5
row_block = 32


def head_body(
    count,
    fsdp,
    batches,
    tokens_in,
    cot_in,
    branch_ref,
    inner_ref,
    out_ref,
    gate_ref,
    up_ref,
    down_ref,
    taps_ref,
    conv_bias_ref,
    gate_bias_ref,
    input_bias_ref,
    rate_ref,
    slope_ref,
    gain_one_ref,
    gain_two_ref,
    resets_ref,
    gate_blocks_ref,
    input_blocks_ref,
    gate_all,
    up_all,
    down_all,
    branch_all_far,
    inner_all_far,
    out_all_far,
    cot_out_far,
    normed_out_far,
    branch_pre_far,
    padded_far,
    conv_low_far,
    gate_pre_far,
    input_pre_far,
    carries_far,
    states_far,
    mixed_low_far,
    gate_square_far,
    input_square_far,
    own_values_far,
    own_middle_far,
    normed_two_far,
    ends,
    gains,
    packed_ref,
    fresh_ref,
    branch_all,
    inner_all,
    out_all,
    cot_out,
    normed_out,
    branch_pre,
    padded,
    conv_low,
    gate_pre,
    input_pre,
    carries,
    states,
    mixed_low,
    gate_square_ref,
    input_square_ref,
    own_values,
    own_middle,
    normed_two,
    tokens_ref,
    cot_ref,
    tokens_low,
    prods,
    local_states,
    edges_sent,
    edges_got,
    ends_sent,
    ends_got,
    half_sent,
    half_kept,
    half_got,
    own_sent,
    own_got,
    local_sems,
    far_sems,
    send_sems,
    recv_sems,
):
    index, unit = lax.axis_index("seq"), lax.axis_index("fsdp")
    place = ring_place(index, count)
    forth, back = {"seq": ring_index(place + 1, count)}, {"seq": ring_index(place - 1, count)}
    along, beside = peers(count, fsdp)
    copies = Copies(send_sems, recv_sems)
    moves = Moves(far_sems)
    moves.start(tokens_in, tokens_ref)
    moves.start(cot_in, cot_ref)
    rows, width = tokens_ref.shape
    units, hidden = branch_ref.shape[0], down_ref.shape[0]
    length, slab = rows // batches, width // count
    core, side = lax.rem(unit, 2), lax.rem(unit // 2, 2)
    mid, own = rows // 2, rows // 4

    greet(along + beside)

    locals_of = []
    for source, target in zip(
        (branch_ref, inner_ref, out_ref, gate_ref, up_ref, down_ref),
        (branch_all, inner_all, out_all, gate_all, up_all, down_all),
    ):
        first = target.at[pl.ds(0, slab)]
        if source.shape[1] == slab:
            first = target.at[:, pl.ds(0, slab)]
        copy = pltpu.make_async_copy(source, first, local_sems.at[len(locals_of)])
        copy.start()
        locals_of.append(copy)

    greeted(along + beside)

    pairs = {
        "front": ((branch_ref, branch_all, 0, units), (inner_ref, inner_all, 0, units)),
        "out": (
            (out_ref, out_all, 0, units // 2),
            (out_ref, out_all, units // 2, units // 2),
        ),
        "mlp": ((gate_ref, gate_all, None, None), (up_ref, up_all, None, None)),
        "down": (
            (down_ref, down_all, 0, hidden // 2),
            (down_ref, down_all, hidden // 2, hidden // 2),
        ),
    }
    under_way = {}

    def start(name, step):
        for way in (0, 1):
            shard, whole, first, size = pairs[name][way]

            def slab_at(k):
                if first is None:
                    return whole.at[pl.ds(k * slab, slab)]
                return whole.at[pl.ds(first, size), pl.ds(k * slab, slab)]

            if step > 1:
                under_way[name, way].wait_recv()
            there = (count - step) % count if way else step
            here = (there + 1) % count if way else step - 1
            if step > 1:
                source = slab_at(here)
            else:
                source = shard if first is None else shard.at[pl.ds(first, size)]
            under_way[name, way] = copies.start(source, slab_at(there), back if way else forth)

    def finish(name):
        for way in (0, 1):
            under_way[name, way].wait_recv()

    start("front", 1)
    start("out", 1)

    packed_ref[...] = jnp.zeros_like(packed_ref)
    packed_ref[0:4, :units] = taps_ref[...].astype(f32)
    vectors = (conv_bias_ref, gate_bias_ref, input_bias_ref, rate_ref, slope_ref)
    for row, vector in enumerate((*vectors, gain_one_ref, gain_two_ref)):
        size = vector.shape[0]
        packed_ref[row + 4 : row + 5, :size] = vector[...].astype(f32).reshape(1, size)
    flags = jnp.concatenate(
        [resets_ref[...].astype(f32), jnp.zeros((8 - batches, length), f32)], 0
    ).T
    for batch in range(batches):
        fresh_ref[batch * length : (batch + 1) * length, :] = flags[:, batch : batch + 1]

    moves.wait(1)
    for k in range(count):
        plain = pl.ds(pl.multiple_of(ring_index(place - k, count) * slab, slab), slab)
        part = slice(k * slab, (k + 1) * slab)
        tokens_low[:, part] = tokens_ref[:, plain]
        gains[0:1, part] = packed_ref[9:10, plain]
        gains[1:2, part] = packed_ref[10:11, plain]
    start("front", 2)
    start("out", 2)

    def norm_block(block, carry):
        at = rows_at(block * row_block, row_block)
        values = tokens_low[at, :].astype(f32)
        scale = lax.rsqrt(jnp.mean(values * values, axis=-1, keepdims=True) + eps)
        normed_out[at, :] = (values * scale * gains[0:1, :]).astype(bf16)
        return carry

    lax.fori_loop(0, rows // row_block, norm_block, 0)
    own_values[...] = tokens_low[rows_at(core * mid + side * own, own), :].astype(f32)
    start("front", 3)
    start("out", 3)
    for blocks, square in (
        (gate_blocks_ref, gate_square_ref),
        (input_blocks_ref, input_square_ref),
    ):
        square[...] = jnp.zeros_like(square)
        size = blocks.shape[1]
        for j in range(blocks.shape[0]):
            square[j * size : (j + 1) * size, j * size : (j + 1) * size] = blocks[j]
    moves.wait(1)
    for k in range(count):
        plain = pl.ds(pl.multiple_of(ring_index(place - k, count) * slab, slab), slab)
        cot_out[:, k * slab : (k + 1) * slab] = cot_ref[:, plain]
    for step in range(4, count):
        start("front", step)
        start("out", step)
    start("mlp", 1)
    start("down", 1)
    for copy in locals_of:
        copy.wait()
    finish("front")

    for batch in range(batches):
        at = slice(batch * length, (batch + 1) * length)
        top = batch * (length + 8)
        inner = dot_nt_here(normed_out[at, :], inner_all[...])
        padded[top + 8 : top + 8 + length, :] = inner.astype(bf16).astype(f32)
        edges_sent[batch] = padded[top + length : top + length + 8, :]
    edge_copy = copies.start(edges_sent, edges_got, along[0])
    for batch in range(batches):
        at = slice(batch * length, (batch + 1) * length)
        branch_pre[at, :] = dot_nt_here(normed_out[at, :], branch_all[...])
    edge_copy.wait_recv()
    for batch in range(batches):
        top = batch * (length + 8)
        padded[top : top + 8, :] = jnp.where(index > 0, edges_got[batch], 0.0)
    start("mlp", 2)
    bias, gate_bias, input_bias, rate = [packed_ref[i : i + 1, :units] for i in range(4, 8)]

    def conv_block(block, carry):
        batch = block // (length // row_block)
        wide = padded[rows_at(block * row_block + batch * 8, row_block + 8, 8), :]
        total = bias + packed_ref[0:1, :units] * wide[8:] + packed_ref[1:2, :units] * wide[7:-1]
        total = total + packed_ref[2:3, :units] * wide[6:-2] + packed_ref[3:4, :units] * wide[5:-3]
        conv_low[rows_at(block * row_block, row_block), :] = total.astype(bf16)
        return carry

    lax.fori_loop(0, rows // row_block, conv_block, 0)
    for batch in range(batches):
        at = slice(batch * length, (batch + 1) * length)
        conv = conv_low[at, :]
        gate_pre[at, :] = (
            jnp.dot(conv, gate_square_ref[...], preferred_element_type=f32) + gate_bias
        )
        input_pre[at, :] = (
            jnp.dot(conv, input_square_ref[...], preferred_element_type=f32) + input_bias
        )
    start("down", 2)

    def gate_block(block, carry):
        at = rows_at(block * row_block, row_block)
        rate_gate = jax.nn.sigmoid(gate_pre[at, :])
        inlet_gate = jax.nn.sigmoid(input_pre[at, :])
        log_decay = rate * rate_gate
        decay = jnp.exp(log_decay)
        fresh = fresh_ref[at, :] > 0
        scale = jnp.sqrt(-jnp.tanh(log_decay) * (1.0 + decay * decay))
        carries[at, :] = jnp.where(fresh, 0.0, decay)
        local_states[at, :] = (
            jnp.where(fresh, 1.0, scale) * inlet_gate * conv_low[at, :].astype(f32)
        )
        return carry

    lax.fori_loop(0, rows // row_block, gate_block, 0)
    scanned = scan_rows(carries, local_states, prods, local_states, batches, False)
    ends_sent[...] = jnp.zeros_like(ends_sent)
    for batch, (prod, state) in enumerate(scanned):
        ends_sent[batch : batch + 1, :] = prod
        ends_sent[batches + batch : batches + batch + 1, :] = state
    ends[...] = ends_sent[...]
    end_copies = [
        copies.start(ends_sent, ends_got.at[distance - 1], along[distance - 1])
        for distance in range(1, count)
    ]
    start("mlp", 3)
    for copy in end_copies:
        copy.wait_recv()
    entries = entry_states(ends, ends_got, index, count, batches, 1)

    for batch in range(batches):
        entry = entries[batch]
        top = batch * (length + 8)
        states[top : top + 8, :] = jnp.broadcast_to(entry, (8, units))

        def state_block(block, carry, batch=batch, entry=entry):
            at = rows_at(batch * length + block * row_block, row_block)
            state = local_states[at, :] + prods[at, :] * entry
            states[rows_at(8 + batch * (length + 8) + block * row_block, row_block, 8), :] = state
            mixed_low[at, :] = (state * gelu_tanh(branch_pre[at, :])).astype(bf16)
            return carry

        lax.fori_loop(0, length // row_block, state_block, 0)
    start("down", 3)
    finish("out")
    for part, result in dot_slabs(
        mixed_low[rows_at((1 - core) * mid, mid), :], out_all, slab, count
    ):
        half_sent[:, part] = result.astype(bf16)
    half_copy = copies.start(half_sent, half_got, beside[0])
    for part, result in dot_slabs(mixed_low[rows_at(core * mid, mid), :], out_all, slab, count):
        half_kept[:, part] = result
    half_copy.wait_recv()
    other, mine = rows_at((1 - side) * own, own), rows_at(side * own, own)
    own_sent[...] = (half_kept[other, :] + half_got[other, :].astype(f32)).astype(bf16)
    own_copy = copies.start(own_sent, own_got, beside[1])
    start("mlp", 4)
    start("down", 4)
    own_copy.wait_recv()
    middle = own_values[...] + (
        half_kept[mine, :] + half_got[mine, :].astype(f32) + own_got[...].astype(f32)
    )
    own_middle[...] = middle
    scale = lax.rsqrt(jnp.mean(middle * middle, axis=-1, keepdims=True) + eps)
    own_at, both_at = rows_at(core * mid + side * own, own), rows_at(core * mid, mid)
    normed_two[own_at, :] = (middle * scale * gains[1:2, :]).astype(bf16)
    join_copy = copies.start(normed_two.at[own_at], normed_two.at[own_at], beside[1])
    start("mlp", 5)
    join_copy.wait_recv()
    join_copy = copies.start(normed_two.at[both_at], normed_two.at[both_at], beside[0])
    start("down", 5)
    join_copy.wait_recv()
    for step in range(6, count):
        start("mlp", step)
        start("down", step)
    for source, target in (
        (branch_all, branch_all_far),
        (inner_all, inner_all_far),
        (out_all, out_all_far),
        (cot_out, cot_out_far),
        (normed_out, normed_out_far),
        (branch_pre, branch_pre_far),
        (padded, padded_far),
        (conv_low, conv_low_far),
        (gate_pre, gate_pre_far),
        (input_pre, input_pre_far),
        (carries, carries_far),
        (states, states_far),
        (mixed_low, mixed_low_far),
        (gate_square_ref, gate_square_far),
        (input_square_ref, input_square_far),
        (own_values, own_values_far),
        (own_middle, own_middle_far),
        (normed_two, normed_two_far),
    ):
        moves.start(source, target)
    finish("mlp")
    finish("down")
    moves.wait(18)
    copies.end()


def head(count, fsdp, batches, *operands):
    tokens = operands[0]
    branch, gate = operands[2], operands[5]
    rows, width = tokens.shape
    units, hidden = branch.shape[0], gate.shape[1]
    whole, place = pl.BlockSpec(memory_space=pltpu.VMEM), pl.BlockSpec(memory_space=pl.ANY)

    def array(dtype, *shape):
        return jax.ShapeDtypeStruct(shape, dtype)

    kept = (
        [array(bf16, units, width)] * 3
        + [array(bf16, rows, width)] * 2
        + [array(f32, rows, units), array(f32, rows + 8 * batches, units), array(bf16, rows, units)]
        + [array(f32, rows, units)] * 3
        + [array(f32, rows + 8 * batches, units), array(bf16, rows, units)]
        + [array(bf16, units, units)] * 2
        + [array(f32, rows // 4, width)] * 2
        + [array(bf16, rows, width)]
    )
    outs = (
        [array(bf16, width, hidden)] * 2
        + [array(bf16, hidden, width)]
        + kept
        + [array(f32, 8, units), array(f32, 8, width)]
        + [array(f32, 16, width), array(f32, rows, 1)]
    )
    return pl.pallas_call(
        functools.partial(head_body, count, fsdp, batches),
        out_shape=tuple(outs),
        in_specs=[place] * 8 + [whole] * 11,
        out_specs=tuple([place] * (len(outs) - 4) + [whole] * 4),
        scratch_shapes=[
            *[pltpu.VMEM(part.shape, part.dtype) for part in kept],
            *[pltpu.VMEM((rows, width), bf16)] * 2,
            pltpu.VMEM((rows, width), bf16),
            pltpu.VMEM((rows, units), f32),
            pltpu.VMEM((rows, units), f32),
            pltpu.VMEM((batches, 8, units), f32),
            pltpu.VMEM((batches, 8, units), f32),
            pltpu.VMEM((8, units), f32),
            pltpu.VMEM((count - 1, 8, units), f32),
            pltpu.VMEM((rows // 2, width), bf16),
            pltpu.VMEM((rows // 2, width), f32),
            pltpu.VMEM((rows // 2, width), bf16),
            pltpu.VMEM((rows // 4, width), bf16),
            pltpu.VMEM((rows // 4, width), bf16),
            pltpu.SemaphoreType.DMA((6,)),
            pltpu.SemaphoreType.DMA((20,)),
            pltpu.SemaphoreType.DMA((head_copies,)),
            pltpu.SemaphoreType.DMA((head_copies,)),
        ],
        compiler_params=pltpu.CompilerParams(
            collective_id=1, has_side_effects=True, vmem_limit_bytes=60 * 1024 * 1024
        ),
    )(*operands)


def gelu_slope(values):
    constant = 0.7978845608028654
    bent = jnp.tanh(constant * (values + 0.044715 * values * values * values))
    inner = constant * (1.0 + 3.0 * 0.044715 * values * values)
    return 0.5 * (1.0 + bent) + 0.5 * values * (1.0 - bent * bent) * inner


ring_slots = 3
back_sends = 2 * 2 * (ring_count - 1)
back_copies = 4 + 4 + (ring_count - 1) + 1 + 3


class RingSum:
    def __init__(self, terms, slots, sends, arrivals, credits, count, neighbours):
        self.terms, self.slots, self.count = terms, slots, count
        self.sends, self.arrivals, self.credits = sends, arrivals, credits
        self.neighbours = neighbours
        self.copies = [[], []]

    def prepare(self):
        for way, k in ((0, 1), (1, self.count - 1)):
            self.slots[way, 0] = self.terms[way](k).astype(bf16)

    def send(self, way, step, total=None):
        here, there = (step - 1) % ring_slots, step % ring_slots
        if step > 1:
            self.slots[way, here] = total.astype(bf16)
        if step >= ring_slots:
            pl.semaphore_wait(self.credits.at[way], 1)
        copy = pltpu.make_async_remote_copy(
            src_ref=self.slots.at[way, here],
            dst_ref=self.slots.at[way, there],
            send_sem=self.sends.at[way, step - 1],
            recv_sem=self.arrivals.at[way, step - 1],
            device_id=self.neighbours[way],
            device_id_type=pl.DeviceIdType.MESH,
        )
        copy.start()
        self.copies[way].append(copy)
        if step >= 2:
            self.copies[way][step - 2].wait_send()
            if step + 1 < self.count:
                pl.semaphore_signal(
                    self.credits.at[way],
                    inc=1,
                    device_id=self.neighbours[1 - way],
                    device_id_type=pl.DeviceIdType.MESH,
                )

    def serve(self, step, end=None):
        if step == 1:
            self.send(0, 1)
            self.send(1, 1)
            return
        slabs = (step % self.count, (self.count - step) % self.count)
        terms = [term(k) for term, k in zip(self.terms, slabs)]
        for way, own in enumerate(terms):
            self.copies[way][step - 2].wait_recv()
            total = self.slots[way, (step - 1) % ring_slots].astype(f32) + own
            if step < self.count:
                self.send(way, step, total)
            else:
                self.copies[way][step - 2].wait_send()
                end(way, total)


def back_body(
    count,
    fsdp,
    batches,
    cot_ref,
    hidden_ref,
    normed_ref,
    gate_low_ref,
    up_low_ref,
    ends_ref,
    own_middle,
    fresh_ref,
    packed_ref,
    gains_ref,
    gate_all,
    up_all,
    down_all,
    out_all,
    branch_pre_in,
    padded_in,
    conv_low_in,
    gate_pre_in,
    input_pre_in,
    carries_in,
    states_in,
    gate_square_in,
    input_square_in,
    small_out,
    blocks_out,
    gain_grad_out,
    down_grad,
    branch_low_out,
    inner_low_out,
    gate_low_out,
    input_low_out,
    gate_grad,
    up_grad,
    mixed_far,
    middle_far,
    own_grad_far,
    half_sent,
    half_kept,
    half_got,
    own_sent,
    own_got,
    prods,
    adjoints,
    conv_grad,
    edges_sent,
    edges_got,
    ends_sent,
    ends_got,
    mlp_slots,
    down_slots,
    stream_one,
    stream_two,
    stream_out,
    stream_down,
    stage,
    branch_pre,
    padded,
    conv_low,
    gate_pre,
    input_pre,
    carries,
    states,
    gate_square_ref,
    input_square_ref,
    branch_low,
    inner_low,
    gate_low,
    input_low,
    blocks,
    blocks_one,
    blocks_two,
    blocks_got_one,
    blocks_got_two,
    blocks_got_three,
    mixed_out,
    middle_low,
    own_grad,
    move_sems,
    stream_sems,
    stage_sems,
    ring_sends,
    ring_arrivals,
    ring_credits,
    send_sems,
    recv_sems,
):
    index, unit = lax.axis_index("seq"), lax.axis_index("fsdp")
    place = ring_place(index, count)
    neighbours = (
        {"seq": ring_index(place + 1, count)},
        {"seq": ring_index(place - 1, count)},
    )
    along, beside = peers(count, fsdp)
    copies = Copies(send_sems, recv_sems)
    rows, width = cot_ref.shape
    units = branch_pre.shape[1]
    moves = Moves(move_sems)
    for source, target in (
        (branch_pre_in, branch_pre),
        (states_in, states),
        (carries_in, carries),
        (gate_pre_in, gate_pre),
        (input_pre_in, input_pre),
        (conv_low_in, conv_low),
        (gate_square_in, gate_square_ref),
        (input_square_in, input_square_ref),
        (padded_in, padded),
    ):
        moves.start(source, target)
    length, slab = rows // batches, width // count
    inner_half = hidden_ref.shape[1] // 2
    core, side = lax.rem(unit, 2), lax.rem(unit // 2, 2)
    mid, own = rows // 2, rows // 4
    kept_at, sent_at = rows_at(core * mid, mid), rows_at((1 - core) * mid, mid)
    mine, other = rows_at(side * own, own), rows_at((1 - side) * own, own)
    own_at = rows_at(core * mid + side * own, own)
    tn = (((0,), (0,)), ((), ()))

    greet(along + beside)

    def mlp_term(right):
        return lambda k: lax.dot_general(
            normed_ref[:, k * slab : (k + 1) * slab], right[...], tn, preferred_element_type=f32
        )

    def down_term(first):
        return lambda k: lax.dot_general(
            hidden_ref[:, first : first + inner_half],
            cot_ref[:, k * slab : (k + 1) * slab],
            tn,
            preferred_element_type=f32,
        )

    mlp = RingSum(
        [mlp_term(gate_low_ref), mlp_term(up_low_ref)],
        mlp_slots,
        ring_sends.at[0],
        ring_arrivals.at[0],
        ring_credits.at[0],
        count,
        neighbours,
    )
    down = RingSum(
        [down_term(0), down_term(inner_half)],
        down_slots,
        ring_sends.at[1],
        ring_arrivals.at[1],
        ring_credits.at[1],
        count,
        neighbours,
    )
    mlp.prepare()
    down.prepare()
    greeted(along + beside)
    mlp.serve(1)
    down.serve(1)

    def streamed(sources, buffers, first_sem, columns=False):
        def fetch(k):
            fetched = []
            for number, (source, buffer) in enumerate(zip(sources, buffers)):
                here = pl.ds(k * slab, slab)
                copy = pltpu.make_async_copy(
                    source.at[:, here] if columns else source.at[here],
                    buffer.at[k % 2],
                    stream_sems.at[first_sem + number * count + k],
                )
                copy.start()
                fetched.append(copy)
            return fetched

        fetched = fetch(0)
        for k in range(count):
            for copy in fetched:
                copy.wait()
            if k + 1 < count:
                fetched = fetch(k + 1)
            yield k, [buffer[k % 2] for buffer in buffers]

    nt = dot_nt_here

    for k, (gate, up) in streamed((gate_all, up_all), (stream_one, stream_two), 0):
        part = slice(k * slab, (k + 1) * slab)
        half_sent[:, part] = (
            nt(gate_low_ref[sent_at, :], gate) + nt(up_low_ref[sent_at, :], up)
        ).astype(bf16)
        half_kept[:, part] = nt(gate_low_ref[kept_at, :], gate) + nt(up_low_ref[kept_at, :], up)
    half_copy = copies.start(half_sent, half_got, beside[0])
    half_copy.wait_recv()
    own_sent[...] = (half_kept[other, :] + half_got[other, :].astype(f32)).astype(bf16)
    own_copy = copies.start(own_sent, own_got, beside[1])
    mlp.serve(2)
    down.serve(2)
    own_copy.wait_recv()
    middle = own_middle[...]
    scale = lax.rsqrt(jnp.mean(middle * middle, axis=-1, keepdims=True) + eps)
    unit_values = middle * scale
    front = half_kept[mine, :] + half_got[mine, :].astype(f32) + own_got[...].astype(f32)
    gain_grad_out[...] = jnp.zeros_like(gain_grad_out)
    gain_grad_out[0:1, :] = jnp.sum(front * unit_values, 0, keepdims=True)
    weighted = front * gains_ref[1:2, :]
    result = cot_ref[own_at, :].astype(f32) + scale * (
        weighted - unit_values * jnp.mean(weighted * unit_values, axis=-1, keepdims=True)
    )
    own_grad[...] = result
    middle_low[own_at, :] = result.astype(bf16)
    join_copy = copies.start(middle_low.at[own_at], middle_low.at[own_at], beside[1])
    mlp.serve(3)
    join_copy.wait_recv()
    join_copy = copies.start(middle_low.at[kept_at], middle_low.at[kept_at], beside[0])
    down.serve(3)
    join_copy.wait_recv()

    for k, (out,) in streamed((out_all,), (stream_out,), 2 * count, True):
        for batch in range(batches):
            at = slice(batch * length, (batch + 1) * length)
            more = nt(middle_low[at, k * slab : (k + 1) * slab], out)
            adjoints[at, :] = more if k == 0 else adjoints[at, :] + more

    moves.wait(9)

    def mixed_block(block, carry):
        batch = block // (length // row_block)
        at = rows_at(block * row_block, row_block)
        back, before = adjoints[at, :], branch_pre[at, :]
        state = states[rows_at(block * row_block + batch * 8 + 8, row_block, 8), :]
        branch_low[at, :] = (back * state * gelu_slope(before)).astype(bf16)
        adjoints[at, :] = back * gelu_tanh(before)
        return carry

    lax.fori_loop(0, rows // row_block, mixed_block, 0)
    moves.start(branch_low, branch_low_out)
    scanned = scan_rows(carries, adjoints, prods, adjoints, batches, True)
    ends_sent[...] = ends_ref[...]
    for batch, (_, state) in enumerate(scanned):
        top = batch * length
        ends_sent[batches + batch : batches + batch + 1, :] = carries[top : top + 1, :] * state
    end_copies = [
        copies.start(ends_sent, ends_got.at[distance - 1], along[count - distance - 1])
        for distance in range(1, count)
    ]
    mlp.serve(4)
    for copy in end_copies:
        copy.wait_recv()
    entries = entry_states(ends_sent, ends_got, index, count, batches, -1)

    rate, slope = [packed_ref[i : i + 1, :units] for i in (7, 8)]
    zero = jnp.zeros((1, units), f32)
    sums = (zero, zero, zero)
    for batch in range(batches):
        entry = entries[batch]

        def gate_block(block, sums, batch=batch, entry=entry):
            top = batch * length + block * row_block
            at = rows_at(top, row_block)
            rate_gate = jax.nn.sigmoid(gate_pre[at, :])
            inlet_gate = jax.nn.sigmoid(input_pre[at, :])
            log_decay = rate * rate_gate
            decay = jnp.exp(log_decay)
            fresh = fresh_ref[at, :] > 0
            scale = jnp.sqrt(-jnp.tanh(log_decay) * (1.0 + decay * decay))
            conv = conv_low[at, :].astype(f32)
            lam = adjoints[at, :] + prods[at, :] * entry
            before = states[rows_at(top + batch * 8, row_block + 8, 8), :][7:-1]
            drawn = inlet_gate * conv
            log_grad = jnp.where(
                fresh, 0.0, lam * before * decay - lam * (decay * decay / scale) * drawn
            )
            passed = lam * jnp.where(fresh, 1.0, scale)
            gate_grad_low = (log_grad * rate * (rate_gate * (1.0 - rate_gate))).astype(bf16)
            input_grad_low = (passed * conv * (inlet_gate * (1.0 - inlet_gate))).astype(bf16)
            gate_low[at, :] = gate_grad_low
            input_low[at, :] = input_grad_low
            conv_grad[rows_at(top + batch * 8, row_block, 8), :] = passed * inlet_gate
            terms = (
                gate_grad_low.astype(f32),
                input_grad_low.astype(f32),
                log_grad * rate_gate,
            )
            return tuple(
                total + jnp.sum(more, 0, keepdims=True) for total, more in zip(sums, terms)
            )

        sums = lax.fori_loop(0, length // row_block, gate_block, sums)
        if batch == 0:
            down.serve(4)
    moves.start(gate_low, gate_low_out)
    moves.start(input_low, input_low_out)
    for batch in range(batches):
        at, top = slice(batch * length, (batch + 1) * length), batch * (length + 8)
        conv_grad[top : top + length, :] = (
            conv_grad[top : top + length, :]
            + nt(gate_low[at, :], gate_square_ref[...])
            + nt(input_low[at, :], input_square_ref[...])
        )
        edges_sent[batch] = conv_grad[top : top + 8, :]
    edge_copy = copies.start(edges_sent, edges_got, along[count - 2])
    mlp.serve(5)
    size = blocks.shape[1] // 2
    tall = blocks.shape[0] * size // units
    blocks[...] = jnp.zeros_like(blocks)
    for number, right in enumerate((gate_low, input_low)):
        square = lax.dot_general(conv_low[...], right[...], tn, preferred_element_type=f32)
        for j in range(units // size):
            at = slice(j * size, (j + 1) * size)
            blocks[j * tall : j * tall + size, number * size : (number + 1) * size] = square[
                at, at
            ].astype(bf16)
    across = [{"seq": partner(index, bit)} for bit in (1, 2, 4)]
    bits = [lax.rem(index // bit, 2) for bit in (1, 2, 4)]
    firsts = [blocks.shape[0] // part for part in (2, 4, 8)]

    def halves(source, stage):
        kept = source[rows_at(bits[stage] * firsts[stage], firsts[stage]), :]
        sent = source.at[rows_at((1 - bits[stage]) * firsts[stage], firsts[stage])]
        got = (blocks_got_one, blocks_got_two, blocks_got_three)[stage]
        return kept, copies.start(sent, got, across[stage]), got

    def halved(kept, copy, got):
        copy.wait_recv()
        return (kept.astype(f32) + got[...].astype(f32)).astype(bf16)

    halving = halves(blocks, 0)

    copies.sent(half_copy)
    copies.sent(own_copy)
    for k, (right,) in streamed((down_all,), (stream_down,), 3 * count, True):
        part = slice(k * slab, (k + 1) * slab)
        half_sent[:, part] = jnp.dot(
            hidden_ref[sent_at, :], right, preferred_element_type=f32
        ).astype(bf16)
        half_kept[:, part] = jnp.dot(
            hidden_ref[kept_at, :], right, preferred_element_type=f32
        )
    mixed_copy = copies.start(half_sent, half_got, beside[0])
    down.serve(5)

    edge_copy.wait_recv()
    for batch in range(batches):
        top = batch * (length + 8) + length
        conv_grad[top : top + 8, :] = jnp.where(index < count - 1, edges_got[batch], 0.0)

    def conv_block(block, sums):
        batch = block // (length // row_block)
        at = rows_at(block * row_block + batch * 8, row_block + 8, 8)
        wide, inner = conv_grad[at, :], padded[at, :]
        total = packed_ref[0:1, :units] * wide[:-8] + packed_ref[1:2, :units] * wide[1:-7]
        total = total + packed_ref[2:3, :units] * wide[2:-6] + packed_ref[3:4, :units] * wide[3:-5]
        inner_low[rows_at(block * row_block, row_block), :] = total.astype(bf16)
        near = wide[:-8]
        terms = [near * inner[8 - k : 8 - k + row_block] for k in range(4)] + [near]
        return tuple(
            total + jnp.sum(more, 0, keepdims=True) for total, more in zip(sums, terms)
        )

    conv_sums = lax.fori_loop(0, rows // row_block, conv_block, (zero,) * 5)
    moves.start(inner_low, inner_low_out)
    for number, total in enumerate((*conv_sums, sums[0], sums[1], sums[2] * slope)):
        small_out[number : number + 1, :] = total

    mixed_copy.wait_recv()
    own_sent[...] = (half_kept[other, :] + half_got[other, :].astype(f32)).astype(bf16)
    own_copy = copies.start(own_sent, own_got, beside[1])
    mlp.serve(6)
    down.serve(6)
    blocks_one[...] = halved(*halving)
    halving = halves(blocks_one, 1)
    own_copy.wait_recv()
    final = own_middle[...] + (
        half_kept[mine, :] + half_got[mine, :].astype(f32) + own_got[...].astype(f32)
    )
    final = final.astype(bf16)
    for k in range(count):
        to = pl.ds(pl.multiple_of(ring_index(place - k, count) * slab, slab), slab)
        mixed_out[own_at, to] = final[:, k * slab : (k + 1) * slab]
    join_copy = copies.start(mixed_out.at[own_at], mixed_out.at[own_at], beside[1])
    mlp.serve(7)
    blocks_two[...] = halved(*halving)
    halving = halves(blocks_two, 2)
    join_copy.wait_recv()
    join_copy = copies.start(mixed_out.at[kept_at], mixed_out.at[kept_at], beside[0])
    down.serve(7)
    join_copy.wait_recv()

    def mlp_end(way, total):
        stage[...] = total
        copy = pltpu.make_async_copy(stage, up_grad if way else gate_grad, stage_sems.at[way])
        copy.start()
        copy.wait()

    def down_end(way, total):
        down_grad[way * inner_half : (way + 1) * inner_half, :] = total

    moves.start(middle_low, middle_far)
    moves.start(own_grad, own_grad_far)
    moves.start(mixed_out, mixed_far)
    mlp.serve(8, mlp_end)
    blocks_out[...] = halved(*halving)
    down.serve(8, down_end)
    moves.wait(7)
    copies.end()


def back(count, fsdp, batches, block_width, *operands):
    cot, hidden = operands[0], operands[1]
    late = operands[-9:]
    rows, width = cot.shape
    units, inner = late[0].shape[1], hidden.shape[1]
    slab = width // count
    high = units // block_width * (-(-block_width // 32) * 32)
    whole, place = pl.BlockSpec(memory_space=pltpu.VMEM), pl.BlockSpec(memory_space=pl.ANY)

    def array(dtype, *shape):
        return jax.ShapeDtypeStruct(shape, dtype)

    outs = [
        array(f32, 8, units),
        array(bf16, high // 8, 2 * block_width),
        array(f32, 8, width),
        array(f32, inner, slab),
        *[array(bf16, rows, units)] * 4,
        *[array(f32, slab, inner)] * 2,
        array(bf16, rows, width),
        array(bf16, rows, width),
        array(f32, rows // 4, width),
    ]
    return pl.pallas_call(
        functools.partial(back_body, count, fsdp, batches),
        out_shape=tuple(outs),
        in_specs=[whole] * (len(operands) - 13) + [place] * 13,
        out_specs=tuple([whole] * 4 + [place] * 9),
        scratch_shapes=[
            pltpu.VMEM((rows // 2, width), bf16),
            pltpu.VMEM((rows // 2, width), f32),
            pltpu.VMEM((rows // 2, width), bf16),
            pltpu.VMEM((rows // 4, width), bf16),
            pltpu.VMEM((rows // 4, width), bf16),
            pltpu.VMEM((rows, units), f32),
            pltpu.VMEM((rows, units), f32),
            pltpu.VMEM((rows + 8 * batches, units), f32),
            pltpu.VMEM((batches, 8, units), f32),
            pltpu.VMEM((batches, 8, units), f32),
            pltpu.VMEM((8, units), f32),
            pltpu.VMEM((count - 1, 8, units), f32),
            pltpu.VMEM((2, ring_slots, slab, inner), bf16),
            pltpu.VMEM((2, ring_slots, inner // 2, slab), bf16),
            pltpu.VMEM((2, slab, inner), bf16),
            pltpu.VMEM((2, slab, inner), bf16),
            pltpu.VMEM((2, units, slab), bf16),
            pltpu.VMEM((2, inner, slab), bf16),
            pltpu.VMEM((slab, inner), f32),
            *[pltpu.VMEM(part.shape, part.dtype) for part in late],
            *[pltpu.VMEM((rows, units), bf16)] * 4,
            *[
                pltpu.VMEM((high // part, 2 * block_width), bf16)
                for part in (1, 2, 4, 2, 4, 8)
            ],
            pltpu.VMEM((rows, width), bf16),
            pltpu.VMEM((rows, width), bf16),
            pltpu.VMEM((rows // 4, width), f32),
            pltpu.SemaphoreType.DMA((16,)),
            pltpu.SemaphoreType.DMA((4 * count,)),
            pltpu.SemaphoreType.DMA((2,)),
            pltpu.SemaphoreType.DMA((2, 2, count - 1)),
            pltpu.SemaphoreType.DMA((2, 2, count - 1)),
            pltpu.SemaphoreType.REGULAR((2, 2)),
            pltpu.SemaphoreType.DMA((back_copies,)),
            pltpu.SemaphoreType.DMA((back_copies,)),
        ],
        compiler_params=pltpu.CompilerParams(
            collective_id=2, has_side_effects=True, vmem_limit_bytes=63 * 1024 * 1024
        ),
    )(*operands)


def mlp_body(normed_ref, cot_ref, gate_ref, up_ref, down_ref, hidden_out, gate_out, up_out):
    gate = jnp.dot(normed_ref[...], gate_ref[...], preferred_element_type=f32)
    up = jnp.dot(normed_ref[...], up_ref[...], preferred_element_type=f32)
    back = dot_nt_here(cot_ref[...], down_ref[...])
    constant = 0.7978845608028654
    square = gate * gate
    bent = jnp.tanh(constant * (gate + 0.044715 * square * gate))
    half = 0.5 * (1.0 + bent)
    active = half * gate
    slope = half + 0.5 * gate * (1.0 - bent * bent) * (
        constant * (1.0 + 3.0 * 0.044715 * square)
    )
    hidden_out[...] = (active * up).astype(bf16)
    gate_out[...] = (back * up * slope).astype(bf16)
    up_out[...] = (back * active).astype(bf16)


def feed_forward(normed, cot, gate_all, up_all, down_all):
    rows, width = normed.shape
    hidden = gate_all.shape[1]
    wide = 256
    resident = pl.BlockSpec((rows, width), lambda j: (0, 0))
    columns = pl.BlockSpec((width, wide), lambda j: (0, j))
    result = pl.BlockSpec((rows, wide), lambda j: (0, j))
    return pl.pallas_call(
        mlp_body,
        grid=(hidden // wide,),
        out_shape=(jax.ShapeDtypeStruct((rows, hidden), bf16),) * 3,
        in_specs=[
            resident,
            resident,
            columns,
            columns,
            pl.BlockSpec((wide, width), lambda j: (j, 0)),
        ],
        out_specs=(result,) * 3,
        compiler_params=pltpu.CompilerParams(vmem_limit_bytes=62 * 1024 * 1024),
    )(normed, cot, gate_all, up_all, down_all)


def finish_body(large, *refs):
    blocks, small, gains = refs[large : large + 3]
    outs = refs[large + 3 :]
    for source, target in zip(refs[:large], outs):
        target[...] = source[...].astype(f32)
    gate_blocks, input_blocks, taps, *vectors = outs[large:]
    size = gate_blocks.shape[0]
    gate_blocks[...] = blocks[0:size, 0:size].astype(f32)
    input_blocks[...] = blocks[0:size, size : 2 * size].astype(f32)
    taps[...] = small[0:4, :]
    for row, vector in enumerate(vectors[:4]):
        vector[...] = small[row + 4 : row + 5, :].reshape(vector.shape[0])
    for row, vector in enumerate(vectors[4:]):
        vector[...] = gains[row : row + 1, :].reshape(vector.shape[0])


def finish(parts, blocks, small, gains, *arrays):
    block_width = blocks.shape[1] // 2
    half = parts * block_width

    def rows_of(count, wide):
        return pl.BlockSpec((count // parts, wide), lambda j: (j, 0))

    def whole(*shape):
        return pl.BlockSpec(shape, lambda j: (0,) * len(shape))

    specs = [rows_of(*part.shape) for part in arrays]
    blocks_out = rows_of(half, block_width)
    vectors = [small.shape[1]] * 4 + [gains.shape[1]] * 2
    shapes = [part.shape for part in arrays] + [(half, block_width)] * 2
    shapes += [(4, small.shape[1])] + [(size,) for size in vectors]
    return pl.pallas_call(
        functools.partial(finish_body, len(arrays)),
        grid=(parts,),
        out_shape=tuple(jax.ShapeDtypeStruct(shape, f32) for shape in shapes),
        in_specs=[
            *specs,
            rows_of(*blocks.shape),
            whole(*small.shape),
            whole(*gains.shape),
        ],
        out_specs=(
            *specs,
            blocks_out,
            blocks_out,
            whole(4, small.shape[1]),
            *[whole(size) for size in vectors],
        ),
        compiler_params=pltpu.CompilerParams(vmem_limit_bytes=62 * 1024 * 1024),
    )(*arrays, blocks, small, gains)


def block_diagonal(blocks):
    count, width = blocks.shape[0], blocks.shape[1]
    return sum(
        jnp.pad(blocks[j], ((j * width, (count - 1 - j) * width),) * 2) for j in range(count)
    )


def rows_joined(slab_pairs):
    return jnp.concatenate([part for pair in zip(*slab_pairs) for part in pair], 0)


def diagonal_blocks(square, count):
    width = square.shape[0] // count
    return jnp.stack(
        [square[j * width : (j + 1) * width, j * width : (j + 1) * width] for j in range(count)], 0
    )


def local(
    tokens,
    resets,
    norm_gain,
    branch_weight,
    inner_weight,
    conv_weight,
    conv_bias,
    gate_blocks,
    input_blocks,
    gate_bias,
    input_bias,
    decay_param,
    out_weight,
    mlp_norm_gain,
    gate_weight,
    up_weight,
    down_weight,
    cotangent,
):
    count = lax.axis_size("seq")
    batches, length, width = tokens.shape
    slab = width // count
    units, hidden = conv_bias.shape[0], down_weight.shape[0]
    rows = batches * length
    ringed = count == ring_count and lax.axis_size("fsdp") == 4
    half = slab // 2
    out_turned, down_turned = out_weight.T, down_weight.T
    ring = Ring(count)
    if ringed:
        gather, scatter = functools.partial(Gather, ring), functools.partial(Scatter, ring)
        to_ring, to_plain = ring.tables()

        def moved(values, dtype):
            return move_slabs(values, to_ring, dtype)

        def restored(values, dtype):
            return move_slabs(values, to_plain, dtype)

        def gain_moved(gain):
            return gain.reshape(count, slab)[to_ring].reshape(width)

        def gain_restored(gain):
            return gain.reshape(count, slab)[to_plain].reshape(width)

    else:
        gather, scatter = functools.partial(PlainGather, ring), functools.partial(PlainScatter, ring)

        def moved(values, dtype):
            return values.astype(dtype)

        restored = moved

        def gain_moved(gain):
            return gain

        gain_restored = gain_moved

    def slab_dots(turned, right, first=0, rows=slab):
        def term(k):
            start = k * slab + first
            return dot_nn(turned[start : start + rows], right)

        return term

    steps = count - 1
    taps = conv_weight.astype(f32)
    decay = decay_param.astype(f32)
    fresh_start = resets[:, :, None] > 0
    gain_one = gain_moved(norm_gain.astype(f32))
    gain_two = gain_moved(mlp_norm_gain.astype(f32))

    def gates(gate_pre, input_pre, conv_value, decay):
        return gate_math(gate_pre, input_pre, conv_value, decay, fresh_start)

    def by_sequence(values):
        return values.reshape(batches, -1, values.shape[-1])

    if ringed:
        (
            gate_all,
            up_all,
            down_all,
            branch_all,
            inner_all,
            out_all,
            cot_low,
            normed,
            branch_pre,
            padded,
            conv_flat,
            gate_pre,
            input_pre,
            carries,
            states,
            mixed_low,
            gate_square,
            input_square,
            own_values,
            own_middle,
            normed_two,
            ends,
            ring_gains,
            packed,
            fresh,
        ) = head(
            count,
            lax.axis_size("fsdp"),
            batches,
            tokens.reshape(rows, width),
            cotangent.reshape(rows, width),
            branch_weight.T,
            inner_weight.T,
            out_weight,
            gate_weight,
            up_weight,
            down_weight,
            conv_weight,
            conv_bias,
            gate_bias,
            input_bias,
            -decay_scale * jax.nn.softplus(-decay),
            decay_scale * jax.nn.sigmoid(-decay),
            norm_gain,
            mlp_norm_gain,
            resets,
            gate_blocks,
            input_blocks,
        )
        hidden_low, gate_mlp_low, up_mlp_low = feed_forward(
            normed_two, cot_low, gate_all, up_all, down_all
        )
        (
            small,
            block_grads,
            gain_two_grad,
            down_grad,
            branch_low,
            inner_grad_low,
            gate_low,
            input_low,
            gate_grad,
            up_grad,
            mixed,
            middle_low,
            own_grad,
        ) = back(
            count,
            lax.axis_size("fsdp"),
            batches,
            gate_blocks.shape[-1],
            cot_low,
            hidden_low,
            normed_two,
            gate_mlp_low,
            up_mlp_low,
            ends,
            own_middle,
            fresh,
            packed,
            ring_gains,
            gate_all,
            up_all,
            down_all,
            out_all,
            branch_pre,
            padded,
            conv_flat,
            gate_pre,
            input_pre,
            carries,
            states,
            gate_square,
            input_square,
        )
        block_count, block_width = gate_blocks.shape[:2]
        branch_grad, inner_grad, out_grad, tokens_grad, gains, small, block_grads = tail(
            count,
            middle_low,
            mixed_low,
            normed,
            branch_low,
            inner_grad_low,
            branch_all,
            inner_all,
            own_values,
            own_grad,
            ring_gains,
            gain_two_grad,
            small,
            block_grads,
        )
        (
            mixed,
            tokens_grad,
            gate_grad,
            up_grad,
            down_grad,
            branch_grad,
            inner_grad,
            out_grad,
            gate_blocks_grad,
            input_blocks_grad,
            taps_grad,
            conv_bias_grad,
            gate_bias_grad,
            input_bias_grad,
            decay_grad,
            gain_one_grad,
            gain_two_grad,
        ) = finish(
            block_count,
            block_grads,
            small,
            gains,
            mixed,
            tokens_grad,
            gate_grad,
            up_grad,
            down_grad,
            branch_grad,
            inner_grad,
            out_grad,
        )
        return (
            mixed.reshape(tokens.shape),
            tokens_grad.reshape(tokens.shape),
            gain_one_grad,
            branch_grad.T,
            inner_grad.T,
            taps_grad,
            conv_bias_grad,
            gate_blocks_grad.reshape(block_count, block_width, block_width),
            input_blocks_grad.reshape(block_count, block_width, block_width),
            gate_bias_grad,
            input_bias_grad,
            decay_grad,
            out_grad,
            gain_two_grad,
            gate_grad,
            up_grad,
            down_grad,
        )
    else:
        branch_all, inner_all, out_all, gate_all, up_all, down_all = [
            lax.all_gather(piece, "seq", axis=0, tiled=True)
            for piece in (
                branch_weight,
                inner_weight,
                out_turned,
                gate_weight,
                up_weight,
                down_turned,
            )
        ]
        gate_square, input_square = block_diagonal(gate_blocks), block_diagonal(input_blocks)
        tokens_low, cot_low = tokens.reshape(rows, width), cotangent.reshape(rows, width)
        values = tokens_low.astype(f32)
        normed = (values * inverse_rms(values) * gain_one).astype(bf16)
        inner_low = by_sequence(dot_nn(normed, inner_all).astype(bf16))
        branch_pre = by_sequence(dot_nn(normed, branch_all))
        edge_rows = passed_along(inner_low[:, -3:], 1)
        padded = jnp.concatenate([edge_rows, inner_low], 1).astype(f32)
        conv_sum = conv_bias.astype(f32) + taps[0] * padded[:, 3:] + taps[1] * padded[:, 2:-1]
        conv_sum = conv_sum + taps[2] * padded[:, 1:-2] + taps[3] * padded[:, :-3]
        conv_flat = conv_sum.astype(bf16).reshape(rows, units)
        gate_pre = by_sequence(dot_nn(conv_flat, gate_square) + gate_bias.astype(f32))
        input_pre = by_sequence(dot_nn(conv_flat, input_square) + input_bias.astype(f32))
        conv_value = by_sequence(conv_flat).astype(f32)
        carries, drives = gates(gate_pre, input_pre, conv_value, decay)
        prods, local_state = local_scan(carries, drives, False)
        prods_end = prods[:, -1:]
        state_in = Entry(prods_end, local_state[:, -1:], 1).state(None)
        states = local_state + prods * state_in
        mixed_low = (states * gelu_tanh(branch_pre)).astype(bf16).reshape(rows, units)
        own_values = own_rows(tokens_low).astype(f32)
        own_middle = own_values + Halves(ring, dot_nt(mixed_low, out_all), "fsdp").run()
        normed_two = own_middle * inverse_rms(own_middle) * gain_two
        normed_two = Joined(ring, normed_two.astype(bf16), "fsdp").run()
    branch, branch_pull = jax.vjp(gelu_tanh, branch_pre)
    scale_two = inverse_rms(own_middle)
    unit_two = own_middle * scale_two

    gate_mlp = dot_nn(normed_two, gate_all)
    up_mlp = dot_nn(normed_two, up_all)
    activated, act_pull = jax.vjp(gated_product, gate_mlp, up_mlp)
    hidden_low = activated.astype(bf16)
    down_grads = scatter(
        slab_dots(cot_low.T, hidden_low, 0, half), slab_dots(cot_low.T, hidden_low, half, half)
    )
    in_turn(down_grads)
    grad_gate_mlp, grad_up_mlp = act_pull(dot_nn(ring.then(cot_low, 0), down_all))
    gate_mlp_low, up_mlp_low = grad_gate_mlp.astype(bf16), grad_up_mlp.astype(bf16)
    in_turn(down_grads)
    ring.first(gate_mlp_low, up_mlp_low)
    in_turn(down_grads)
    mlp_grads = scatter(
        slab_dots(normed_two.T, gate_mlp_low), slab_dots(normed_two.T, up_mlp_low)
    )
    in_turn(mlp_grads, down_grads)
    gate_mlp_low, up_mlp_low = lax.optimization_barrier(
        (ring.then(gate_mlp_low, 2), up_mlp_low)
    )
    back_sum = Halves(
        ring, dot_nt(gate_mlp_low, gate_all) + dot_nt(up_mlp_low, up_all), "fsdp"
    )
    back_sum.step()
    ring.first(back_sum.step())
    in_turn(mlp_grads, down_grads)
    own_back = back_sum.run(2)
    gain_two_grad = jnp.sum(own_back * unit_two, 0)
    weighted = own_back * gain_two
    own_grad = own_rows(cot_low).astype(f32) + scale_two * (
        weighted - unit_two * jnp.mean(weighted * unit_two, axis=-1, keepdims=True)
    )
    middle_join = Joined(ring, own_grad.astype(bf16), "fsdp")
    ring.first(middle_join.step())
    in_turn(mlp_grads)
    mixed_sum = Halves(ring, dot_nt(ring.then(hidden_low, 2), down_all), "fsdp")
    mixed_sum.step()
    ring.first(mixed_sum.step())
    in_turn(down_grads)
    middle_join.step(2)
    middle_low = middle_join.run()

    grad_mixed = dot_nn(middle_low, out_all).reshape(batches, length, units)
    (grad_branch_pre,) = branch_pull(grad_mixed * states)
    branch_low = grad_branch_pre.astype(bf16).reshape(rows, units)
    following = jnp.concatenate([carries[:, 1:], jnp.ones_like(carries[:, :1])], 1)
    tail_prods, local_adjoint = local_scan(following, grad_mixed * branch, True)
    entry = Entry(prods_end, carries[:, :1] * local_adjoint[:, :1], -1)
    ring.first(local_adjoint, branch_low)
    in_turn(mlp_grads)
    entry.between(ring.then)
    in_turn(down_grads)
    adjoint_in = entry.state(lambda part: ring.then(part, 1))
    adjoint = local_adjoint + tail_prods * adjoint_in
    state_before = jnp.concatenate([state_in, states[:, :-1]], 1)
    _, gate_pull = jax.vjp(gates, gate_pre, input_pre, conv_value, decay)
    grad_gate_pre, grad_input_pre, grad_conv, decay_grad = gate_pull(
        (adjoint * state_before, adjoint)
    )
    gate_low = grad_gate_pre.astype(bf16).reshape(rows, units)
    input_low = grad_input_pre.astype(bf16).reshape(rows, units)
    ring.first(gate_low, input_low)
    in_turn(mlp_grads)
    back_conv = dot_nt(gate_low, gate_square) + dot_nt(input_low, input_square)
    grad_conv = grad_conv + back_conv.reshape(batches, length, units)

    border = jnp.zeros((batches, 3, units), f32)
    spread = jnp.concatenate([border, grad_conv, border], 1)
    stop = length + 3
    grad_padded = taps[0] * spread[:, :stop] + taps[1] * spread[:, 1 : stop + 1]
    grad_padded = grad_padded + taps[2] * spread[:, 2 : stop + 2] + taps[3] * spread[:, 3:]
    returned = passed_along(grad_padded[:, :3], -1)
    mixed_join = Joined(ring, restored(own_middle + mixed_sum.run(1), bf16), "fsdp")
    ring.first(grad_padded, mixed_join.step())
    in_turn(mlp_grads)
    grad_inner = jnp.concatenate(
        [grad_padded[:, 3:-3], grad_padded[:, -3:] + ring.then(returned)], 1
    )
    inner_grad_low = grad_inner.astype(bf16).reshape(rows, units)
    in_turn(*[mlp_grads] * (steps - 6))

    block_count = gate_blocks.shape[0]
    block_grads = jnp.concatenate(
        [
            diagonal_blocks(dot_tn(conv_flat, gate_low), block_count),
            diagonal_blocks(dot_tn(conv_flat, input_low), block_count),
        ],
        0,
    )
    block_width = block_grads.shape[-1]
    taps_grad = jnp.stack(
        [jnp.sum(grad_conv * padded[:, 3 - k : 3 - k + length], (0, 1)) for k in range(4)], 0
    )
    small = jnp.concatenate(
        [
            taps_grad,
            jnp.sum(grad_conv, (0, 1))[None],
            jnp.sum(gate_low.astype(f32), 0)[None],
            jnp.sum(input_low.astype(f32), 0)[None],
            decay_grad[None],
        ],
        0,
    )
    mixed_join.step()
    mixed = mixed_join.run().astype(f32).reshape(tokens.shape)
    gate_grad, up_grad = mlp_grads.sums()
    if ringed:
        branch_grad, inner_grad, out_grad, tokens_grad, gains, small, block_grads = tail(
            count,
            middle_low.T,
            mixed_low,
            normed.T,
            branch_low,
            inner_grad_low,
            branch_all,
            inner_all,
            own_values,
            own_grad,
            gain_one[None],
            gain_two_grad[None],
            small,
            block_grads.reshape(-1, block_width).astype(bf16),
        )
        block_grads = block_grads.astype(f32)
    else:
        out_grads = scatter(
            slab_dots(middle_low.T, mixed_low, 0, half),
            slab_dots(middle_low.T, mixed_low, half, half),
        )
        front_grads = scatter(
            slab_dots(normed.T, branch_low), slab_dots(normed.T, inner_grad_low)
        )
        branch_grad, inner_grad = front_grads.sums()
        out_grad = jnp.concatenate(out_grads.sums(), 0)
        own_front = Halves(
            ring, dot_nt(branch_low, branch_all) + dot_nt(inner_grad_low, inner_all), "fsdp"
        ).run()
        scale_one = inverse_rms(own_values)
        unit_one = own_values * scale_one
        weighted = own_front * gain_one
        own_tokens = own_grad + scale_one * (
            weighted - unit_one * jnp.mean(weighted * unit_one, axis=-1, keepdims=True)
        )
        gains = jnp.stack([jnp.sum(own_front * unit_one, 0), gain_two_grad], 0)
        gains = lax.psum(gains, ("seq", "fsdp"))
        small, block_grads = lax.psum((small, block_grads), "seq")
        tokens_grad = Joined(ring, own_tokens.astype(bf16), "fsdp").run()
    tokens_grad = tokens_grad.astype(f32).reshape(tokens.shape)
    block_grads = block_grads.reshape(2, block_count, block_width, block_width)
    down_grad = jnp.concatenate(down_grads.sums(), 0)
    return (
        mixed,
        tokens_grad,
        gains[0],
        branch_grad,
        inner_grad,
        small[:4],
        small[4],
        block_grads[0],
        block_grads[1],
        small[5],
        small[6],
        small[7],
        out_grad.T,
        gains[1],
        gate_grad,
        up_grad,
        down_grad.T,
    )


def solution(mesh):
    units, both = P("fsdp"), P("seq", "fsdp")
    blocks, turned = P("fsdp", None, None), P("fsdp", "seq")
    rows = P(None, "seq", None)
    return jax.shard_map(
        local,
        mesh=mesh,
        in_specs=(
            rows,
            P(None, "seq"),
            P(),
            both,
            both,
            P(None, "fsdp"),
            units,
            blocks,
            blocks,
            units,
            units,
            units,
            turned,
            P(),
            both,
            both,
            turned,
            rows,
        ),
        out_specs=(
            rows,
            rows,
            P(),
            both,
            both,
            P(None, "fsdp"),
            units,
            blocks,
            blocks,
            units,
            units,
            units,
            turned,
            P(),
            both,
            both,
            turned,
        ),
        check_vma=False,
    )
```

```python
import functools

import jax
import jax.numpy as jnp
from jax import lax
from jax.experimental import pallas as pl
from jax.experimental.pallas import tpu as pltpu
from jax.sharding import PartitionSpec as P

eps = 1e-06
decay_scale = 8.0
f32 = jnp.float32
bf16 = jnp.bfloat16
ring_count = 8


def gelu_tanh(values):
    return jax.nn.gelu(values, approximate=True)


def gated_product(gate_pre, up_pre):
    return gelu_tanh(gate_pre) * up_pre


def gate_math(gate_pre, input_pre, conv_value, decay_param, fresh_start):
    rate_gate = jax.nn.sigmoid(gate_pre)
    inlet_gate = jax.nn.sigmoid(input_pre)
    log_decay = -decay_scale * jax.nn.softplus(-decay_param) * rate_gate
    input_scale = jnp.where(fresh_start, 1.0, jnp.sqrt(-jnp.expm1(2.0 * log_decay)))
    carries = jnp.where(fresh_start, 0.0, jnp.exp(log_decay))
    return (carries, input_scale * inlet_gate * conv_value)


def dot_nn(left, right):
    return jnp.dot(left, right, preferred_element_type=f32)


def dot_nt(left, right):
    return lax.dot_general(left, right, (((1,), (1,)), ((), ())), preferred_element_type=f32)


def dot_tn(left, right):
    return lax.dot_general(left, right, (((0,), (0,)), ((), ())), preferred_element_type=f32)


def inverse_rms(values):
    return lax.rsqrt(jnp.mean(values * values, axis=-1, keepdims=True) + eps)


def scan_body(backward, a_ref, b_ref, prod_ref, state_ref):
    batches, length, units = a_ref.shape
    tiles = length // 8
    rows = lax.broadcasted_iota(jnp.int32, (8, units), 0)

    def step(index, carry):
        tile = tiles - 1 - index if backward else index
        where_rows = pl.ds(pl.multiple_of(tile * 8, 8), 8)
        following = []
        for batch in range(batches):
            prod_in, state_in = carry[batch]
            a = a_ref[batch, where_rows, :]
            b = b_ref[batch, where_rows, :]
            for shift in (1, 2, 4):
                turn = 8 - shift if backward else shift
                inside = rows < 8 - shift if backward else rows >= shift
                a_moved = jnp.where(inside, pltpu.roll(a, turn, 0), 1.0)
                b_moved = jnp.where(inside, pltpu.roll(b, turn, 0), 0.0)
                b = a * b_moved + b
                a = a * a_moved
            b = b + a * state_in
            a = a * prod_in
            prod_ref[batch, where_rows, :] = a
            state_ref[batch, where_rows, :] = b
            edge = 0 if backward else 7
            following.append((a[edge : edge + 1], b[edge : edge + 1]))
        return tuple(following)

    first = tuple(
        (jnp.ones((1, units), f32), jnp.zeros((1, units), f32)) for _ in range(batches)
    )
    lax.fori_loop(0, tiles, step, first)


def local_scan(a, b, backward):
    shape = jax.ShapeDtypeStruct(a.shape, f32)
    elements = a.shape[0] * a.shape[1] * a.shape[2]
    return pl.pallas_call(
        functools.partial(scan_body, backward),
        out_shape=(shape, shape),
        in_specs=[pl.BlockSpec(memory_space=pltpu.VMEM)] * 2,
        out_specs=(pl.BlockSpec(memory_space=pltpu.VMEM),) * 2,
        compiler_params=pltpu.CompilerParams(vmem_limit_bytes=32 * 1024 * 1024),
        cost_estimate=pl.CostEstimate(
            flops=20 * elements, bytes_accessed=16 * elements, transcendentals=0
        ),
    )(a, b)


def move_body(table_ref, in_ref, out_ref):
    out_ref[...] = in_ref[...].astype(out_ref.dtype)


def move_slabs(values, table, dtype):
    rows, width = values.shape
    slabs = table.shape[0]
    return pl.pallas_call(
        move_body,
        out_shape=jax.ShapeDtypeStruct((rows, width), dtype),
        grid_spec=pltpu.PrefetchScalarGridSpec(
            num_scalar_prefetch=1,
            grid=(slabs,),
            in_specs=[pl.BlockSpec((rows, width // slabs), lambda k, where: (0, where[k]))],
            out_specs=pl.BlockSpec((rows, width // slabs), lambda k, where: (0, k)),
        ),
        cost_estimate=pl.CostEstimate(
            flops=0, bytes_accessed=8 * rows * width, transcendentals=0
        ),
    )(table, values)


class Ring:
    def __init__(self, count):
        self.count = count
        self.order = list(range(0, count, 2)) + list(range(count - 1, 0, -2))
        self.place = [self.order.index(i) for i in range(count)]
        self.forth = [(self.order[i], self.order[(i + 1) % count]) for i in range(count)]
        self.back = [(there, here) for here, there in self.forth]
        self.sent, self.awaited = [], []

    def tables(self):
        here = jnp.asarray(self.place, jnp.int32)[lax.axis_index("seq")]
        steps = jnp.arange(self.count, dtype=jnp.int32)
        to_ring = jnp.asarray(self.order, jnp.int32)[(here - steps) % self.count]
        to_plain = (here - jnp.asarray(self.place, jnp.int32)) % self.count
        return to_ring, to_plain

    def send(self, forth, back):
        earlier = list(self.sent[-2]) if len(self.sent) > 1 else []
        if earlier or self.awaited:
            forth, back = lax.optimization_barrier((forth, back, *earlier, *self.awaited))[:2]
        self.awaited = []
        self.sent.append(
            (lax.ppermute(forth, "seq", self.forth), lax.ppermute(back, "seq", self.back))
        )
        return self.sent[-1]

    def first(self, *values):
        self.awaited.extend(values)

    def then(self, value, under_way=1):
        if len(self.sent) <= under_way:
            return value
        return lax.optimization_barrier((value, *self.sent[-1 - under_way]))[0]


class Gather:
    def __init__(self, ring, forth, back):
        self.ring, self.forth, self.back = ring, [forth], [back]

    def step(self):
        forth, back = self.ring.send(self.forth[-1], self.back[-1])
        self.forth.append(forth)
        self.back.append(back)

    def slabs(self):
        count = self.ring.count
        return self.forth, [self.back[-k % count] for k in range(count)]


class Scatter:
    def __init__(self, ring, forth_slab, back_slab):
        self.ring, self.forth_slab, self.back_slab = ring, forth_slab, back_slab
        self.at = 1
        self.forth = forth_slab(1).astype(bf16)
        self.back = back_slab(ring.count - 1).astype(bf16)

    def step(self):
        count = self.ring.count
        forth, back = self.ring.send(self.forth, self.back)
        self.at += 1
        self.forth = forth.astype(f32) + self.forth_slab(self.at % count)
        self.back = back.astype(f32) + self.back_slab(count - self.at)
        if self.at < count:
            self.forth, self.back = self.forth.astype(bf16), self.back.astype(bf16)

    def sums(self):
        return self.forth, self.back


class PlainGather:
    def __init__(self, ring, forth, back):
        self.pieces = (forth, back)

    def step(self):
        pass

    def slabs(self):
        return tuple(list(lax.all_gather(piece, "seq")) for piece in self.pieces)


class PlainScatter:
    def __init__(self, ring, forth_slab, back_slab):
        self.terms = (forth_slab, back_slab)

    def step(self):
        pass

    def sums(self):
        count = lax.axis_size("seq")
        return tuple(
            lax.psum_scatter(
                jnp.concatenate([term(k) for k in range(count)], 0),
                "seq",
                scatter_dimension=0,
                tiled=True,
            )
            for term in self.terms
        )


def in_turn(*transfers):
    for transfer in transfers:
        transfer.step()


def swapped(values, axis, bit):
    return lax.ppermute(values, axis, [(i, i ^ bit) for i in range(lax.axis_size(axis))])


class Exchange:
    def __init__(self, ring, values, axis):
        self.ring, self.values, self.axis = ring, values, axis
        self.got = None
        count = lax.axis_size(axis)
        self.bits = [1 << i for i in range(count.bit_length() - 1)]
        self.stages = self.plan()

    def upper(self, bit):
        return (lax.axis_index(self.axis) // bit) % 2 > 0

    def step(self, under_way=None):
        if self.got is not None:
            got, bit, end = self.got
            self.got = None
            end(got if under_way is None else self.ring.then(got, under_way), bit)
        if self.stages:
            start, end, bit = self.stages.pop(0)
            self.got = (swapped(start(bit), self.axis, bit), bit, end)
        return self.values

    def run(self, under_way=None):
        while self.stages or self.got is not None:
            self.step(under_way)
        return self.values

    def start_half(self, bit):
        half = self.values.shape[0] // 2
        kept, sent = [
            jnp.where(self.upper(bit) == side, self.values[half:], self.values[:half])
            for side in (True, False)
        ]
        self.values = kept
        return sent.astype(bf16)

    def end_half(self, got, bit):
        self.values = self.values.astype(f32) + got.astype(f32)

    def start_join(self, bit):
        return self.values

    def end_join(self, got, bit):
        upper, own = self.upper(bit), self.values
        self.values = jnp.concatenate([jnp.where(upper, got, own), jnp.where(upper, own, got)], 0)

    def end_sum(self, got, bit):
        self.values = self.values + got

    def halving(self):
        return [(self.start_half, self.end_half, bit) for bit in self.bits]

    def joining(self):
        return [(self.start_join, self.end_join, bit) for bit in reversed(self.bits)]


class Halves(Exchange):
    def plan(self):
        return self.halving()


class Joined(Exchange):
    def plan(self):
        return self.joining()


class Everywhere(Exchange):
    def plan(self):
        stages = self.halving() + self.joining()
        middle = len(self.bits)

        def start_first_join(bit):
            self.values = self.values.astype(bf16)
            return self.values

        if stages:
            stages[middle] = (start_first_join, self.end_join, stages[middle][2])
        return stages


class SmallSum(Exchange):
    def plan(self):
        return [(self.start_join, self.end_sum, bit) for bit in self.bits]


def own_rows(values):
    count, mine = lax.axis_size("fsdp"), lax.axis_index("fsdp")
    bit = 1
    while bit < count:
        half = values.shape[0] // 2
        values = lax.dynamic_slice_in_dim(values, ((mine // bit) % 2) * half, half, 0)
        bit *= 2
    return values


def halves_joined(own):
    count, mine = lax.axis_size("fsdp"), lax.axis_index("fsdp")
    bit = count // 2
    while bit:
        got = lax.ppermute(own, "fsdp", [(i, i ^ bit) for i in range(count)])
        upper = (mine // bit) % 2 > 0
        own = jnp.concatenate([jnp.where(upper, got, own), jnp.where(upper, own, got)], 0)
        bit //= 2
    return own


def passed_along(block, distance):
    devices = range(lax.axis_size("seq"))
    route = [(i - distance, i) for i in devices if i - distance in devices]
    return lax.ppermute(block, "seq", route)


def joined_maps(earlier, later):
    return jnp.stack([earlier[0] * later[0], later[1] + later[0] * earlier[1]], 0)


class Entry:
    def __init__(self, prods, states, sign):
        self.pair, self.sign = jnp.stack([prods, states], 0), sign
        self.count = lax.axis_size("seq")
        self.direct = self.count == ring_count
        if self.direct:
            self.other = swapped(self.pair, "seq", 1)

    def between(self, hold):
        if not self.direct:
            return
        self.other = hold(self.other)
        self.second = lax.axis_index("seq") % 2 == (1 if self.sign > 0 else 0)
        earlier = jnp.where(self.second, self.other, self.pair)
        later = jnp.where(self.second, self.pair, self.other)
        both = joined_maps(earlier, later)
        self.parts = [
            passed_along(both, self.sign * distance) for distance in range(self.count - 2, 0, -2)
        ]

    def state(self, hold):
        if self.direct:
            parts = [hold(self.parts[0])] + self.parts[1:]
            state = parts[0][1]
            for part in parts[1:]:
                state = part[1] + part[0] * state
            return jnp.where(self.second, self.other[1] + self.other[0] * state, state)
        pair = passed_along(self.pair, self.sign)
        distance = 1
        while distance < self.count:
            pair = joined_maps(passed_along(pair, self.sign * distance), pair)
            distance *= 2
        return pair[1]


def ring_index(place, count):
    place = lax.rem(place + 2 * count, count)
    odd = place // (count // 2)
    return (1 - odd) * (2 * place) + odd * (2 * count - 1 - 2 * place)


def ring_place(index, count):
    odd = lax.rem(index, 2)
    return (1 - odd) * (index // 2) + odd * (count - 1 - index // 2)


def partner(index, bit):
    return index + bit * (1 - 2 * lax.rem(index // bit, 2))


class Copies:
    def __init__(self, send_sems, recv_sems):
        self.send_sems, self.recv_sems = send_sems, recv_sems
        self.started, self.waiting = 0, []

    def start(self, source, target, device):
        slot = self.started
        copy = pltpu.make_async_remote_copy(
            src_ref=source,
            dst_ref=target,
            send_sem=self.send_sems.at[slot],
            recv_sem=self.recv_sems.at[slot],
            device_id=device,
            device_id_type=pl.DeviceIdType.MESH,
        )
        copy.start()
        self.started += 1
        self.waiting.append(copy)
        return copy

    def sent(self, copy):
        copy.wait_send()
        self.waiting.remove(copy)

    def end(self):
        for copy in self.waiting:
            copy.wait_send()


class Moves:
    def __init__(self, sems):
        self.sems, self.started, self.waiting = sems, 0, []

    def start(self, source, target):
        copy = pltpu.make_async_copy(source, target, self.sems.at[self.started])
        copy.start()
        self.started += 1
        self.waiting.append(copy)
        return copy

    def wait(self, number):
        for copy in self.waiting[:number]:
            copy.wait()
        self.waiting = self.waiting[number:]


def greet(devices):
    for device in devices:
        pl.semaphore_signal(
            pltpu.get_barrier_semaphore(),
            inc=1,
            device_id=device,
            device_id_type=pl.DeviceIdType.MESH,
        )


def greeted(devices):
    pl.semaphore_wait(pltpu.get_barrier_semaphore(), len(devices))


tail_copies = 28 + 4 + 3 + 3 + 5


def tail_body(
    count,
    emb_ref,
    mixed_ref,
    normed_ref,
    branch_ref,
    inner_ref,
    branch_all_in,
    inner_all_in,
    values_in,
    grad_in,
    gain_ref,
    gain_two_ref,
    small_ref,
    blocks_ref,
    branch_out,
    inner_out,
    out_out,
    tokens_out,
    gains_out,
    small_out,
    blocks_out,
    wide_sent,
    wide_got,
    slim_sent,
    slim_got,
    half_sent,
    half_kept,
    half_got,
    own_sent,
    own_got,
    small_sums,
    small_got,
    gain_sums,
    gain_got,
    branch_all_ref,
    inner_all_ref,
    values_ref,
    grad_ref,
    move_sems,
    send_sems,
    recv_sems,
):
    index, unit = lax.axis_index("seq"), lax.axis_index("fsdp")
    place = ring_place(index, count)
    forth, back = {"seq": ring_index(place + 1, count)}, {"seq": ring_index(place - 1, count)}
    across = [{"seq": partner(index, bit)} for bit in (1, 2, 4)]
    beside = [{"fsdp": partner(unit, bit)} for bit in (1, 2)]
    copies = Copies(send_sems, recv_sems)
    rows, units = branch_ref.shape
    slab = normed_ref.shape[1] // count
    tn = (((0,), (0,)), ((), ()))
    moves = Moves(move_sems)
    moves.start(branch_all_in, branch_all_ref)
    moves.start(inner_all_in, inner_all_ref)
    moves.start(values_in, values_ref)
    moves.start(grad_in, grad_ref)

    others = [forth, back] + across + beside
    greet(others)

    cut = slim_got.shape[2]
    parts = (slice(0, cut), slice(cut, units))

    def out_term(k, way):
        return lax.dot_general(
            mixed_ref[:, parts[way]],
            emb_ref[:, k * slab : (k + 1) * slab],
            tn,
            preferred_element_type=f32,
        )

    def front_term(k, way):
        return lax.dot_general(
            (inner_ref if way else branch_ref)[...],
            normed_ref[:, k * slab : (k + 1) * slab],
            tn,
            preferred_element_type=f32,
        )

    rings = {}

    def send(name, way, step, total):
        sent, got = (slim_sent, slim_got) if name == "out" else (wide_sent, wide_got)
        there = pl.ds(0, total.shape[0])
        if step > 0:
            sent[way, step, there, :] = total.astype(bf16)
        rings[name, way] = copies.start(
            sent.at[way, step, there], got.at[way, step, there], back if way else forth
        )

    def term(name, way, step):
        k = (count - step) % count if way else step % count
        return out_term(k, way) if name == "out" else front_term(k, way)

    def serve(name, step):
        got = slim_got if name == "out" else wide_got
        terms = [term(name, way, step) for way in (0, 1)]
        for way, own in enumerate(terms):
            rings[name, way].wait_recv()
            total = got[way, step - 2, pl.ds(0, own.shape[0]), :].astype(f32) + own
            if step < count:
                send(name, way, step - 1, total)
            elif name == "out":
                out_out[parts[way], :] = total
            else:
                (inner_out if way else branch_out)[...] = total

    firsts = [(name, way, term(name, way, 1)) for name in ("out", "front") for way in (0, 1)]
    for name, way, first in firsts:
        sent = slim_sent if name == "out" else wide_sent
        sent[way, 0, pl.ds(0, first.shape[0]), :] = first.astype(bf16)
    greeted(others)
    for name, way, first in firsts:
        send(name, way, 0, first)
    moves.wait(2)

    high = blocks_out.shape[0]
    bits = [lax.rem(index // bit, 2) for bit in (1, 2, 4)]
    sizes = [high // 2, high // 4, high // 8]
    starts = [bits[0] * sizes[0]]
    for bit, size in zip(bits[1:], sizes[1:]):
        starts.append(starts[-1] + bit * size)
    at = [rows_at(start, size) for start, size in zip(starts, sizes)]
    blocks_out[at[2], :] = blocks_ref[...]
    blocks_copy = copies.start(blocks_out.at[at[2]], blocks_out.at[at[2]], across[2])
    small_sums[0] = small_ref[...]
    small_copy = copies.start(small_sums.at[0], small_got.at[0], across[0])

    core, side = lax.rem(unit, 2), lax.rem(unit // 2, 2)
    mid, own = rows // 2, rows // 4

    def front_back(start, k):
        columns = slice(k * slab, (k + 1) * slab)
        return jnp.dot(
            branch_ref[rows_at(start, mid), :],
            branch_all_ref[:, columns],
            preferred_element_type=f32,
        ) + jnp.dot(
            inner_ref[rows_at(start, mid), :],
            inner_all_ref[:, columns],
            preferred_element_type=f32,
        )

    for k in range(count):
        half_sent[:, k * slab : (k + 1) * slab] = front_back((1 - core) * mid, k).astype(bf16)
    half_copy = copies.start(half_sent, half_got, beside[0])
    serve("out", 2)
    for k in range(count):
        half_kept[:, k * slab : (k + 1) * slab] = front_back(core * mid, k)
    half_copy.wait_recv()
    other = rows_at((1 - side) * own, own)
    mine = rows_at(side * own, own)
    own_sent[...] = (half_kept[other, :] + half_got[other, :].astype(f32)).astype(bf16)
    own_copy = copies.start(own_sent, own_got, beside[1])
    serve("front", 2)

    blocks_copy.wait_recv()
    blocks_copy = copies.start(blocks_out.at[at[1]], blocks_out.at[at[1]], across[1])
    small_copy.wait_recv()
    small_sums[1] = small_sums[0] + small_got[0]
    small_copy = copies.start(small_sums.at[1], small_got.at[1], across[1])
    serve("out", 3)
    serve("front", 3)

    own_copy.wait_recv()
    moves.wait(2)
    values = values_ref[...]
    scale = lax.rsqrt(jnp.mean(values * values, axis=-1, keepdims=True) + eps)
    unit_values = values * scale
    front = half_kept[mine, :] + half_got[mine, :].astype(f32) + own_got[...].astype(f32)
    gain_grad = jnp.sum(front * unit_values, 0, keepdims=True)
    weighted = front * gain_ref[0:1, :]
    result = grad_ref[...] + scale * (
        weighted - unit_values * jnp.mean(weighted * unit_values, axis=-1, keepdims=True)
    )
    low = result.astype(bf16)
    own_at = rows_at(core * mid + side * own, own)
    gain_sums[0] = jnp.zeros_like(gain_sums[0])
    for k in range(count):
        to = pl.ds(pl.multiple_of(ring_index(place - k, count) * slab, slab), slab)
        part = slice(k * slab, (k + 1) * slab)
        tokens_out[own_at, to] = low[:, part]
        gain_sums[0, 0:1, to] = gain_grad[:, part]
        gain_sums[0, 1:2, to] = gain_two_ref[0:1, part]
    tokens_copy = copies.start(tokens_out.at[own_at], tokens_out.at[own_at], beside[1])
    gain_copy = copies.start(gain_sums.at[0], gain_got.at[0], across[0])
    serve("out", 4)
    serve("front", 4)

    blocks_copy.wait_recv()
    blocks_copy = copies.start(blocks_out.at[at[0]], blocks_out.at[at[0]], across[0])
    small_copy.wait_recv()
    small_sums[2] = small_sums[1] + small_got[1]
    small_copy = copies.start(small_sums.at[2], small_got.at[2], across[2])
    gain_copy.wait_recv()
    gain_sums[1] = gain_sums[0] + gain_got[0]
    gain_copy = copies.start(gain_sums.at[1], gain_got.at[1], across[1])
    tokens_copy.wait_recv()
    both_at = rows_at(core * mid, mid)
    tokens_copy = copies.start(tokens_out.at[both_at], tokens_out.at[both_at], beside[0])
    serve("out", 5)
    serve("front", 5)

    blocks_copy.wait_recv()
    gain_copy.wait_recv()
    gain_sums[2] = gain_sums[1] + gain_got[1]
    gain_copy = copies.start(gain_sums.at[2], gain_got.at[2], across[2])
    small_copy.wait_recv()
    small_out[...] = small_sums[2] + small_got[2]
    serve("out", 6)
    serve("front", 6)

    gain_copy.wait_recv()
    gain_sums[3] = gain_sums[2] + gain_got[2]
    gain_copy = copies.start(gain_sums.at[3], gain_got.at[3], beside[0])
    serve("out", 7)
    gain_copy.wait_recv()
    gain_sums[4] = gain_sums[3] + gain_got[3]
    gain_copy = copies.start(gain_sums.at[4], gain_got.at[4], beside[1])
    serve("front", 7)
    serve("out", 8)
    gain_copy.wait_recv()
    gains_out[...] = gain_sums[4] + gain_got[4]
    tokens_copy.wait_recv()
    serve("front", 8)
    copies.end()


def tail(count, *operands):
    emb, mixed, normed, *_ = operands
    small, blocks = operands[-2:]
    rows, width = emb.shape
    units = mixed.shape[1]
    slab, cut = width // count, units // 2
    high, block_width = blocks.shape
    whole = pl.BlockSpec(memory_space=pltpu.VMEM)
    grad = jax.ShapeDtypeStruct((units, slab), f32)
    steps = count - 1
    return pl.pallas_call(
        functools.partial(tail_body, count),
        out_shape=(
            grad,
            grad,
            grad,
            jax.ShapeDtypeStruct((rows, width), bf16),
            jax.ShapeDtypeStruct((8, width), f32),
            jax.ShapeDtypeStruct(small.shape, f32),
            jax.ShapeDtypeStruct((8 * high, block_width), bf16),
        ),
        in_specs=[whole] * 5
        + [pl.BlockSpec(memory_space=pl.ANY)] * 4
        + [whole] * (len(operands) - 9),
        out_specs=(whole,) * 7,
        scratch_shapes=[
            pltpu.VMEM((2, steps, units, slab), bf16),
            pltpu.VMEM((2, steps, units, slab), bf16),
            pltpu.VMEM((2, steps, cut, slab), bf16),
            pltpu.VMEM((2, steps, cut, slab), bf16),
            pltpu.VMEM((rows // 2, width), bf16),
            pltpu.VMEM((rows // 2, width), f32),
            pltpu.VMEM((rows // 2, width), bf16),
            pltpu.VMEM((rows // 4, width), bf16),
            pltpu.VMEM((rows // 4, width), bf16),
            pltpu.VMEM((3, *small.shape), f32),
            pltpu.VMEM((3, *small.shape), f32),
            pltpu.VMEM((5, 8, width), f32),
            pltpu.VMEM((5, 8, width), f32),
            pltpu.VMEM((units, width), bf16),
            pltpu.VMEM((units, width), bf16),
            pltpu.VMEM((rows // 4, width), f32),
            pltpu.VMEM((rows // 4, width), f32),
            pltpu.SemaphoreType.DMA((4,)),
            pltpu.SemaphoreType.DMA((tail_copies,)),
            pltpu.SemaphoreType.DMA((tail_copies,)),
        ],
        compiler_params=pltpu.CompilerParams(
            collective_id=0, has_side_effects=True, vmem_limit_bytes=60 * 1024 * 1024
        ),
    )(*operands)


def peers(count, units):
    index, unit = lax.axis_index("seq"), lax.axis_index("fsdp")
    along = [{"seq": lax.rem(index + distance, count)} for distance in range(1, count)]
    beside = [{"fsdp": partner(unit, 1 << i)} for i in range(units.bit_length() - 1)]
    return along, beside


def rows_at(start, size, multiple=16):
    return pl.ds(pl.multiple_of(start, multiple), size)


def dot_nt_here(left, right):
    return lax.dot_general(left, right, (((1,), (1,)), ((), ())), preferred_element_type=f32)


def dot_slabs(left, right_ref, slab, count):
    for k in range(count):
        columns = slice(k * slab, (k + 1) * slab)
        yield columns, jnp.dot(left, right_ref[:, columns], preferred_element_type=f32)


def scan_rows(a_ref, b_ref, prod_ref, state_ref, batches, backward):
    length, units = a_ref.shape[0] // batches, a_ref.shape[1]
    tiles = length // 8
    rows = lax.broadcasted_iota(jnp.int32, (8, units), 0)

    def step(index, carry):
        tile = tiles - 1 - index if backward else index
        following = []
        for batch in range(batches):
            prod_in, state_in, a_next = carry[batch]
            at = rows_at(batch * length + tile * 8, 8, 8)
            a, b = a_ref[at, :], b_ref[at, :]
            a_first = a[0:1]
            if backward:
                a = jnp.where(rows < 7, pltpu.roll(a, 7, 0), a_next)
            for shift in (1, 2, 4):
                turn = 8 - shift if backward else shift
                inside = rows < 8 - shift if backward else rows >= shift
                a_moved = jnp.where(inside, pltpu.roll(a, turn, 0), 1.0)
                b_moved = jnp.where(inside, pltpu.roll(b, turn, 0), 0.0)
                b = a * b_moved + b
                a = a * a_moved
            b = b + a * state_in
            a = a * prod_in
            prod_ref[at, :] = a
            state_ref[at, :] = b
            edge = 0 if backward else 7
            following.append((a[edge : edge + 1], b[edge : edge + 1], a_first))
        return tuple(following)

    one, zero = jnp.ones((1, units), f32), jnp.zeros((1, units), f32)
    maps = lax.fori_loop(0, tiles, step, ((one, zero, one),) * batches)
    return [(prod, state) for prod, state, _ in maps]


def entry_states(ends_ref, got_ref, index, count, batches, sign):
    states = []
    for batch in range(batches):
        state = jnp.zeros_like(ends_ref[0:1, :])
        for distance in range(count - 1, 0, -1):
            there = index - distance >= 0 if sign > 0 else index + distance < count
            prods = got_ref[distance - 1, batch : batch + 1, :]
            longer = got_ref[distance - 1, batches + batch : batches + batch + 1, :] + prods * state
            state = jnp.where(there, longer, 0.0)
        states.append(state)
    return states


head_copies = 9 * (ring_count - 1) + 5
row_block = 32


def head_body(
    count,
    fsdp,
    batches,
    tokens_in,
    cot_in,
    branch_ref,
    inner_ref,
    out_ref,
    gate_ref,
    up_ref,
    down_ref,
    taps_ref,
    conv_bias_ref,
    gate_bias_ref,
    input_bias_ref,
    rate_ref,
    slope_ref,
    gain_one_ref,
    gain_two_ref,
    resets_ref,
    gate_blocks_ref,
    input_blocks_ref,
    gate_all,
    up_all,
    down_all,
    branch_all_far,
    inner_all_far,
    out_all_far,
    cot_out_far,
    normed_out_far,
    branch_pre_far,
    padded_far,
    conv_low_far,
    gate_pre_far,
    input_pre_far,
    carries_far,
    states_far,
    mixed_low_far,
    gate_square_far,
    input_square_far,
    own_values_far,
    own_middle_far,
    normed_two_far,
    ends,
    gains,
    packed_ref,
    fresh_ref,
    branch_all,
    inner_all,
    out_all,
    cot_out,
    normed_out,
    branch_pre,
    padded,
    conv_low,
    gate_pre,
    input_pre,
    carries,
    states,
    mixed_low,
    gate_square_ref,
    input_square_ref,
    own_values,
    own_middle,
    normed_two,
    tokens_ref,
    cot_ref,
    tokens_low,
    prods,
    local_states,
    edges_sent,
    edges_got,
    ends_sent,
    ends_got,
    half_sent,
    half_kept,
    half_got,
    own_sent,
    own_got,
    local_sems,
    far_sems,
    send_sems,
    recv_sems,
):
    index, unit = lax.axis_index("seq"), lax.axis_index("fsdp")
    place = ring_place(index, count)
    forth, back = {"seq": ring_index(place + 1, count)}, {"seq": ring_index(place - 1, count)}
    along, beside = peers(count, fsdp)
    copies = Copies(send_sems, recv_sems)
    moves = Moves(far_sems)
    moves.start(tokens_in, tokens_ref)
    moves.start(cot_in, cot_ref)
    rows, width = tokens_ref.shape
    units, hidden = branch_ref.shape[0], down_ref.shape[0]
    length, slab = rows // batches, width // count
    core, side = lax.rem(unit, 2), lax.rem(unit // 2, 2)
    mid, own = rows // 2, rows // 4

    greet(along + beside)

    locals_of = []
    for source, target in zip(
        (branch_ref, inner_ref, out_ref, gate_ref, up_ref, down_ref),
        (branch_all, inner_all, out_all, gate_all, up_all, down_all),
    ):
        first = target.at[pl.ds(0, slab)]
        if source.shape[1] == slab:
            first = target.at[:, pl.ds(0, slab)]
        copy = pltpu.make_async_copy(source, first, local_sems.at[len(locals_of)])
        copy.start()
        locals_of.append(copy)

    greeted(along + beside)

    pairs = {
        "front": ((branch_ref, branch_all, 0, units), (inner_ref, inner_all, 0, units)),
        "out": (
            (out_ref, out_all, 0, units // 2),
            (out_ref, out_all, units // 2, units // 2),
        ),
        "mlp": ((gate_ref, gate_all, None, None), (up_ref, up_all, None, None)),
        "down": (
            (down_ref, down_all, 0, hidden // 2),
            (down_ref, down_all, hidden // 2, hidden // 2),
        ),
    }
    under_way = {}

    def start(name, step):
        for way in (0, 1):
            shard, whole, first, size = pairs[name][way]

            def slab_at(k):
                if first is None:
                    return whole.at[pl.ds(k * slab, slab)]
                return whole.at[pl.ds(first, size), pl.ds(k * slab, slab)]

            if step > 1:
                under_way[name, way].wait_recv()
            there = (count - step) % count if way else step
            here = (there + 1) % count if way else step - 1
            if step > 1:
                source = slab_at(here)
            else:
                source = shard if first is None else shard.at[pl.ds(first, size)]
            under_way[name, way] = copies.start(source, slab_at(there), back if way else forth)

    def finish(name):
        for way in (0, 1):
            under_way[name, way].wait_recv()

    start("front", 1)
    start("out", 1)

    packed_ref[...] = jnp.zeros_like(packed_ref)
    packed_ref[0:4, :units] = taps_ref[...].astype(f32)
    vectors = (conv_bias_ref, gate_bias_ref, input_bias_ref, rate_ref, slope_ref)
    for row, vector in enumerate((*vectors, gain_one_ref, gain_two_ref)):
        size = vector.shape[0]
        packed_ref[row + 4 : row + 5, :size] = vector[...].astype(f32).reshape(1, size)
    flags = jnp.concatenate(
        [resets_ref[...].astype(f32), jnp.zeros((8 - batches, length), f32)], 0
    ).T
    for batch in range(batches):
        fresh_ref[batch * length : (batch + 1) * length, :] = flags[:, batch : batch + 1]

    moves.wait(1)
    for k in range(count):
        plain = pl.ds(pl.multiple_of(ring_index(place - k, count) * slab, slab), slab)
        part = slice(k * slab, (k + 1) * slab)
        tokens_low[:, part] = tokens_ref[:, plain]
        gains[0:1, part] = packed_ref[9:10, plain]
        gains[1:2, part] = packed_ref[10:11, plain]
    start("front", 2)
    start("out", 2)

    def norm_block(block, carry):
        at = rows_at(block * row_block, row_block)
        values = tokens_low[at, :].astype(f32)
        scale = lax.rsqrt(jnp.mean(values * values, axis=-1, keepdims=True) + eps)
        normed_out[at, :] = (values * scale * gains[0:1, :]).astype(bf16)
        return carry

    lax.fori_loop(0, rows // row_block, norm_block, 0)
    own_values[...] = tokens_low[rows_at(core * mid + side * own, own), :].astype(f32)
    start("front", 3)
    start("out", 3)
    for blocks, square in (
        (gate_blocks_ref, gate_square_ref),
        (input_blocks_ref, input_square_ref),
    ):
        square[...] = jnp.zeros_like(square)
        size = blocks.shape[1]
        for j in range(blocks.shape[0]):
            square[j * size : (j + 1) * size, j * size : (j + 1) * size] = blocks[j]
    moves.wait(1)
    for k in range(count):
        plain = pl.ds(pl.multiple_of(ring_index(place - k, count) * slab, slab), slab)
        cot_out[:, k * slab : (k + 1) * slab] = cot_ref[:, plain]
    for step in range(4, count):
        start("front", step)
        start("out", step)
    start("mlp", 1)
    start("down", 1)
    for copy in locals_of:
        copy.wait()
    finish("front")

    for batch in range(batches):
        at = slice(batch * length, (batch + 1) * length)
        top = batch * (length + 8)
        inner = dot_nt_here(normed_out[at, :], inner_all[...])
        padded[top + 8 : top + 8 + length, :] = inner.astype(bf16).astype(f32)
        edges_sent[batch] = padded[top + length : top + length + 8, :]
    edge_copy = copies.start(edges_sent, edges_got, along[0])
    for batch in range(batches):
        at = slice(batch * length, (batch + 1) * length)
        branch_pre[at, :] = dot_nt_here(normed_out[at, :], branch_all[...])
    edge_copy.wait_recv()
    for batch in range(batches):
        top = batch * (length + 8)
        padded[top : top + 8, :] = jnp.where(index > 0, edges_got[batch], 0.0)
    start("mlp", 2)
    bias, gate_bias, input_bias, rate = [packed_ref[i : i + 1, :units] for i in range(4, 8)]

    def conv_block(block, carry):
        batch = block // (length // row_block)
        wide = padded[rows_at(block * row_block + batch * 8, row_block + 8, 8), :]
        total = bias + packed_ref[0:1, :units] * wide[8:] + packed_ref[1:2, :units] * wide[7:-1]
        total = total + packed_ref[2:3, :units] * wide[6:-2] + packed_ref[3:4, :units] * wide[5:-3]
        conv_low[rows_at(block * row_block, row_block), :] = total.astype(bf16)
        return carry

    lax.fori_loop(0, rows // row_block, conv_block, 0)
    for batch in range(batches):
        at = slice(batch * length, (batch + 1) * length)
        conv = conv_low[at, :]
        gate_pre[at, :] = (
            jnp.dot(conv, gate_square_ref[...], preferred_element_type=f32) + gate_bias
        )
        input_pre[at, :] = (
            jnp.dot(conv, input_square_ref[...], preferred_element_type=f32) + input_bias
        )
    start("down", 2)

    def gate_block(block, carry):
        at = rows_at(block * row_block, row_block)
        rate_gate = jax.nn.sigmoid(gate_pre[at, :])
        inlet_gate = jax.nn.sigmoid(input_pre[at, :])
        log_decay = rate * rate_gate
        decay = jnp.exp(log_decay)
        fresh = fresh_ref[at, :] > 0
        scale = jnp.sqrt(-jnp.tanh(log_decay) * (1.0 + decay * decay))
        carries[at, :] = jnp.where(fresh, 0.0, decay)
        local_states[at, :] = (
            jnp.where(fresh, 1.0, scale) * inlet_gate * conv_low[at, :].astype(f32)
        )
        return carry

    lax.fori_loop(0, rows // row_block, gate_block, 0)
    scanned = scan_rows(carries, local_states, prods, local_states, batches, False)
    ends_sent[...] = jnp.zeros_like(ends_sent)
    for batch, (prod, state) in enumerate(scanned):
        ends_sent[batch : batch + 1, :] = prod
        ends_sent[batches + batch : batches + batch + 1, :] = state
    ends[...] = ends_sent[...]
    end_copies = [
        copies.start(ends_sent, ends_got.at[distance - 1], along[distance - 1])
        for distance in range(1, count)
    ]
    start("mlp", 3)
    for copy in end_copies:
        copy.wait_recv()
    entries = entry_states(ends, ends_got, index, count, batches, 1)

    for batch in range(batches):
        entry = entries[batch]
        top = batch * (length + 8)
        states[top : top + 8, :] = jnp.broadcast_to(entry, (8, units))

        def state_block(block, carry, batch=batch, entry=entry):
            at = rows_at(batch * length + block * row_block, row_block)
            state = local_states[at, :] + prods[at, :] * entry
            states[rows_at(8 + batch * (length + 8) + block * row_block, row_block, 8), :] = state
            mixed_low[at, :] = (state * gelu_tanh(branch_pre[at, :])).astype(bf16)
            return carry

        lax.fori_loop(0, length // row_block, state_block, 0)
    start("down", 3)
    finish("out")
    for part, result in dot_slabs(
        mixed_low[rows_at((1 - core) * mid, mid), :], out_all, slab, count
    ):
        half_sent[:, part] = result.astype(bf16)
    half_copy = copies.start(half_sent, half_got, beside[0])
    for part, result in dot_slabs(mixed_low[rows_at(core * mid, mid), :], out_all, slab, count):
        half_kept[:, part] = result
    half_copy.wait_recv()
    other, mine = rows_at((1 - side) * own, own), rows_at(side * own, own)
    own_sent[...] = (half_kept[other, :] + half_got[other, :].astype(f32)).astype(bf16)
    own_copy = copies.start(own_sent, own_got, beside[1])
    start("mlp", 4)
    start("down", 4)
    own_copy.wait_recv()
    middle = own_values[...] + (
        half_kept[mine, :] + half_got[mine, :].astype(f32) + own_got[...].astype(f32)
    )
    own_middle[...] = middle
    scale = lax.rsqrt(jnp.mean(middle * middle, axis=-1, keepdims=True) + eps)
    own_at, both_at = rows_at(core * mid + side * own, own), rows_at(core * mid, mid)
    normed_two[own_at, :] = (middle * scale * gains[1:2, :]).astype(bf16)
    join_copy = copies.start(normed_two.at[own_at], normed_two.at[own_at], beside[1])
    start("mlp", 5)
    join_copy.wait_recv()
    join_copy = copies.start(normed_two.at[both_at], normed_two.at[both_at], beside[0])
    start("down", 5)
    join_copy.wait_recv()
    for step in range(6, count):
        start("mlp", step)
        start("down", step)
    for source, target in (
        (branch_all, branch_all_far),
        (inner_all, inner_all_far),
        (out_all, out_all_far),
        (cot_out, cot_out_far),
        (normed_out, normed_out_far),
        (branch_pre, branch_pre_far),
        (padded, padded_far),
        (conv_low, conv_low_far),
        (gate_pre, gate_pre_far),
        (input_pre, input_pre_far),
        (carries, carries_far),
        (states, states_far),
        (mixed_low, mixed_low_far),
        (gate_square_ref, gate_square_far),
        (input_square_ref, input_square_far),
        (own_values, own_values_far),
        (own_middle, own_middle_far),
        (normed_two, normed_two_far),
    ):
        moves.start(source, target)
    finish("mlp")
    finish("down")
    moves.wait(18)
    copies.end()


def head(count, fsdp, batches, *operands):
    tokens = operands[0]
    branch, gate = operands[2], operands[5]
    rows, width = tokens.shape
    units, hidden = branch.shape[0], gate.shape[1]
    whole, place = pl.BlockSpec(memory_space=pltpu.VMEM), pl.BlockSpec(memory_space=pl.ANY)

    def array(dtype, *shape):
        return jax.ShapeDtypeStruct(shape, dtype)

    kept = (
        [array(bf16, units, width)] * 3
        + [array(bf16, rows, width)] * 2
        + [array(f32, rows, units), array(f32, rows + 8 * batches, units), array(bf16, rows, units)]
        + [array(f32, rows, units)] * 3
        + [array(f32, rows + 8 * batches, units), array(bf16, rows, units)]
        + [array(bf16, units, units)] * 2
        + [array(f32, rows // 4, width)] * 2
        + [array(bf16, rows, width)]
    )
    outs = (
        [array(bf16, width, hidden)] * 2
        + [array(bf16, hidden, width)]
        + kept
        + [array(f32, 8, units), array(f32, 8, width)]
        + [array(f32, 16, width), array(f32, rows, 1)]
    )
    return pl.pallas_call(
        functools.partial(head_body, count, fsdp, batches),
        out_shape=tuple(outs),
        in_specs=[place] * 8 + [whole] * 11,
        out_specs=tuple([place] * (len(outs) - 4) + [whole] * 4),
        scratch_shapes=[
            *[pltpu.VMEM(part.shape, part.dtype) for part in kept],
            *[pltpu.VMEM((rows, width), bf16)] * 2,
            pltpu.VMEM((rows, width), bf16),
            pltpu.VMEM((rows, units), f32),
            pltpu.VMEM((rows, units), f32),
            pltpu.VMEM((batches, 8, units), f32),
            pltpu.VMEM((batches, 8, units), f32),
            pltpu.VMEM((8, units), f32),
            pltpu.VMEM((count - 1, 8, units), f32),
            pltpu.VMEM((rows // 2, width), bf16),
            pltpu.VMEM((rows // 2, width), f32),
            pltpu.VMEM((rows // 2, width), bf16),
            pltpu.VMEM((rows // 4, width), bf16),
            pltpu.VMEM((rows // 4, width), bf16),
            pltpu.SemaphoreType.DMA((6,)),
            pltpu.SemaphoreType.DMA((20,)),
            pltpu.SemaphoreType.DMA((head_copies,)),
            pltpu.SemaphoreType.DMA((head_copies,)),
        ],
        compiler_params=pltpu.CompilerParams(
            collective_id=1, has_side_effects=True, vmem_limit_bytes=60 * 1024 * 1024
        ),
    )(*operands)


def gelu_slope(values):
    constant = 0.7978845608028654
    bent = jnp.tanh(constant * (values + 0.044715 * values * values * values))
    inner = constant * (1.0 + 3.0 * 0.044715 * values * values)
    return 0.5 * (1.0 + bent) + 0.5 * values * (1.0 - bent * bent) * inner


ring_slots = 3
back_sends = 2 * 2 * (ring_count - 1)
back_copies = 4 + 4 + (ring_count - 1) + 1 + 3


class RingSum:
    def __init__(self, terms, slots, sends, arrivals, credits, count, neighbours):
        self.terms, self.slots, self.count = terms, slots, count
        self.sends, self.arrivals, self.credits = sends, arrivals, credits
        self.neighbours = neighbours
        self.copies = [[], []]

    def prepare(self):
        for way, k in ((0, 1), (1, self.count - 1)):
            self.slots[way, 0] = self.terms[way](k).astype(bf16)

    def send(self, way, step, total=None):
        here, there = (step - 1) % ring_slots, step % ring_slots
        if step > 1:
            self.slots[way, here] = total.astype(bf16)
        if step >= ring_slots:
            pl.semaphore_wait(self.credits.at[way], 1)
        copy = pltpu.make_async_remote_copy(
            src_ref=self.slots.at[way, here],
            dst_ref=self.slots.at[way, there],
            send_sem=self.sends.at[way, step - 1],
            recv_sem=self.arrivals.at[way, step - 1],
            device_id=self.neighbours[way],
            device_id_type=pl.DeviceIdType.MESH,
        )
        copy.start()
        self.copies[way].append(copy)
        if step >= 2:
            self.copies[way][step - 2].wait_send()
            if step + 1 < self.count:
                pl.semaphore_signal(
                    self.credits.at[way],
                    inc=1,
                    device_id=self.neighbours[1 - way],
                    device_id_type=pl.DeviceIdType.MESH,
                )

    def serve(self, step, end=None):
        if step == 1:
            self.send(0, 1)
            self.send(1, 1)
            return
        slabs = (step % self.count, (self.count - step) % self.count)
        terms = [term(k) for term, k in zip(self.terms, slabs)]
        for way, own in enumerate(terms):
            self.copies[way][step - 2].wait_recv()
            total = self.slots[way, (step - 1) % ring_slots].astype(f32) + own
            if step < self.count:
                self.send(way, step, total)
            else:
                self.copies[way][step - 2].wait_send()
                end(way, total)


def back_body(
    count,
    fsdp,
    batches,
    cot_ref,
    hidden_ref,
    normed_ref,
    gate_low_ref,
    up_low_ref,
    ends_ref,
    own_middle,
    fresh_ref,
    packed_ref,
    gains_ref,
    gate_all,
    up_all,
    down_all,
    out_all,
    branch_pre_in,
    padded_in,
    conv_low_in,
    gate_pre_in,
    input_pre_in,
    carries_in,
    states_in,
    gate_square_in,
    input_square_in,
    small_out,
    blocks_out,
    gain_grad_out,
    down_grad,
    branch_low_out,
    inner_low_out,
    gate_low_out,
    input_low_out,
    gate_grad,
    up_grad,
    mixed_far,
    middle_far,
    own_grad_far,
    half_sent,
    half_kept,
    half_got,
    own_sent,
    own_got,
    prods,
    adjoints,
    conv_grad,
    edges_sent,
    edges_got,
    ends_sent,
    ends_got,
    mlp_slots,
    down_slots,
    stream_one,
    stream_two,
    stream_out,
    stream_down,
    stage,
    branch_pre,
    padded,
    conv_low,
    gate_pre,
    input_pre,
    carries,
    states,
    gate_square_ref,
    input_square_ref,
    branch_low,
    inner_low,
    gate_low,
    input_low,
    blocks,
    blocks_one,
    blocks_two,
    blocks_got_one,
    blocks_got_two,
    blocks_got_three,
    mixed_out,
    middle_low,
    own_grad,
    move_sems,
    stream_sems,
    stage_sems,
    ring_sends,
    ring_arrivals,
    ring_credits,
    send_sems,
    recv_sems,
):
    index, unit = lax.axis_index("seq"), lax.axis_index("fsdp")
    place = ring_place(index, count)
    neighbours = (
        {"seq": ring_index(place + 1, count)},
        {"seq": ring_index(place - 1, count)},
    )
    along, beside = peers(count, fsdp)
    copies = Copies(send_sems, recv_sems)
    rows, width = cot_ref.shape
    units = branch_pre.shape[1]
    moves = Moves(move_sems)
    for source, target in (
        (branch_pre_in, branch_pre),
        (states_in, states),
        (carries_in, carries),
        (gate_pre_in, gate_pre),
        (input_pre_in, input_pre),
        (conv_low_in, conv_low),
        (gate_square_in, gate_square_ref),
        (input_square_in, input_square_ref),
        (padded_in, padded),
    ):
        moves.start(source, target)
    length, slab = rows // batches, width // count
    inner_half = hidden_ref.shape[1] // 2
    core, side = lax.rem(unit, 2), lax.rem(unit // 2, 2)
    mid, own = rows // 2, rows // 4
    kept_at, sent_at = rows_at(core * mid, mid), rows_at((1 - core) * mid, mid)
    mine, other = rows_at(side * own, own), rows_at((1 - side) * own, own)
    own_at = rows_at(core * mid + side * own, own)
    tn = (((0,), (0,)), ((), ()))

    greet(along + beside)

    def mlp_term(right):
        return lambda k: lax.dot_general(
            normed_ref[:, k * slab : (k + 1) * slab], right[...], tn, preferred_element_type=f32
        )

    def down_term(first):
        return lambda k: lax.dot_general(
            hidden_ref[:, first : first + inner_half],
            cot_ref[:, k * slab : (k + 1) * slab],
            tn,
            preferred_element_type=f32,
        )

    mlp = RingSum(
        [mlp_term(gate_low_ref), mlp_term(up_low_ref)],
        mlp_slots,
        ring_sends.at[0],
        ring_arrivals.at[0],
        ring_credits.at[0],
        count,
        neighbours,
    )
    down = RingSum(
        [down_term(0), down_term(inner_half)],
        down_slots,
        ring_sends.at[1],
        ring_arrivals.at[1],
        ring_credits.at[1],
        count,
        neighbours,
    )
    mlp.prepare()
    down.prepare()
    greeted(along + beside)
    mlp.serve(1)
    down.serve(1)

    def streamed(sources, buffers, first_sem, columns=False):
        def fetch(k):
            fetched = []
            for number, (source, buffer) in enumerate(zip(sources, buffers)):
                here = pl.ds(k * slab, slab)
                copy = pltpu.make_async_copy(
                    source.at[:, here] if columns else source.at[here],
                    buffer.at[k % 2],
                    stream_sems.at[first_sem + number * count + k],
                )
                copy.start()
                fetched.append(copy)
            return fetched

        fetched = fetch(0)
        for k in range(count):
            for copy in fetched:
                copy.wait()
            if k + 1 < count:
                fetched = fetch(k + 1)
            yield k, [buffer[k % 2] for buffer in buffers]

    nt = dot_nt_here

    for k, (gate, up) in streamed((gate_all, up_all), (stream_one, stream_two), 0):
        part = slice(k * slab, (k + 1) * slab)
        half_sent[:, part] = (
            nt(gate_low_ref[sent_at, :], gate) + nt(up_low_ref[sent_at, :], up)
        ).astype(bf16)
        half_kept[:, part] = nt(gate_low_ref[kept_at, :], gate) + nt(up_low_ref[kept_at, :], up)
    half_copy = copies.start(half_sent, half_got, beside[0])
    half_copy.wait_recv()
    own_sent[...] = (half_kept[other, :] + half_got[other, :].astype(f32)).astype(bf16)
    own_copy = copies.start(own_sent, own_got, beside[1])
    mlp.serve(2)
    down.serve(2)
    own_copy.wait_recv()
    middle = own_middle[...]
    scale = lax.rsqrt(jnp.mean(middle * middle, axis=-1, keepdims=True) + eps)
    unit_values = middle * scale
    front = half_kept[mine, :] + half_got[mine, :].astype(f32) + own_got[...].astype(f32)
    gain_grad_out[...] = jnp.zeros_like(gain_grad_out)
    gain_grad_out[0:1, :] = jnp.sum(front * unit_values, 0, keepdims=True)
    weighted = front * gains_ref[1:2, :]
    result = cot_ref[own_at, :].astype(f32) + scale * (
        weighted - unit_values * jnp.mean(weighted * unit_values, axis=-1, keepdims=True)
    )
    own_grad[...] = result
    middle_low[own_at, :] = result.astype(bf16)
    join_copy = copies.start(middle_low.at[own_at], middle_low.at[own_at], beside[1])
    mlp.serve(3)
    join_copy.wait_recv()
    join_copy = copies.start(middle_low.at[kept_at], middle_low.at[kept_at], beside[0])
    down.serve(3)
    join_copy.wait_recv()

    for k, (out,) in streamed((out_all,), (stream_out,), 2 * count, True):
        for batch in range(batches):
            at = slice(batch * length, (batch + 1) * length)
            more = nt(middle_low[at, k * slab : (k + 1) * slab], out)
            adjoints[at, :] = more if k == 0 else adjoints[at, :] + more

    moves.wait(9)

    def mixed_block(block, carry):
        batch = block // (length // row_block)
        at = rows_at(block * row_block, row_block)
        back, before = adjoints[at, :], branch_pre[at, :]
        state = states[rows_at(block * row_block + batch * 8 + 8, row_block, 8), :]
        branch_low[at, :] = (back * state * gelu_slope(before)).astype(bf16)
        adjoints[at, :] = back * gelu_tanh(before)
        return carry

    lax.fori_loop(0, rows // row_block, mixed_block, 0)
    moves.start(branch_low, branch_low_out)
    scanned = scan_rows(carries, adjoints, prods, adjoints, batches, True)
    ends_sent[...] = ends_ref[...]
    for batch, (_, state) in enumerate(scanned):
        top = batch * length
        ends_sent[batches + batch : batches + batch + 1, :] = carries[top : top + 1, :] * state
    end_copies = [
        copies.start(ends_sent, ends_got.at[distance - 1], along[count - distance - 1])
        for distance in range(1, count)
    ]
    mlp.serve(4)
    for copy in end_copies:
        copy.wait_recv()
    entries = entry_states(ends_sent, ends_got, index, count, batches, -1)

    rate, slope = [packed_ref[i : i + 1, :units] for i in (7, 8)]
    zero = jnp.zeros((1, units), f32)
    sums = (zero, zero, zero)
    for batch in range(batches):
        entry = entries[batch]

        def gate_block(block, sums, batch=batch, entry=entry):
            top = batch * length + block * row_block
            at = rows_at(top, row_block)
            rate_gate = jax.nn.sigmoid(gate_pre[at, :])
            inlet_gate = jax.nn.sigmoid(input_pre[at, :])
            log_decay = rate * rate_gate
            decay = jnp.exp(log_decay)
            fresh = fresh_ref[at, :] > 0
            scale = jnp.sqrt(-jnp.tanh(log_decay) * (1.0 + decay * decay))
            conv = conv_low[at, :].astype(f32)
            lam = adjoints[at, :] + prods[at, :] * entry
            before = states[rows_at(top + batch * 8, row_block + 8, 8), :][7:-1]
            drawn = inlet_gate * conv
            log_grad = jnp.where(
                fresh, 0.0, lam * before * decay - lam * (decay * decay / scale) * drawn
            )
            passed = lam * jnp.where(fresh, 1.0, scale)
            gate_grad_low = (log_grad * rate * (rate_gate * (1.0 - rate_gate))).astype(bf16)
            input_grad_low = (passed * conv * (inlet_gate * (1.0 - inlet_gate))).astype(bf16)
            gate_low[at, :] = gate_grad_low
            input_low[at, :] = input_grad_low
            conv_grad[rows_at(top + batch * 8, row_block, 8), :] = passed * inlet_gate
            terms = (
                gate_grad_low.astype(f32),
                input_grad_low.astype(f32),
                log_grad * rate_gate,
            )
            return tuple(
                total + jnp.sum(more, 0, keepdims=True) for total, more in zip(sums, terms)
            )

        sums = lax.fori_loop(0, length // row_block, gate_block, sums)
        if batch == 0:
            down.serve(4)
    moves.start(gate_low, gate_low_out)
    moves.start(input_low, input_low_out)
    for batch in range(batches):
        at, top = slice(batch * length, (batch + 1) * length), batch * (length + 8)
        conv_grad[top : top + length, :] = (
            conv_grad[top : top + length, :]
            + nt(gate_low[at, :], gate_square_ref[...])
            + nt(input_low[at, :], input_square_ref[...])
        )
        edges_sent[batch] = conv_grad[top : top + 8, :]
    edge_copy = copies.start(edges_sent, edges_got, along[count - 2])
    mlp.serve(5)
    size = blocks.shape[1] // 2
    tall = blocks.shape[0] * size // units
    blocks[...] = jnp.zeros_like(blocks)
    for number, right in enumerate((gate_low, input_low)):
        square = lax.dot_general(conv_low[...], right[...], tn, preferred_element_type=f32)
        for j in range(units // size):
            at = slice(j * size, (j + 1) * size)
            blocks[j * tall : j * tall + size, number * size : (number + 1) * size] = square[
                at, at
            ].astype(bf16)
    across = [{"seq": partner(index, bit)} for bit in (1, 2, 4)]
    bits = [lax.rem(index // bit, 2) for bit in (1, 2, 4)]
    firsts = [blocks.shape[0] // part for part in (2, 4, 8)]

    def halves(source, stage):
        kept = source[rows_at(bits[stage] * firsts[stage], firsts[stage]), :]
        sent = source.at[rows_at((1 - bits[stage]) * firsts[stage], firsts[stage])]
        got = (blocks_got_one, blocks_got_two, blocks_got_three)[stage]
        return kept, copies.start(sent, got, across[stage]), got

    def halved(kept, copy, got):
        copy.wait_recv()
        return (kept.astype(f32) + got[...].astype(f32)).astype(bf16)

    halving = halves(blocks, 0)

    copies.sent(half_copy)
    copies.sent(own_copy)
    for k, (right,) in streamed((down_all,), (stream_down,), 3 * count, True):
        part = slice(k * slab, (k + 1) * slab)
        half_sent[:, part] = jnp.dot(
            hidden_ref[sent_at, :], right, preferred_element_type=f32
        ).astype(bf16)
        half_kept[:, part] = jnp.dot(
            hidden_ref[kept_at, :], right, preferred_element_type=f32
        )
    mixed_copy = copies.start(half_sent, half_got, beside[0])
    down.serve(5)

    edge_copy.wait_recv()
    for batch in range(batches):
        top = batch * (length + 8) + length
        conv_grad[top : top + 8, :] = jnp.where(index < count - 1, edges_got[batch], 0.0)

    def conv_block(block, sums):
        batch = block // (length // row_block)
        at = rows_at(block * row_block + batch * 8, row_block + 8, 8)
        wide, inner = conv_grad[at, :], padded[at, :]
        total = packed_ref[0:1, :units] * wide[:-8] + packed_ref[1:2, :units] * wide[1:-7]
        total = total + packed_ref[2:3, :units] * wide[2:-6] + packed_ref[3:4, :units] * wide[3:-5]
        inner_low[rows_at(block * row_block, row_block), :] = total.astype(bf16)
        near = wide[:-8]
        terms = [near * inner[8 - k : 8 - k + row_block] for k in range(4)] + [near]
        return tuple(
            total + jnp.sum(more, 0, keepdims=True) for total, more in zip(sums, terms)
        )

    conv_sums = lax.fori_loop(0, rows // row_block, conv_block, (zero,) * 5)
    moves.start(inner_low, inner_low_out)
    for number, total in enumerate((*conv_sums, sums[0], sums[1], sums[2] * slope)):
        small_out[number : number + 1, :] = total

    mixed_copy.wait_recv()
    own_sent[...] = (half_kept[other, :] + half_got[other, :].astype(f32)).astype(bf16)
    own_copy = copies.start(own_sent, own_got, beside[1])
    mlp.serve(6)
    down.serve(6)
    blocks_one[...] = halved(*halving)
    halving = halves(blocks_one, 1)
    own_copy.wait_recv()
    final = own_middle[...] + (
        half_kept[mine, :] + half_got[mine, :].astype(f32) + own_got[...].astype(f32)
    )
    final = final.astype(bf16)
    for k in range(count):
        to = pl.ds(pl.multiple_of(ring_index(place - k, count) * slab, slab), slab)
        mixed_out[own_at, to] = final[:, k * slab : (k + 1) * slab]
    join_copy = copies.start(mixed_out.at[own_at], mixed_out.at[own_at], beside[1])
    mlp.serve(7)
    blocks_two[...] = halved(*halving)
    halving = halves(blocks_two, 2)
    join_copy.wait_recv()
    join_copy = copies.start(mixed_out.at[kept_at], mixed_out.at[kept_at], beside[0])
    down.serve(7)
    join_copy.wait_recv()

    def mlp_end(way, total):
        stage[...] = total
        copy = pltpu.make_async_copy(stage, up_grad if way else gate_grad, stage_sems.at[way])
        copy.start()
        copy.wait()

    def down_end(way, total):
        down_grad[way * inner_half : (way + 1) * inner_half, :] = total

    moves.start(middle_low, middle_far)
    moves.start(own_grad, own_grad_far)
    moves.start(mixed_out, mixed_far)
    mlp.serve(8, mlp_end)
    blocks_out[...] = halved(*halving)
    down.serve(8, down_end)
    moves.wait(7)
    copies.end()


def back(count, fsdp, batches, block_width, *operands):
    cot, hidden = operands[0], operands[1]
    late = operands[-9:]
    rows, width = cot.shape
    units, inner = late[0].shape[1], hidden.shape[1]
    slab = width // count
    high = units // block_width * (-(-block_width // 32) * 32)
    whole, place = pl.BlockSpec(memory_space=pltpu.VMEM), pl.BlockSpec(memory_space=pl.ANY)

    def array(dtype, *shape):
        return jax.ShapeDtypeStruct(shape, dtype)

    outs = [
        array(f32, 8, units),
        array(bf16, high // 8, 2 * block_width),
        array(f32, 8, width),
        array(f32, inner, slab),
        *[array(bf16, rows, units)] * 4,
        *[array(f32, slab, inner)] * 2,
        array(bf16, rows, width),
        array(bf16, rows, width),
        array(f32, rows // 4, width),
    ]
    return pl.pallas_call(
        functools.partial(back_body, count, fsdp, batches),
        out_shape=tuple(outs),
        in_specs=[whole] * (len(operands) - 13) + [place] * 13,
        out_specs=tuple([whole] * 4 + [place] * 9),
        scratch_shapes=[
            pltpu.VMEM((rows // 2, width), bf16),
            pltpu.VMEM((rows // 2, width), f32),
            pltpu.VMEM((rows // 2, width), bf16),
            pltpu.VMEM((rows // 4, width), bf16),
            pltpu.VMEM((rows // 4, width), bf16),
            pltpu.VMEM((rows, units), f32),
            pltpu.VMEM((rows, units), f32),
            pltpu.VMEM((rows + 8 * batches, units), f32),
            pltpu.VMEM((batches, 8, units), f32),
            pltpu.VMEM((batches, 8, units), f32),
            pltpu.VMEM((8, units), f32),
            pltpu.VMEM((count - 1, 8, units), f32),
            pltpu.VMEM((2, ring_slots, slab, inner), bf16),
            pltpu.VMEM((2, ring_slots, inner // 2, slab), bf16),
            pltpu.VMEM((2, slab, inner), bf16),
            pltpu.VMEM((2, slab, inner), bf16),
            pltpu.VMEM((2, units, slab), bf16),
            pltpu.VMEM((2, inner, slab), bf16),
            pltpu.VMEM((slab, inner), f32),
            *[pltpu.VMEM(part.shape, part.dtype) for part in late],
            *[pltpu.VMEM((rows, units), bf16)] * 4,
            *[
                pltpu.VMEM((high // part, 2 * block_width), bf16)
                for part in (1, 2, 4, 2, 4, 8)
            ],
            pltpu.VMEM((rows, width), bf16),
            pltpu.VMEM((rows, width), bf16),
            pltpu.VMEM((rows // 4, width), f32),
            pltpu.SemaphoreType.DMA((16,)),
            pltpu.SemaphoreType.DMA((4 * count,)),
            pltpu.SemaphoreType.DMA((2,)),
            pltpu.SemaphoreType.DMA((2, 2, count - 1)),
            pltpu.SemaphoreType.DMA((2, 2, count - 1)),
            pltpu.SemaphoreType.REGULAR((2, 2)),
            pltpu.SemaphoreType.DMA((back_copies,)),
            pltpu.SemaphoreType.DMA((back_copies,)),
        ],
        compiler_params=pltpu.CompilerParams(
            collective_id=2, has_side_effects=True, vmem_limit_bytes=63 * 1024 * 1024
        ),
    )(*operands)


def mlp_body(normed_ref, cot_ref, gate_ref, up_ref, down_ref, hidden_out, gate_out, up_out):
    gate = jnp.dot(normed_ref[...], gate_ref[...], preferred_element_type=f32)
    up = jnp.dot(normed_ref[...], up_ref[...], preferred_element_type=f32)
    back = dot_nt_here(cot_ref[...], down_ref[...])
    constant = 0.7978845608028654
    square = gate * gate
    bent = jnp.tanh(constant * (gate + 0.044715 * square * gate))
    half = 0.5 * (1.0 + bent)
    active = half * gate
    slope = half + 0.5 * gate * (1.0 - bent * bent) * (
        constant * (1.0 + 3.0 * 0.044715 * square)
    )
    hidden_out[...] = (active * up).astype(bf16)
    gate_out[...] = (back * up * slope).astype(bf16)
    up_out[...] = (back * active).astype(bf16)


def feed_forward(normed, cot, gate_all, up_all, down_all):
    rows, width = normed.shape
    hidden = gate_all.shape[1]
    wide = 256
    resident = pl.BlockSpec((rows, width), lambda j: (0, 0))
    columns = pl.BlockSpec((width, wide), lambda j: (0, j))
    result = pl.BlockSpec((rows, wide), lambda j: (0, j))
    return pl.pallas_call(
        mlp_body,
        grid=(hidden // wide,),
        out_shape=(jax.ShapeDtypeStruct((rows, hidden), bf16),) * 3,
        in_specs=[
            resident,
            resident,
            columns,
            columns,
            pl.BlockSpec((wide, width), lambda j: (j, 0)),
        ],
        out_specs=(result,) * 3,
        compiler_params=pltpu.CompilerParams(vmem_limit_bytes=62 * 1024 * 1024),
    )(normed, cot, gate_all, up_all, down_all)


def finish_body(large, *refs):
    blocks, small, gains = refs[large : large + 3]
    outs = refs[large + 3 :]
    for source, target in zip(refs[:large], outs):
        target[...] = source[...].astype(f32)
    gate_blocks, input_blocks, taps, *vectors = outs[large:]
    size = gate_blocks.shape[0]
    gate_blocks[...] = blocks[0:size, 0:size].astype(f32)
    input_blocks[...] = blocks[0:size, size : 2 * size].astype(f32)
    taps[...] = small[0:4, :]
    for row, vector in enumerate(vectors[:4]):
        vector[...] = small[row + 4 : row + 5, :].reshape(vector.shape[0])
    for row, vector in enumerate(vectors[4:]):
        vector[...] = gains[row : row + 1, :].reshape(vector.shape[0])


def finish(parts, blocks, small, gains, *arrays):
    block_width = blocks.shape[1] // 2
    half = parts * block_width

    def rows_of(count, wide):
        return pl.BlockSpec((count // parts, wide), lambda j: (j, 0))

    def whole(*shape):
        return pl.BlockSpec(shape, lambda j: (0,) * len(shape))

    specs = [rows_of(*part.shape) for part in arrays]
    blocks_out = rows_of(half, block_width)
    vectors = [small.shape[1]] * 4 + [gains.shape[1]] * 2
    shapes = [part.shape for part in arrays] + [(half, block_width)] * 2
    shapes += [(4, small.shape[1])] + [(size,) for size in vectors]
    return pl.pallas_call(
        functools.partial(finish_body, len(arrays)),
        grid=(parts,),
        out_shape=tuple(jax.ShapeDtypeStruct(shape, f32) for shape in shapes),
        in_specs=[
            *specs,
            rows_of(*blocks.shape),
            whole(*small.shape),
            whole(*gains.shape),
        ],
        out_specs=(
            *specs,
            blocks_out,
            blocks_out,
            whole(4, small.shape[1]),
            *[whole(size) for size in vectors],
        ),
        compiler_params=pltpu.CompilerParams(vmem_limit_bytes=62 * 1024 * 1024),
    )(*arrays, blocks, small, gains)


def block_diagonal(blocks):
    count, width = blocks.shape[0], blocks.shape[1]
    return sum(
        jnp.pad(blocks[j], ((j * width, (count - 1 - j) * width),) * 2) for j in range(count)
    )


def rows_joined(slab_pairs):
    return jnp.concatenate([part for pair in zip(*slab_pairs) for part in pair], 0)


def diagonal_blocks(square, count):
    width = square.shape[0] // count
    return jnp.stack(
        [square[j * width : (j + 1) * width, j * width : (j + 1) * width] for j in range(count)], 0
    )


def local(
    tokens,
    resets,
    norm_gain,
    branch_weight,
    inner_weight,
    conv_weight,
    conv_bias,
    gate_blocks,
    input_blocks,
    gate_bias,
    input_bias,
    decay_param,
    out_weight,
    mlp_norm_gain,
    gate_weight,
    up_weight,
    down_weight,
    cotangent,
):
    count = lax.axis_size("seq")
    batches, length, width = tokens.shape
    slab = width // count
    units, hidden = conv_bias.shape[0], down_weight.shape[0]
    rows = batches * length
    ringed = count == ring_count and lax.axis_size("fsdp") == 4
    half = slab // 2
    out_turned, down_turned = out_weight.T, down_weight.T
    ring = Ring(count)
    if ringed:
        gather, scatter = functools.partial(Gather, ring), functools.partial(Scatter, ring)
        to_ring, to_plain = ring.tables()

        def moved(values, dtype):
            return move_slabs(values, to_ring, dtype)

        def restored(values, dtype):
            return move_slabs(values, to_plain, dtype)

        def gain_moved(gain):
            return gain.reshape(count, slab)[to_ring].reshape(width)

        def gain_restored(gain):
            return gain.reshape(count, slab)[to_plain].reshape(width)

    else:
        gather, scatter = functools.partial(PlainGather, ring), functools.partial(PlainScatter, ring)

        def moved(values, dtype):
            return values.astype(dtype)

        restored = moved

        def gain_moved(gain):
            return gain

        gain_restored = gain_moved

    def slab_dots(turned, right, first=0, rows=slab):
        def term(k):
            start = k * slab + first
            return dot_nn(turned[start : start + rows], right)

        return term

    steps = count - 1
    taps = conv_weight.astype(f32)
    decay = decay_param.astype(f32)
    fresh_start = resets[:, :, None] > 0
    gain_one = gain_moved(norm_gain.astype(f32))
    gain_two = gain_moved(mlp_norm_gain.astype(f32))

    def gates(gate_pre, input_pre, conv_value, decay):
        return gate_math(gate_pre, input_pre, conv_value, decay, fresh_start)

    def by_sequence(values):
        return values.reshape(batches, -1, values.shape[-1])

    if ringed:
        (
            gate_all,
            up_all,
            down_all,
            branch_all,
            inner_all,
            out_all,
            cot_low,
            normed,
            branch_pre,
            padded,
            conv_flat,
            gate_pre,
            input_pre,
            carries,
            states,
            mixed_low,
            gate_square,
            input_square,
            own_values,
            own_middle,
            normed_two,
            ends,
            ring_gains,
            packed,
            fresh,
        ) = head(
            count,
            lax.axis_size("fsdp"),
            batches,
            tokens.reshape(rows, width),
            cotangent.reshape(rows, width),
            branch_weight.T,
            inner_weight.T,
            out_weight,
            gate_weight,
            up_weight,
            down_weight,
            conv_weight,
            conv_bias,
            gate_bias,
            input_bias,
            -decay_scale * jax.nn.softplus(-decay),
            decay_scale * jax.nn.sigmoid(-decay),
            norm_gain,
            mlp_norm_gain,
            resets,
            gate_blocks,
            input_blocks,
        )
        hidden_low, gate_mlp_low, up_mlp_low = feed_forward(
            normed_two, cot_low, gate_all, up_all, down_all
        )
        (
            small,
            block_grads,
            gain_two_grad,
            down_grad,
            branch_low,
            inner_grad_low,
            gate_low,
            input_low,
            gate_grad,
            up_grad,
            mixed,
            middle_low,
            own_grad,
        ) = back(
            count,
            lax.axis_size("fsdp"),
            batches,
            gate_blocks.shape[-1],
            cot_low,
            hidden_low,
            normed_two,
            gate_mlp_low,
            up_mlp_low,
            ends,
            own_middle,
            fresh,
            packed,
            ring_gains,
            gate_all,
            up_all,
            down_all,
            out_all,
            branch_pre,
            padded,
            conv_flat,
            gate_pre,
            input_pre,
            carries,
            states,
            gate_square,
            input_square,
        )
        block_count, block_width = gate_blocks.shape[:2]
        branch_grad, inner_grad, out_grad, tokens_grad, gains, small, block_grads = tail(
            count,
            middle_low,
            mixed_low,
            normed,
            branch_low,
            inner_grad_low,
            branch_all,
            inner_all,
            own_values,
            own_grad,
            ring_gains,
            gain_two_grad,
            small,
            block_grads,
        )
        (
            mixed,
            tokens_grad,
            gate_grad,
            up_grad,
            down_grad,
            branch_grad,
            inner_grad,
            out_grad,
            gate_blocks_grad,
            input_blocks_grad,
            taps_grad,
            conv_bias_grad,
            gate_bias_grad,
            input_bias_grad,
            decay_grad,
            gain_one_grad,
            gain_two_grad,
        ) = finish(
            block_count,
            block_grads,
            small,
            gains,
            mixed,
            tokens_grad,
            gate_grad,
            up_grad,
            down_grad,
            branch_grad,
            inner_grad,
            out_grad,
        )
        return (
            mixed.reshape(tokens.shape),
            tokens_grad.reshape(tokens.shape),
            gain_one_grad,
            branch_grad.T,
            inner_grad.T,
            taps_grad,
            conv_bias_grad,
            gate_blocks_grad.reshape(block_count, block_width, block_width),
            input_blocks_grad.reshape(block_count, block_width, block_width),
            gate_bias_grad,
            input_bias_grad,
            decay_grad,
            out_grad,
            gain_two_grad,
            gate_grad,
            up_grad,
            down_grad,
        )
    else:
        branch_all, inner_all, out_all, gate_all, up_all, down_all = [
            lax.all_gather(piece, "seq", axis=0, tiled=True)
            for piece in (
                branch_weight,
                inner_weight,
                out_turned,
                gate_weight,
                up_weight,
                down_turned,
            )
        ]
        gate_square, input_square = block_diagonal(gate_blocks), block_diagonal(input_blocks)
        tokens_low, cot_low = tokens.reshape(rows, width), cotangent.reshape(rows, width)
        values = tokens_low.astype(f32)
        normed = (values * inverse_rms(values) * gain_one).astype(bf16)
        inner_low = by_sequence(dot_nn(normed, inner_all).astype(bf16))
        branch_pre = by_sequence(dot_nn(normed, branch_all))
        edge_rows = passed_along(inner_low[:, -3:], 1)
        padded = jnp.concatenate([edge_rows, inner_low], 1).astype(f32)
        conv_sum = conv_bias.astype(f32) + taps[0] * padded[:, 3:] + taps[1] * padded[:, 2:-1]
        conv_sum = conv_sum + taps[2] * padded[:, 1:-2] + taps[3] * padded[:, :-3]
        conv_flat = conv_sum.astype(bf16).reshape(rows, units)
        gate_pre = by_sequence(dot_nn(conv_flat, gate_square) + gate_bias.astype(f32))
        input_pre = by_sequence(dot_nn(conv_flat, input_square) + input_bias.astype(f32))
        conv_value = by_sequence(conv_flat).astype(f32)
        carries, drives = gates(gate_pre, input_pre, conv_value, decay)
        prods, local_state = local_scan(carries, drives, False)
        prods_end = prods[:, -1:]
        state_in = Entry(prods_end, local_state[:, -1:], 1).state(None)
        states = local_state + prods * state_in
        mixed_low = (states * gelu_tanh(branch_pre)).astype(bf16).reshape(rows, units)
        own_values = own_rows(tokens_low).astype(f32)
        own_middle = own_values + Halves(ring, dot_nt(mixed_low, out_all), "fsdp").run()
        normed_two = own_middle * inverse_rms(own_middle) * gain_two
        normed_two = Joined(ring, normed_two.astype(bf16), "fsdp").run()
    branch, branch_pull = jax.vjp(gelu_tanh, branch_pre)
    scale_two = inverse_rms(own_middle)
    unit_two = own_middle * scale_two

    gate_mlp = dot_nn(normed_two, gate_all)
    up_mlp = dot_nn(normed_two, up_all)
    activated, act_pull = jax.vjp(gated_product, gate_mlp, up_mlp)
    hidden_low = activated.astype(bf16)
    down_grads = scatter(
        slab_dots(cot_low.T, hidden_low, 0, half), slab_dots(cot_low.T, hidden_low, half, half)
    )
    in_turn(down_grads)
    grad_gate_mlp, grad_up_mlp = act_pull(dot_nn(ring.then(cot_low, 0), down_all))
    gate_mlp_low, up_mlp_low = grad_gate_mlp.astype(bf16), grad_up_mlp.astype(bf16)
    in_turn(down_grads)
    ring.first(gate_mlp_low, up_mlp_low)
    in_turn(down_grads)
    mlp_grads = scatter(
        slab_dots(normed_two.T, gate_mlp_low), slab_dots(normed_two.T, up_mlp_low)
    )
    in_turn(mlp_grads, down_grads)
    gate_mlp_low, up_mlp_low = lax.optimization_barrier(
        (ring.then(gate_mlp_low, 2), up_mlp_low)
    )
    back_sum = Halves(
        ring, dot_nt(gate_mlp_low, gate_all) + dot_nt(up_mlp_low, up_all), "fsdp"
    )
    back_sum.step()
    ring.first(back_sum.step())
    in_turn(mlp_grads, down_grads)
    own_back = back_sum.run(2)
    gain_two_grad = jnp.sum(own_back * unit_two, 0)
    weighted = own_back * gain_two
    own_grad = own_rows(cot_low).astype(f32) + scale_two * (
        weighted - unit_two * jnp.mean(weighted * unit_two, axis=-1, keepdims=True)
    )
    middle_join = Joined(ring, own_grad.astype(bf16), "fsdp")
    ring.first(middle_join.step())
    in_turn(mlp_grads)
    mixed_sum = Halves(ring, dot_nt(ring.then(hidden_low, 2), down_all), "fsdp")
    mixed_sum.step()
    ring.first(mixed_sum.step())
    in_turn(down_grads)
    middle_join.step(2)
    middle_low = middle_join.run()

    grad_mixed = dot_nn(middle_low, out_all).reshape(batches, length, units)
    (grad_branch_pre,) = branch_pull(grad_mixed * states)
    branch_low = grad_branch_pre.astype(bf16).reshape(rows, units)
    following = jnp.concatenate([carries[:, 1:], jnp.ones_like(carries[:, :1])], 1)
    tail_prods, local_adjoint = local_scan(following, grad_mixed * branch, True)
    entry = Entry(prods_end, carries[:, :1] * local_adjoint[:, :1], -1)
    ring.first(local_adjoint, branch_low)
    in_turn(mlp_grads)
    entry.between(ring.then)
    in_turn(down_grads)
    adjoint_in = entry.state(lambda part: ring.then(part, 1))
    adjoint = local_adjoint + tail_prods * adjoint_in
    state_before = jnp.concatenate([state_in, states[:, :-1]], 1)
    _, gate_pull = jax.vjp(gates, gate_pre, input_pre, conv_value, decay)
    grad_gate_pre, grad_input_pre, grad_conv, decay_grad = gate_pull(
        (adjoint * state_before, adjoint)
    )
    gate_low = grad_gate_pre.astype(bf16).reshape(rows, units)
    input_low = grad_input_pre.astype(bf16).reshape(rows, units)
    ring.first(gate_low, input_low)
    in_turn(mlp_grads)
    back_conv = dot_nt(gate_low, gate_square) + dot_nt(input_low, input_square)
    grad_conv = grad_conv + back_conv.reshape(batches, length, units)

    border = jnp.zeros((batches, 3, units), f32)
    spread = jnp.concatenate([border, grad_conv, border], 1)
    stop = length + 3
    grad_padded = taps[0] * spread[:, :stop] + taps[1] * spread[:, 1 : stop + 1]
    grad_padded = grad_padded + taps[2] * spread[:, 2 : stop + 2] + taps[3] * spread[:, 3:]
    returned = passed_along(grad_padded[:, :3], -1)
    mixed_join = Joined(ring, restored(own_middle + mixed_sum.run(1), bf16), "fsdp")
    ring.first(grad_padded, mixed_join.step())
    in_turn(mlp_grads)
    grad_inner = jnp.concatenate(
        [grad_padded[:, 3:-3], grad_padded[:, -3:] + ring.then(returned)], 1
    )
    inner_grad_low = grad_inner.astype(bf16).reshape(rows, units)
    in_turn(*[mlp_grads] * (steps - 6))

    block_count = gate_blocks.shape[0]
    block_grads = jnp.concatenate(
        [
            diagonal_blocks(dot_tn(conv_flat, gate_low), block_count),
            diagonal_blocks(dot_tn(conv_flat, input_low), block_count),
        ],
        0,
    )
    block_width = block_grads.shape[-1]
    taps_grad = jnp.stack(
        [jnp.sum(grad_conv * padded[:, 3 - k : 3 - k + length], (0, 1)) for k in range(4)], 0
    )
    small = jnp.concatenate(
        [
            taps_grad,
            jnp.sum(grad_conv, (0, 1))[None],
            jnp.sum(gate_low.astype(f32), 0)[None],
            jnp.sum(input_low.astype(f32), 0)[None],
            decay_grad[None],
        ],
        0,
    )
    mixed_join.step()
    mixed = mixed_join.run().astype(f32).reshape(tokens.shape)
    gate_grad, up_grad = mlp_grads.sums()
    if ringed:
        branch_grad, inner_grad, out_grad, tokens_grad, gains, small, block_grads = tail(
            count,
            middle_low.T,
            mixed_low,
            normed.T,
            branch_low,
            inner_grad_low,
            branch_all,
            inner_all,
            own_values,
            own_grad,
            gain_one[None],
            gain_two_grad[None],
            small,
            block_grads.reshape(-1, block_width).astype(bf16),
        )
        block_grads = block_grads.astype(f32)
    else:
        out_grads = scatter(
            slab_dots(middle_low.T, mixed_low, 0, half),
            slab_dots(middle_low.T, mixed_low, half, half),
        )
        front_grads = scatter(
            slab_dots(normed.T, branch_low), slab_dots(normed.T, inner_grad_low)
        )
        branch_grad, inner_grad = front_grads.sums()
        out_grad = jnp.concatenate(out_grads.sums(), 0)
        own_front = Halves(
            ring, dot_nt(branch_low, branch_all) + dot_nt(inner_grad_low, inner_all), "fsdp"
        ).run()
        scale_one = inverse_rms(own_values)
        unit_one = own_values * scale_one
        weighted = own_front * gain_one
        own_tokens = own_grad + scale_one * (
            weighted - unit_one * jnp.mean(weighted * unit_one, axis=-1, keepdims=True)
        )
        gains = jnp.stack([jnp.sum(own_front * unit_one, 0), gain_two_grad], 0)
        gains = lax.psum(gains, ("seq", "fsdp"))
        small, block_grads = lax.psum((small, block_grads), "seq")
        tokens_grad = Joined(ring, own_tokens.astype(bf16), "fsdp").run()
    tokens_grad = tokens_grad.astype(f32).reshape(tokens.shape)
    block_grads = block_grads.reshape(2, block_count, block_width, block_width)
    down_grad = jnp.concatenate(down_grads.sums(), 0)
    return (
        mixed,
        tokens_grad,
        gains[0],
        branch_grad,
        inner_grad,
        small[:4],
        small[4],
        block_grads[0],
        block_grads[1],
        small[5],
        small[6],
        small[7],
        out_grad.T,
        gains[1],
        gate_grad,
        up_grad,
        down_grad.T,
    )


def solution(mesh):
    units, both = P("fsdp"), P("seq", "fsdp")
    blocks, turned = P("fsdp", None, None), P("fsdp", "seq")
    rows = P(None, "seq", None)
    return jax.shard_map(
        local,
        mesh=mesh,
        in_specs=(
            rows,
            P(None, "seq"),
            P(),
            both,
            both,
            P(None, "fsdp"),
            units,
            blocks,
            blocks,
            units,
            units,
            units,
            turned,
            P(),
            both,
            both,
            turned,
            rows,
        ),
        out_specs=(
            rows,
            rows,
            P(),
            both,
            both,
            P(None, "fsdp"),
            units,
            blocks,
            blocks,
            units,
            units,
            units,
            turned,
            P(),
            both,
            both,
            turned,
        ),
        check_vma=False,
    )
```
